32 devices in a mesh: dp: 4 (over y, x), row: 2 (over core), col: 4 (over z).
Axes of the slice: x: 2, y: 2, z: 4, core: 2. Of those that a mesh axis runs over, the one named last changes fastest.
Arguments:
- tokens: bfloat16 [1280, 16384], P('row', ('dp', 'col')), may hold values from -6 to 6
- segment_ids: int32 [8, 2048], P(('dp', 'row')), may hold values from 0 to 3, never falling along the last dimension, each value on 1 to 1024 neighbouring positions
- padding_mask: int32 [8, 2048], P(('dp', 'row')), may hold values from 0 to 1, as said below
- w_qkv: bfloat16 [4915200], P(('row', 'col')), may hold values from -0.15625 to 0.15625
- w_out: bfloat16 [1638400], P(('row', 'col')), may hold values from -1.25 to 1.25
- w_up: bfloat16 [1638400], P(('row', 'col')), may hold values from -0.15625 to 0.15625
- w_down: bfloat16 [1638400], P(('row', 'col')), may hold values from -0.15625 to 0.15625
- gain_attn: float32 [1280], replicated, may hold values from 0.5 to 1.5
- gain_mlp: float32 [1280], replicated, may hold values from 0.5 to 1.5
- scale_raw: float32 [80], replicated, may hold values from -0.5 to 1.5
- cotangent: bfloat16 [1280, 16384], P('row', ('dp', 'col')), may hold values from -6 to 6
Outputs:
- result: float32 [1280, 16384], P('row', ('dp', 'col'))
- grad_tokens: float32 [1280, 16384], P('row', ('dp', 'col'))
- grad_qkv: float32 [4915200], P(('row', 'col'))
- grad_wout: float32 [1638400], P(('row', 'col'))
- grad_up: float32 [1638400], P(('row', 'col'))
- grad_down: float32 [1638400], P(('row', 'col'))
- grad_gain_attn: float32 [1280], replicated
- grad_gain_mlp: float32 [1280], replicated
- grad_scale: float32 [80], replicated
The draws below stay inside these ranges and needn't reach their ends.
Inputs may be any that keep to these rules, and one draw needn't show every extreme that they name: `segment_ids`: within each row the document numbers never fall; a document holds at most 1024 tokens. `padding_mask`: each row is a nonempty run of ones followed by a nonempty run of zeros.
All inputs are finite; a program needn't handle non-finite values.
Results may differ from the reference program's by a relative error of at most 0.012.
The reference program's roundings to bfloat16 on the way count: a program that leaves them out, or rounds other values in their place, can miss the bound.
Values may be sent and summed in bfloat16 or wider, within the bound.
A program may use at most 256 MiB of HBM per device.

```python
import math
import jax
import jax.numpy as jnp
import numpy as np
from jax import lax

D = 1280
FF = 1280
HEADS = 16
HEAD = 80
SEQ_LEN = 2048
SEQS = 8
TOKENS = 16384
N_ROW = 2
N_COL = 4


def draw_padding_mask(key, part):
    key = jax.random.fold_in(key, 7)
    valid = jax.random.randint(key, (SEQS, 1), SEQ_LEN // 2, SEQ_LEN - SEQ_LEN // 16 + 1)
    places = lax.broadcasted_iota(jnp.int32, (SEQS, SEQ_LEN), 1)
    return (places < valid).astype(jnp.int32)


def block_scale(key, dims, cuts, least, top_value):
    factor_of = 1.0
    for axis_at, shards_of in cuts:
        steps = jax.random.uniform(jax.random.fold_in(jax.random.fold_in(key, 6), axis_at), (shards_of,), jnp.float32, least / len(cuts), top_value / len(cuts))
        factor_of = factor_of * jnp.repeat(jnp.exp(steps), dims[axis_at] // shards_of).reshape((-1,) + (1,) * (len(dims) - 1 - axis_at))
    return factor_of


def profile(number_of, total, limit, slope):
    loads = [(1 << 20) // math.isqrt(grade ** slope) + 1 for grade in range(2, number_of + 1)]
    surplus, given = total - limit - (number_of - 1), [1] * (number_of - 1)
    while surplus > 0:
        candidates = [i for i in range(number_of - 1) if given[i] < limit]
        whole, left = sum([loads[i] for i in candidates]), surplus
        for i in candidates:
            more = min(limit - given[i], max(1, left * loads[i] // whole), surplus)
            given[i] = given[i] + more
            surplus = surplus - more
    return np.array([limit] + given)


def ragged_sizes(stream_key, number_of, total, bound, lean):
    if number_of == 2:
        one = jax.random.randint(stream_key, (), max(1, total - bound), min(bound, total - 1) + 1)
        return jnp.stack([one, total - one])
    sizes = jnp.asarray(profile(number_of, total, bound, lean), jnp.int32)
    twos = (number_of - 1) // 2
    donor, receiver = sizes[1:1 + 2 * twos:2], sizes[2:2 + 2 * twos:2]
    slack = jnp.minimum(donor - 1, bound - receiver)
    shifted = jax.random.randint(jax.random.fold_in(stream_key, 1), (twos,), 0, 1 << 20) % (slack + 1)
    sizes = sizes.at[1:1 + 2 * twos:2].set(donor - shifted).at[2:2 + 2 * twos:2].set(receiver + shifted)
    return sizes[jax.random.permutation(jax.random.fold_in(stream_key, 2), number_of)]


def centred(key, extent, scale, bound, split=(), kind=jnp.bfloat16):
    values = jax.random.normal(key, extent, jnp.float32) * scale
    if len(split) > 0:
        values = block_scale(key, extent, split, -0.22, 0.18) * values
    return jnp.clip(values, min=-bound, max=bound).astype(kind)


def setup_inputs(seed: int = 0) -> dict:
    key_list = jax.random.split(jax.random.key(seed), 12)
    return {
        "tokens": centred(key_list[0], (D, TOKENS), 1.0, 6.0, ((0, 2), (1, 16))),
        "segment_ids": jax.vmap(lambda own: jnp.searchsorted(jnp.cumsum(ragged_sizes(own, 4, SEQ_LEN, SEQ_LEN // 2, 0)), jnp.arange(SEQ_LEN), side="right"))(jax.random.split(key_list[1], SEQS)).reshape((SEQS, SEQ_LEN)).astype(jnp.int32),
        "padding_mask": draw_padding_mask(jax.random.fold_in(key_list[11], 71), 0),
        "w_qkv": centred(key_list[3], (N_ROW * N_COL * (D // N_ROW) * 3 * (HEADS * HEAD // N_COL),), D ** -0.5, 0.15625, ((0, 8),)),
        "w_out": centred(key_list[4], (N_ROW * N_COL * (HEADS * HEAD // N_COL) * (D // N_ROW),), (HEADS * HEAD // 64) ** -0.5, 1.25, ((0, 8),)),
        "w_up": centred(key_list[5], (N_ROW * N_COL * (D // N_ROW) * (FF // N_COL),), D ** -0.5, 0.15625, ((0, 8),)),
        "w_down": centred(key_list[6], (N_ROW * N_COL * (FF // N_COL) * (D // N_ROW),), FF ** -0.5, 0.15625, ((0, 8),)),
        "gain_attn": jnp.clip(1.0 + 0.1 * jax.random.normal(key_list[7], (D,), jnp.float32), 0.5, 1.5),
        "gain_mlp": jnp.clip(1.0 + 0.1 * jax.random.normal(key_list[8], (D,), jnp.float32), 0.5, 1.5),
        "scale_raw": jnp.clip(jax.random.uniform(key_list[9], (HEAD,), jnp.float32, -0.5, 1.5), -0.5, 1.5),
        "cotangent": centred(key_list[10], (D, TOKENS), 1.0, 6.0, ((0, 2), (1, 16))),
    }


EPSILON = 1e-06
LOG_TWO_E = 1.442695041
precise = lax.Precision.HIGHEST

@jax.custom_vjp
def low(v):
    return lax.optimization_barrier(v.astype(jnp.bfloat16)).astype(jnp.float32)

@jax.custom_vjp
def low_back(v):
    return v

def low_keep(v):
    return (low(v), None)

def low_pass(kept, grad):
    return (grad,)

def back_keep(v):
    return (v, None)

def back_low(kept, grad):
    return (low(grad),)
low.defvjp(low_keep, low_pass)
low_back.defvjp(back_keep, back_low)

def qkv_matrix(flat):
    width = HEADS * HEAD
    return flat.reshape(N_ROW, N_COL, D // N_ROW, 3, width // N_COL).transpose(0, 2, 3, 1, 4).reshape(D, 3, width)

def qkv_blocks(matrix):
    width = HEADS * HEAD
    return matrix.reshape(N_ROW, D // N_ROW, 3, N_COL, width // N_COL).transpose(0, 3, 1, 2, 4).reshape(-1)

def in_matrix(flat, width):
    return flat.reshape(N_ROW, N_COL, D // N_ROW, width // N_COL).transpose(0, 2, 1, 3).reshape(D, width)

def in_blocks(matrix, width):
    return matrix.reshape(N_ROW, D // N_ROW, N_COL, width // N_COL).transpose(0, 2, 1, 3).reshape(-1)

def out_matrix(flat, width):
    return flat.reshape(N_ROW, N_COL, width // N_COL, D // N_ROW).transpose(1, 2, 0, 3).reshape(width, D)

def out_blocks(matrix, width):
    return matrix.reshape(N_COL, width // N_COL, N_ROW, D // N_ROW).transpose(2, 0, 1, 3).reshape(-1)

def product_high(left, right):
    return jnp.dot(left, right, precision=precise)

def rms_norm(inputs, gain):
    return inputs * lax.rsqrt(lax.optimization_barrier(jnp.mean(inputs * inputs, axis=-1, keepdims=True)) + EPSILON) * gain

def softplus(values):
    return jnp.log1p(jnp.exp(values))

def attend(queries, key_heads, values, segments, padding):
    block_size = min(512, SEQ_LEN)
    positions = jnp.arange(SEQ_LEN, dtype=jnp.int32)

    def one_block(block_index):
        offset = block_index * block_size
        row_places = offset + jnp.arange(block_size, dtype=jnp.int32)
        query_rows = lax.dynamic_slice_in_dim(queries, offset, block_size, 0)
        seg_rows = lax.dynamic_slice_in_dim(segments, offset, block_size, 0)
        matching = seg_rows[:, None] == segments[None, :]
        causal = positions[None, :] <= row_places[:, None]
        visible = (padding[None, :] == 1) | (positions[None, :] == row_places[:, None])
        allowed = matching & causal & visible
        scores = low_back(jnp.einsum('qhe,khe->hqk', query_rows, key_heads, precision=precise))
        scores = jnp.where(allowed[None], scores, -1e+30)
        row_peak = lax.optimization_barrier(jnp.max(scores, axis=2, keepdims=True))
        exponent = jnp.exp(scores - row_peak)
        probabilities = exponent / lax.optimization_barrier(jnp.sum(exponent, axis=2, keepdims=True))
        return jnp.einsum('hqk,khe->qhe', low(probabilities), values, precision=precise)
    blocks_out = lax.map(jax.checkpoint(one_block), jnp.arange(SEQ_LEN // block_size, dtype=jnp.int32))
    return blocks_out.reshape(SEQ_LEN, HEADS * HEAD)

def layer(inputs, w_qkv, w_out, w_up, w_down, gain_attn, gain_mlp, scale_raw, segments, padding):
    normed_one = low(rms_norm(inputs, gain_attn))
    projected = low_back(product_high(normed_one, w_qkv.reshape(D, 3 * HEADS * HEAD)))
    projected = projected.reshape(SEQ_LEN, 3, HEADS, HEAD)
    factor = LOG_TWO_E / math.sqrt(HEAD) * softplus(scale_raw)
    queries = low(projected[:, 0] * factor)
    key_heads = low(projected[:, 1])
    values = low(projected[:, 2])
    attended = low(low_back(attend(queries, key_heads, values, segments, padding)))
    middle = inputs + low_back(product_high(attended, w_out))
    normed_two = low(rms_norm(middle, gain_mlp))
    hidden = low_back(product_high(normed_two, w_up))
    active = low(jax.nn.silu(hidden))
    return middle + low_back(product_high(active, w_down))

def reference(tokens, segment_ids, padding_mask, w_qkv, w_out, w_up, w_down, gain_attn, gain_mlp, scale_raw, cotangent):
    params = (qkv_matrix(w_qkv.astype(jnp.float32)), out_matrix(w_out.astype(jnp.float32), HEADS * HEAD), in_matrix(w_up.astype(jnp.float32), FF), out_matrix(w_down.astype(jnp.float32), FF), gain_attn.astype(jnp.float32), gain_mlp.astype(jnp.float32), scale_raw.astype(jnp.float32))
    inputs_all = tokens.astype(jnp.float32).T.reshape(SEQS, SEQ_LEN, D)
    grads_all = cotangent.astype(jnp.float32).T.reshape(SEQS, SEQ_LEN, D)

    def one_sequence(running, item):
        inputs, grad_out, segments, padding = item

        def forward(layer_in, p_qkv, p_out, p_up, p_down, p_gone, p_gtwo, p_scale):
            return layer(layer_in, p_qkv, p_out, p_up, p_down, p_gone, p_gtwo, p_scale, segments, padding)
        output, pullback = jax.vjp(forward, inputs, *params)
        grads = pullback(grad_out)
        updated = tuple((total + update for total, update in zip(running, grads[1:])))
        return (updated, (output, grads[0]))
    zeros = tuple((jnp.zeros_like(param) for param in params))
    sums, (outputs, grad_inputs) = lax.scan(one_sequence, zeros, (inputs_all, grads_all, segment_ids, padding_mask))
    return (outputs.reshape(TOKENS, D).T, grad_inputs.reshape(TOKENS, D).T, qkv_blocks(sums[0]), out_blocks(sums[1], HEADS * HEAD), in_blocks(sums[2], FF), out_blocks(sums[3], FF), sums[4], sums[5], sums[6])
```

```python
import functools
import math

import jax
import jax.numpy as jnp
import numpy as np
from jax import lax
from jax.experimental import pallas as pl
from jax.experimental.pallas import tpu as pltpu
from jax.sharding import Mesh, PartitionSpec as P

D = 1280
HEAD = 80
EPSILON = 1e-06
LOG_TWO_E = 1.442695041
BLOCK = 256
LOW = jnp.bfloat16
FULL = jnp.float32
COLS = ("cs", "cp")


def mm(left, right, left_axis, right_axis):
    return lax.dot_general(
        left, right, (((left_axis,), (right_axis,)), ((), ())), preferred_element_type=FULL
    )


def shift(x, axis, k):
    n = lax.axis_size(axis)
    return lax.ppermute(x, axis, [(i, i ^ k) for i in range(n)])


def sibling(x):
    return shift(x, "row", 1)


def place(pieces, me, axis):
    n = len(pieces)
    if n == 1:
        return pieces[0]
    if n == 2:
        first = me == 0
        return jnp.concatenate(
            [jnp.where(first, pieces[0], pieces[1]), jnp.where(first, pieces[1], pieces[0])], axis
        )
    shape = list(pieces[0].shape)
    step = shape[axis]
    shape[axis] = step * n
    out = jnp.zeros(shape, pieces[0].dtype)
    for k, piece in enumerate(pieces):
        out = lax.dynamic_update_slice_in_dim(out, piece, (me ^ k) * step, axis)
    return out


def cut(x, index, count, axis):
    step = x.shape[axis] // count
    return lax.dynamic_slice_in_dim(x, index * step, step, axis)


def gather(x, axis):
    return [x] + [shift(x, axis, k) for k in range(1, lax.axis_size(axis))]


def swap(x, name, axis):
    me, n = lax.axis_index(name), lax.axis_size(name)
    parts = [cut(x, me ^ k, n, axis) for k in range(n)]
    return [parts[0]] + [shift(parts[k], name, k) for k in range(1, n)]


def reduce_pieces(pieces):
    total = pieces[0].astype(FULL)
    for piece in pieces[1:]:
        total = total + piece.astype(FULL)
    return total


def diag_mask(segq, segk):
    size = segk.shape[0], segq.shape[1]
    ki = lax.broadcasted_iota(jnp.int32, size, 0)
    qi = lax.broadcasted_iota(jnp.int32, size, 1)
    return ((segk == segq) & (ki <= qi)) | (ki == qi)


def forward_kernel(heads, lo_ref, hi_ref, q_ref, k_ref, v_ref, segq_ref, segk_ref, o_ref, log_ref, ks):
    i = pl.program_id(0)

    @pl.when(i == 0)
    def _():
        for h in range(heads):
            ks[h] = k_ref[h * HEAD:(h + 1) * HEAD, :].T

    segq = segq_ref[...]

    def visit(kb, carry, diagonal):
        at = pl.ds(pl.multiple_of(kb * BLOCK, BLOCK), BLOCK)
        segk = segk_ref[at, :]
        mask = diag_mask(segq, segk) if diagonal else segk == segq
        out = []
        for h in range(heads):
            rows = slice(h * HEAD, (h + 1) * HEAD)
            s = jnp.dot(ks[h, at, :], q_ref[rows, :], preferred_element_type=FULL)
            s = jnp.where(mask, s, -1e30)
            peak = jnp.max(s, axis=0, keepdims=True)
            if not diagonal:
                m, l, acc = carry[h]
                peak = jnp.maximum(m, peak)
            p = jnp.exp(s - peak)
            total = jnp.sum(p, axis=0, keepdims=True)
            new = jnp.dot(v_ref[rows, at], p.astype(LOW), preferred_element_type=FULL)
            if not diagonal:
                keep = jnp.exp(m - peak)
                total = l * keep + total
                new = acc * keep + new
            out.append((peak, total, new))
        return tuple(out)

    carry = visit(i, None, True)
    carry = lax.fori_loop(lo_ref[i], hi_ref[i], lambda kb, c: visit(kb, c, False), carry)
    for h in range(heads):
        m, l, acc = carry[h]
        o_ref[h * HEAD:(h + 1) * HEAD, :] = (acc / l).astype(LOW)
        log_ref[h] = m + jnp.log(l)


def attention_forward(q, k, v, segq, segk, lo, hi):
    cols, length = q.shape
    heads = cols // HEAD
    steps = length // BLOCK
    whole = pl.BlockSpec((cols, length), lambda i, *_: (0, 0))
    part = pl.BlockSpec((cols, BLOCK), lambda i, *_: (0, i))
    return pl.pallas_call(
        functools.partial(forward_kernel, heads),
        out_shape=(
            jax.ShapeDtypeStruct((cols, length), LOW),
            jax.ShapeDtypeStruct((heads, 1, length), FULL),
        ),
        grid_spec=pltpu.PrefetchScalarGridSpec(
            num_scalar_prefetch=2,
            grid=(steps,),
            in_specs=[
                part,
                whole,
                whole,
                pl.BlockSpec((1, BLOCK), lambda i, *_: (0, i)),
                pl.BlockSpec((length, 1), lambda i, *_: (0, 0)),
            ],
            out_specs=(part, pl.BlockSpec((heads, 1, BLOCK), lambda i, *_: (0, 0, i))),
            scratch_shapes=[pltpu.VMEM((heads, length, HEAD), LOW)],
        ),
        compiler_params=pltpu.CompilerParams(vmem_limit_bytes=48 * 2**20),
        cost_estimate=pl.CostEstimate(
            flops=8 * 2 * length * length * cols,
            bytes_accessed=4 * cols * length * 2,
            transcendentals=heads * length * length // 3,
        ),
    )(lo, hi, q, k, v, segq, segk)


def backward_kernel(
    heads, lo_ref, hi_ref, q_ref, k_ref, v_ref, o_ref, go_ref, log_ref, raw_ref, factor_ref,
    segq_ref, segk_ref, dq_ref, dk_ref, dv_ref, scale_ref, ks, vs, dks, dvs, dqs,
):
    i = pl.program_id(0)

    @pl.when(i == 0)
    def _():
        for h in range(heads):
            ks[h] = k_ref[h * HEAD:(h + 1) * HEAD, :].T
            vs[h] = v_ref[h * HEAD:(h + 1) * HEAD, :].T
        dks[...] = jnp.zeros_like(dks)
        dvs[...] = jnp.zeros_like(dvs)
        scale_ref[...] = jnp.zeros_like(scale_ref)

    segq = segq_ref[...]
    inner = [
        jnp.sum(
            o_ref[h * HEAD:(h + 1) * HEAD, :].astype(FULL)
            * go_ref[h * HEAD:(h + 1) * HEAD, :].astype(FULL),
            axis=0,
            keepdims=True,
        )
        for h in range(heads)
    ]

    def visit(kb, diagonal):
        at = pl.ds(pl.multiple_of(kb * BLOCK, BLOCK), BLOCK)
        segk = segk_ref[at, :]
        mask = diag_mask(segq, segk) if diagonal else segk == segq
        for h in range(heads):
            rows = slice(h * HEAD, (h + 1) * HEAD)
            q = q_ref[rows, :]
            go = go_ref[rows, :]
            s = jnp.dot(ks[h, at, :], q, preferred_element_type=FULL)
            p = jnp.where(mask, jnp.exp(s - log_ref[h]), 0.0)
            dp = jnp.dot(vs[h, at, :], go, preferred_element_type=FULL)
            ds = (p * (dp - inner[h])).astype(LOW)
            new = jnp.dot(k_ref[rows, at], ds, preferred_element_type=FULL)
            if diagonal:
                dqs[rows, :] = new
            else:
                dqs[rows, :] += new
            dks[rows, at] += mm(q, ds, 1, 1)
            dvs[rows, at] += mm(go, p.astype(LOW), 1, 1)

    visit(i, True)

    @pl.loop(lo_ref[i], hi_ref[i])
    def _(kb):
        visit(kb, False)

    factor = factor_ref[...]
    part = jnp.zeros((HEAD, 1), FULL)
    for h in range(heads):
        rows = slice(h * HEAD, (h + 1) * HEAD)
        dq = dqs[rows, :]
        part = part + jnp.sum(dq * raw_ref[rows, :], axis=1, keepdims=True)
        dq_ref[rows, :] = (dq * factor).astype(LOW)
    scale_ref[...] += part

    @pl.when(i == pl.num_programs(0) - 1)
    def _():
        dk_ref[...] = dks[...].astype(LOW)
        dv_ref[...] = dvs[...].astype(LOW)


def attention_backward(q, k, v, o, go, logs, raw, factor, segq, segk, lo, hi):
    cols, length = q.shape
    heads = cols // HEAD
    steps = length // BLOCK
    whole = pl.BlockSpec((cols, length), lambda i, *_: (0, 0))
    part = pl.BlockSpec((cols, BLOCK), lambda i, *_: (0, i))
    column = pl.BlockSpec((HEAD, 1), lambda i, *_: (0, 0))
    shape = jax.ShapeDtypeStruct((cols, length), LOW)
    return pl.pallas_call(
        functools.partial(backward_kernel, heads),
        out_shape=(shape, shape, shape, jax.ShapeDtypeStruct((HEAD, 1), FULL)),
        grid_spec=pltpu.PrefetchScalarGridSpec(
            num_scalar_prefetch=2,
            grid=(steps,),
            in_specs=[
                part,
                whole,
                whole,
                part,
                part,
                pl.BlockSpec((heads, 1, BLOCK), lambda i, *_: (0, 0, i)),
                part,
                column,
                pl.BlockSpec((1, BLOCK), lambda i, *_: (0, i)),
                pl.BlockSpec((length, 1), lambda i, *_: (0, 0)),
            ],
            out_specs=(part, whole, whole, column),
            scratch_shapes=[
                pltpu.VMEM((heads, length, HEAD), LOW),
                pltpu.VMEM((heads, length, HEAD), LOW),
                pltpu.VMEM((cols, length), FULL),
                pltpu.VMEM((cols, length), FULL),
                pltpu.VMEM((cols, BLOCK), FULL),
            ],
        ),
        compiler_params=pltpu.CompilerParams(vmem_limit_bytes=48 * 2**20),
        cost_estimate=pl.CostEstimate(
            flops=8 * 5 * length * length * cols,
            bytes_accessed=8 * cols * length * 2,
            transcendentals=heads * length * length // 3,
        ),
    )(lo, hi, q, k, v, o, go, logs, raw, factor, segq, segk)


def on_device(
    tokens,
    segment_ids,
    padding_mask,
    w_qkv,
    w_out,
    w_up,
    w_down,
    gain_attn,
    gain_mlp,
    scale_raw,
    cotangent,
):
    width, here = tokens.shape
    r, s = lax.axis_index("row"), lax.axis_index("cs")
    j, d = lax.axis_index("cp"), lax.axis_index("dp")
    n_pair, n_dp, n_col = lax.axis_size("cp"), lax.axis_size("dp"), lax.axis_size(COLS)
    c = s * n_pair + j
    head_cols = w_qkv.shape[0] // (3 * width)
    heads = head_cols // HEAD
    near = r == s

    segments = jnp.where(s == r, segment_ids[0], sibling(segment_ids)[0])
    padding = jnp.where(s == r, padding_mask[0], sibling(padding_mask)[0])
    length = segments.shape[0]
    firsts = segments[::BLOCK]
    starts = jnp.sum((segments[None, :] < firsts[:, None]).astype(jnp.int32), axis=1)
    filled = (jnp.sum(padding) + BLOCK - 1) // BLOCK
    blocks = jnp.arange(length // BLOCK, dtype=jnp.int32)
    lo = starts // BLOCK
    hi = jnp.minimum(blocks, filled)
    segq = segments[None, :]
    segk = jnp.where(padding == 1, segments, -1)[:, None]

    token_pieces = gather(tokens, "cp")
    token_others = [sibling(piece) for piece in token_pieces]
    grad_out = cotangent
    grad_out_full = jnp.concatenate([grad_out, sibling(grad_out)], 0)

    def halves(vector):
        whole = vector.reshape(2, width)
        own = lax.dynamic_index_in_dim(whole, r, 0, keepdims=False)
        other = lax.dynamic_index_in_dim(whole, 1 - r, 0, keepdims=False)
        return own[:, None], other[:, None]

    gain_one, gain_one_other = halves(gain_attn)
    gain_two, _ = halves(gain_mlp)

    block = w_qkv.reshape(width, 3 * head_cols)
    remote = place(gather(shift(cut(block, d, n_dp, 0), "cs", 1), "dp"), d, 0)
    qkv = jnp.concatenate(
        [jnp.where(near, block, remote), sibling(jnp.where(near, remote, block))], 0
    )

    stacked = jnp.stack([w_out.reshape(-1, width), w_up.reshape(width, -1).T, w_down.reshape(-1, width)])
    unit = stacked.shape[1]
    quarter = cut(stacked, d, n_dp, 1)[:, None, None]
    along_z = [quarter] + [
        lax.ppermute(quarter, COLS, [(i, i ^ k) for i in range(n_col)]) for k in range(1, n_col)
    ]
    c_first = c ^ (r * n_pair)
    along_z = place(along_z, c_first, 1)
    gathered = place(gather(along_z, "dp"), d, 2)
    gathered = gathered.reshape(3, n_col * unit, width)
    half_units = n_col * unit // 2
    crossed = sibling(gathered[:, half_units:])
    out_own, up_own, down_own = gathered
    out_half, up_half, down_half = jnp.concatenate([gathered[:, :half_units], crossed], 2)

    def project(own, other):
        own, other = own.astype(FULL), other.astype(FULL)
        squares = jnp.sum(own * own, axis=0) + jnp.sum(other * other, axis=0)
        inverse = lax.rsqrt(squares / D + EPSILON)[None, :]
        normed = jnp.concatenate(
            [
                (own * inverse * gain_one).astype(LOW),
                (other * inverse * gain_one_other).astype(LOW),
            ],
            0,
        )
        return inverse, normed, mm(qkv, normed, 0, 0)

    pieces = [project(own, other) for own, other in zip(token_pieces, token_others)]
    inverse_one = pieces[0][0]
    normed_one = place([piece[1] for piece in pieces], j, 1)
    projected = place([piece[2] for piece in pieces], j, 1)
    factor = (LOG_TWO_E / math.sqrt(HEAD) * jnp.log1p(jnp.exp(scale_raw)))[:, None]
    query_raw = projected[:head_cols]
    queries = (query_raw * jnp.tile(factor, (heads, 1))).astype(LOW)
    key_heads = projected[head_cols:2 * head_cols].astype(LOW)
    values = projected[2 * head_cols:].astype(LOW)

    attended, logs = attention_forward(queries, key_heads, values, segq, segk, lo, hi)
    mine = place(swap(attended, "cp", 1), j, 0)
    att_full = jnp.concatenate([mine, sibling(mine)], 0)

    inputs = tokens.astype(FULL)
    middle = inputs + mm(out_own, att_full, 0, 0)
    squares = jnp.sum(middle * middle, axis=0, keepdims=True)
    inverse_two = lax.rsqrt((squares + sibling(squares)) / D + EPSILON)
    normed_two = (middle * inverse_two * gain_two).astype(LOW)
    normed_full = jnp.concatenate([normed_two, sibling(normed_two)], 0)
    hidden = mm(up_half, normed_full, 1, 0)
    sigmoid = jax.nn.sigmoid(hidden)
    active = (hidden * sigmoid).astype(LOW)
    active_full = jnp.concatenate([active, sibling(active)], 0)
    result = middle + mm(down_own, active_full, 0, 0)

    grad_active = mm(down_half, grad_out_full, 1, 0)
    grad_hidden = (grad_active * sigmoid * (1.0 + hidden * (1.0 - sigmoid))).astype(LOW)
    grad_hidden_full = jnp.concatenate([grad_hidden, sibling(grad_hidden)], 0)
    grad_normed_two = mm(up_own, grad_hidden_full, 0, 0)
    scaled = grad_normed_two * gain_two
    inner = jnp.sum(scaled * middle, axis=0, keepdims=True)
    inner = inner + sibling(inner)
    grad_middle = (
        grad_out.astype(FULL)
        + inverse_two * scaled
        - middle * (inverse_two * inverse_two * inverse_two * inner / D)
    )
    gain_two_part = jnp.sum(grad_normed_two * middle * inverse_two, axis=1)
    grad_branch = grad_middle.astype(LOW)
    grad_branch_full = jnp.concatenate([grad_branch, sibling(grad_branch)], 0)
    grad_mine = mm(out_half, grad_branch_full, 1, 0).astype(LOW)
    grad_attended = place(swap(grad_mine, "cp", 0), j, 1)

    grads = jnp.stack(
        [
            mm(att_full, grad_branch, 1, 1).astype(LOW),
            mm(grad_hidden_full, normed_two, 1, 1).astype(LOW),
            mm(active_full, grad_out, 1, 1).astype(LOW),
        ]
    ).reshape(3, n_col, n_dp, unit // n_dp, width)
    summed = reduce_pieces(swap(grads, "dp", 2)).astype(LOW)
    parts = [
        lax.dynamic_slice_in_dim(summed, c_first ^ k, 1, 1) for k in range(n_col)
    ]
    parts = [parts[0]] + [
        lax.ppermute(parts[k], COLS, [(i, i ^ k) for i in range(n_col)]) for k in range(1, n_col)
    ]
    final = reduce_pieces(parts).astype(LOW)
    final = place(gather(final, "dp"), d, 2).astype(FULL).reshape(3, unit, width)

    dq, dk, dv, scale_part = attention_backward(
        queries, key_heads, values, attended, grad_attended, logs, query_raw, factor,
        segq, segk, lo, hi,
    )
    grad_projected = jnp.concatenate([dq, dk, dv], 0)

    grad_qkv = mm(normed_one, grad_projected, 1, 1).astype(LOW)
    grad_qkv = grad_qkv.reshape(2, n_dp, width // n_dp, 3 * head_cols)
    grad_qkv = reduce_pieces(swap(grad_qkv, "dp", 1))[:, 0].astype(LOW)
    crossed_grad = sibling(grad_qkv[1])
    stay = jnp.where(near, grad_qkv[0], crossed_grad).astype(FULL)
    leave = jnp.where(near, crossed_grad, grad_qkv[0])
    grad_qkv = (stay + shift(leave, "cs", 1).astype(FULL)).astype(LOW)
    grad_qkv = place(gather(grad_qkv, "dp"), d, 0).astype(FULL)

    grad_normed = mm(qkv, grad_projected, 1, 0)
    grad_normed = grad_normed[:width] + sibling(grad_normed[width:].astype(LOW)).astype(FULL)
    own_part = cut(grad_normed, j, n_pair, 1)
    for k in range(1, n_pair):
        own_part = own_part + shift(
            cut(grad_normed, j ^ k, n_pair, 1).astype(LOW), "cp", k
        ).astype(FULL)
    scaled = own_part * gain_one
    inner = jnp.sum(scaled * inputs, axis=0, keepdims=True)
    inner = inner + sibling(inner)
    grad_tokens = (
        grad_middle
        + inverse_one * scaled
        - inputs * (inverse_one * inverse_one * inverse_one * inner / D)
    )
    gain_one_part = jnp.sum(own_part * inputs * inverse_one, axis=1)

    scale_part = (
        scale_part[:, 0] * (LOG_TWO_E / math.sqrt(HEAD)) * jax.nn.sigmoid(scale_raw)
    )
    sums = jnp.stack(
        [gain_one_part, gain_two_part, jnp.pad(scale_part, (0, width - HEAD))]
    )
    for name in ("dp", "cs", "cp"):
        k = 1
        while k < lax.axis_size(name):
            sums = sums + shift(sums, name, k)
            k *= 2
    other = sibling(sums)
    first = r == 0
    gains = jnp.concatenate(
        [jnp.where(first, sums[:2], other[:2]), jnp.where(first, other[:2], sums[:2])], 1
    )
    scale_total = (sums[2] + other[2])[:HEAD]
    return (
        result,
        grad_tokens,
        grad_qkv.reshape(-1),
        final[0].reshape(-1),
        final[1].T.reshape(-1),
        final[2].reshape(-1),
        gains[0],
        gains[1],
        scale_total,
    )


def solution(mesh):
    n_dp, n_row, n_col = (mesh.shape[name] for name in ("dp", "row", "col"))
    split = Mesh(
        np.asarray(mesh.devices).reshape(n_dp, n_row, n_row, n_col // n_row),
        ("dp", "row", "cs", "cp"),
    )
    rows = P("row", ("dp", "cs", "cp"))
    ids = P(("dp", "row"), None)
    blocks = P(("row", "cs", "cp"))
    return jax.shard_map(
        on_device,
        mesh=split,
        in_specs=(rows, ids, ids, blocks, blocks, blocks, blocks, P(), P(), P(), rows),
        out_specs=(rows, rows, blocks, blocks, blocks, blocks, P(), P(), P()),
        check_vma=False,
    )
```

```python
import functools
import math

import jax
import jax.numpy as jnp
import numpy as np
from jax import lax
from jax.experimental import pallas as pl
from jax.experimental.pallas import tpu as pltpu
from jax.sharding import Mesh, PartitionSpec as P

D = 1280
HEAD = 80
EPSILON = 1e-06
LOG_TWO_E = 1.442695041
BLOCK = 256
LOW = jnp.bfloat16
FULL = jnp.float32
COLS = ("cs", "cp")


def mm(left, right, left_axis, right_axis):
    return lax.dot_general(
        left, right, (((left_axis,), (right_axis,)), ((), ())), preferred_element_type=FULL
    )


def shift(x, axis, k):
    n = lax.axis_size(axis)
    return lax.ppermute(x, axis, [(i, i ^ k) for i in range(n)])


def sibling(x):
    return shift(x, "row", 1)


def place(pieces, me, axis):
    n = len(pieces)
    if n == 1:
        return pieces[0]
    if n == 2:
        first = me == 0
        return jnp.concatenate(
            [jnp.where(first, pieces[0], pieces[1]), jnp.where(first, pieces[1], pieces[0])], axis
        )
    shape = list(pieces[0].shape)
    step = shape[axis]
    shape[axis] = step * n
    out = jnp.zeros(shape, pieces[0].dtype)
    for k, piece in enumerate(pieces):
        out = lax.dynamic_update_slice_in_dim(out, piece, (me ^ k) * step, axis)
    return out


def cut(x, index, count, axis):
    step = x.shape[axis] // count
    return lax.dynamic_slice_in_dim(x, index * step, step, axis)


def gather(x, axis):
    return [x] + [shift(x, axis, k) for k in range(1, lax.axis_size(axis))]


def swap(x, name, axis):
    me, n = lax.axis_index(name), lax.axis_size(name)
    parts = [cut(x, me ^ k, n, axis) for k in range(n)]
    return [parts[0]] + [shift(parts[k], name, k) for k in range(1, n)]


def reduce_pieces(pieces):
    total = pieces[0].astype(FULL)
    for piece in pieces[1:]:
        total = total + piece.astype(FULL)
    return total


def diag_mask(segq, segk):
    size = segk.shape[0], segq.shape[1]
    ki = lax.broadcasted_iota(jnp.int32, size, 0)
    qi = lax.broadcasted_iota(jnp.int32, size, 1)
    return ((segk == segq) & (ki <= qi)) | (ki == qi)


def forward_kernel(heads, lo_ref, hi_ref, q_ref, k_ref, v_ref, segq_ref, segk_ref, o_ref, log_ref, ks):
    i = pl.program_id(0)

    @pl.when(i == 0)
    def _():
        for h in range(heads):
            ks[h] = k_ref[h * HEAD:(h + 1) * HEAD, :].T

    segq = segq_ref[...]

    def visit(kb, carry, diagonal):
        at = pl.ds(pl.multiple_of(kb * BLOCK, BLOCK), BLOCK)
        segk = segk_ref[at, :]
        mask = diag_mask(segq, segk) if diagonal else segk == segq
        out = []
        for h in range(heads):
            rows = slice(h * HEAD, (h + 1) * HEAD)
            s = jnp.dot(ks[h, at, :], q_ref[rows, :], preferred_element_type=FULL)
            s = jnp.where(mask, s, -1e30)
            peak = jnp.max(s, axis=0, keepdims=True)
            if not diagonal:
                m, l, acc = carry[h]
                peak = jnp.maximum(m, peak)
            p = jnp.exp(s - peak)
            total = jnp.sum(p, axis=0, keepdims=True)
            new = jnp.dot(v_ref[rows, at], p.astype(LOW), preferred_element_type=FULL)
            if not diagonal:
                keep = jnp.exp(m - peak)
                total = l * keep + total
                new = acc * keep + new
            out.append((peak, total, new))
        return tuple(out)

    carry = visit(i, None, True)
    carry = lax.fori_loop(lo_ref[i], hi_ref[i], lambda kb, c: visit(kb, c, False), carry)
    for h in range(heads):
        m, l, acc = carry[h]
        o_ref[h * HEAD:(h + 1) * HEAD, :] = (acc / l).astype(LOW)
        log_ref[h] = m + jnp.log(l)


def attention_forward(q, k, v, segq, segk, lo, hi):
    cols, length = q.shape
    heads = cols // HEAD
    steps = length // BLOCK
    whole = pl.BlockSpec((cols, length), lambda i, *_: (0, 0))
    part = pl.BlockSpec((cols, BLOCK), lambda i, *_: (0, i))
    return pl.pallas_call(
        functools.partial(forward_kernel, heads),
        out_shape=(
            jax.ShapeDtypeStruct((cols, length), LOW),
            jax.ShapeDtypeStruct((heads, 1, length), FULL),
        ),
        grid_spec=pltpu.PrefetchScalarGridSpec(
            num_scalar_prefetch=2,
            grid=(steps,),
            in_specs=[
                part,
                whole,
                whole,
                pl.BlockSpec((1, BLOCK), lambda i, *_: (0, i)),
                pl.BlockSpec((length, 1), lambda i, *_: (0, 0)),
            ],
            out_specs=(part, pl.BlockSpec((heads, 1, BLOCK), lambda i, *_: (0, 0, i))),
            scratch_shapes=[pltpu.VMEM((heads, length, HEAD), LOW)],
        ),
        compiler_params=pltpu.CompilerParams(vmem_limit_bytes=48 * 2**20),
        cost_estimate=pl.CostEstimate(
            flops=8 * 2 * length * length * cols,
            bytes_accessed=4 * cols * length * 2,
            transcendentals=heads * length * length // 3,
        ),
    )(lo, hi, q, k, v, segq, segk)


def backward_kernel(
    heads, lo_ref, hi_ref, q_ref, k_ref, v_ref, o_ref, go_ref, log_ref, raw_ref, factor_ref,
    segq_ref, segk_ref, dq_ref, dk_ref, dv_ref, scale_ref, ks, vs, dks, dvs, dqs,
):
    i = pl.program_id(0)

    @pl.when(i == 0)
    def _():
        for h in range(heads):
            ks[h] = k_ref[h * HEAD:(h + 1) * HEAD, :].T
            vs[h] = v_ref[h * HEAD:(h + 1) * HEAD, :].T
        dks[...] = jnp.zeros_like(dks)
        dvs[...] = jnp.zeros_like(dvs)
        scale_ref[...] = jnp.zeros_like(scale_ref)

    segq = segq_ref[...]
    inner = [
        jnp.sum(
            o_ref[h * HEAD:(h + 1) * HEAD, :].astype(FULL)
            * go_ref[h * HEAD:(h + 1) * HEAD, :].astype(FULL),
            axis=0,
            keepdims=True,
        )
        for h in range(heads)
    ]

    def visit(kb, diagonal):
        at = pl.ds(pl.multiple_of(kb * BLOCK, BLOCK), BLOCK)
        segk = segk_ref[at, :]
        mask = diag_mask(segq, segk) if diagonal else segk == segq
        for h in range(heads):
            rows = slice(h * HEAD, (h + 1) * HEAD)
            q = q_ref[rows, :]
            go = go_ref[rows, :]
            s = jnp.dot(ks[h, at, :], q, preferred_element_type=FULL)
            p = jnp.where(mask, jnp.exp(s - log_ref[h]), 0.0)
            dp = jnp.dot(vs[h, at, :], go, preferred_element_type=FULL)
            ds = (p * (dp - inner[h])).astype(LOW)
            new = jnp.dot(k_ref[rows, at], ds, preferred_element_type=FULL)
            if diagonal:
                dqs[rows, :] = new
            else:
                dqs[rows, :] += new
            dks[rows, at] += mm(q, ds, 1, 1)
            dvs[rows, at] += mm(go, p.astype(LOW), 1, 1)

    visit(i, True)

    @pl.loop(lo_ref[i], hi_ref[i])
    def _(kb):
        visit(kb, False)

    factor = factor_ref[...]
    part = jnp.zeros((HEAD, 1), FULL)
    for h in range(heads):
        rows = slice(h * HEAD, (h + 1) * HEAD)
        dq = dqs[rows, :]
        part = part + jnp.sum(dq * raw_ref[rows, :], axis=1, keepdims=True)
        dq_ref[rows, :] = (dq * factor).astype(LOW)
    scale_ref[...] += part

    @pl.when(i == pl.num_programs(0) - 1)
    def _():
        dk_ref[...] = dks[...].astype(LOW)
        dv_ref[...] = dvs[...].astype(LOW)


def attention_backward(q, k, v, o, go, logs, raw, factor, segq, segk, lo, hi):
    cols, length = q.shape
    heads = cols // HEAD
    steps = length // BLOCK
    whole = pl.BlockSpec((cols, length), lambda i, *_: (0, 0))
    part = pl.BlockSpec((cols, BLOCK), lambda i, *_: (0, i))
    column = pl.BlockSpec((HEAD, 1), lambda i, *_: (0, 0))
    shape = jax.ShapeDtypeStruct((cols, length), LOW)
    return pl.pallas_call(
        functools.partial(backward_kernel, heads),
        out_shape=(shape, shape, shape, jax.ShapeDtypeStruct((HEAD, 1), FULL)),
        grid_spec=pltpu.PrefetchScalarGridSpec(
            num_scalar_prefetch=2,
            grid=(steps,),
            in_specs=[
                part,
                whole,
                whole,
                part,
                part,
                pl.BlockSpec((heads, 1, BLOCK), lambda i, *_: (0, 0, i)),
                part,
                column,
                pl.BlockSpec((1, BLOCK), lambda i, *_: (0, i)),
                pl.BlockSpec((length, 1), lambda i, *_: (0, 0)),
            ],
            out_specs=(part, whole, whole, column),
            scratch_shapes=[
                pltpu.VMEM((heads, length, HEAD), LOW),
                pltpu.VMEM((heads, length, HEAD), LOW),
                pltpu.VMEM((cols, length), FULL),
                pltpu.VMEM((cols, length), FULL),
                pltpu.VMEM((cols, BLOCK), FULL),
            ],
        ),
        compiler_params=pltpu.CompilerParams(vmem_limit_bytes=48 * 2**20),
        cost_estimate=pl.CostEstimate(
            flops=8 * 5 * length * length * cols,
            bytes_accessed=8 * cols * length * 2,
            transcendentals=heads * length * length // 3,
        ),
    )(lo, hi, q, k, v, o, go, logs, raw, factor, segq, segk)


def remote(src, dst, sems, index, device):
    return pltpu.make_async_remote_copy(
        src_ref=src,
        dst_ref=dst,
        send_sem=sems[0].at[index],
        recv_sem=sems[1].at[index],
        device_id=device,
        device_id_type=pl.DeviceIdType.MESH,
    )


def greet(peers):
    barrier = pltpu.get_barrier_semaphore()
    for peer in peers:
        pl.semaphore_signal(barrier, inc=1, device_id=peer, device_id_type=pl.DeviceIdType.MESH)
    pl.semaphore_wait(barrier, len(peers))


def tail_kernel(
    n_dp, n_pair, gain_ref, inverse_ref, sums_ref, qkv_hbm, dq_hbm, dk_hbm, dv_hbm, normed_hbm,
    tokens_hbm, middle_hbm, grads_hbm,
    result_hbm, qkv_out, grads_out, sums_out,
    qkv, dproj, normed, tokens, middle, result, row_send, row_recv, own, pair_send, pair_recv,
    dp_send, dp_recv, dp_own, cross_send, cross_recv, cs_send, cs_recv, final, grads_recv,
    grads_own, grads_final, inner_send, inner_recv, sums_send, sums_recv,
    send_sems, recv_sems, local_sems,
):
    r, s = lax.axis_index("row"), lax.axis_index("cs")
    j, d = lax.axis_index("cp"), lax.axis_index("dp")
    n_col = 2 * n_pair
    width, here = tokens.shape
    cols = dq_hbm.shape[0]
    share = width // n_dp
    subs = row_send.shape[1]
    piece = here // subs
    c_first = (s * n_pair + j) ^ (r * n_pair)
    sems = (send_sems, recv_sems)
    counter = iter(range(1000))
    sent = []

    def send(src, dst, device):
        copy = remote(src, dst, sems, next(counter), device)
        copy.start()
        sent.append(copy)
        return copy

    local = []

    def load(src, dst):
        copy = pltpu.make_async_copy(src, dst, local_sems.at[len(local)])
        copy.start()
        local.append(copy)
        return copy

    early = [
        load(qkv_hbm, qkv),
        load(dq_hbm, dproj.at[pl.ds(0, cols)]),
        load(dk_hbm, dproj.at[pl.ds(cols, cols)]),
        load(dv_hbm, dproj.at[pl.ds(2 * cols, cols)]),
    ]
    load_normed = load(normed_hbm, normed)
    late = [load(tokens_hbm, tokens), load(middle_hbm, middle), load(grads_hbm.at[c_first], grads_own)]

    sibling_id = {"row": 1 - r}
    dp_ids = [{"dp": d ^ k} for k in range(1, n_dp)]
    col_ids = [
        {"cs": s ^ (k // n_pair), "cp": j ^ (k % n_pair)} for k in range(1, n_col)
    ]
    greet([sibling_id] + dp_ids + col_ids)

    for copy in early:
        copy.wait()

    def rows_of(half, chunk, u):
        at = pl.ds(pl.multiple_of(chunk * here + u * piece, 128), piece)
        return jnp.dot(
            qkv[half * width:(half + 1) * width, :], dproj[:, at], preferred_element_type=FULL
        )

    row_copies = {}
    for k in range(1, n_pair):
        for u in range(subs):
            row_send[k, u] = rows_of(1, j ^ k, u).astype(LOW)
            row_copies[k, u] = send(row_send.at[k, u], row_recv.at[k, u], sibling_id)
    pair_copies = []
    for k in range(1, n_pair):
        for u in range(subs):
            part = rows_of(0, j ^ k, u)
            row_copies[k, u].wait_recv()
            pair_send[k - 1, u] = (part + row_recv[k, u].astype(FULL)).astype(LOW)
            pair_copies.append(
                send(pair_send.at[k - 1, u], pair_recv.at[k - 1, u], {"cp": j ^ k})
            )

    load_normed.wait()

    def quarter(half, owner):
        at = pl.ds(pl.multiple_of(half * width + owner * share, 32), share)
        return mm(normed[at, :], dproj[...], 1, 1)

    dp_copies = []
    for k in range(1, n_dp):
        for half in range(2):
            dp_send[k - 1, half] = quarter(half, d ^ k).astype(LOW)
        dp_copies.append(send(dp_send.at[k - 1], dp_recv.at[k - 1], dp_ids[k - 1]))
    for half in range(2):
        dp_own[half] = quarter(half, d)

    grads_copies = [
        send(grads_hbm.at[c_first ^ k], grads_recv.at[k - 1], col_ids[k - 1])
        for k in range(1, n_col)
    ]

    for u in range(subs):
        row_send[0, u] = rows_of(1, j, u).astype(LOW)
        row_copies[0, u] = send(row_send.at[0, u], row_recv.at[0, u], sibling_id)
    for u in range(subs):
        own[u] = rows_of(0, j, u)
    for copy in late:
        copy.wait()

    for copy in dp_copies:
        copy.wait_recv()

    def total(half):
        value = dp_own[half]
        for k in range(1, n_dp):
            value = value + dp_recv[k - 1, half].astype(FULL)
        return value

    cross_send[...] = total(1).astype(LOW)
    cross_copy = send(cross_send, cross_recv, sibling_id)
    dp_own[0] = total(0)
    cross_copy.wait_recv()
    near = r == s
    kept, crossed = dp_own[0], cross_recv[...].astype(FULL)
    cs_send[...] = jnp.where(near, crossed, kept).astype(LOW)
    cs_copy = send(cs_send, cs_recv, {"cs": 1 - s})
    dp_own[1] = jnp.where(near, kept, crossed)

    for copy in pair_copies:
        copy.wait_recv()
    inverse = inverse_ref[...]
    for u in range(subs):
        row_copies[0, u].wait_recv()
        at = slice(u * piece, (u + 1) * piece)
        value = own[u] + row_recv[0, u].astype(FULL)
        for k in range(1, n_pair):
            value = value + pair_recv[k - 1, u].astype(FULL)
        own[u] = value
        inner_send[:, at] = jnp.sum(
            value * gain_ref[...] * tokens[:, at].astype(FULL), axis=0, keepdims=True
        )
    inner_copy = send(inner_send, inner_recv, sibling_id)
    narrow = jnp.zeros((width, 128), FULL)
    for u in range(subs):
        at = slice(u * piece, (u + 1) * piece)
        wide = own[u] * tokens[:, at].astype(FULL) * inverse[:, at]
        for v in range(piece // 128):
            narrow = narrow + wide[:, v * 128:(v + 1) * 128]
    gain_part = jnp.sum(narrow.T, axis=0, keepdims=True)
    sums_send[0] = jnp.concatenate([gain_part, sums_ref[1:]], 0)
    inner_copy.wait_recv()
    inner = (inner_send[...] + inner_recv[...]) / D
    for u in range(subs):
        at = slice(u * piece, (u + 1) * piece)
        result[:, at] = (
            middle[:, at]
            + inverse[:, at] * (own[u] * gain_ref[...])
            - tokens[:, at].astype(FULL)
            * (inverse[:, at] * inverse[:, at] * inverse[:, at] * inner[:, at])
        )
    result_copy = pltpu.make_async_copy(result, result_hbm, local_sems.at[len(local)])
    result_copy.start()

    cs_copy.wait_recv()
    final[...] = (dp_own[1] + cs_recv[...].astype(FULL)).astype(LOW)
    out_copies = [send(final, qkv_out.at[d], peer) for peer in dp_ids]
    final_copy = pltpu.make_async_copy(final, qkv_out.at[d], local_sems.at[len(local) + 1])
    final_copy.start()

    for copy in grads_copies:
        copy.wait_recv()
    value = grads_own[...].astype(FULL)
    for k in range(1, n_col):
        value = value + grads_recv[k - 1].astype(FULL)
    grads_final[...] = value.astype(LOW)
    out_copies += [send(grads_final, grads_out.at[d], peer) for peer in dp_ids]
    grads_copy = pltpu.make_async_copy(grads_final, grads_out.at[d], local_sems.at[len(local) + 2])
    grads_copy.start()

    steps = []
    for name, me, n in (("dp", d, n_dp), ("cs", s, 2), ("cp", j, n_pair)):
        k = 1
        while k < n:
            steps.append({name: me ^ k})
            k *= 2
    for t, peer in enumerate(steps):
        copy = send(sums_send.at[t], sums_recv.at[t], peer)
        copy.wait_recv()
        sums_send[t + 1] = sums_send[t] + sums_recv[t]
    last = len(steps)
    copy = send(sums_send.at[last], sums_recv.at[last], sibling_id)
    copy.wait_recv()
    sums_out[0] = sums_send[last]
    sums_out[1] = sums_recv[last]

    for copy in out_copies:
        copy.wait_recv()
    result_copy.wait()
    final_copy.wait()
    grads_copy.wait()
    for copy in sent:
        copy.wait_send()


def tail(n_dp, n_pair, gain, inverse, sums, qkv, dq, dk, dv, normed, tokens, middle, grads):
    width, here = tokens.shape
    length = normed.shape[1]
    cols = dq.shape[0]
    share = width // n_dp
    subs = 2
    piece = here // subs
    n_col = 2 * n_pair
    part = grads.shape[1:]
    wide = 3 * cols
    steps = (n_dp * n_col).bit_length()
    count = 2 * n_pair * subs + 3 * n_dp + n_col + steps + 6
    hbm = pl.BlockSpec(memory_space=pl.ANY)
    vmem = pl.BlockSpec(memory_space=pltpu.VMEM)
    V = pltpu.VMEM
    return pl.pallas_call(
        functools.partial(tail_kernel, n_dp, n_pair),
        out_shape=(
            jax.ShapeDtypeStruct((width, here), FULL),
            jax.ShapeDtypeStruct((n_dp, share, wide), LOW),
            jax.ShapeDtypeStruct((n_dp,) + part, LOW),
            jax.ShapeDtypeStruct((2,) + sums.shape, FULL),
        ),
        in_specs=[vmem] * 3 + [hbm] * 8,
        out_specs=(hbm, hbm, hbm, vmem),
        scratch_shapes=[
            V((2 * width, wide), LOW),
            V((wide, length), LOW),
            V((2 * width, length), LOW),
            V((width, here), LOW),
            V((width, here), FULL),
            V((width, here), FULL),
            V((n_pair, subs, width, piece), LOW),
            V((n_pair, subs, width, piece), LOW),
            V((subs, width, piece), FULL),
            V((n_pair - 1, subs, width, piece), LOW),
            V((n_pair - 1, subs, width, piece), LOW),
            V((n_dp - 1, 2, share, wide), LOW),
            V((n_dp - 1, 2, share, wide), LOW),
            V((2, share, wide), FULL),
            V((share, wide), LOW),
            V((share, wide), LOW),
            V((share, wide), LOW),
            V((share, wide), LOW),
            V((share, wide), LOW),
            V((n_col - 1,) + part, LOW),
            V(part, LOW),
            V(part, LOW),
            V((1, here), FULL),
            V((1, here), FULL),
            V((steps + 1,) + sums.shape, FULL),
            V((steps + 1,) + sums.shape, FULL),
            pltpu.SemaphoreType.DMA((count,)),
            pltpu.SemaphoreType.DMA((count,)),
            pltpu.SemaphoreType.DMA((12,)),
        ],
        compiler_params=pltpu.CompilerParams(
            collective_id=1, has_side_effects=True, vmem_limit_bytes=60 * 2**20
        ),
        cost_estimate=pl.CostEstimate(
            flops=8 * wide * width * length, bytes_accessed=2**25, transcendentals=0
        ),
    )(gain, inverse, sums, qkv, dq, dk, dv, normed, tokens, middle, grads)


def on_device(
    tokens,
    segment_ids,
    padding_mask,
    w_qkv,
    w_out,
    w_up,
    w_down,
    gain_attn,
    gain_mlp,
    scale_raw,
    cotangent,
):
    width, here = tokens.shape
    r, s = lax.axis_index("row"), lax.axis_index("cs")
    j, d = lax.axis_index("cp"), lax.axis_index("dp")
    n_pair, n_dp, n_col = lax.axis_size("cp"), lax.axis_size("dp"), lax.axis_size(COLS)
    c = s * n_pair + j
    head_cols = w_qkv.shape[0] // (3 * width)
    heads = head_cols // HEAD
    near = r == s

    segments = jnp.where(s == r, segment_ids[0], sibling(segment_ids)[0])
    padding = jnp.where(s == r, padding_mask[0], sibling(padding_mask)[0])
    length = segments.shape[0]
    firsts = segments[::BLOCK]
    starts = jnp.sum((segments[None, :] < firsts[:, None]).astype(jnp.int32), axis=1)
    filled = (jnp.sum(padding) + BLOCK - 1) // BLOCK
    blocks = jnp.arange(length // BLOCK, dtype=jnp.int32)
    lo = starts // BLOCK
    hi = jnp.minimum(blocks, filled)
    segq = segments[None, :]
    segk = jnp.where(padding == 1, segments, -1)[:, None]

    token_pieces = gather(tokens, "cp")
    token_others = [sibling(piece) for piece in token_pieces]
    grad_out = cotangent
    grad_out_full = jnp.concatenate([grad_out, sibling(grad_out)], 0)

    def halves(vector):
        whole = vector.reshape(2, width)
        own = lax.dynamic_index_in_dim(whole, r, 0, keepdims=False)
        other = lax.dynamic_index_in_dim(whole, 1 - r, 0, keepdims=False)
        return own[:, None], other[:, None]

    gain_one, gain_one_other = halves(gain_attn)
    gain_two, _ = halves(gain_mlp)

    block = w_qkv.reshape(width, 3 * head_cols)
    remote = place(gather(shift(cut(block, d, n_dp, 0), "cs", 1), "dp"), d, 0)
    qkv = jnp.concatenate(
        [jnp.where(near, block, remote), sibling(jnp.where(near, remote, block))], 0
    )

    stacked = jnp.stack([w_out.reshape(-1, width), w_up.reshape(width, -1).T, w_down.reshape(-1, width)])
    unit = stacked.shape[1]
    quarter = cut(stacked, d, n_dp, 1)[:, None, None]
    along_z = [quarter] + [
        lax.ppermute(quarter, COLS, [(i, i ^ k) for i in range(n_col)]) for k in range(1, n_col)
    ]
    c_first = c ^ (r * n_pair)
    along_z = place(along_z, c_first, 1)
    gathered = place(gather(along_z, "dp"), d, 2)
    gathered = gathered.reshape(3, n_col * unit, width)
    half_units = n_col * unit // 2
    crossed = sibling(gathered[:, half_units:])
    out_own, up_own, down_own = gathered
    out_half, up_half, down_half = jnp.concatenate([gathered[:, :half_units], crossed], 2)

    def project(own, other):
        own, other = own.astype(FULL), other.astype(FULL)
        squares = jnp.sum(own * own, axis=0) + jnp.sum(other * other, axis=0)
        inverse = lax.rsqrt(squares / D + EPSILON)[None, :]
        normed = jnp.concatenate(
            [
                (own * inverse * gain_one).astype(LOW),
                (other * inverse * gain_one_other).astype(LOW),
            ],
            0,
        )
        return inverse, normed, mm(qkv, normed, 0, 0)

    pieces = [project(own, other) for own, other in zip(token_pieces, token_others)]
    inverse_one = pieces[0][0]
    normed_one = place([piece[1] for piece in pieces], j, 1)
    projected = place([piece[2] for piece in pieces], j, 1)
    factor = (LOG_TWO_E / math.sqrt(HEAD) * jnp.log1p(jnp.exp(scale_raw)))[:, None]
    query_raw = projected[:head_cols]
    queries = (query_raw * jnp.tile(factor, (heads, 1))).astype(LOW)
    key_heads = projected[head_cols:2 * head_cols].astype(LOW)
    values = projected[2 * head_cols:].astype(LOW)

    attended, logs = attention_forward(queries, key_heads, values, segq, segk, lo, hi)
    mine = place(swap(attended, "cp", 1), j, 0)
    att_full = jnp.concatenate([mine, sibling(mine)], 0)

    inputs = tokens.astype(FULL)
    middle = inputs + mm(out_own, att_full, 0, 0)
    squares = jnp.sum(middle * middle, axis=0, keepdims=True)
    inverse_two = lax.rsqrt((squares + sibling(squares)) / D + EPSILON)
    normed_two = (middle * inverse_two * gain_two).astype(LOW)
    normed_full = jnp.concatenate([normed_two, sibling(normed_two)], 0)
    hidden = mm(up_half, normed_full, 1, 0)
    sigmoid = jax.nn.sigmoid(hidden)
    active = (hidden * sigmoid).astype(LOW)
    active_full = jnp.concatenate([active, sibling(active)], 0)
    result = middle + mm(down_own, active_full, 0, 0)

    grad_active = mm(down_half, grad_out_full, 1, 0)
    grad_hidden = (grad_active * sigmoid * (1.0 + hidden * (1.0 - sigmoid))).astype(LOW)
    grad_hidden_full = jnp.concatenate([grad_hidden, sibling(grad_hidden)], 0)
    grad_normed_two = mm(up_own, grad_hidden_full, 0, 0)
    scaled = grad_normed_two * gain_two
    inner = jnp.sum(scaled * middle, axis=0, keepdims=True)
    inner = inner + sibling(inner)
    grad_middle = (
        grad_out.astype(FULL)
        + inverse_two * scaled
        - middle * (inverse_two * inverse_two * inverse_two * inner / D)
    )
    gain_two_part = jnp.sum(grad_normed_two * middle * inverse_two, axis=1)
    grad_branch = grad_middle.astype(LOW)
    grad_branch_full = jnp.concatenate([grad_branch, sibling(grad_branch)], 0)
    grad_mine = mm(out_half, grad_branch_full, 1, 0).astype(LOW)
    grad_attended = place(swap(grad_mine, "cp", 0), j, 1)

    grads = jnp.stack(
        [
            mm(att_full, grad_branch, 1, 1).astype(LOW),
            mm(grad_hidden_full, normed_two, 1, 1).astype(LOW),
            mm(active_full, grad_out, 1, 1).astype(LOW),
        ],
    ).reshape(3, n_col, n_dp, unit // n_dp, width)
    grads = jnp.transpose(grads, (2, 1, 0, 3, 4)).reshape(n_dp, n_col, 3 * unit // n_dp, width)
    received = swap(grads, "dp", 0)

    dq, dk, dv, scale_part = attention_backward(
        queries, key_heads, values, attended, grad_attended, logs, query_raw, factor,
        segq, segk, lo, hi,
    )
    received, dq = lax.optimization_barrier((received, dq))
    grads = reduce_pieces(received)[0].astype(LOW)
    scale_part = (
        scale_part[:, 0] * (LOG_TWO_E / math.sqrt(HEAD)) * jax.nn.sigmoid(scale_raw)
    )
    sums = jnp.concatenate(
        [
            jnp.zeros((1, width), FULL),
            gain_two_part[None],
            jnp.pad(scale_part, (0, width - HEAD))[None],
            jnp.zeros((5, width), FULL),
        ]
    )
    grad_tokens, grad_qkv, final, sums = tail(
        n_dp, n_pair, gain_one, inverse_one, sums, qkv, dq, dk, dv, normed_one, tokens,
        grad_middle, grads,
    )
    grad_qkv = grad_qkv.astype(FULL)
    final = final.reshape(n_dp, 3, unit // n_dp, width).astype(FULL)
    final = [final[:, i].reshape(unit, width) for i in range(3)]
    own, other = sums[0], sums[1]
    first = r == 0
    gains = jnp.concatenate(
        [jnp.where(first, own[:2], other[:2]), jnp.where(first, other[:2], own[:2])], 1
    )
    scale_total = (own[2] + other[2])[:HEAD]
    return (
        result,
        grad_tokens,
        grad_qkv.reshape(-1),
        final[0].reshape(-1),
        final[1].T.reshape(-1),
        final[2].reshape(-1),
        gains[0],
        gains[1],
        scale_total,
    )


def solution(mesh):
    n_dp, n_row, n_col = (mesh.shape[name] for name in ("dp", "row", "col"))
    split = Mesh(
        np.asarray(mesh.devices).reshape(n_dp, n_row, n_row, n_col // n_row),
        ("dp", "row", "cs", "cp"),
    )
    rows = P("row", ("dp", "cs", "cp"))
    ids = P(("dp", "row"), None)
    blocks = P(("row", "cs", "cp"))
    return jax.shard_map(
        on_device,
        mesh=split,
        in_specs=(rows, ids, ids, blocks, blocks, blocks, blocks, P(), P(), P(), rows),
        out_specs=(rows, rows, blocks, blocks, blocks, blocks, P(), P(), P()),
        check_vma=False,
    )
```

```python
import functools
import math

import jax
import jax.numpy as jnp
import numpy as np
from jax import lax
from jax.experimental import pallas as pl
from jax.experimental.pallas import tpu as pltpu
from jax.sharding import Mesh, PartitionSpec as P

D = 1280
HEAD = 80
EPSILON = 1e-06
LOG_TWO_E = 1.442695041
BLOCK = 256
LOW = jnp.bfloat16
FULL = jnp.float32
COLS = ("cs", "cp")


def mm(left, right, left_axis, right_axis):
    return lax.dot_general(
        left, right, (((left_axis,), (right_axis,)), ((), ())), preferred_element_type=FULL
    )


def shift(x, axis, k):
    n = lax.axis_size(axis)
    return lax.ppermute(x, axis, [(i, i ^ k) for i in range(n)])


def sibling(x):
    return shift(x, "row", 1)


def place(pieces, me, axis):
    n = len(pieces)
    if n == 1:
        return pieces[0]
    if n == 2:
        first = me == 0
        return jnp.concatenate(
            [jnp.where(first, pieces[0], pieces[1]), jnp.where(first, pieces[1], pieces[0])], axis
        )
    shape = list(pieces[0].shape)
    step = shape[axis]
    shape[axis] = step * n
    out = jnp.zeros(shape, pieces[0].dtype)
    for k, piece in enumerate(pieces):
        out = lax.dynamic_update_slice_in_dim(out, piece, (me ^ k) * step, axis)
    return out


def cut(x, index, count, axis):
    step = x.shape[axis] // count
    return lax.dynamic_slice_in_dim(x, index * step, step, axis)


def gather(x, axis):
    return [x] + [shift(x, axis, k) for k in range(1, lax.axis_size(axis))]


def swap(x, name, axis):
    me, n = lax.axis_index(name), lax.axis_size(name)
    parts = [cut(x, me ^ k, n, axis) for k in range(n)]
    return [parts[0]] + [shift(parts[k], name, k) for k in range(1, n)]


def reduce_pieces(pieces):
    total = pieces[0].astype(FULL)
    for piece in pieces[1:]:
        total = total + piece.astype(FULL)
    return total


def diag_mask(segq, segk):
    size = segk.shape[0], segq.shape[1]
    ki = lax.broadcasted_iota(jnp.int32, size, 0)
    qi = lax.broadcasted_iota(jnp.int32, size, 1)
    return ((segk == segq) & (ki <= qi)) | (ki == qi)


def forward_kernel(heads, lo_ref, hi_ref, q_ref, k_ref, v_ref, segq_ref, segk_ref, o_ref, log_ref, ks):
    i = pl.program_id(0)

    @pl.when(i == 0)
    def _():
        for h in range(heads):
            ks[h] = k_ref[h * HEAD:(h + 1) * HEAD, :].T

    segq = segq_ref[...]

    def visit(kb, carry, diagonal):
        at = pl.ds(pl.multiple_of(kb * BLOCK, BLOCK), BLOCK)
        segk = segk_ref[at, :]
        mask = diag_mask(segq, segk) if diagonal else segk == segq
        out = []
        for h in range(heads):
            rows = slice(h * HEAD, (h + 1) * HEAD)
            s = jnp.dot(ks[h, at, :], q_ref[rows, :], preferred_element_type=FULL)
            s = jnp.where(mask, s, -1e30)
            peak = jnp.max(s, axis=0, keepdims=True)
            if not diagonal:
                m, l, acc = carry[h]
                peak = jnp.maximum(m, peak)
            p = jnp.exp(s - peak)
            total = jnp.sum(p, axis=0, keepdims=True)
            new = jnp.dot(v_ref[rows, at], p.astype(LOW), preferred_element_type=FULL)
            if not diagonal:
                keep = jnp.exp(m - peak)
                total = l * keep + total
                new = acc * keep + new
            out.append((peak, total, new))
        return tuple(out)

    carry = visit(i, None, True)
    carry = lax.fori_loop(lo_ref[i], hi_ref[i], lambda kb, c: visit(kb, c, False), carry)
    for h in range(heads):
        m, l, acc = carry[h]
        o_ref[h * HEAD:(h + 1) * HEAD, :] = (acc / l).astype(LOW)
        log_ref[h] = m + jnp.log(l)


def attention_forward(q, k, v, segq, segk, lo, hi):
    cols, length = q.shape
    heads = cols // HEAD
    steps = length // BLOCK
    whole = pl.BlockSpec((cols, length), lambda i, *_: (0, 0))
    part = pl.BlockSpec((cols, BLOCK), lambda i, *_: (0, i))
    return pl.pallas_call(
        functools.partial(forward_kernel, heads),
        out_shape=(
            jax.ShapeDtypeStruct((cols, length), LOW),
            jax.ShapeDtypeStruct((heads, 1, length), FULL),
        ),
        grid_spec=pltpu.PrefetchScalarGridSpec(
            num_scalar_prefetch=2,
            grid=(steps,),
            in_specs=[
                part,
                whole,
                whole,
                pl.BlockSpec((1, BLOCK), lambda i, *_: (0, i)),
                pl.BlockSpec((length, 1), lambda i, *_: (0, 0)),
            ],
            out_specs=(part, pl.BlockSpec((heads, 1, BLOCK), lambda i, *_: (0, 0, i))),
            scratch_shapes=[pltpu.VMEM((heads, length, HEAD), LOW)],
        ),
        compiler_params=pltpu.CompilerParams(vmem_limit_bytes=48 * 2**20),
        cost_estimate=pl.CostEstimate(
            flops=8 * 2 * length * length * cols,
            bytes_accessed=4 * cols * length * 2,
            transcendentals=heads * length * length // 3,
        ),
    )(lo, hi, q, k, v, segq, segk)


def backward_kernel(
    heads, lo_ref, hi_ref, q_ref, k_ref, v_ref, o_ref, go_ref, log_ref, raw_ref, factor_ref,
    segq_ref, segk_ref, dq_ref, dk_ref, dv_ref, scale_ref, ks, vs, dks, dvs, dqs,
):
    i = pl.program_id(0)

    @pl.when(i == 0)
    def _():
        for h in range(heads):
            ks[h] = k_ref[h * HEAD:(h + 1) * HEAD, :].T
            vs[h] = v_ref[h * HEAD:(h + 1) * HEAD, :].T
        dks[...] = jnp.zeros_like(dks)
        dvs[...] = jnp.zeros_like(dvs)
        scale_ref[...] = jnp.zeros_like(scale_ref)

    segq = segq_ref[...]
    inner = [
        jnp.sum(
            o_ref[h * HEAD:(h + 1) * HEAD, :].astype(FULL)
            * go_ref[h * HEAD:(h + 1) * HEAD, :].astype(FULL),
            axis=0,
            keepdims=True,
        )
        for h in range(heads)
    ]

    def visit(kb, diagonal):
        at = pl.ds(pl.multiple_of(kb * BLOCK, BLOCK), BLOCK)
        segk = segk_ref[at, :]
        mask = diag_mask(segq, segk) if diagonal else segk == segq
        for h in range(heads):
            rows = slice(h * HEAD, (h + 1) * HEAD)
            q = q_ref[rows, :]
            go = go_ref[rows, :]
            s = jnp.dot(ks[h, at, :], q, preferred_element_type=FULL)
            p = jnp.where(mask, jnp.exp(s - log_ref[h]), 0.0)
            dp = jnp.dot(vs[h, at, :], go, preferred_element_type=FULL)
            ds = (p * (dp - inner[h])).astype(LOW)
            new = jnp.dot(k_ref[rows, at], ds, preferred_element_type=FULL)
            if diagonal:
                dqs[rows, :] = new
            else:
                dqs[rows, :] += new
            dks[rows, at] += mm(q, ds, 1, 1)
            dvs[rows, at] += mm(go, p.astype(LOW), 1, 1)

    visit(i, True)

    @pl.loop(lo_ref[i], hi_ref[i])
    def _(kb):
        visit(kb, False)

    factor = factor_ref[...]
    part = jnp.zeros((HEAD, 1), FULL)
    for h in range(heads):
        rows = slice(h * HEAD, (h + 1) * HEAD)
        dq = dqs[rows, :]
        part = part + jnp.sum(dq * raw_ref[rows, :], axis=1, keepdims=True)
        dq_ref[rows, :] = (dq * factor).astype(LOW)
    scale_ref[...] += part

    @pl.when(i == pl.num_programs(0) - 1)
    def _():
        dk_ref[...] = dks[...].astype(LOW)
        dv_ref[...] = dvs[...].astype(LOW)


def attention_backward(q, k, v, o, go, logs, raw, factor, segq, segk, lo, hi):
    cols, length = q.shape
    heads = cols // HEAD
    steps = length // BLOCK
    whole = pl.BlockSpec((cols, length), lambda i, *_: (0, 0))
    part = pl.BlockSpec((cols, BLOCK), lambda i, *_: (0, i))
    column = pl.BlockSpec((HEAD, 1), lambda i, *_: (0, 0))
    shape = jax.ShapeDtypeStruct((cols, length), LOW)
    return pl.pallas_call(
        functools.partial(backward_kernel, heads),
        out_shape=(shape, shape, shape, jax.ShapeDtypeStruct((HEAD, 1), FULL)),
        grid_spec=pltpu.PrefetchScalarGridSpec(
            num_scalar_prefetch=2,
            grid=(steps,),
            in_specs=[
                part,
                whole,
                whole,
                part,
                part,
                pl.BlockSpec((heads, 1, BLOCK), lambda i, *_: (0, 0, i)),
                part,
                column,
                pl.BlockSpec((1, BLOCK), lambda i, *_: (0, i)),
                pl.BlockSpec((length, 1), lambda i, *_: (0, 0)),
            ],
            out_specs=(part, whole, whole, column),
            scratch_shapes=[
                pltpu.VMEM((heads, length, HEAD), LOW),
                pltpu.VMEM((heads, length, HEAD), LOW),
                pltpu.VMEM((cols, length), FULL),
                pltpu.VMEM((cols, length), FULL),
                pltpu.VMEM((cols, BLOCK), FULL),
            ],
        ),
        compiler_params=pltpu.CompilerParams(vmem_limit_bytes=48 * 2**20),
        cost_estimate=pl.CostEstimate(
            flops=8 * 5 * length * length * cols,
            bytes_accessed=8 * cols * length * 2,
            transcendentals=heads * length * length // 3,
        ),
    )(lo, hi, q, k, v, o, go, logs, raw, factor, segq, segk)


def remote(src, dst, sems, index, device):
    return pltpu.make_async_remote_copy(
        src_ref=src,
        dst_ref=dst,
        send_sem=sems[0].at[index],
        recv_sem=sems[1].at[index],
        device_id=device,
        device_id_type=pl.DeviceIdType.MESH,
    )


def greet(peers):
    barrier = pltpu.get_barrier_semaphore()
    for peer in peers:
        pl.semaphore_signal(barrier, inc=1, device_id=peer, device_id_type=pl.DeviceIdType.MESH)
    pl.semaphore_wait(barrier, len(peers))


def head_kernel(
    n_dp, n_pair, gain_ref, factor_ref, tokens_hbm, block_hbm, slab_hbm,
    q_hbm, k_hbm, v_hbm, raw_hbm, normed_hbm, qkv_hbm, slabs_hbm, inverse_ref,
    tokens, others, block, cs_recv, remote_block, pass_on, qkv, turned, normed, q, k, v, raw,
    send_sems, recv_sems, local_sems,
):
    r, s = lax.axis_index("row"), lax.axis_index("cs")
    j, d = lax.axis_index("cp"), lax.axis_index("dp")
    n_col = 2 * n_pair
    subs, width, piece = tokens.shape[1:]
    here = subs * piece
    share = cs_recv.shape[0]
    cols = q.shape[0]
    c_first = (s * n_pair + j) ^ (r * n_pair)
    near = r == s
    sems = (send_sems, recv_sems)
    counter, local_counter = iter(range(1000)), iter(range(1000))
    sent, stored = [], []

    def send(src, dst, device):
        copy = remote(src, dst, sems, next(counter), device)
        copy.start()
        sent.append(copy)
        return copy

    def move(src, dst):
        copy = pltpu.make_async_copy(src, dst, local_sems.at[next(local_counter)])
        copy.start()
        return copy

    def store(src, dst):
        stored.append(move(src, dst))

    def columns(u):
        return pl.ds(u * piece, piece)

    own_tokens = [move(tokens_hbm.at[:, columns(u)], tokens.at[0, u]) for u in range(subs)]
    own_block = move(block_hbm, block)
    store(slab_hbm, slabs_hbm.at[c_first])
    sibling_id = {"row": 1 - r}
    dp_ids = [{"dp": d ^ k} for k in range(1, n_dp)]
    col_ids = [{"cs": s ^ (k // n_pair), "cp": j ^ (k % n_pair)} for k in range(1, n_col)]
    greet([sibling_id] + dp_ids + col_ids)

    cs_copy = send(block_hbm.at[d], cs_recv, {"cs": 1 - s})
    other_copies = {}
    for u in range(subs):
        other_copies[0, u] = send(tokens_hbm.at[:, columns(u)], others.at[0, u], sibling_id)
    pair_copies = {}
    for u in range(subs):
        for m in range(1, n_pair):
            pair_copies[m, u] = send(
                tokens_hbm.at[:, columns(u)], tokens.at[m, u], {"cp": j ^ m}
            )

    def norm(m, u):
        own, other = tokens[m, u].astype(FULL), others[m, u].astype(FULL)
        squares = jnp.sum(own * own, axis=0, keepdims=True)
        squares = squares + jnp.sum(other * other, axis=0, keepdims=True)
        inverse = lax.rsqrt(squares / D + EPSILON)
        at = pl.ds(pl.multiple_of((j ^ m) * here + u * piece, 128), piece)
        normed[:width, at] = (own * inverse * gain_ref[:width]).astype(LOW)
        normed[width:, at] = (other * inverse * gain_ref[width:]).astype(LOW)
        store(normed.at[:, at], normed_hbm.at[:, at])
        if m == 0:
            inverse_ref[:, columns(u)] = inverse

    def project(m, u):
        at = pl.ds(pl.multiple_of((j ^ m) * here + u * piece, 128), piece)
        for part, out in ((0, None), (1, k), (2, v)):
            value = jnp.dot(
                turned[part * cols:(part + 1) * cols, :], normed[:, at],
                preferred_element_type=FULL,
            )
            if part == 0:
                raw[:, at] = value
                q[:, at] = (value * factor_ref[...]).astype(LOW)
            else:
                out[:, at] = value.astype(LOW)
        for src, dst in ((q, q_hbm), (k, k_hbm), (v, v_hbm), (raw, raw_hbm)):
            store(src.at[:, at], dst.at[:, at])

    for u in range(subs):
        own_tokens[u].wait()
        other_copies[0, u].wait_recv()
        norm(0, u)
    own_block.wait()

    cs_copy.wait_recv()
    dp_copies = [send(cs_recv, remote_block.at[d], peer) for peer in dp_ids]
    slab_copies = [send(slab_hbm, slabs_hbm.at[c_first], peer) for peer in col_ids]
    remote_block[d] = cs_recv[...]
    for u in range(subs - 1):
        for m in range(1, n_pair):
            pair_copies[m, u].wait_recv()
            other_copies[m, u] = send(tokens.at[m, u], others.at[m, u], sibling_id)
    cross_copies = []
    for m in range(n_dp):
        owner = d ^ m
        if m:
            dp_copies[m - 1].wait_recv()
        mine, its = block[owner], remote_block[owner]
        at = pl.multiple_of(owner * share, 32)
        qkv[pl.ds(at, share)] = jnp.where(near, mine, its)
        pass_on[owner] = jnp.where(near, its, mine)
        cross_copies.append(
            send(pass_on.at[owner], qkv.at[pl.ds(width + at, share)], sibling_id)
        )
    u = subs - 1
    for m in range(1, n_pair):
        pair_copies[m, u].wait_recv()
        other_copies[m, u] = send(tokens.at[m, u], others.at[m, u], sibling_id)
    turned[:, :width] = qkv[:width].T
    for copy in cross_copies:
        copy.wait_recv()
    turned[:, width:] = qkv[width:].T
    store(qkv, qkv_hbm)

    for u in range(subs):
        project(0, u)
    for u in range(subs):
        for m in range(1, n_pair):
            other_copies[m, u].wait_recv()
            norm(m, u)
            project(m, u)

    for copy in stored:
        copy.wait()
    for copy in slab_copies:
        copy.wait_recv()
    for copy in sent:
        copy.wait_send()


def head(n_dp, n_pair, gain, factor, tokens, block, slab):
    width, here = tokens.shape
    wide = block.shape[1]
    cols = wide // 3
    share = width // n_dp
    length = n_pair * here
    n_col = 2 * n_pair
    subs = 2
    piece = here // subs
    count = subs * n_pair * 2 + 2 * n_dp + n_col + 4
    moves = 3 + subs + 5 * subs * n_pair + 4
    hbm = pl.BlockSpec(memory_space=pl.ANY)
    vmem = pl.BlockSpec(memory_space=pltpu.VMEM)
    V = pltpu.VMEM
    shape = jax.ShapeDtypeStruct((cols, length), LOW)
    return pl.pallas_call(
        functools.partial(head_kernel, n_dp, n_pair),
        out_shape=(
            shape,
            shape,
            shape,
            jax.ShapeDtypeStruct((cols, length), FULL),
            jax.ShapeDtypeStruct((2 * width, length), LOW),
            jax.ShapeDtypeStruct((2 * width, wide), LOW),
            jax.ShapeDtypeStruct((n_col,) + slab.shape, LOW),
            jax.ShapeDtypeStruct((1, here), FULL),
        ),
        in_specs=[vmem] * 2 + [hbm] * 3,
        out_specs=(hbm,) * 7 + (vmem,),
        scratch_shapes=[
            V((n_pair, subs, width, piece), LOW),
            V((n_pair, subs, width, piece), LOW),
            V((n_dp, share, wide), LOW),
            V((share, wide), LOW),
            V((n_dp, share, wide), LOW),
            V((n_dp, share, wide), LOW),
            V((2 * width, wide), LOW),
            V((wide, 2 * width), LOW),
            V((2 * width, length), LOW),
            V((cols, length), LOW),
            V((cols, length), LOW),
            V((cols, length), LOW),
            V((cols, length), FULL),
            pltpu.SemaphoreType.DMA((count,)),
            pltpu.SemaphoreType.DMA((count,)),
            pltpu.SemaphoreType.DMA((moves,)),
        ],
        compiler_params=pltpu.CompilerParams(
            collective_id=2, has_side_effects=True, vmem_limit_bytes=60 * 2**20
        ),
        cost_estimate=pl.CostEstimate(
            flops=4 * wide * width * length, bytes_accessed=2**25, transcendentals=0
        ),
    )(gain, factor, tokens, block.reshape(n_dp, share, wide), slab)


def tail_kernel(
    n_dp, n_pair, gain_ref, inverse_ref, sums_ref, qkv_hbm, dq_hbm, dk_hbm, dv_hbm, normed_hbm,
    tokens_hbm, middle_hbm, grads_hbm,
    result_hbm, qkv_out, grads_out, sums_out,
    qkv, dproj, normed, tokens, middle, result, row_send, row_recv, own, pair_send, pair_recv,
    dp_send, dp_recv, dp_own, cross_send, cross_recv, cs_send, cs_recv, final, grads_recv,
    grads_own, grads_final, inner_send, inner_recv, sums_send, sums_recv,
    send_sems, recv_sems, local_sems,
):
    r, s = lax.axis_index("row"), lax.axis_index("cs")
    j, d = lax.axis_index("cp"), lax.axis_index("dp")
    n_col = 2 * n_pair
    width, here = tokens.shape
    cols = dq_hbm.shape[0]
    share = width // n_dp
    subs = row_send.shape[1]
    piece = here // subs
    c_first = (s * n_pair + j) ^ (r * n_pair)
    sems = (send_sems, recv_sems)
    counter = iter(range(1000))
    sent = []

    def send(src, dst, device):
        copy = remote(src, dst, sems, next(counter), device)
        copy.start()
        sent.append(copy)
        return copy

    local = []

    def load(src, dst):
        copy = pltpu.make_async_copy(src, dst, local_sems.at[len(local)])
        copy.start()
        local.append(copy)
        return copy

    early = [
        load(qkv_hbm, qkv),
        load(dq_hbm, dproj.at[pl.ds(0, cols)]),
        load(dk_hbm, dproj.at[pl.ds(cols, cols)]),
        load(dv_hbm, dproj.at[pl.ds(2 * cols, cols)]),
    ]
    load_normed = load(normed_hbm, normed)
    late = [load(tokens_hbm, tokens), load(middle_hbm, middle), load(grads_hbm.at[c_first], grads_own)]

    sibling_id = {"row": 1 - r}
    dp_ids = [{"dp": d ^ k} for k in range(1, n_dp)]
    col_ids = [
        {"cs": s ^ (k // n_pair), "cp": j ^ (k % n_pair)} for k in range(1, n_col)
    ]
    greet([sibling_id] + dp_ids + col_ids)

    for copy in early:
        copy.wait()

    def rows_of(half, chunk, u):
        at = pl.ds(pl.multiple_of(chunk * here + u * piece, 128), piece)
        return jnp.dot(
            qkv[half * width:(half + 1) * width, :], dproj[:, at], preferred_element_type=FULL
        )

    row_copies = {}
    for k in range(1, n_pair):
        for u in range(subs):
            row_send[k, u] = rows_of(1, j ^ k, u).astype(LOW)
            row_copies[k, u] = send(row_send.at[k, u], row_recv.at[k, u], sibling_id)
    pair_copies = []
    for k in range(1, n_pair):
        for u in range(subs):
            part = rows_of(0, j ^ k, u)
            row_copies[k, u].wait_recv()
            pair_send[k - 1, u] = (part + row_recv[k, u].astype(FULL)).astype(LOW)
            pair_copies.append(
                send(pair_send.at[k - 1, u], pair_recv.at[k - 1, u], {"cp": j ^ k})
            )

    load_normed.wait()

    def quarter(half, owner):
        at = pl.ds(pl.multiple_of(half * width + owner * share, 32), share)
        return mm(normed[at, :], dproj[...], 1, 1)

    dp_copies = []
    for k in range(1, n_dp):
        for half in range(2):
            dp_send[k - 1, half] = quarter(half, d ^ k).astype(LOW)
        dp_copies.append(send(dp_send.at[k - 1], dp_recv.at[k - 1], dp_ids[k - 1]))
    for half in range(2):
        dp_own[half] = quarter(half, d)

    grads_copies = [
        send(grads_hbm.at[c_first ^ k], grads_recv.at[k - 1], col_ids[k - 1])
        for k in range(1, n_col)
    ]

    for u in range(subs):
        row_send[0, u] = rows_of(1, j, u).astype(LOW)
        row_copies[0, u] = send(row_send.at[0, u], row_recv.at[0, u], sibling_id)
    for u in range(subs):
        own[u] = rows_of(0, j, u)
    for copy in late:
        copy.wait()

    for copy in dp_copies:
        copy.wait_recv()

    def total(half):
        value = dp_own[half]
        for k in range(1, n_dp):
            value = value + dp_recv[k - 1, half].astype(FULL)
        return value

    cross_send[...] = total(1).astype(LOW)
    cross_copy = send(cross_send, cross_recv, sibling_id)
    dp_own[0] = total(0)
    cross_copy.wait_recv()
    near = r == s
    kept, crossed = dp_own[0], cross_recv[...].astype(FULL)
    cs_send[...] = jnp.where(near, crossed, kept).astype(LOW)
    cs_copy = send(cs_send, cs_recv, {"cs": 1 - s})
    dp_own[1] = jnp.where(near, kept, crossed)

    for copy in pair_copies:
        copy.wait_recv()
    inverse = inverse_ref[...]
    for u in range(subs):
        row_copies[0, u].wait_recv()
        at = slice(u * piece, (u + 1) * piece)
        value = own[u] + row_recv[0, u].astype(FULL)
        for k in range(1, n_pair):
            value = value + pair_recv[k - 1, u].astype(FULL)
        own[u] = value
        inner_send[:, at] = jnp.sum(
            value * gain_ref[...] * tokens[:, at].astype(FULL), axis=0, keepdims=True
        )
    inner_copy = send(inner_send, inner_recv, sibling_id)
    narrow = jnp.zeros((width, 128), FULL)
    for u in range(subs):
        at = slice(u * piece, (u + 1) * piece)
        wide = own[u] * tokens[:, at].astype(FULL) * inverse[:, at]
        for v in range(piece // 128):
            narrow = narrow + wide[:, v * 128:(v + 1) * 128]
    gain_part = jnp.sum(narrow.T, axis=0, keepdims=True)
    sums_send[0] = jnp.concatenate([gain_part, sums_ref[1:]], 0)
    inner_copy.wait_recv()
    inner = (inner_send[...] + inner_recv[...]) / D
    for u in range(subs):
        at = slice(u * piece, (u + 1) * piece)
        result[:, at] = (
            middle[:, at]
            + inverse[:, at] * (own[u] * gain_ref[...])
            - tokens[:, at].astype(FULL)
            * (inverse[:, at] * inverse[:, at] * inverse[:, at] * inner[:, at])
        )
    result_copy = pltpu.make_async_copy(result, result_hbm, local_sems.at[len(local)])
    result_copy.start()

    cs_copy.wait_recv()
    final[...] = (dp_own[1] + cs_recv[...].astype(FULL)).astype(LOW)
    out_copies = [send(final, qkv_out.at[d], peer) for peer in dp_ids]
    final_copy = pltpu.make_async_copy(final, qkv_out.at[d], local_sems.at[len(local) + 1])
    final_copy.start()

    for copy in grads_copies:
        copy.wait_recv()
    value = grads_own[...].astype(FULL)
    for k in range(1, n_col):
        value = value + grads_recv[k - 1].astype(FULL)
    grads_final[...] = value.astype(LOW)
    out_copies += [send(grads_final, grads_out.at[d], peer) for peer in dp_ids]
    grads_copy = pltpu.make_async_copy(grads_final, grads_out.at[d], local_sems.at[len(local) + 2])
    grads_copy.start()

    steps = []
    for name, me, n in (("dp", d, n_dp), ("cs", s, 2), ("cp", j, n_pair)):
        k = 1
        while k < n:
            steps.append({name: me ^ k})
            k *= 2
    for t, peer in enumerate(steps):
        copy = send(sums_send.at[t], sums_recv.at[t], peer)
        copy.wait_recv()
        sums_send[t + 1] = sums_send[t] + sums_recv[t]
    last = len(steps)
    copy = send(sums_send.at[last], sums_recv.at[last], sibling_id)
    copy.wait_recv()
    sums_out[0] = sums_send[last]
    sums_out[1] = sums_recv[last]

    for copy in out_copies:
        copy.wait_recv()
    result_copy.wait()
    final_copy.wait()
    grads_copy.wait()
    for copy in sent:
        copy.wait_send()


def tail(n_dp, n_pair, gain, inverse, sums, qkv, dq, dk, dv, normed, tokens, middle, grads):
    width, here = tokens.shape
    length = normed.shape[1]
    cols = dq.shape[0]
    share = width // n_dp
    subs = 2
    piece = here // subs
    n_col = 2 * n_pair
    part = grads.shape[1:]
    wide = 3 * cols
    steps = (n_dp * n_col).bit_length()
    count = 2 * n_pair * subs + 3 * n_dp + n_col + steps + 6
    hbm = pl.BlockSpec(memory_space=pl.ANY)
    vmem = pl.BlockSpec(memory_space=pltpu.VMEM)
    V = pltpu.VMEM
    return pl.pallas_call(
        functools.partial(tail_kernel, n_dp, n_pair),
        out_shape=(
            jax.ShapeDtypeStruct((width, here), FULL),
            jax.ShapeDtypeStruct((n_dp, share, wide), LOW),
            jax.ShapeDtypeStruct((n_dp,) + part, LOW),
            jax.ShapeDtypeStruct((2,) + sums.shape, FULL),
        ),
        in_specs=[vmem] * 3 + [hbm] * 8,
        out_specs=(hbm, hbm, hbm, vmem),
        scratch_shapes=[
            V((2 * width, wide), LOW),
            V((wide, length), LOW),
            V((2 * width, length), LOW),
            V((width, here), LOW),
            V((width, here), FULL),
            V((width, here), FULL),
            V((n_pair, subs, width, piece), LOW),
            V((n_pair, subs, width, piece), LOW),
            V((subs, width, piece), FULL),
            V((n_pair - 1, subs, width, piece), LOW),
            V((n_pair - 1, subs, width, piece), LOW),
            V((n_dp - 1, 2, share, wide), LOW),
            V((n_dp - 1, 2, share, wide), LOW),
            V((2, share, wide), FULL),
            V((share, wide), LOW),
            V((share, wide), LOW),
            V((share, wide), LOW),
            V((share, wide), LOW),
            V((share, wide), LOW),
            V((n_col - 1,) + part, LOW),
            V(part, LOW),
            V(part, LOW),
            V((1, here), FULL),
            V((1, here), FULL),
            V((steps + 1,) + sums.shape, FULL),
            V((steps + 1,) + sums.shape, FULL),
            pltpu.SemaphoreType.DMA((count,)),
            pltpu.SemaphoreType.DMA((count,)),
            pltpu.SemaphoreType.DMA((12,)),
        ],
        compiler_params=pltpu.CompilerParams(
            collective_id=1, has_side_effects=True, vmem_limit_bytes=60 * 2**20
        ),
        cost_estimate=pl.CostEstimate(
            flops=8 * wide * width * length, bytes_accessed=2**25, transcendentals=0
        ),
    )(gain, inverse, sums, qkv, dq, dk, dv, normed, tokens, middle, grads)


def on_device(
    tokens,
    segment_ids,
    padding_mask,
    w_qkv,
    w_out,
    w_up,
    w_down,
    gain_attn,
    gain_mlp,
    scale_raw,
    cotangent,
):
    width, here = tokens.shape
    r, s = lax.axis_index("row"), lax.axis_index("cs")
    j, d = lax.axis_index("cp"), lax.axis_index("dp")
    n_pair, n_dp, n_col = lax.axis_size("cp"), lax.axis_size("dp"), lax.axis_size(COLS)
    c = s * n_pair + j
    head_cols = w_qkv.shape[0] // (3 * width)
    heads = head_cols // HEAD
    near = r == s

    segments = jnp.where(s == r, segment_ids[0], sibling(segment_ids)[0])
    padding = jnp.where(s == r, padding_mask[0], sibling(padding_mask)[0])
    length = segments.shape[0]
    firsts = segments[::BLOCK]
    starts = jnp.sum((segments[None, :] < firsts[:, None]).astype(jnp.int32), axis=1)
    filled = (jnp.sum(padding) + BLOCK - 1) // BLOCK
    blocks = jnp.arange(length // BLOCK, dtype=jnp.int32)
    lo = starts // BLOCK
    hi = jnp.minimum(blocks, filled)
    segq = segments[None, :]
    segk = jnp.where(padding == 1, segments, -1)[:, None]

    grad_out = cotangent
    grad_out_full = jnp.concatenate([grad_out, sibling(grad_out)], 0)

    def halves(vector):
        whole = vector.reshape(2, width)
        own = lax.dynamic_index_in_dim(whole, r, 0, keepdims=False)
        other = lax.dynamic_index_in_dim(whole, 1 - r, 0, keepdims=False)
        return own[:, None], other[:, None]

    gain_one, gain_one_other = halves(gain_attn)
    gain_two, _ = halves(gain_mlp)
    factor = (LOG_TWO_E / math.sqrt(HEAD) * jnp.log1p(jnp.exp(scale_raw)))[:, None]

    block = w_qkv.reshape(width, 3 * head_cols)
    unit = w_up.shape[0] // width
    slab = jnp.concatenate([w_out.reshape(-1, width), w_up.reshape(width, -1).T], 0)
    slab_rows = -(-2 * unit // (16 * n_dp)) * 16
    slab = jnp.pad(slab, ((0, n_dp * slab_rows - 2 * unit), (0, 0)))
    slab = cut(slab, d, n_dp, 0)
    queries, key_heads, values, query_raw, normed_one, qkv, slabs, inverse_one = head(
        n_dp, n_pair, jnp.concatenate([gain_one, gain_one_other], 0), jnp.tile(factor, (heads, 1)),
        tokens, block, slab,
    )
    slabs = place(gather(slabs, "dp"), d, 1)[:, :2 * unit].reshape(n_col, 2, unit, width)
    down = w_down.reshape(-1, width)
    c_first = c ^ (r * n_pair)
    down_own = place(
        [down]
        + [lax.ppermute(down, COLS, [(i, i ^ k) for i in range(n_col)]) for k in range(1, n_col)],
        c_first,
        0,
    )
    out_own, up_own = (slabs[:, i].reshape(n_col * unit, width) for i in range(2))
    half_units = n_col * unit // 2
    gathered = jnp.stack([out_own, up_own, down_own])
    crossed = sibling(gathered[:, half_units:])
    out_half, up_half, down_half = jnp.concatenate([gathered[:, :half_units], crossed], 2)

    attended, logs = attention_forward(queries, key_heads, values, segq, segk, lo, hi)
    mine = place(swap(attended, "cp", 1), j, 0)
    att_full = jnp.concatenate([mine, sibling(mine)], 0)

    inputs = tokens.astype(FULL)
    middle = inputs + mm(out_own, att_full, 0, 0)
    squares = jnp.sum(middle * middle, axis=0, keepdims=True)
    inverse_two = lax.rsqrt((squares + sibling(squares)) / D + EPSILON)
    normed_two = (middle * inverse_two * gain_two).astype(LOW)
    normed_full = jnp.concatenate([normed_two, sibling(normed_two)], 0)
    hidden = mm(up_half, normed_full, 1, 0)
    sigmoid = jax.nn.sigmoid(hidden)
    active = (hidden * sigmoid).astype(LOW)
    active_full = jnp.concatenate([active, sibling(active)], 0)
    result = middle + mm(down_own, active_full, 0, 0)

    grad_active = mm(down_half, grad_out_full, 1, 0)
    grad_hidden = (grad_active * sigmoid * (1.0 + hidden * (1.0 - sigmoid))).astype(LOW)
    grad_hidden_full = jnp.concatenate([grad_hidden, sibling(grad_hidden)], 0)
    grad_normed_two = mm(up_own, grad_hidden_full, 0, 0)
    scaled = grad_normed_two * gain_two
    inner = jnp.sum(scaled * middle, axis=0, keepdims=True)
    inner = inner + sibling(inner)
    grad_middle = (
        grad_out.astype(FULL)
        + inverse_two * scaled
        - middle * (inverse_two * inverse_two * inverse_two * inner / D)
    )
    gain_two_part = jnp.sum(grad_normed_two * middle * inverse_two, axis=1)
    grad_branch = grad_middle.astype(LOW)
    grad_branch_full = jnp.concatenate([grad_branch, sibling(grad_branch)], 0)
    grad_mine = mm(out_half, grad_branch_full, 1, 0).astype(LOW)
    grad_attended = place(swap(grad_mine, "cp", 0), j, 1)

    grads = jnp.stack(
        [
            mm(att_full, grad_branch, 1, 1).astype(LOW),
            mm(grad_hidden_full, normed_two, 1, 1).astype(LOW),
            mm(active_full, grad_out, 1, 1).astype(LOW),
        ],
    ).reshape(3, n_col, n_dp, unit // n_dp, width)
    grads = jnp.transpose(grads, (2, 1, 0, 3, 4)).reshape(n_dp, n_col, 3 * unit // n_dp, width)
    received = swap(grads, "dp", 0)

    dq, dk, dv, scale_part = attention_backward(
        queries, key_heads, values, attended, grad_attended, logs, query_raw, factor,
        segq, segk, lo, hi,
    )
    received, dq = lax.optimization_barrier((received, dq))
    grads = reduce_pieces(received)[0].astype(LOW)
    scale_part = (
        scale_part[:, 0] * (LOG_TWO_E / math.sqrt(HEAD)) * jax.nn.sigmoid(scale_raw)
    )
    sums = jnp.concatenate(
        [
            jnp.zeros((1, width), FULL),
            gain_two_part[None],
            jnp.pad(scale_part, (0, width - HEAD))[None],
            jnp.zeros((5, width), FULL),
        ]
    )
    grad_tokens, grad_qkv, final, sums = tail(
        n_dp, n_pair, gain_one, inverse_one, sums, qkv, dq, dk, dv, normed_one, tokens,
        grad_middle, grads,
    )
    grad_qkv = grad_qkv.astype(FULL)
    final = final.reshape(n_dp, 3, unit // n_dp, width).astype(FULL)
    final = [final[:, i].reshape(unit, width) for i in range(3)]
    own, other = sums[0], sums[1]
    first = r == 0
    gains = jnp.concatenate(
        [jnp.where(first, own[:2], other[:2]), jnp.where(first, other[:2], own[:2])], 1
    )
    scale_total = (own[2] + other[2])[:HEAD]
    return (
        result,
        grad_tokens,
        grad_qkv.reshape(-1),
        final[0].reshape(-1),
        final[1].T.reshape(-1),
        final[2].reshape(-1),
        gains[0],
        gains[1],
        scale_total,
    )


def solution(mesh):
    n_dp, n_row, n_col = (mesh.shape[name] for name in ("dp", "row", "col"))
    split = Mesh(
        np.asarray(mesh.devices).reshape(n_dp, n_row, n_row, n_col // n_row),
        ("dp", "row", "cs", "cp"),
    )
    rows = P("row", ("dp", "cs", "cp"))
    ids = P(("dp", "row"), None)
    blocks = P(("row", "cs", "cp"))
    return jax.shard_map(
        on_device,
        mesh=split,
        in_specs=(rows, ids, ids, blocks, blocks, blocks, blocks, P(), P(), P(), rows),
        out_specs=(rows, rows, blocks, blocks, blocks, blocks, P(), P(), P()),
        check_vma=False,
    )
```

```python
import functools
import math

import jax
import jax.numpy as jnp
import numpy as np
from jax import lax
from jax.experimental import pallas as pl
from jax.experimental.pallas import tpu as pltpu
from jax.sharding import Mesh, PartitionSpec as P

D = 1280
HEAD = 80
EPSILON = 1e-06
LOG_TWO_E = 1.442695041
BLOCK = 256
LOW = jnp.bfloat16
FULL = jnp.float32
COLS = ("cs", "cp")


def mm(left, right, left_axis, right_axis):
    return lax.dot_general(
        left, right, (((left_axis,), (right_axis,)), ((), ())), preferred_element_type=FULL
    )


def shift(x, axis, k):
    n = lax.axis_size(axis)
    return lax.ppermute(x, axis, [(i, i ^ k) for i in range(n)])


def sibling(x):
    return shift(x, "row", 1)


def place(pieces, me, axis):
    n = len(pieces)
    if n == 1:
        return pieces[0]
    if n == 2:
        first = me == 0
        return jnp.concatenate(
            [jnp.where(first, pieces[0], pieces[1]), jnp.where(first, pieces[1], pieces[0])], axis
        )
    shape = list(pieces[0].shape)
    step = shape[axis]
    shape[axis] = step * n
    out = jnp.zeros(shape, pieces[0].dtype)
    for k, piece in enumerate(pieces):
        out = lax.dynamic_update_slice_in_dim(out, piece, (me ^ k) * step, axis)
    return out


def cut(x, index, count, axis):
    step = x.shape[axis] // count
    return lax.dynamic_slice_in_dim(x, index * step, step, axis)


def gather(x, axis):
    return [x] + [shift(x, axis, k) for k in range(1, lax.axis_size(axis))]


def swap(x, name, axis):
    me, n = lax.axis_index(name), lax.axis_size(name)
    parts = [cut(x, me ^ k, n, axis) for k in range(n)]
    return [parts[0]] + [shift(parts[k], name, k) for k in range(1, n)]


def reduce_pieces(pieces):
    total = pieces[0].astype(FULL)
    for piece in pieces[1:]:
        total = total + piece.astype(FULL)
    return total


def diag_mask(segq, segk):
    size = segk.shape[0], segq.shape[1]
    ki = lax.broadcasted_iota(jnp.int32, size, 0)
    qi = lax.broadcasted_iota(jnp.int32, size, 1)
    return ((segk == segq) & (ki <= qi)) | (ki == qi)


def forward_kernel(heads, lo_ref, hi_ref, q_ref, k_ref, v_ref, segq_ref, segk_ref, o_ref, log_ref, ks):
    i = pl.program_id(0)

    @pl.when(i == 0)
    def _():
        for h in range(heads):
            ks[h] = k_ref[h * HEAD:(h + 1) * HEAD, :].T

    segq = segq_ref[...]

    def visit(kb, carry, diagonal):
        at = pl.ds(pl.multiple_of(kb * BLOCK, BLOCK), BLOCK)
        segk = segk_ref[at, :]
        mask = diag_mask(segq, segk) if diagonal else segk == segq
        out = []
        for h in range(heads):
            rows = slice(h * HEAD, (h + 1) * HEAD)
            s = jnp.dot(ks[h, at, :], q_ref[rows, :], preferred_element_type=FULL)
            s = jnp.where(mask, s, -1e30)
            peak = jnp.max(s, axis=0, keepdims=True)
            if not diagonal:
                m, l, acc = carry[h]
                peak = jnp.maximum(m, peak)
            p = jnp.exp(s - peak)
            total = jnp.sum(p, axis=0, keepdims=True)
            new = jnp.dot(v_ref[rows, at], p.astype(LOW), preferred_element_type=FULL)
            if not diagonal:
                keep = jnp.exp(m - peak)
                total = l * keep + total
                new = acc * keep + new
            out.append((peak, total, new))
        return tuple(out)

    carry = visit(i, None, True)
    carry = lax.fori_loop(lo_ref[i], hi_ref[i], lambda kb, c: visit(kb, c, False), carry)
    for h in range(heads):
        m, l, acc = carry[h]
        o_ref[h * HEAD:(h + 1) * HEAD, :] = (acc / l).astype(LOW)
        log_ref[h] = m + jnp.log(l)


def attention_forward(q, k, v, segq, segk, lo, hi):
    cols, length = q.shape
    heads = cols // HEAD
    steps = length // BLOCK
    whole = pl.BlockSpec((cols, length), lambda i, *_: (0, 0))
    part = pl.BlockSpec((cols, BLOCK), lambda i, *_: (0, i))
    return pl.pallas_call(
        functools.partial(forward_kernel, heads),
        out_shape=(
            jax.ShapeDtypeStruct((cols, length), LOW),
            jax.ShapeDtypeStruct((heads, 1, length), FULL),
        ),
        grid_spec=pltpu.PrefetchScalarGridSpec(
            num_scalar_prefetch=2,
            grid=(steps,),
            in_specs=[
                part,
                whole,
                whole,
                pl.BlockSpec((1, BLOCK), lambda i, *_: (0, i)),
                pl.BlockSpec((length, 1), lambda i, *_: (0, 0)),
            ],
            out_specs=(part, pl.BlockSpec((heads, 1, BLOCK), lambda i, *_: (0, 0, i))),
            scratch_shapes=[pltpu.VMEM((heads, length, HEAD), LOW)],
        ),
        compiler_params=pltpu.CompilerParams(vmem_limit_bytes=48 * 2**20),
        cost_estimate=pl.CostEstimate(
            flops=8 * 2 * length * length * cols,
            bytes_accessed=4 * cols * length * 2,
            transcendentals=heads * length * length // 3,
        ),
    )(lo, hi, q, k, v, segq, segk)


def backward_kernel(
    heads, lo_ref, hi_ref, q_ref, k_ref, v_ref, o_ref, go_ref, log_ref, raw_ref, factor_ref,
    segq_ref, segk_ref, dq_ref, dk_ref, dv_ref, scale_ref, ks, vs, dks, dvs, dqs,
):
    i = pl.program_id(0)

    @pl.when(i == 0)
    def _():
        for h in range(heads):
            ks[h] = k_ref[h * HEAD:(h + 1) * HEAD, :].T
            vs[h] = v_ref[h * HEAD:(h + 1) * HEAD, :].T
        dks[...] = jnp.zeros_like(dks)
        dvs[...] = jnp.zeros_like(dvs)
        scale_ref[...] = jnp.zeros_like(scale_ref)

    segq = segq_ref[...]
    inner = [
        jnp.sum(
            o_ref[h * HEAD:(h + 1) * HEAD, :].astype(FULL)
            * go_ref[h * HEAD:(h + 1) * HEAD, :].astype(FULL),
            axis=0,
            keepdims=True,
        )
        for h in range(heads)
    ]

    def visit(kb, diagonal):
        at = pl.ds(pl.multiple_of(kb * BLOCK, BLOCK), BLOCK)
        segk = segk_ref[at, :]
        mask = diag_mask(segq, segk) if diagonal else segk == segq
        for h in range(heads):
            rows = slice(h * HEAD, (h + 1) * HEAD)
            q = q_ref[rows, :]
            go = go_ref[rows, :]
            s = jnp.dot(ks[h, at, :], q, preferred_element_type=FULL)
            p = jnp.where(mask, jnp.exp(s - log_ref[h]), 0.0)
            dp = jnp.dot(vs[h, at, :], go, preferred_element_type=FULL)
            ds = (p * (dp - inner[h])).astype(LOW)
            new = jnp.dot(k_ref[rows, at], ds, preferred_element_type=FULL)
            if diagonal:
                dqs[rows, :] = new
            else:
                dqs[rows, :] += new
            dks[rows, at] += mm(q, ds, 1, 1)
            dvs[rows, at] += mm(go, p.astype(LOW), 1, 1)

    visit(i, True)

    @pl.loop(lo_ref[i], hi_ref[i])
    def _(kb):
        visit(kb, False)

    factor = factor_ref[...]
    part = jnp.zeros((HEAD, 1), FULL)
    for h in range(heads):
        rows = slice(h * HEAD, (h + 1) * HEAD)
        dq = dqs[rows, :]
        part = part + jnp.sum(dq * raw_ref[rows, :], axis=1, keepdims=True)
        dq_ref[rows, :] = (dq * factor).astype(LOW)
    scale_ref[...] += part

    @pl.when(i == pl.num_programs(0) - 1)
    def _():
        dk_ref[...] = dks[...].astype(LOW)
        dv_ref[...] = dvs[...].astype(LOW)


def attention_backward(q, k, v, o, go, logs, raw, factor, segq, segk, lo, hi):
    cols, length = q.shape
    heads = cols // HEAD
    steps = length // BLOCK
    whole = pl.BlockSpec((cols, length), lambda i, *_: (0, 0))
    part = pl.BlockSpec((cols, BLOCK), lambda i, *_: (0, i))
    column = pl.BlockSpec((HEAD, 1), lambda i, *_: (0, 0))
    shape = jax.ShapeDtypeStruct((cols, length), LOW)
    return pl.pallas_call(
        functools.partial(backward_kernel, heads),
        out_shape=(shape, shape, shape, jax.ShapeDtypeStruct((HEAD, 1), FULL)),
        grid_spec=pltpu.PrefetchScalarGridSpec(
            num_scalar_prefetch=2,
            grid=(steps,),
            in_specs=[
                part,
                whole,
                whole,
                part,
                part,
                pl.BlockSpec((heads, 1, BLOCK), lambda i, *_: (0, 0, i)),
                part,
                column,
                pl.BlockSpec((1, BLOCK), lambda i, *_: (0, i)),
                pl.BlockSpec((length, 1), lambda i, *_: (0, 0)),
            ],
            out_specs=(part, whole, whole, column),
            scratch_shapes=[
                pltpu.VMEM((heads, length, HEAD), LOW),
                pltpu.VMEM((heads, length, HEAD), LOW),
                pltpu.VMEM((cols, length), FULL),
                pltpu.VMEM((cols, length), FULL),
                pltpu.VMEM((cols, BLOCK), FULL),
            ],
        ),
        compiler_params=pltpu.CompilerParams(vmem_limit_bytes=48 * 2**20),
        cost_estimate=pl.CostEstimate(
            flops=8 * 5 * length * length * cols,
            bytes_accessed=8 * cols * length * 2,
            transcendentals=heads * length * length // 3,
        ),
    )(lo, hi, q, k, v, o, go, logs, raw, factor, segq, segk)


def remote(src, dst, sems, index, device):
    return pltpu.make_async_remote_copy(
        src_ref=src,
        dst_ref=dst,
        send_sem=sems[0].at[index],
        recv_sem=sems[1].at[index],
        device_id=device,
        device_id_type=pl.DeviceIdType.MESH,
    )


def greet(peers):
    barrier = pltpu.get_barrier_semaphore()
    for peer in peers:
        pl.semaphore_signal(barrier, inc=1, device_id=peer, device_id_type=pl.DeviceIdType.MESH)
    pl.semaphore_wait(barrier, len(peers))


def head_kernel(
    n_dp, n_pair, gain_ref, factor_ref, tokens_hbm, block_hbm, slab_hbm,
    q_hbm, k_hbm, v_hbm, raw_hbm, normed_hbm, qkv_hbm, slabs_hbm, inverse_ref,
    tokens, others, block, cs_recv, remote_block, pass_on, qkv, turned, normed, q, k, v, raw,
    send_sems, recv_sems, local_sems,
):
    r, s = lax.axis_index("row"), lax.axis_index("cs")
    j, d = lax.axis_index("cp"), lax.axis_index("dp")
    n_col = 2 * n_pair
    subs, width, piece = tokens.shape[1:]
    here = subs * piece
    share = cs_recv.shape[0]
    cols = q.shape[0]
    c_first = (s * n_pair + j) ^ (r * n_pair)
    near = r == s
    sems = (send_sems, recv_sems)
    counter, local_counter = iter(range(1000)), iter(range(1000))
    sent, stored = [], []

    def send(src, dst, device):
        copy = remote(src, dst, sems, next(counter), device)
        copy.start()
        sent.append(copy)
        return copy

    def move(src, dst):
        copy = pltpu.make_async_copy(src, dst, local_sems.at[next(local_counter)])
        copy.start()
        return copy

    def store(src, dst):
        stored.append(move(src, dst))

    def columns(u):
        return pl.ds(u * piece, piece)

    own_tokens = [move(tokens_hbm.at[:, columns(u)], tokens.at[0, u]) for u in range(subs)]
    own_block = move(block_hbm, block)
    store(slab_hbm, slabs_hbm.at[c_first])
    sibling_id = {"row": 1 - r}
    dp_ids = [{"dp": d ^ k} for k in range(1, n_dp)]
    col_ids = [{"cs": s ^ (k // n_pair), "cp": j ^ (k % n_pair)} for k in range(1, n_col)]
    greet([sibling_id] + dp_ids + col_ids)

    cs_copy = send(block_hbm.at[d], cs_recv, {"cs": 1 - s})
    other_copies = {}
    for u in range(subs):
        other_copies[0, u] = send(tokens_hbm.at[:, columns(u)], others.at[0, u], sibling_id)
    pair_copies = {}
    for u in range(subs):
        for m in range(1, n_pair):
            pair_copies[m, u] = send(
                tokens_hbm.at[:, columns(u)], tokens.at[m, u], {"cp": j ^ m}
            )

    def norm(m, u):
        own, other = tokens[m, u].astype(FULL), others[m, u].astype(FULL)
        squares = jnp.sum(own * own, axis=0, keepdims=True)
        squares = squares + jnp.sum(other * other, axis=0, keepdims=True)
        inverse = lax.rsqrt(squares / D + EPSILON)
        at = pl.ds(pl.multiple_of((j ^ m) * here + u * piece, 128), piece)
        normed[:width, at] = (own * inverse * gain_ref[:width]).astype(LOW)
        normed[width:, at] = (other * inverse * gain_ref[width:]).astype(LOW)
        store(normed.at[:, at], normed_hbm.at[:, at])
        if m == 0:
            inverse_ref[:, columns(u)] = inverse

    def project(m, u):
        at = pl.ds(pl.multiple_of((j ^ m) * here + u * piece, 128), piece)
        for part, out in ((0, None), (1, k), (2, v)):
            value = jnp.dot(
                turned[part * cols:(part + 1) * cols, :], normed[:, at],
                preferred_element_type=FULL,
            )
            if part == 0:
                raw[:, at] = value
                q[:, at] = (value * factor_ref[...]).astype(LOW)
            else:
                out[:, at] = value.astype(LOW)
        for src, dst in ((q, q_hbm), (k, k_hbm), (v, v_hbm), (raw, raw_hbm)):
            store(src.at[:, at], dst.at[:, at])

    for u in range(subs):
        own_tokens[u].wait()
        other_copies[0, u].wait_recv()
        norm(0, u)
    own_block.wait()

    cs_copy.wait_recv()
    dp_copies = [send(cs_recv, remote_block.at[d], peer) for peer in dp_ids]
    slab_copies = [send(slab_hbm, slabs_hbm.at[c_first], peer) for peer in col_ids]
    remote_block[d] = cs_recv[...]
    for u in range(subs - 1):
        for m in range(1, n_pair):
            pair_copies[m, u].wait_recv()
            other_copies[m, u] = send(tokens.at[m, u], others.at[m, u], sibling_id)
    cross_copies = []
    for m in range(n_dp):
        owner = d ^ m
        if m:
            dp_copies[m - 1].wait_recv()
        mine, its = block[owner], remote_block[owner]
        at = pl.multiple_of(owner * share, 32)
        qkv[pl.ds(at, share)] = jnp.where(near, mine, its)
        pass_on[owner] = jnp.where(near, its, mine)
        cross_copies.append(
            send(pass_on.at[owner], qkv.at[pl.ds(width + at, share)], sibling_id)
        )
    u = subs - 1
    for m in range(1, n_pair):
        pair_copies[m, u].wait_recv()
        other_copies[m, u] = send(tokens.at[m, u], others.at[m, u], sibling_id)
    turned[:, :width] = qkv[:width].T
    for copy in cross_copies:
        copy.wait_recv()
    turned[:, width:] = qkv[width:].T
    store(qkv, qkv_hbm)

    for u in range(subs):
        project(0, u)
    for u in range(subs):
        for m in range(1, n_pair):
            other_copies[m, u].wait_recv()
            norm(m, u)
            project(m, u)

    for copy in stored:
        copy.wait()
    for copy in slab_copies:
        copy.wait_recv()
    for copy in sent:
        copy.wait_send()


def head(n_dp, n_pair, gain, factor, tokens, block, slab):
    width, here = tokens.shape
    wide = block.shape[1]
    cols = wide // 3
    share = width // n_dp
    length = n_pair * here
    n_col = 2 * n_pair
    subs = 2
    piece = here // subs
    count = subs * n_pair * 2 + 2 * n_dp + n_col + 4
    moves = 3 + subs + 5 * subs * n_pair + 4
    hbm = pl.BlockSpec(memory_space=pl.ANY)
    vmem = pl.BlockSpec(memory_space=pltpu.VMEM)
    V = pltpu.VMEM
    shape = jax.ShapeDtypeStruct((cols, length), LOW)
    return pl.pallas_call(
        functools.partial(head_kernel, n_dp, n_pair),
        out_shape=(
            shape,
            shape,
            shape,
            jax.ShapeDtypeStruct((cols, length), FULL),
            jax.ShapeDtypeStruct((2 * width, length), LOW),
            jax.ShapeDtypeStruct((2 * width, wide), LOW),
            jax.ShapeDtypeStruct((n_col,) + slab.shape, LOW),
            jax.ShapeDtypeStruct((1, here), FULL),
        ),
        in_specs=[vmem] * 2 + [hbm] * 3,
        out_specs=(hbm,) * 7 + (vmem,),
        scratch_shapes=[
            V((n_pair, subs, width, piece), LOW),
            V((n_pair, subs, width, piece), LOW),
            V((n_dp, share, wide), LOW),
            V((share, wide), LOW),
            V((n_dp, share, wide), LOW),
            V((n_dp, share, wide), LOW),
            V((2 * width, wide), LOW),
            V((wide, 2 * width), LOW),
            V((2 * width, length), LOW),
            V((cols, length), LOW),
            V((cols, length), LOW),
            V((cols, length), LOW),
            V((cols, length), FULL),
            pltpu.SemaphoreType.DMA((count,)),
            pltpu.SemaphoreType.DMA((count,)),
            pltpu.SemaphoreType.DMA((moves,)),
        ],
        compiler_params=pltpu.CompilerParams(
            collective_id=2, has_side_effects=True, vmem_limit_bytes=60 * 2**20
        ),
        cost_estimate=pl.CostEstimate(
            flops=4 * wide * width * length, bytes_accessed=2**25, transcendentals=0
        ),
    )(gain, factor, tokens, block.reshape(n_dp, share, wide), slab)


def middle_kernel(n_dp, n_pair, unit, gain_ref, att_hbm, tokens_hbm, cot_hbm, *refs):
    n_col = 2 * n_pair
    slab_hbms, refs = refs[:n_dp], refs[n_dp:]
    down_hbms, refs = refs[:n_col], refs[n_col:]
    result_hbm, middle_hbm, out_hbm, refs = refs[0], refs[1], refs[2], refs[3:]
    grads_hbms, refs = refs[:n_dp], refs[n_dp:]
    (
        gain_out, tokens, cot, slab, out_w, up_w, down_w, out_t, up_t, down_t, out_half, up_half,
        down_half, att, normed, active, grad_hidden, branch, middle, grad, result, grad_att, grads,
        square_send, square_recv, inner_send, inner_recv, inverse, narrow,
        send_sems, recv_sems, local_sems,
    ) = refs
    r, s = lax.axis_index("row"), lax.axis_index("cs")
    j, d = lax.axis_index("cp"), lax.axis_index("dp")
    width, here = tokens.shape
    pieces, _, piece = square_send.shape
    cols = att_hbm.shape[0]
    half = n_col * unit // 2
    rows_q = slab_hbms[0].shape[1]
    rows_g = grads_hbms[0].shape[1]
    c_first = (s * n_pair + j) ^ (r * n_pair)
    sems = (send_sems, recv_sems)
    counter, local_counter = iter(range(1000)), iter(range(1000))
    sent, stored = [], []

    def send(src, dst, device):
        copy = remote(src, dst, sems, next(counter), device)
        copy.start()
        sent.append(copy)
        return copy

    def move(src, dst):
        copy = pltpu.make_async_copy(src, dst, local_sems.at[next(local_counter)])
        copy.start()
        return copy

    def columns(u):
        return pl.ds(u * piece, piece)

    def span(u):
        return slice(u * piece, (u + 1) * piece)

    own_rows, other_rows = pl.ds(0, width), pl.ds(width, width)
    weight_loads = [
        move(slab_hbms[m], slab.at[:, pl.ds(pl.multiple_of((d ^ m) * rows_q, 16), rows_q)])
        for m in range(n_dp)
    ] + [
        move(down_hbms[m], down_w.at[pl.ds(pl.multiple_of((c_first ^ m) * unit, 16), unit)])
        for m in range(n_col)
    ]
    att_loads = [
        move(
            att_hbm.at[:, pl.ds(pl.multiple_of(j * here + u * piece, 128), piece)],
            att.at[pl.ds(pl.multiple_of(j * cols, 16), cols), columns(u)],
        )
        for u in range(pieces)
    ]
    token_load = move(tokens_hbm, tokens)
    cot_load = move(cot_hbm, cot.at[own_rows])
    sibling_id = {"row": 1 - r}
    pair_ids = [{"cp": j ^ m} for m in range(1, n_pair)]
    greet([sibling_id] + pair_ids)

    att_copies = {}
    for u in range(pieces):
        for m in range(1, n_pair):
            att_copies[u, m] = send(
                att_hbm.at[:, pl.ds(pl.multiple_of((j ^ m) * here + u * piece, 128), piece)],
                att.at[pl.ds(pl.multiple_of(j * cols, 16), cols), columns(u)],
                pair_ids[m - 1],
            )
    cot_copy = send(cot_hbm, cot.at[other_rows], sibling_id)

    for copy in weight_loads:
        copy.wait()
    for m in range(n_col):
        at = slice(m * unit, (m + 1) * unit)
        out_w[at] = slab[m, :unit]
        up_w[at] = slab[m, unit:2 * unit]
    cross_copies = [
        send(whole.at[pl.ds(half, half)], part.at[:, other_rows], sibling_id)
        for whole, part in ((up_w, up_half), (down_w, down_half), (out_w, out_half))
    ]
    for whole, part in ((up_w, up_half), (down_w, down_half), (out_w, out_half)):
        part[:, :width] = whole[:half]
    out_t[...] = out_w[...].T
    narrow[...] = jnp.zeros_like(narrow)

    copies = {}

    def exchange(name, u, ref):
        copies[name, u] = send(
            ref.at[own_rows, columns(u)], ref.at[other_rows, columns(u)], sibling_id
        )

    def share_heads(u):
        att_loads[u].wait()
        for m in range(1, n_pair):
            att_copies[u, m].wait_recv()
        exchange("att", u, att)

    def first_branch(u):
        if u == 0:
            token_load.wait()
        copies["att", u].wait_recv()
        value = tokens[:, span(u)].astype(FULL) + jnp.dot(
            out_t[...], att[:, span(u)], preferred_element_type=FULL
        )
        middle[:, span(u)] = value
        square_send[u] = jnp.sum(value * value, axis=0, keepdims=True)
        copies["square", u] = send(square_send.at[u], square_recv.at[u], sibling_id)

    def second_norm(u):
        copies["square", u].wait_recv()
        scale = lax.rsqrt((square_send[u] + square_recv[u]) / D + EPSILON)
        inverse[u] = scale
        normed[:width, span(u)] = (middle[:, span(u)] * scale * gain_ref[...]).astype(LOW)
        exchange("normed", u, normed)

    def hidden_units(u):
        if u == 0:
            cot_load.wait()
            cot_copy.wait_recv()
            for copy in cross_copies:
                copy.wait_recv()
            up_t[...] = up_w[...].T
            down_t[...] = down_w[...].T
        grad_active = jnp.dot(down_half[...], cot[:, span(u)], preferred_element_type=FULL)
        copies["normed", u].wait_recv()
        hidden = jnp.dot(up_half[...], normed[:, span(u)], preferred_element_type=FULL)
        sigmoid = jax.nn.sigmoid(hidden)
        grad_hidden[:half, span(u)] = (
            grad_active * sigmoid * (1.0 + hidden * (1.0 - sigmoid))
        ).astype(LOW)
        exchange("grad_hidden", u, grad_hidden)
        active[:half, span(u)] = (hidden * sigmoid).astype(LOW)
        exchange("active", u, active)

    def second_branch(u):
        copies["grad_hidden", u].wait_recv()
        value = jnp.dot(up_t[...], grad_hidden[:, span(u)], preferred_element_type=FULL)
        grad[:, span(u)] = value
        product = value * middle[:, span(u)]
        inner_send[u] = jnp.sum(product * gain_ref[...], axis=0, keepdims=True)
        copies["inner", u] = send(inner_send.at[u], inner_recv.at[u], sibling_id)
        product = product * inverse[u]
        total = narrow[...]
        for v in range(piece // 128):
            total = total + product[:, v * 128:(v + 1) * 128]
        narrow[...] = total
        copies["active", u].wait_recv()
        result[:, span(u)] = middle[:, span(u)] + jnp.dot(
            down_t[...], active[:, span(u)], preferred_element_type=FULL
        )
        stored.append(move(result.at[:, columns(u)], result_hbm.at[:, columns(u)]))

    def norm_back(u):
        copies["inner", u].wait_recv()
        scale = inverse[u]
        inner = scale * scale * scale * ((inner_send[u] + inner_recv[u]) / D)
        value = (
            cot[:width, span(u)].astype(FULL)
            + scale * (grad[:, span(u)] * gain_ref[...])
            - middle[:, span(u)] * inner
        )
        grad[:, span(u)] = value
        stored.append(move(grad.at[:, columns(u)], middle_hbm.at[:, columns(u)]))
        branch[:width, span(u)] = value.astype(LOW)
        exchange("branch", u, branch)

    def heads_back(u):
        copies["branch", u].wait_recv()
        grad_att[:, span(u)] = jnp.dot(
            out_half[...], branch[:, span(u)], preferred_element_type=FULL
        ).astype(LOW)
        target = pl.ds(pl.multiple_of(j * here + u * piece, 128), piece)
        for m in range(n_pair):
            source = grad_att.at[
                pl.ds(pl.multiple_of((j ^ m) * cols, 16), cols), columns(u)
            ]
            if m:
                copies["out", u, m] = send(source, out_hbm.at[:, target], pair_ids[m - 1])
            else:
                stored.append(move(source, out_hbm.at[:, target]))

    stages = (
        share_heads, first_branch, second_norm, hidden_units, second_branch, norm_back, heads_back,
    )
    for t in range(pieces + len(stages) - 1):
        for number in reversed(range(len(stages))):
            if 0 <= t - number < pieces:
                stages[number](t - number)

    if grads.shape[1] > 3 * unit:
        grads[...] = jnp.zeros_like(grads)
    for m, (left, right) in enumerate(((active, cot), (grad_hidden, normed), (att, branch))):
        turned = right[:width].T
        for n in range(n_col):
            grads[n, (2 - m) * unit:(3 - m) * unit] = jnp.dot(
                left[n * unit:(n + 1) * unit], turned, preferred_element_type=FULL
            ).astype(LOW)
    for m in range(n_dp):
        at = pl.ds(pl.multiple_of((d ^ m) * rows_g, 16), rows_g)
        stored.append(move(grads.at[:, at], grads_hbms[m]))
    gain_out[...] = jnp.sum(narrow[...].T, axis=0, keepdims=True)

    for u in range(pieces):
        for m in range(1, n_pair):
            copies["out", u, m].wait_recv()
    for copy in stored:
        copy.wait()
    for copy in sent:
        copy.wait_send()


def middle_part(n_dp, n_pair, gain, attended, tokens, cotangent, slabs, downs):
    width, here = tokens.shape
    n_col = 2 * n_pair
    cols, length = attended.shape
    unit = downs[0].shape[0]
    half = n_col * unit // 2
    rows_q = slabs[0].shape[1]
    rows_g = quarter_rows(3 * unit, n_dp)
    pieces = max(2, here // 256)
    piece = here // pieces
    count = 2 * pieces * (n_pair - 1) + 7 * pieces + 8
    moves = n_dp + n_col + 4 * pieces + 4 + n_dp
    hbm = pl.BlockSpec(memory_space=pl.ANY)
    vmem = pl.BlockSpec(memory_space=pltpu.VMEM)
    V = pltpu.VMEM
    S = jax.ShapeDtypeStruct
    weight = V((2 * half, width), LOW)
    weight_t = V((width, 2 * half), LOW)
    both = V((2 * width, here), LOW)
    whole = V((width, here), FULL)
    row = V((pieces, 1, piece), FULL)
    out = pl.pallas_call(
        functools.partial(middle_kernel, n_dp, n_pair, unit),
        out_shape=(
            S((width, here), FULL),
            S((width, here), FULL),
            S((cols, length), LOW),
        )
        + (S((n_col, rows_g, width), LOW),) * n_dp
        + (S((1, width), FULL),),
        in_specs=[vmem] + [hbm] * (3 + n_dp + n_col),
        out_specs=(hbm,) * (3 + n_dp) + (vmem,),
        scratch_shapes=[
            V((width, here), LOW),
            both,
            V((n_col, n_dp * rows_q, width), LOW),
            weight,
            weight,
            weight,
            weight_t,
            weight_t,
            weight_t,
            V((half, 2 * width), LOW),
            V((half, 2 * width), LOW),
            V((half, 2 * width), LOW),
            both,
            both,
            V((2 * half, here), LOW),
            V((2 * half, here), LOW),
            both,
            whole,
            whole,
            whole,
            V((width, here), LOW),
            V((n_col, n_dp * rows_g, width), LOW),
            row,
            row,
            row,
            row,
            row,
            V((width, 128), FULL),
            pltpu.SemaphoreType.DMA((count,)),
            pltpu.SemaphoreType.DMA((count,)),
            pltpu.SemaphoreType.DMA((moves,)),
        ],
        compiler_params=pltpu.CompilerParams(
            collective_id=3, has_side_effects=True, vmem_limit_bytes=62 * 2**20
        ),
        cost_estimate=pl.CostEstimate(
            flops=18 * 2 * half * width * here, bytes_accessed=2**25, transcendentals=0
        ),
    )(gain, attended, tokens, cotangent, *slabs, *downs)
    return out[0], out[1], out[2], out[3:3 + n_dp], out[3 + n_dp]


def quarter_rows(rows, n_dp):
    return -(-rows // (16 * n_dp)) * 16


def tail_kernel(
    n_dp, n_pair, gain_ref, inverse_ref, sums_ref, qkv_hbm, dq_hbm, dk_hbm, dv_hbm, normed_hbm,
    tokens_hbm, middle_hbm, *refs,
):
    grads_hbms, refs = refs[:n_dp], refs[n_dp:]
    (
    result_hbm, qkv_out, grads_out, sums_out,
    qkv, dproj, normed, tokens, middle, result, row_send, row_recv, own, pair_send, pair_recv,
    dp_send, dp_recv, dp_own, cross_send, cross_recv, cs_send, cs_recv, final, grads_parts,
    grads_send, grads_recv, grads_final, inner_send, inner_recv, sums_send, sums_recv,
    send_sems, recv_sems, local_sems,
    ) = refs
    r, s = lax.axis_index("row"), lax.axis_index("cs")
    j, d = lax.axis_index("cp"), lax.axis_index("dp")
    n_col = 2 * n_pair
    width, here = tokens.shape
    cols = dq_hbm.shape[0]
    share = width // n_dp
    subs = row_send.shape[1]
    piece = here // subs
    c_first = (s * n_pair + j) ^ (r * n_pair)
    sems = (send_sems, recv_sems)
    counter = iter(range(1000))
    sent = []

    def send(src, dst, device):
        copy = remote(src, dst, sems, next(counter), device)
        copy.start()
        sent.append(copy)
        return copy

    local = []

    def load(src, dst):
        copy = pltpu.make_async_copy(src, dst, local_sems.at[len(local)])
        copy.start()
        local.append(copy)
        return copy

    early = [
        load(qkv_hbm, qkv),
        load(dq_hbm, dproj.at[pl.ds(0, cols)]),
        load(dk_hbm, dproj.at[pl.ds(cols, cols)]),
        load(dv_hbm, dproj.at[pl.ds(2 * cols, cols)]),
    ]
    load_normed = load(normed_hbm, normed)
    load_grads = [load(grads_hbms[k], grads_parts.at[k]) for k in range(n_dp)]
    late = [load(tokens_hbm, tokens), load(middle_hbm, middle)]

    sibling_id = {"row": 1 - r}
    dp_ids = [{"dp": d ^ k} for k in range(1, n_dp)]
    col_ids = [
        {"cs": s ^ (k // n_pair), "cp": j ^ (k % n_pair)} for k in range(1, n_col)
    ]
    greet([sibling_id] + dp_ids + col_ids)

    for copy in early:
        copy.wait()

    def rows_of(half, chunk, u):
        at = pl.ds(pl.multiple_of(chunk * here + u * piece, 128), piece)
        return jnp.dot(
            qkv[half * width:(half + 1) * width, :], dproj[:, at], preferred_element_type=FULL
        )

    row_copies = {}
    for k in range(1, n_pair):
        for u in range(subs):
            row_send[k, u] = rows_of(1, j ^ k, u).astype(LOW)
            row_copies[k, u] = send(row_send.at[k, u], row_recv.at[k, u], sibling_id)
    pair_copies = []
    for k in range(1, n_pair):
        for u in range(subs):
            part = rows_of(0, j ^ k, u)
            row_copies[k, u].wait_recv()
            pair_send[k - 1, u] = (part + row_recv[k, u].astype(FULL)).astype(LOW)
            pair_copies.append(
                send(pair_send.at[k - 1, u], pair_recv.at[k - 1, u], {"cp": j ^ k})
            )

    load_normed.wait()

    def quarter(half, owner):
        at = pl.ds(pl.multiple_of(half * width + owner * share, 32), share)
        return mm(normed[at, :], dproj[...], 1, 1)

    dp_copies = []
    for k in range(1, n_dp):
        for half in range(2):
            dp_send[k - 1, half] = quarter(half, d ^ k).astype(LOW)
        dp_copies.append(send(dp_send.at[k - 1], dp_recv.at[k - 1], dp_ids[k - 1]))
    for half in range(2):
        dp_own[half] = quarter(half, d)

    for copy in load_grads:
        copy.wait()

    def summed(place_at):
        value = grads_parts[0, place_at].astype(FULL)
        for k in range(1, n_dp):
            value = value + grads_parts[k, place_at].astype(FULL)
        return value

    grads_copies = []
    for k in range(1, n_col):
        grads_send[k - 1] = summed(c_first ^ k).astype(LOW)
        grads_copies.append(send(grads_send.at[k - 1], grads_recv.at[k - 1], col_ids[k - 1]))

    for u in range(subs):
        row_send[0, u] = rows_of(1, j, u).astype(LOW)
        row_copies[0, u] = send(row_send.at[0, u], row_recv.at[0, u], sibling_id)
    for u in range(subs):
        own[u] = rows_of(0, j, u)
    for copy in late:
        copy.wait()

    for copy in dp_copies:
        copy.wait_recv()

    def total(half):
        value = dp_own[half]
        for k in range(1, n_dp):
            value = value + dp_recv[k - 1, half].astype(FULL)
        return value

    cross_send[...] = total(1).astype(LOW)
    cross_copy = send(cross_send, cross_recv, sibling_id)
    dp_own[0] = total(0)
    cross_copy.wait_recv()
    near = r == s
    kept, crossed = dp_own[0], cross_recv[...].astype(FULL)
    cs_send[...] = jnp.where(near, crossed, kept).astype(LOW)
    cs_copy = send(cs_send, cs_recv, {"cs": 1 - s})
    dp_own[1] = jnp.where(near, kept, crossed)

    for copy in pair_copies:
        copy.wait_recv()
    inverse = inverse_ref[...]
    for u in range(subs):
        row_copies[0, u].wait_recv()
        at = slice(u * piece, (u + 1) * piece)
        value = own[u] + row_recv[0, u].astype(FULL)
        for k in range(1, n_pair):
            value = value + pair_recv[k - 1, u].astype(FULL)
        own[u] = value
        inner_send[:, at] = jnp.sum(
            value * gain_ref[...] * tokens[:, at].astype(FULL), axis=0, keepdims=True
        )
    inner_copy = send(inner_send, inner_recv, sibling_id)
    narrow = jnp.zeros((width, 128), FULL)
    for u in range(subs):
        at = slice(u * piece, (u + 1) * piece)
        wide = own[u] * tokens[:, at].astype(FULL) * inverse[:, at]
        for v in range(piece // 128):
            narrow = narrow + wide[:, v * 128:(v + 1) * 128]
    gain_part = jnp.sum(narrow.T, axis=0, keepdims=True)
    sums_send[0] = jnp.concatenate([gain_part, sums_ref[1:]], 0)
    inner_copy.wait_recv()
    inner = (inner_send[...] + inner_recv[...]) / D
    for u in range(subs):
        at = slice(u * piece, (u + 1) * piece)
        result[:, at] = (
            middle[:, at]
            + inverse[:, at] * (own[u] * gain_ref[...])
            - tokens[:, at].astype(FULL)
            * (inverse[:, at] * inverse[:, at] * inverse[:, at] * inner[:, at])
        )
    result_copy = pltpu.make_async_copy(result, result_hbm, local_sems.at[len(local)])
    result_copy.start()

    cs_copy.wait_recv()
    final[...] = (dp_own[1] + cs_recv[...].astype(FULL)).astype(LOW)
    out_copies = [send(final, qkv_out.at[d], peer) for peer in dp_ids]
    final_copy = pltpu.make_async_copy(final, qkv_out.at[d], local_sems.at[len(local) + 1])
    final_copy.start()

    for copy in grads_copies:
        copy.wait_recv()
    value = summed(c_first)
    for k in range(1, n_col):
        value = value + grads_recv[k - 1].astype(FULL)
    grads_final[...] = value.astype(LOW)
    out_copies += [send(grads_final, grads_out.at[d], peer) for peer in dp_ids]
    grads_copy = pltpu.make_async_copy(grads_final, grads_out.at[d], local_sems.at[len(local) + 2])
    grads_copy.start()

    steps = []
    for name, me, n in (("dp", d, n_dp), ("cs", s, 2), ("cp", j, n_pair)):
        k = 1
        while k < n:
            steps.append({name: me ^ k})
            k *= 2
    for t, peer in enumerate(steps):
        copy = send(sums_send.at[t], sums_recv.at[t], peer)
        copy.wait_recv()
        sums_send[t + 1] = sums_send[t] + sums_recv[t]
    last = len(steps)
    copy = send(sums_send.at[last], sums_recv.at[last], sibling_id)
    copy.wait_recv()
    sums_out[0] = sums_send[last]
    sums_out[1] = sums_recv[last]

    for copy in out_copies:
        copy.wait_recv()
    result_copy.wait()
    final_copy.wait()
    grads_copy.wait()
    for copy in sent:
        copy.wait_send()


def tail(n_dp, n_pair, gain, inverse, sums, qkv, dq, dk, dv, normed, tokens, middle, grads):
    width, here = tokens.shape
    length = normed.shape[1]
    cols = dq.shape[0]
    share = width // n_dp
    subs = 2
    piece = here // subs
    n_col = 2 * n_pair
    part = grads[0].shape[1:]
    wide = 3 * cols
    steps = (n_dp * n_col).bit_length()
    count = 2 * n_pair * subs + 3 * n_dp + n_col + steps + 6
    hbm = pl.BlockSpec(memory_space=pl.ANY)
    vmem = pl.BlockSpec(memory_space=pltpu.VMEM)
    V = pltpu.VMEM
    return pl.pallas_call(
        functools.partial(tail_kernel, n_dp, n_pair),
        out_shape=(
            jax.ShapeDtypeStruct((width, here), FULL),
            jax.ShapeDtypeStruct((n_dp, share, wide), LOW),
            jax.ShapeDtypeStruct((n_dp,) + part, LOW),
            jax.ShapeDtypeStruct((2,) + sums.shape, FULL),
        ),
        in_specs=[vmem] * 3 + [hbm] * (7 + n_dp),
        out_specs=(hbm, hbm, hbm, vmem),
        scratch_shapes=[
            V((2 * width, wide), LOW),
            V((wide, length), LOW),
            V((2 * width, length), LOW),
            V((width, here), LOW),
            V((width, here), FULL),
            V((width, here), FULL),
            V((n_pair, subs, width, piece), LOW),
            V((n_pair, subs, width, piece), LOW),
            V((subs, width, piece), FULL),
            V((n_pair - 1, subs, width, piece), LOW),
            V((n_pair - 1, subs, width, piece), LOW),
            V((n_dp - 1, 2, share, wide), LOW),
            V((n_dp - 1, 2, share, wide), LOW),
            V((2, share, wide), FULL),
            V((share, wide), LOW),
            V((share, wide), LOW),
            V((share, wide), LOW),
            V((share, wide), LOW),
            V((share, wide), LOW),
            V((n_dp, n_col) + part, LOW),
            V((n_col - 1,) + part, LOW),
            V((n_col - 1,) + part, LOW),
            V(part, LOW),
            V((1, here), FULL),
            V((1, here), FULL),
            V((steps + 1,) + sums.shape, FULL),
            V((steps + 1,) + sums.shape, FULL),
            pltpu.SemaphoreType.DMA((count,)),
            pltpu.SemaphoreType.DMA((count,)),
            pltpu.SemaphoreType.DMA((11 + n_dp,)),
        ],
        compiler_params=pltpu.CompilerParams(
            collective_id=1, has_side_effects=True, vmem_limit_bytes=60 * 2**20
        ),
        cost_estimate=pl.CostEstimate(
            flops=8 * wide * width * length, bytes_accessed=2**25, transcendentals=0
        ),
    )(gain, inverse, sums, qkv, dq, dk, dv, normed, tokens, middle, *grads)


def on_device(
    tokens,
    segment_ids,
    padding_mask,
    w_qkv,
    w_out,
    w_up,
    w_down,
    gain_attn,
    gain_mlp,
    scale_raw,
    cotangent,
):
    width, here = tokens.shape
    r, s = lax.axis_index("row"), lax.axis_index("cs")
    j, d = lax.axis_index("cp"), lax.axis_index("dp")
    n_pair, n_dp, n_col = lax.axis_size("cp"), lax.axis_size("dp"), lax.axis_size(COLS)
    c = s * n_pair + j
    head_cols = w_qkv.shape[0] // (3 * width)
    heads = head_cols // HEAD
    near = r == s

    segments = jnp.where(s == r, segment_ids[0], sibling(segment_ids)[0])
    padding = jnp.where(s == r, padding_mask[0], sibling(padding_mask)[0])
    length = segments.shape[0]
    firsts = segments[::BLOCK]
    starts = jnp.sum((segments[None, :] < firsts[:, None]).astype(jnp.int32), axis=1)
    filled = (jnp.sum(padding) + BLOCK - 1) // BLOCK
    blocks = jnp.arange(length // BLOCK, dtype=jnp.int32)
    lo = starts // BLOCK
    hi = jnp.minimum(blocks, filled)
    segq = segments[None, :]
    segk = jnp.where(padding == 1, segments, -1)[:, None]

    def halves(vector):
        whole = vector.reshape(2, width)
        own = lax.dynamic_index_in_dim(whole, r, 0, keepdims=False)
        other = lax.dynamic_index_in_dim(whole, 1 - r, 0, keepdims=False)
        return own[:, None], other[:, None]

    gain_one, gain_one_other = halves(gain_attn)
    gain_two, _ = halves(gain_mlp)
    factor = (LOG_TWO_E / math.sqrt(HEAD) * jnp.log1p(jnp.exp(scale_raw)))[:, None]

    block = w_qkv.reshape(width, 3 * head_cols)
    unit = w_up.shape[0] // width
    slab = jnp.concatenate([w_out.reshape(-1, width), w_up.reshape(width, -1).T], 0)
    slab_rows = quarter_rows(2 * unit, n_dp)
    slab = jnp.pad(slab, ((0, n_dp * slab_rows - 2 * unit), (0, 0)))
    slab = cut(slab, d, n_dp, 0)
    queries, key_heads, values, query_raw, normed_one, qkv, slabs, inverse_one = head(
        n_dp, n_pair, jnp.concatenate([gain_one, gain_one_other], 0), jnp.tile(factor, (heads, 1)),
        tokens, block, slab,
    )
    slabs = gather(slabs, "dp")
    down = w_down.reshape(-1, width)
    downs = [down] + [
        lax.ppermute(down, COLS, [(i, i ^ k) for i in range(n_col)]) for k in range(1, n_col)
    ]
    attended, logs = attention_forward(queries, key_heads, values, segq, segk, lo, hi)
    result, grad_middle, grad_attended, grads, gain_two_part = middle_part(
        n_dp, n_pair, gain_two, attended, tokens, cotangent, slabs, downs
    )
    received = [grads[0]] + [shift(grads[k], "dp", k) for k in range(1, n_dp)]

    dq, dk, dv, scale_part = attention_backward(
        queries, key_heads, values, attended, grad_attended, logs, query_raw, factor,
        segq, segk, lo, hi,
    )
    scale_part = (
        scale_part[:, 0] * (LOG_TWO_E / math.sqrt(HEAD)) * jax.nn.sigmoid(scale_raw)
    )
    sums = jnp.concatenate(
        [
            jnp.zeros((1, width), FULL),
            gain_two_part,
            jnp.pad(scale_part, (0, width - HEAD))[None],
            jnp.zeros((5, width), FULL),
        ]
    )
    grad_tokens, grad_qkv, final, sums = tail(
        n_dp, n_pair, gain_one, inverse_one, sums, qkv, dq, dk, dv, normed_one, tokens,
        grad_middle, received,
    )
    grad_qkv = grad_qkv.astype(FULL)
    final = final.reshape(-1, width)
    final = [final[i * unit:(i + 1) * unit].astype(FULL) for i in range(3)]
    own, other = sums[0], sums[1]
    first = r == 0
    gains = jnp.concatenate(
        [jnp.where(first, own[:2], other[:2]), jnp.where(first, other[:2], own[:2])], 1
    )
    scale_total = (own[2] + other[2])[:HEAD]
    return (
        result,
        grad_tokens,
        grad_qkv.reshape(-1),
        final[0].reshape(-1),
        final[1].T.reshape(-1),
        final[2].reshape(-1),
        gains[0],
        gains[1],
        scale_total,
    )


def solution(mesh):
    n_dp, n_row, n_col = (mesh.shape[name] for name in ("dp", "row", "col"))
    split = Mesh(
        np.asarray(mesh.devices).reshape(n_dp, n_row, n_row, n_col // n_row),
        ("dp", "row", "cs", "cp"),
    )
    rows = P("row", ("dp", "cs", "cp"))
    ids = P(("dp", "row"), None)
    blocks = P(("row", "cs", "cp"))
    return jax.shard_map(
        on_device,
        mesh=split,
        in_specs=(rows, ids, ids, blocks, blocks, blocks, blocks, P(), P(), P(), rows),
        out_specs=(rows, rows, blocks, blocks, blocks, blocks, P(), P(), P()),
        check_vma=False,
    )
```

```python
import functools
import math

import jax
import jax.numpy as jnp
import numpy as np
from jax import lax
from jax.experimental import pallas as pl
from jax.experimental.pallas import tpu as pltpu
from jax.sharding import Mesh, PartitionSpec as P

D = 1280
HEAD = 80
EPSILON = 1e-06
LOG_TWO_E = 1.442695041
BLOCK = 256
LOW = jnp.bfloat16
FULL = jnp.float32
COLS = ("cs", "cp")


def mm(left, right, left_axis, right_axis):
    return lax.dot_general(
        left, right, (((left_axis,), (right_axis,)), ((), ())), preferred_element_type=FULL
    )


def shift(x, axis, k):
    n = lax.axis_size(axis)
    return lax.ppermute(x, axis, [(i, i ^ k) for i in range(n)])


def sibling(x):
    return shift(x, "row", 1)


def cut(x, index, count, axis):
    step = x.shape[axis] // count
    return lax.dynamic_slice_in_dim(x, index * step, step, axis)


def gather(x, axis):
    return [x] + [shift(x, axis, k) for k in range(1, lax.axis_size(axis))]


def diag_mask(segq, segk):
    size = segk.shape[0], segq.shape[1]
    ki = lax.broadcasted_iota(jnp.int32, size, 0)
    qi = lax.broadcasted_iota(jnp.int32, size, 1)
    return ((segk == segq) & (ki <= qi)) | (ki == qi)


def forward_kernel(heads, lo_ref, hi_ref, q_ref, k_ref, v_ref, segq_ref, segk_ref, o_ref, log_ref, ks):
    i = pl.program_id(0)

    @pl.when(i == 0)
    def _():
        for h in range(heads):
            ks[h] = k_ref[h * HEAD:(h + 1) * HEAD, :].T

    segq = segq_ref[...]

    def visit(kb, carry, diagonal):
        at = pl.ds(pl.multiple_of(kb * BLOCK, BLOCK), BLOCK)
        segk = segk_ref[at, :]
        mask = diag_mask(segq, segk) if diagonal else segk == segq
        out = []
        for h in range(heads):
            rows = slice(h * HEAD, (h + 1) * HEAD)
            s = jnp.dot(ks[h, at, :], q_ref[rows, :], preferred_element_type=FULL)
            s = jnp.where(mask, s, -1e30)
            peak = jnp.max(s, axis=0, keepdims=True)
            if not diagonal:
                m, l, acc = carry[h]
                peak = jnp.maximum(m, peak)
            p = jnp.exp(s - peak)
            total = jnp.sum(p, axis=0, keepdims=True)
            new = jnp.dot(v_ref[rows, at], p.astype(LOW), preferred_element_type=FULL)
            if not diagonal:
                keep = jnp.exp(m - peak)
                total = l * keep + total
                new = acc * keep + new
            out.append((peak, total, new))
        return tuple(out)

    carry = visit(i, None, True)
    carry = lax.fori_loop(lo_ref[i], hi_ref[i], lambda kb, c: visit(kb, c, False), carry)
    for h in range(heads):
        m, l, acc = carry[h]
        o_ref[h * HEAD:(h + 1) * HEAD, :] = (acc / l).astype(LOW)
        log_ref[h] = m + jnp.log(l)


def attention_forward(q, k, v, segq, segk, lo, hi):
    cols, length = q.shape
    heads = cols // HEAD
    steps = length // BLOCK
    whole = pl.BlockSpec((cols, length), lambda i, *_: (0, 0))
    part = pl.BlockSpec((cols, BLOCK), lambda i, *_: (0, i))
    return pl.pallas_call(
        functools.partial(forward_kernel, heads),
        out_shape=(
            jax.ShapeDtypeStruct((cols, length), LOW),
            jax.ShapeDtypeStruct((heads, 1, length), FULL),
        ),
        grid_spec=pltpu.PrefetchScalarGridSpec(
            num_scalar_prefetch=2,
            grid=(steps,),
            in_specs=[
                part,
                whole,
                whole,
                pl.BlockSpec((1, BLOCK), lambda i, *_: (0, i)),
                pl.BlockSpec((length, 1), lambda i, *_: (0, 0)),
            ],
            out_specs=(part, pl.BlockSpec((heads, 1, BLOCK), lambda i, *_: (0, 0, i))),
            scratch_shapes=[pltpu.VMEM((heads, length, HEAD), LOW)],
        ),
        compiler_params=pltpu.CompilerParams(vmem_limit_bytes=62 * 2**20),
        cost_estimate=pl.CostEstimate(
            flops=8 * 2 * length * length * cols,
            bytes_accessed=4 * cols * length * 2,
            transcendentals=heads * length * length // 3,
        ),
    )(lo, hi, q, k, v, segq, segk)


def backward_kernel(
    heads, lo_ref, hi_ref, q_ref, k_ref, v_ref, o_ref, go_ref, log_ref, raw_ref, factor_ref,
    segq_ref, segk_ref, dq_ref, dk_ref, dv_ref, scale_ref, ks, vs, dks, dvs, dqs,
):
    i = pl.program_id(0)

    @pl.when(i == 0)
    def _():
        for h in range(heads):
            ks[h] = k_ref[h * HEAD:(h + 1) * HEAD, :].T
            vs[h] = v_ref[h * HEAD:(h + 1) * HEAD, :].T
        dks[...] = jnp.zeros_like(dks)
        dvs[...] = jnp.zeros_like(dvs)
        scale_ref[...] = jnp.zeros_like(scale_ref)

    segq = segq_ref[...]
    inner = [
        jnp.sum(
            o_ref[h * HEAD:(h + 1) * HEAD, :].astype(FULL)
            * go_ref[h * HEAD:(h + 1) * HEAD, :].astype(FULL),
            axis=0,
            keepdims=True,
        )
        for h in range(heads)
    ]

    def visit(kb, diagonal):
        at = pl.ds(pl.multiple_of(kb * BLOCK, BLOCK), BLOCK)
        segk = segk_ref[at, :]
        mask = diag_mask(segq, segk) if diagonal else segk == segq
        for h in range(heads):
            rows = slice(h * HEAD, (h + 1) * HEAD)
            q = q_ref[rows, :]
            go = go_ref[rows, :]
            s = jnp.dot(ks[h, at, :], q, preferred_element_type=FULL)
            p = jnp.where(mask, jnp.exp(s - log_ref[h]), 0.0)
            dp = jnp.dot(vs[h, at, :], go, preferred_element_type=FULL)
            ds = (p * (dp - inner[h])).astype(LOW)
            new = jnp.dot(k_ref[rows, at], ds, preferred_element_type=FULL)
            if diagonal:
                dqs[rows, :] = new
            else:
                dqs[rows, :] += new
            dks[rows, at] += mm(q, ds, 1, 1)
            dvs[rows, at] += mm(go, p.astype(LOW), 1, 1)

    visit(i, True)

    @pl.loop(lo_ref[i], hi_ref[i])
    def _(kb):
        visit(kb, False)

    factor = factor_ref[...]
    part = jnp.zeros((HEAD, 1), FULL)
    for h in range(heads):
        rows = slice(h * HEAD, (h + 1) * HEAD)
        dq = dqs[rows, :]
        part = part + jnp.sum(dq * raw_ref[rows, :], axis=1, keepdims=True)
        dq_ref[rows, :] = (dq * factor).astype(LOW)
    scale_ref[...] += part

    @pl.when(i == pl.num_programs(0) - 1)
    def _():
        dk_ref[...] = dks[...].astype(LOW)
        dv_ref[...] = dvs[...].astype(LOW)


def attention_backward(q, k, v, o, go, logs, raw, factor, segq, segk, lo, hi):
    cols, length = q.shape
    heads = cols // HEAD
    steps = length // BLOCK
    whole = pl.BlockSpec((cols, length), lambda i, *_: (0, 0))
    part = pl.BlockSpec((cols, BLOCK), lambda i, *_: (0, i))
    column = pl.BlockSpec((HEAD, 1), lambda i, *_: (0, 0))
    shape = jax.ShapeDtypeStruct((cols, length), LOW)
    return pl.pallas_call(
        functools.partial(backward_kernel, heads),
        out_shape=(shape, shape, shape, jax.ShapeDtypeStruct((HEAD, 1), FULL)),
        grid_spec=pltpu.PrefetchScalarGridSpec(
            num_scalar_prefetch=2,
            grid=(steps,),
            in_specs=[
                part,
                whole,
                whole,
                part,
                part,
                pl.BlockSpec((heads, 1, BLOCK), lambda i, *_: (0, 0, i)),
                part,
                column,
                pl.BlockSpec((1, BLOCK), lambda i, *_: (0, i)),
                pl.BlockSpec((length, 1), lambda i, *_: (0, 0)),
            ],
            out_specs=(part, whole, whole, column),
            scratch_shapes=[
                pltpu.VMEM((heads, length, HEAD), LOW),
                pltpu.VMEM((heads, length, HEAD), LOW),
                pltpu.VMEM((cols, length), FULL),
                pltpu.VMEM((cols, length), FULL),
                pltpu.VMEM((cols, BLOCK), FULL),
            ],
        ),
        compiler_params=pltpu.CompilerParams(vmem_limit_bytes=62 * 2**20),
        cost_estimate=pl.CostEstimate(
            flops=8 * 5 * length * length * cols,
            bytes_accessed=8 * cols * length * 2,
            transcendentals=heads * length * length // 3,
        ),
    )(lo, hi, q, k, v, o, go, logs, raw, factor, segq, segk)


def remote(src, dst, sems, index, device):
    return pltpu.make_async_remote_copy(
        src_ref=src,
        dst_ref=dst,
        send_sem=sems[0].at[index],
        recv_sem=sems[1].at[index],
        device_id=device,
        device_id_type=pl.DeviceIdType.MESH,
    )


def greet(peers):
    barrier = pltpu.get_barrier_semaphore()
    for peer in peers:
        pl.semaphore_signal(barrier, inc=1, device_id=peer, device_id_type=pl.DeviceIdType.MESH)
    pl.semaphore_wait(barrier, len(peers))


def head_kernel(
    n_dp, n_pair, gain_ref, factor_ref, tokens_hbm, cot_hbm, block_hbm, slab_hbm,
    q_hbm, k_hbm, v_hbm, raw_hbm, normed_hbm, qkv_hbm, slabs_hbm, cot_out, inverse_ref,
    tokens, others, block, cs_recv, remote_block, pass_on, qkv, turned, normed, q, k, v, raw,
    send_sems, recv_sems, local_sems,
):
    r, s = lax.axis_index("row"), lax.axis_index("cs")
    j, d = lax.axis_index("cp"), lax.axis_index("dp")
    n_col = 2 * n_pair
    subs, width, piece = tokens.shape[1:]
    here = subs * piece
    share = cs_recv.shape[0]
    cols = q.shape[0]
    c_first = (s * n_pair + j) ^ (r * n_pair)
    near = r == s
    sems = (send_sems, recv_sems)
    counter, local_counter = iter(range(1000)), iter(range(1000))
    sent, stored = [], []

    def send(src, dst, device):
        copy = remote(src, dst, sems, next(counter), device)
        copy.start()
        sent.append(copy)
        return copy

    def move(src, dst):
        copy = pltpu.make_async_copy(src, dst, local_sems.at[next(local_counter)])
        copy.start()
        return copy

    def store(src, dst):
        stored.append(move(src, dst))

    def columns(u):
        return pl.ds(u * piece, piece)

    own_tokens = [move(tokens_hbm.at[:, columns(u)], tokens.at[0, u]) for u in range(subs)]
    own_block = move(block_hbm, block)
    store(slab_hbm, slabs_hbm.at[c_first])
    sibling_id = {"row": 1 - r}
    dp_ids = [{"dp": d ^ k} for k in range(1, n_dp)]
    col_ids = [{"cs": s ^ (k // n_pair), "cp": j ^ (k % n_pair)} for k in range(1, n_col)]
    greet([sibling_id] + dp_ids + col_ids)

    cs_copy = send(block_hbm.at[d], cs_recv, {"cs": 1 - s})
    other_copies = {}
    for u in range(subs):
        other_copies[0, u] = send(tokens_hbm.at[:, columns(u)], others.at[0, u], sibling_id)
    pair_copies = {}
    for u in range(subs):
        for m in range(1, n_pair):
            pair_copies[m, u] = send(
                tokens_hbm.at[:, columns(u)], tokens.at[m, u], {"cp": j ^ m}
            )

    cot_copy = send(cot_hbm, cot_out, sibling_id)

    def norm(m, u):
        own, other = tokens[m, u].astype(FULL), others[m, u].astype(FULL)
        squares = jnp.sum(own * own, axis=0, keepdims=True)
        squares = squares + jnp.sum(other * other, axis=0, keepdims=True)
        inverse = lax.rsqrt(squares / D + EPSILON)
        at = pl.ds(pl.multiple_of((j ^ m) * here + u * piece, 128), piece)
        normed[:width, at] = (own * inverse * gain_ref[:width]).astype(LOW)
        normed[width:, at] = (other * inverse * gain_ref[width:]).astype(LOW)
        store(normed.at[:, at], normed_hbm.at[:, at])
        if m == 0:
            inverse_ref[:, columns(u)] = inverse

    def project(m, u):
        at = pl.ds(pl.multiple_of((j ^ m) * here + u * piece, 128), piece)
        for part, out in ((0, None), (1, k), (2, v)):
            value = jnp.dot(
                turned[part * cols:(part + 1) * cols, :], normed[:, at],
                preferred_element_type=FULL,
            )
            if part == 0:
                raw[:, at] = value
                q[:, at] = (value * factor_ref[...]).astype(LOW)
            else:
                out[:, at] = value.astype(LOW)
        for src, dst in ((q, q_hbm), (k, k_hbm), (v, v_hbm), (raw, raw_hbm)):
            store(src.at[:, at], dst.at[:, at])

    for u in range(subs):
        own_tokens[u].wait()
        other_copies[0, u].wait_recv()
        norm(0, u)
    own_block.wait()

    cs_copy.wait_recv()
    dp_copies = [send(cs_recv, remote_block.at[d], peer) for peer in dp_ids]
    slab_copies = [send(slab_hbm, slabs_hbm.at[c_first], peer) for peer in col_ids]
    remote_block[d] = cs_recv[...]
    for u in range(subs - 1):
        for m in range(1, n_pair):
            pair_copies[m, u].wait_recv()
            other_copies[m, u] = send(tokens.at[m, u], others.at[m, u], sibling_id)
    cross_copies = []
    for m in range(n_dp):
        owner = d ^ m
        if m:
            dp_copies[m - 1].wait_recv()
        mine, its = block[owner], remote_block[owner]
        at = pl.multiple_of(owner * share, 32)
        qkv[pl.ds(at, share)] = jnp.where(near, mine, its)
        pass_on[owner] = jnp.where(near, its, mine)
        cross_copies.append(
            send(pass_on.at[owner], qkv.at[pl.ds(width + at, share)], sibling_id)
        )
    u = subs - 1
    for m in range(1, n_pair):
        pair_copies[m, u].wait_recv()
        other_copies[m, u] = send(tokens.at[m, u], others.at[m, u], sibling_id)
    turned[:, :width] = qkv[:width].T
    for copy in cross_copies:
        copy.wait_recv()
    turned[:, width:] = qkv[width:].T
    store(qkv, qkv_hbm)

    for u in range(subs):
        project(0, u)
    for u in range(subs):
        for m in range(1, n_pair):
            other_copies[m, u].wait_recv()
            norm(m, u)
            project(m, u)

    for copy in stored:
        copy.wait()
    for copy in slab_copies + [cot_copy]:
        copy.wait_recv()
    for copy in sent:
        copy.wait_send()


def head(n_dp, n_pair, gain, factor, tokens, cotangent, block, slab):
    width, here = tokens.shape
    wide = block.shape[1]
    cols = wide // 3
    share = width // n_dp
    length = n_pair * here
    n_col = 2 * n_pair
    subs = 2
    piece = here // subs
    count = subs * n_pair * 2 + 2 * n_dp + n_col + 5
    moves = 3 + subs + 5 * subs * n_pair + 4
    hbm = pl.BlockSpec(memory_space=pl.ANY)
    vmem = pl.BlockSpec(memory_space=pltpu.VMEM)
    V = pltpu.VMEM
    shape = jax.ShapeDtypeStruct((cols, length), LOW)
    return pl.pallas_call(
        functools.partial(head_kernel, n_dp, n_pair),
        out_shape=(
            shape,
            shape,
            shape,
            jax.ShapeDtypeStruct((cols, length), FULL),
            jax.ShapeDtypeStruct((2 * width, length), LOW),
            jax.ShapeDtypeStruct((2 * width, wide), LOW),
            jax.ShapeDtypeStruct((n_col,) + slab.shape, LOW),
            jax.ShapeDtypeStruct((width, here), LOW),
            jax.ShapeDtypeStruct((1, here), FULL),
        ),
        in_specs=[vmem] * 2 + [hbm] * 4,
        out_specs=(hbm,) * 8 + (vmem,),
        scratch_shapes=[
            V((n_pair, subs, width, piece), LOW),
            V((n_pair, subs, width, piece), LOW),
            V((n_dp, share, wide), LOW),
            V((share, wide), LOW),
            V((n_dp, share, wide), LOW),
            V((n_dp, share, wide), LOW),
            V((2 * width, wide), LOW),
            V((wide, 2 * width), LOW),
            V((2 * width, length), LOW),
            V((cols, length), LOW),
            V((cols, length), LOW),
            V((cols, length), LOW),
            V((cols, length), FULL),
            pltpu.SemaphoreType.DMA((count,)),
            pltpu.SemaphoreType.DMA((count,)),
            pltpu.SemaphoreType.DMA((moves,)),
        ],
        compiler_params=pltpu.CompilerParams(
            collective_id=2, has_side_effects=True, vmem_limit_bytes=60 * 2**20
        ),
        cost_estimate=pl.CostEstimate(
            flops=4 * wide * width * length, bytes_accessed=2**25, transcendentals=0
        ),
    )(gain, factor, tokens, cotangent, block.reshape(n_dp, share, wide), slab)


def middle_kernel(n_dp, n_pair, unit, gain_ref, att_hbm, tokens_hbm, cot_hbm, cot_other, *refs):
    n_col = 2 * n_pair
    slab_hbms, refs = refs[:n_dp], refs[n_dp:]
    down_hbms, refs = refs[:n_col], refs[n_col:]
    result_hbm, middle_hbm, out_hbm, refs = refs[0], refs[1], refs[2], refs[3:]
    grads_hbms, refs = refs[:n_dp], refs[n_dp:]
    down_outs, refs = refs[:n_col], refs[n_col:]
    (
        gain_out, tokens, cot, slab, out_w, up_w, down_w, out_t, up_t, down_t, out_half, up_half,
        down_half, att, scaled, normed, active, grad_hidden, branch, middle, grad, result, grad_att,
        grads, down_grads, square_send, square_recv, inner_send, inner_recv, inverse, narrow,
        send_sems, recv_sems, local_sems,
    ) = refs
    r, s = lax.axis_index("row"), lax.axis_index("cs")
    j, d = lax.axis_index("cp"), lax.axis_index("dp")
    width, here = tokens.shape
    pieces, _, piece = square_send.shape
    cols = att_hbm.shape[0]
    half = n_col * unit // 2
    rows_q = slab_hbms[0].shape[1]
    rows_g = grads_hbms[0].shape[1]
    c_first = (s * n_pair + j) ^ (r * n_pair)
    sems = (send_sems, recv_sems)
    counter, local_counter = iter(range(1000)), iter(range(1000))
    sent, stored = [], []

    def send(src, dst, device):
        copy = remote(src, dst, sems, next(counter), device)
        copy.start()
        sent.append(copy)
        return copy

    def move(src, dst):
        copy = pltpu.make_async_copy(src, dst, local_sems.at[next(local_counter)])
        copy.start()
        return copy

    def columns(u):
        return pl.ds(u * piece, piece)

    def span(u):
        return slice(u * piece, (u + 1) * piece)

    own_rows, other_rows = pl.ds(0, width), pl.ds(width, width)
    weight_loads = [
        move(slab_hbms[m], slab.at[:, pl.ds(pl.multiple_of((d ^ m) * rows_q, 16), rows_q)])
        for m in range(n_dp)
    ] + [
        move(down_hbms[m], down_w.at[pl.ds(pl.multiple_of((c_first ^ m) * unit, 16), unit)])
        for m in range(n_col)
    ]
    att_loads = [
        move(
            att_hbm.at[:, pl.ds(pl.multiple_of(j * here + u * piece, 128), piece)],
            att.at[pl.ds(pl.multiple_of(j * cols, 16), cols), columns(u)],
        )
        for u in range(pieces)
    ]
    token_load = move(tokens_hbm, tokens)
    cot_loads = [move(cot_hbm, cot.at[own_rows]), move(cot_other, cot.at[other_rows])]
    sibling_id = {"row": 1 - r}
    pair_ids = [{"cp": j ^ m} for m in range(1, n_pair)]
    greet([sibling_id] + pair_ids)

    att_copies = {}
    for u in range(pieces):
        for m in range(1, n_pair):
            att_copies[u, m] = send(
                att_hbm.at[:, pl.ds(pl.multiple_of((j ^ m) * here + u * piece, 128), piece)],
                att.at[pl.ds(pl.multiple_of(j * cols, 16), cols), columns(u)],
                pair_ids[m - 1],
            )

    for copy in weight_loads:
        copy.wait()
    for m in range(n_col):
        at = slice(m * unit, (m + 1) * unit)
        out_w[at] = slab[m, :unit]
        up_w[at] = slab[m, unit:2 * unit]
    cross_copies = [
        send(whole.at[pl.ds(half, half)], part.at[:, other_rows], sibling_id)
        for whole, part in ((up_w, up_half), (down_w, down_half), (out_w, out_half))
    ]
    for whole, part in ((up_w, up_half), (down_w, down_half), (out_w, out_half)):
        part[:, :width] = whole[:half]
    out_t[...] = out_w[...].T
    narrow[...] = jnp.zeros_like(narrow)

    copies = {}

    def exchange(name, u, ref):
        copies[name, u] = send(
            ref.at[own_rows, columns(u)], ref.at[other_rows, columns(u)], sibling_id
        )

    def share_heads(u):
        att_loads[u].wait()
        for m in range(1, n_pair):
            att_copies[u, m].wait_recv()
        exchange("att", u, att)

    def first_branch(u):
        if u == 0:
            token_load.wait()
        copies["att", u].wait_recv()
        value = tokens[:, span(u)].astype(FULL) + jnp.dot(
            out_t[...], att[:, span(u)], preferred_element_type=FULL
        )
        scaled[:width, span(u)] = (value * gain_ref[...]).astype(LOW)
        exchange("scaled", u, scaled)
        square_send[u] = jnp.sum(value * value, axis=0, keepdims=True)
        copies["square", u] = send(square_send.at[u], square_recv.at[u], sibling_id)
        middle[:, span(u)] = value

    def hidden_units(u):
        if u == 0:
            for copy in cot_loads:
                copy.wait()
            for copy in cross_copies:
                copy.wait_recv()
            up_t[...] = up_w[...].T
            down_t[...] = down_w[...].T
        grad_active = jnp.dot(down_half[...], cot[:, span(u)], preferred_element_type=FULL)
        copies["scaled", u].wait_recv()
        copies["square", u].wait_recv()
        scale = lax.rsqrt((square_send[u] + square_recv[u]) / D + EPSILON)
        inverse[u] = scale
        hidden = scale * jnp.dot(up_half[...], scaled[:, span(u)], preferred_element_type=FULL)
        sigmoid = jax.nn.sigmoid(hidden)
        value = (grad_active * sigmoid * (1.0 + hidden * (1.0 - sigmoid))).astype(LOW)
        grad_hidden[:half, span(u)] = value
        exchange("grad_hidden", u, grad_hidden)
        active[:half, span(u)] = (hidden * sigmoid).astype(LOW)
        exchange("active", u, active)
        inner_send[u] = jnp.sum(value.astype(FULL) * hidden, axis=0, keepdims=True)
        copies["inner", u] = send(inner_send.at[u], inner_recv.at[u], sibling_id)
        normed[:, span(u)] = (middle[:, span(u)] * scale * gain_ref[...]).astype(LOW)

    def second_branch(u):
        copies["grad_hidden", u].wait_recv()
        copies["inner", u].wait_recv()
        scale = inverse[u]
        inner = scale * scale * ((inner_send[u] + inner_recv[u]) / D)
        back = jnp.dot(up_t[...], grad_hidden[:, span(u)], preferred_element_type=FULL)
        value = (
            cot[:width, span(u)].astype(FULL)
            + scale * (back * gain_ref[...])
            - middle[:, span(u)] * inner
        )
        branch[:width, span(u)] = value.astype(LOW)
        exchange("branch", u, branch)
        grad[:, span(u)] = value
        stored.append(move(grad.at[:, columns(u)], middle_hbm.at[:, columns(u)]))
        product = back * middle[:, span(u)] * scale
        total = narrow[...]
        for v in range(piece // 128):
            total = total + product[:, v * 128:(v + 1) * 128]
        narrow[...] = total
        copies["active", u].wait_recv()
        result[:, span(u)] = middle[:, span(u)] + jnp.dot(
            down_t[...], active[:, span(u)], preferred_element_type=FULL
        )
        stored.append(move(result.at[:, columns(u)], result_hbm.at[:, columns(u)]))

    def heads_back(u):
        copies["branch", u].wait_recv()
        grad_att[:, span(u)] = jnp.dot(
            out_half[...], branch[:, span(u)], preferred_element_type=FULL
        ).astype(LOW)
        target = pl.ds(pl.multiple_of(j * here + u * piece, 128), piece)
        for m in range(n_pair):
            source = grad_att.at[
                pl.ds(pl.multiple_of((j ^ m) * cols, 16), cols), columns(u)
            ]
            if m:
                copies["out", u, m] = send(source, out_hbm.at[:, target], pair_ids[m - 1])
            else:
                stored.append(move(source, out_hbm.at[:, target]))

    stages = (share_heads, first_branch, hidden_units, second_branch, heads_back)
    for t in range(pieces + len(stages) - 1):
        for number in reversed(range(len(stages))):
            if 0 <= t - number < pieces:
                stages[number](t - number)

    def product(left, right, target, first):
        turned = right[:width].T
        for n in range(n_col):
            target[n, first:first + unit] = jnp.dot(
                left[n * unit:(n + 1) * unit], turned, preferred_element_type=FULL
            ).astype(LOW)

    product(active, cot, down_grads, 0)
    for m in range(n_col):
        stored.append(move(down_grads.at[c_first ^ m], down_outs[m]))
    if grads.shape[1] > 2 * unit:
        grads[...] = jnp.zeros_like(grads)
    product(grad_hidden, normed, grads, unit)
    product(att, branch, grads, 0)
    for m in range(n_dp):
        at = pl.ds(pl.multiple_of((d ^ m) * rows_g, 16), rows_g)
        stored.append(move(grads.at[:, at], grads_hbms[m]))
    gain_out[...] = jnp.sum(narrow[...].T, axis=0, keepdims=True)

    for u in range(pieces):
        for m in range(1, n_pair):
            copies["out", u, m].wait_recv()
    for copy in stored:
        copy.wait()
    for copy in sent:
        copy.wait_send()


def middle_part(n_dp, n_pair, gain, attended, tokens, cotangent, cot_other, slabs, downs):
    width, here = tokens.shape
    n_col = 2 * n_pair
    cols, length = attended.shape
    unit = downs[0].shape[0]
    half = n_col * unit // 2
    rows_q = slabs[0].shape[1]
    rows_g = quarter_rows(2 * unit, n_dp)
    pieces = max(2, here // 256)
    piece = here // pieces
    count = 2 * pieces * (n_pair - 1) + 7 * pieces + 8
    moves = 2 * n_dp + 2 * n_col + 4 * pieces + 4
    hbm = pl.BlockSpec(memory_space=pl.ANY)
    vmem = pl.BlockSpec(memory_space=pltpu.VMEM)
    V = pltpu.VMEM
    S = jax.ShapeDtypeStruct
    weight = V((2 * half, width), LOW)
    weight_t = V((width, 2 * half), LOW)
    both = V((2 * width, here), LOW)
    whole = V((width, here), FULL)
    row = V((pieces, 1, piece), FULL)
    out = pl.pallas_call(
        functools.partial(middle_kernel, n_dp, n_pair, unit),
        out_shape=(
            S((width, here), FULL),
            S((width, here), FULL),
            S((cols, length), LOW),
        )
        + (S((n_col, rows_g, width), LOW),) * n_dp
        + (S((unit, width), LOW),) * n_col
        + (S((1, width), FULL),),
        in_specs=[vmem] + [hbm] * (4 + n_dp + n_col),
        out_specs=(hbm,) * (3 + n_dp + n_col) + (vmem,),
        scratch_shapes=[
            V((width, here), LOW),
            both,
            V((n_col, n_dp * rows_q, width), LOW),
            weight,
            weight,
            weight,
            weight_t,
            weight_t,
            weight_t,
            V((half, 2 * width), LOW),
            V((half, 2 * width), LOW),
            V((half, 2 * width), LOW),
            both,
            both,
            V((width, here), LOW),
            V((2 * half, here), LOW),
            V((2 * half, here), LOW),
            both,
            whole,
            whole,
            whole,
            V((width, here), LOW),
            V((n_col, n_dp * rows_g, width), LOW),
            V((n_col, unit, width), LOW),
            row,
            row,
            row,
            row,
            row,
            V((width, 128), FULL),
            pltpu.SemaphoreType.DMA((count,)),
            pltpu.SemaphoreType.DMA((count,)),
            pltpu.SemaphoreType.DMA((moves,)),
        ],
        compiler_params=pltpu.CompilerParams(
            collective_id=3, has_side_effects=True, vmem_limit_bytes=62 * 2**20
        ),
        cost_estimate=pl.CostEstimate(
            flops=18 * 2 * half * width * here, bytes_accessed=2**25, transcendentals=0
        ),
    )(gain, attended, tokens, cotangent, cot_other, *slabs, *downs)
    return out[0], out[1], out[2], out[3:3 + n_dp], out[3 + n_dp:-1], out[-1]


def quarter_rows(rows, n_dp):
    return -(-rows // (16 * n_dp)) * 16


def tail_kernel(
    n_dp, n_pair, gain_ref, inverse_ref, sums_ref, qkv_hbm, dq_hbm, dk_hbm, dv_hbm, normed_hbm,
    tokens_hbm, middle_hbm, *refs,
):
    n_col = 2 * n_pair
    grads_hbms, refs = refs[:n_dp], refs[n_dp:]
    down_hbms, refs = refs[:n_col], refs[n_col:]
    (
        result_hbm, qkv_out, grads_out, down_out, sums_out,
        qkv, dproj, normed, tokens, middle, result, row_send, row_recv, own, pair_send, pair_recv,
        dp_send, dp_recv, dp_own, cross_send, cross_recv, cs_send, cs_recv, final, grads_parts,
        grads_send, grads_recv, grads_final, down_parts, down_send, down_recv, down_final,
        inner_send, inner_recv, sums_send, sums_recv, send_sems, recv_sems, local_sems,
    ) = refs
    r, s = lax.axis_index("row"), lax.axis_index("cs")
    j, d = lax.axis_index("cp"), lax.axis_index("dp")
    width, here = tokens.shape
    cols = dq_hbm.shape[0]
    unit = down_parts.shape[1]
    share = width // n_dp
    part = share // 2
    rows_d = down_final.shape[0]
    subs = row_send.shape[1]
    piece = here // subs
    c_first = (s * n_pair + j) ^ (r * n_pair)
    near = r == s
    sems = (send_sems, recv_sems)
    counter, local_counter = iter(range(1000)), iter(range(1000))
    sent, stored = [], []

    def send(src, dst, device):
        copy = remote(src, dst, sems, next(counter), device)
        copy.start()
        sent.append(copy)
        return copy

    def move(src, dst):
        copy = pltpu.make_async_copy(src, dst, local_sems.at[next(local_counter)])
        copy.start()
        return copy

    early = [
        move(dq_hbm, dproj.at[pl.ds(0, cols)]),
        move(dk_hbm, dproj.at[pl.ds(cols, cols)]),
        move(dv_hbm, dproj.at[pl.ds(2 * cols, cols)]),
        move(normed_hbm, normed),
    ]
    load_qkv = move(qkv_hbm, qkv)
    load_down = [move(down_hbms[k], down_parts.at[k]) for k in range(n_col)]
    load_grads = [move(grads_hbms[k], grads_parts.at[k]) for k in range(n_dp)]
    late = [move(tokens_hbm, tokens), move(middle_hbm, middle)]

    sibling_id = {"row": 1 - r}
    cs_id = {"cs": 1 - s}
    dp_ids = [{"dp": d ^ k} for k in range(1, n_dp)]
    col_ids = [{"cs": s ^ (k // n_pair), "cp": j ^ (k % n_pair)} for k in range(1, n_col)]
    greet([sibling_id] + dp_ids + col_ids)

    def quarter(half, owner):
        at = pl.ds(pl.multiple_of(half * width + owner * share, 32), share)
        return mm(normed[at, :], dproj[...], 1, 1)

    def rows_of(half, chunk, u):
        at = pl.ds(pl.multiple_of(chunk * here + u * piece, 128), piece)
        return jnp.dot(
            qkv[half * width:(half + 1) * width, :], dproj[:, at], preferred_element_type=FULL
        )

    dp_copies = {}

    def send_part(k, p):
        rows = pl.ds(p * part, part)
        dp_copies[k, p] = send(
            dp_send.at[k - 1, :, rows], dp_recv.at[k - 1, :, rows], dp_ids[k - 1]
        )

    def quarters(k):
        for half in range(2):
            dp_send[k - 1, half] = quarter(half, d ^ k).astype(LOW)
        send_part(k, 0)

    row_copies, pair_copies = {}, []
    for copy in early:
        copy.wait()
    quarters(1)
    load_qkv.wait()
    for k in range(1, n_pair):
        for u in range(subs):
            row_send[k, u] = rows_of(1, j ^ k, u).astype(LOW)
            row_copies[k, u] = send(row_send.at[k, u], row_recv.at[k, u], sibling_id)
    for k in range(1, n_pair):
        for u in range(subs):
            value = rows_of(0, j ^ k, u)
            row_copies[k, u].wait_recv()
            pair_send[k - 1, u] = (value + row_recv[k, u].astype(FULL)).astype(LOW)
            pair_copies.append(
                send(pair_send.at[k - 1, u], pair_recv.at[k - 1, u], {"cp": j ^ k})
            )
    for k in range(2, n_dp):
        quarters(k)
    for copy in load_down:
        copy.wait()
    value = down_parts[0].astype(FULL)
    for k in range(1, n_col):
        value = value + down_parts[k].astype(FULL)
    if down_send.shape[0] > unit:
        down_send[...] = jnp.zeros_like(down_send)
    down_send[:unit] = value.astype(LOW)

    def down_rows(owner):
        return pl.ds(pl.multiple_of(owner * rows_d, 16), rows_d)

    down_copies = [
        send(down_send.at[down_rows(d ^ k)], down_recv.at[k - 1], dp_ids[k - 1])
        for k in range(1, n_dp)
    ]
    for k in range(1, n_dp):
        send_part(k, 1)
    for half in range(2):
        dp_own[half] = quarter(half, d)

    for u in range(subs):
        row_send[0, u] = rows_of(1, j, u).astype(LOW)
        row_copies[0, u] = send(row_send.at[0, u], row_recv.at[0, u], sibling_id)
    for u in range(subs):
        own[u] = rows_of(0, j, u)

    cs_copies = []

    def reduce_part(p):
        rows = slice(p * part, (p + 1) * part)
        for k in range(1, n_dp):
            dp_copies[k, p].wait_recv()

        def total(half):
            value = dp_own[half, rows]
            for k in range(1, n_dp):
                value = value + dp_recv[k - 1, half, rows].astype(FULL)
            return value

        cross_send[p] = total(1).astype(LOW)
        cross_copy = send(cross_send.at[p], cross_recv.at[p], sibling_id)
        kept = total(0)
        cross_copy.wait_recv()
        crossed = cross_recv[p].astype(FULL)
        cs_send[p] = jnp.where(near, crossed, kept).astype(LOW)
        cs_copies.append(send(cs_send.at[p], cs_recv.at[p], cs_id))
        dp_own[0, rows] = jnp.where(near, kept, crossed)

    reduce_part(0)

    for copy in load_grads:
        copy.wait()

    def summed(place_at):
        value = grads_parts[0, place_at].astype(FULL)
        for k in range(1, n_dp):
            value = value + grads_parts[k, place_at].astype(FULL)
        return value

    grads_copies = []
    for k in range(1, n_col):
        grads_send[k - 1] = summed(c_first ^ k).astype(LOW)
        grads_copies.append(send(grads_send.at[k - 1], grads_recv.at[k - 1], col_ids[k - 1]))

    value = down_send[down_rows(d)].astype(FULL)
    for k in range(1, n_dp):
        down_copies[k - 1].wait_recv()
        value = value + down_recv[k - 1].astype(FULL)
    down_final[...] = value.astype(LOW)
    out_copies = [send(down_final, down_out.at[d], peer) for peer in dp_ids]
    stored.append(move(down_final, down_out.at[d]))
    reduce_part(1)

    for copy in late:
        copy.wait()
    for copy in pair_copies:
        copy.wait_recv()
    inverse = inverse_ref[...]
    for u in range(subs):
        row_copies[0, u].wait_recv()
        at = slice(u * piece, (u + 1) * piece)
        value = own[u] + row_recv[0, u].astype(FULL)
        for k in range(1, n_pair):
            value = value + pair_recv[k - 1, u].astype(FULL)
        own[u] = value
        inner_send[:, at] = jnp.sum(
            value * gain_ref[...] * tokens[:, at].astype(FULL), axis=0, keepdims=True
        )
    inner_copy = send(inner_send, inner_recv, sibling_id)

    def finish_part(p):
        cs_copies[p].wait_recv()
        rows = slice(p * part, (p + 1) * part)
        final[p] = (dp_own[0, rows] + cs_recv[p].astype(FULL)).astype(LOW)
        target = qkv_out.at[d, pl.ds(p * part, part)]
        out_copies.extend([send(final.at[p], target, peer) for peer in dp_ids])
        stored.append(move(final.at[p], target))

    finish_part(0)
    narrow = jnp.zeros((width, 128), FULL)
    for u in range(subs):
        at = slice(u * piece, (u + 1) * piece)
        wide = own[u] * tokens[:, at].astype(FULL) * inverse[:, at]
        for v in range(piece // 128):
            narrow = narrow + wide[:, v * 128:(v + 1) * 128]
    gain_part = jnp.sum(narrow.T, axis=0, keepdims=True)
    sums_send[0] = jnp.concatenate([gain_part, sums_ref[1:]], 0)
    inner_copy.wait_recv()
    inner = (inner_send[...] + inner_recv[...]) / D
    for u in range(subs):
        at = slice(u * piece, (u + 1) * piece)
        result[:, at] = (
            middle[:, at]
            + inverse[:, at] * (own[u] * gain_ref[...])
            - tokens[:, at].astype(FULL)
            * (inverse[:, at] * inverse[:, at] * inverse[:, at] * inner[:, at])
        )
    stored.append(move(result, result_hbm))
    finish_part(1)

    value = summed(c_first)
    for k in range(1, n_col):
        grads_copies[k - 1].wait_recv()
        value = value + grads_recv[k - 1].astype(FULL)
    grads_final[...] = value.astype(LOW)
    out_copies += [send(grads_final, grads_out.at[d], peer) for peer in dp_ids]
    stored.append(move(grads_final, grads_out.at[d]))

    steps = []
    for name, me, n in (("dp", d, n_dp), ("cs", s, 2), ("cp", j, n_pair)):
        k = 1
        while k < n:
            steps.append({name: me ^ k})
            k *= 2
    for t, peer in enumerate(steps):
        copy = send(sums_send.at[t], sums_recv.at[t], peer)
        copy.wait_recv()
        sums_send[t + 1] = sums_send[t] + sums_recv[t]
    last = len(steps)
    copy = send(sums_send.at[last], sums_recv.at[last], sibling_id)
    copy.wait_recv()
    sums_out[0] = sums_send[last]
    sums_out[1] = sums_recv[last]

    for copy in out_copies:
        copy.wait_recv()
    for copy in stored:
        copy.wait()
    for copy in sent:
        copy.wait_send()


def tail(n_dp, n_pair, gain, inverse, sums, qkv, dq, dk, dv, normed, tokens, middle, grads, downs):
    width, here = tokens.shape
    length = normed.shape[1]
    cols = dq.shape[0]
    unit = downs[0].shape[0]
    rows_d = quarter_rows(unit, n_dp)
    share = width // n_dp
    subs = 2
    piece = here // subs
    n_col = 2 * n_pair
    part = grads[0].shape[1:]
    wide = 3 * cols
    steps = (n_dp * n_col).bit_length()
    count = 2 * n_pair * subs + 7 * n_dp + n_col + steps + 10
    moves = 13 + n_dp + n_col
    hbm = pl.BlockSpec(memory_space=pl.ANY)
    vmem = pl.BlockSpec(memory_space=pltpu.VMEM)
    V = pltpu.VMEM
    halves = V((2, share // 2, wide), LOW)
    return pl.pallas_call(
        functools.partial(tail_kernel, n_dp, n_pair),
        out_shape=(
            jax.ShapeDtypeStruct((width, here), FULL),
            jax.ShapeDtypeStruct((n_dp, share, wide), LOW),
            jax.ShapeDtypeStruct((n_dp,) + part, LOW),
            jax.ShapeDtypeStruct((n_dp, rows_d, width), LOW),
            jax.ShapeDtypeStruct((2,) + sums.shape, FULL),
        ),
        in_specs=[vmem] * 3 + [hbm] * (7 + n_dp + n_col),
        out_specs=(hbm,) * 4 + (vmem,),
        scratch_shapes=[
            V((2 * width, wide), LOW),
            V((wide, length), LOW),
            V((2 * width, length), LOW),
            V((width, here), LOW),
            V((width, here), FULL),
            V((width, here), FULL),
            V((n_pair, subs, width, piece), LOW),
            V((n_pair, subs, width, piece), LOW),
            V((subs, width, piece), FULL),
            V((n_pair - 1, subs, width, piece), LOW),
            V((n_pair - 1, subs, width, piece), LOW),
            V((n_dp - 1, 2, share, wide), LOW),
            V((n_dp - 1, 2, share, wide), LOW),
            V((2, share, wide), FULL),
            halves,
            halves,
            halves,
            halves,
            halves,
            V((n_dp, n_col) + part, LOW),
            V((n_col - 1,) + part, LOW),
            V((n_col - 1,) + part, LOW),
            V(part, LOW),
            V((n_col, unit, width), LOW),
            V((n_dp * rows_d, width), LOW),
            V((n_dp - 1, rows_d, width), LOW),
            V((rows_d, width), LOW),
            V((1, here), FULL),
            V((1, here), FULL),
            V((steps + 1,) + sums.shape, FULL),
            V((steps + 1,) + sums.shape, FULL),
            pltpu.SemaphoreType.DMA((count,)),
            pltpu.SemaphoreType.DMA((count,)),
            pltpu.SemaphoreType.DMA((moves,)),
        ],
        compiler_params=pltpu.CompilerParams(
            collective_id=1, has_side_effects=True, vmem_limit_bytes=62 * 2**20
        ),
        cost_estimate=pl.CostEstimate(
            flops=8 * wide * width * length, bytes_accessed=2**25, transcendentals=0
        ),
    )(gain, inverse, sums, qkv, dq, dk, dv, normed, tokens, middle, *grads, *downs)


def on_device(
    tokens,
    segment_ids,
    padding_mask,
    w_qkv,
    w_out,
    w_up,
    w_down,
    gain_attn,
    gain_mlp,
    scale_raw,
    cotangent,
):
    width, here = tokens.shape
    r, s = lax.axis_index("row"), lax.axis_index("cs")
    j, d = lax.axis_index("cp"), lax.axis_index("dp")
    n_pair, n_dp, n_col = lax.axis_size("cp"), lax.axis_size("dp"), lax.axis_size(COLS)
    c = s * n_pair + j
    head_cols = w_qkv.shape[0] // (3 * width)
    heads = head_cols // HEAD
    near = r == s

    segments = jnp.where(s == r, segment_ids[0], sibling(segment_ids)[0])
    padding = jnp.where(s == r, padding_mask[0], sibling(padding_mask)[0])
    length = segments.shape[0]
    firsts = segments[::BLOCK]
    starts = jnp.sum((segments[None, :] < firsts[:, None]).astype(jnp.int32), axis=1)
    filled = (jnp.sum(padding) + BLOCK - 1) // BLOCK
    blocks = jnp.arange(length // BLOCK, dtype=jnp.int32)
    lo = starts // BLOCK
    hi = jnp.minimum(blocks, filled)
    segq = segments[None, :]
    segk = jnp.where(padding == 1, segments, -1)[:, None]

    def halves(vector):
        whole = vector.reshape(2, width)
        own = lax.dynamic_index_in_dim(whole, r, 0, keepdims=False)
        other = lax.dynamic_index_in_dim(whole, 1 - r, 0, keepdims=False)
        return own[:, None], other[:, None]

    gain_one, gain_one_other = halves(gain_attn)
    gain_two, _ = halves(gain_mlp)
    factor = (LOG_TWO_E / math.sqrt(HEAD) * jnp.log1p(jnp.exp(scale_raw)))[:, None]

    block = w_qkv.reshape(width, 3 * head_cols)
    unit = w_up.shape[0] // width
    slab = jnp.concatenate([w_out.reshape(-1, width), w_up.reshape(width, -1).T], 0)
    slab_rows = quarter_rows(2 * unit, n_dp)
    slab = jnp.pad(slab, ((0, n_dp * slab_rows - 2 * unit), (0, 0)))
    slab = cut(slab, d, n_dp, 0)
    queries, key_heads, values, query_raw, normed_one, qkv, slabs, cot_other, inverse_one = head(
        n_dp, n_pair, jnp.concatenate([gain_one, gain_one_other], 0), jnp.tile(factor, (heads, 1)),
        tokens, cotangent, block, slab,
    )
    slabs = gather(slabs, "dp")
    down = w_down.reshape(-1, width)
    downs = [down] + [
        lax.ppermute(down, COLS, [(i, i ^ k) for i in range(n_col)]) for k in range(1, n_col)
    ]
    attended, logs = attention_forward(queries, key_heads, values, segq, segk, lo, hi)
    result, grad_middle, grad_attended, grads, down_grads, gain_two_part = middle_part(
        n_dp, n_pair, gain_two, attended, tokens, cotangent, cot_other, slabs, downs
    )
    received = [grads[0]] + [shift(grads[k], "dp", k) for k in range(1, n_dp)]
    down_received = [down_grads[0]] + [
        lax.ppermute(down_grads[k], COLS, [(i, i ^ k) for i in range(n_col)])
        for k in range(1, n_col)
    ]

    dq, dk, dv, scale_part = attention_backward(
        queries, key_heads, values, attended, grad_attended, logs, query_raw, factor,
        segq, segk, lo, hi,
    )
    scale_part = (
        scale_part[:, 0] * (LOG_TWO_E / math.sqrt(HEAD)) * jax.nn.sigmoid(scale_raw)
    )
    sums = jnp.concatenate(
        [
            jnp.zeros((1, width), FULL),
            gain_two_part,
            jnp.pad(scale_part, (0, width - HEAD))[None],
            jnp.zeros((5, width), FULL),
        ]
    )
    grad_tokens, grad_qkv, final, final_down, sums = tail(
        n_dp, n_pair, gain_one, inverse_one, sums, qkv, dq, dk, dv, normed_one, tokens,
        grad_middle, received, down_received,
    )
    grad_qkv = grad_qkv.astype(FULL)
    final = final.reshape(-1, width)
    final = [final[i * unit:(i + 1) * unit].astype(FULL) for i in range(2)]
    final.append(final_down.reshape(-1, width)[:unit].astype(FULL))
    own, other = sums[0], sums[1]
    first = r == 0
    gains = jnp.concatenate(
        [jnp.where(first, own[:2], other[:2]), jnp.where(first, other[:2], own[:2])], 1
    )
    scale_total = (own[2] + other[2])[:HEAD]
    return (
        result,
        grad_tokens,
        grad_qkv.reshape(-1),
        final[0].reshape(-1),
        final[1].T.reshape(-1),
        final[2].reshape(-1),
        gains[0],
        gains[1],
        scale_total,
    )


def solution(mesh):
    n_dp, n_row, n_col = (mesh.shape[name] for name in ("dp", "row", "col"))
    split = Mesh(
        np.asarray(mesh.devices).reshape(n_dp, n_row, n_row, n_col // n_row),
        ("dp", "row", "cs", "cp"),
    )
    rows = P("row", ("dp", "cs", "cp"))
    ids = P(("dp", "row"), None)
    blocks = P(("row", "cs", "cp"))
    return jax.shard_map(
        on_device,
        mesh=split,
        in_specs=(rows, ids, ids, blocks, blocks, blocks, blocks, P(), P(), P(), rows),
        out_specs=(rows, rows, blocks, blocks, blocks, blocks, P(), P(), P()),
        check_vma=False,
    )
```

```python
import functools
import math

import jax
import jax.numpy as jnp
import numpy as np
from jax import lax
from jax.experimental import pallas as pl
from jax.experimental.pallas import tpu as pltpu
from jax.sharding import Mesh, PartitionSpec as P

D = 1280
HEAD = 80
EPSILON = 1e-06
LOG_TWO_E = 1.442695041
BLOCK = 256
LOW = jnp.bfloat16
FULL = jnp.float32
COLS = ("cs", "cp")


def mm(left, right, left_axis, right_axis):
    return lax.dot_general(
        left, right, (((left_axis,), (right_axis,)), ((), ())), preferred_element_type=FULL
    )


def shift(x, axis, k):
    n = lax.axis_size(axis)
    return lax.ppermute(x, axis, [(i, i ^ k) for i in range(n)])


def sibling(x):
    return shift(x, "row", 1)


def cut(x, index, count, axis):
    step = x.shape[axis] // count
    return lax.dynamic_slice_in_dim(x, index * step, step, axis)


def gather(x, axis):
    return [x] + [shift(x, axis, k) for k in range(1, lax.axis_size(axis))]


def diag_mask(segq, segk):
    size = segk.shape[0], segq.shape[1]
    ki = lax.broadcasted_iota(jnp.int32, size, 0)
    qi = lax.broadcasted_iota(jnp.int32, size, 1)
    return ((segk == segq) & (ki <= qi)) | (ki == qi)


def forward_kernel(heads, lo_ref, hi_ref, q_ref, k_ref, v_ref, segq_ref, segk_ref, o_ref, log_ref, ks):
    i = pl.program_id(0)

    @pl.when(i == 0)
    def _():
        for h in range(heads):
            ks[h] = k_ref[h * HEAD:(h + 1) * HEAD, :].T

    segq = segq_ref[...]

    def visit(kb, carry, diagonal):
        at = pl.ds(pl.multiple_of(kb * BLOCK, BLOCK), BLOCK)
        segk = segk_ref[at, :]
        mask = diag_mask(segq, segk) if diagonal else segk == segq
        out = []
        for h in range(heads):
            rows = slice(h * HEAD, (h + 1) * HEAD)
            s = jnp.dot(ks[h, at, :], q_ref[rows, :], preferred_element_type=FULL)
            s = jnp.where(mask, s, -1e30)
            peak = jnp.max(s, axis=0, keepdims=True)
            if not diagonal:
                m, l, acc = carry[h]
                peak = jnp.maximum(m, peak)
            p = jnp.exp(s - peak)
            total = jnp.sum(p, axis=0, keepdims=True)
            new = jnp.dot(v_ref[rows, at], p.astype(LOW), preferred_element_type=FULL)
            if not diagonal:
                keep = jnp.exp(m - peak)
                total = l * keep + total
                new = acc * keep + new
            out.append((peak, total, new))
        return tuple(out)

    carry = visit(i, None, True)
    carry = lax.fori_loop(lo_ref[i], hi_ref[i], lambda kb, c: visit(kb, c, False), carry)
    for h in range(heads):
        m, l, acc = carry[h]
        o_ref[h * HEAD:(h + 1) * HEAD, :] = (acc / l).astype(LOW)
        log_ref[h] = m + jnp.log(l)


def attention_forward(q, k, v, segq, segk, lo, hi):
    cols, length = q.shape
    heads = cols // HEAD
    steps = length // BLOCK
    whole = pl.BlockSpec((cols, length), lambda i, *_: (0, 0))
    part = pl.BlockSpec((cols, BLOCK), lambda i, *_: (0, i))
    return pl.pallas_call(
        functools.partial(forward_kernel, heads),
        out_shape=(
            jax.ShapeDtypeStruct((cols, length), LOW),
            jax.ShapeDtypeStruct((heads, 1, length), FULL),
        ),
        grid_spec=pltpu.PrefetchScalarGridSpec(
            num_scalar_prefetch=2,
            grid=(steps,),
            in_specs=[
                part,
                whole,
                whole,
                pl.BlockSpec((1, BLOCK), lambda i, *_: (0, i)),
                pl.BlockSpec((length, 1), lambda i, *_: (0, 0)),
            ],
            out_specs=(part, pl.BlockSpec((heads, 1, BLOCK), lambda i, *_: (0, 0, i))),
            scratch_shapes=[pltpu.VMEM((heads, length, HEAD), LOW)],
        ),
        compiler_params=pltpu.CompilerParams(vmem_limit_bytes=62 * 2**20),
        cost_estimate=pl.CostEstimate(
            flops=8 * 2 * length * length * cols,
            bytes_accessed=4 * cols * length * 2,
            transcendentals=heads * length * length // 3,
        ),
    )(lo, hi, q, k, v, segq, segk)


def backward_kernel(
    heads, lo_ref, hi_ref, q_ref, k_ref, v_ref, o_ref, go_ref, log_ref, raw_ref, factor_ref,
    segq_ref, segk_ref, dq_ref, dk_ref, dv_ref, scale_ref, ks, vs, dks, dvs, dqs,
):
    i = pl.program_id(0)

    @pl.when(i == 0)
    def _():
        for h in range(heads):
            ks[h] = k_ref[h * HEAD:(h + 1) * HEAD, :].T
            vs[h] = v_ref[h * HEAD:(h + 1) * HEAD, :].T
        dks[...] = jnp.zeros_like(dks)
        dvs[...] = jnp.zeros_like(dvs)
        scale_ref[...] = jnp.zeros_like(scale_ref)

    segq = segq_ref[...]
    inner = [
        jnp.sum(
            o_ref[h * HEAD:(h + 1) * HEAD, :].astype(FULL)
            * go_ref[h * HEAD:(h + 1) * HEAD, :].astype(FULL),
            axis=0,
            keepdims=True,
        )
        for h in range(heads)
    ]

    def visit(kb, diagonal):
        at = pl.ds(pl.multiple_of(kb * BLOCK, BLOCK), BLOCK)
        segk = segk_ref[at, :]
        mask = diag_mask(segq, segk) if diagonal else segk == segq
        for h in range(heads):
            rows = slice(h * HEAD, (h + 1) * HEAD)
            q = q_ref[rows, :]
            go = go_ref[rows, :]
            s = jnp.dot(ks[h, at, :], q, preferred_element_type=FULL)
            p = jnp.where(mask, jnp.exp(s - log_ref[h]), 0.0)
            dp = jnp.dot(vs[h, at, :], go, preferred_element_type=FULL)
            ds = (p * (dp - inner[h])).astype(LOW)
            new = jnp.dot(k_ref[rows, at], ds, preferred_element_type=FULL)
            if diagonal:
                dqs[rows, :] = new
            else:
                dqs[rows, :] += new
            dks[rows, at] += mm(q, ds, 1, 1)
            dvs[rows, at] += mm(go, p.astype(LOW), 1, 1)

    visit(i, True)

    @pl.loop(lo_ref[i], hi_ref[i])
    def _(kb):
        visit(kb, False)

    factor = factor_ref[...]
    part = jnp.zeros((HEAD, 1), FULL)
    for h in range(heads):
        rows = slice(h * HEAD, (h + 1) * HEAD)
        dq = dqs[rows, :]
        part = part + jnp.sum(dq * raw_ref[rows, :], axis=1, keepdims=True)
        dq_ref[rows, :] = (dq * factor).astype(LOW)
    scale_ref[...] += part

    @pl.when(i == pl.num_programs(0) - 1)
    def _():
        dk_ref[...] = dks[...].astype(LOW)
        dv_ref[...] = dvs[...].astype(LOW)


def attention_backward(q, k, v, o, go, logs, raw, factor, segq, segk, lo, hi):
    cols, length = q.shape
    heads = cols // HEAD
    steps = length // BLOCK
    whole = pl.BlockSpec((cols, length), lambda i, *_: (0, 0))
    part = pl.BlockSpec((cols, BLOCK), lambda i, *_: (0, i))
    column = pl.BlockSpec((HEAD, 1), lambda i, *_: (0, 0))
    shape = jax.ShapeDtypeStruct((cols, length), LOW)
    return pl.pallas_call(
        functools.partial(backward_kernel, heads),
        out_shape=(shape, shape, shape, jax.ShapeDtypeStruct((HEAD, 1), FULL)),
        grid_spec=pltpu.PrefetchScalarGridSpec(
            num_scalar_prefetch=2,
            grid=(steps,),
            in_specs=[
                part,
                whole,
                whole,
                part,
                part,
                pl.BlockSpec((heads, 1, BLOCK), lambda i, *_: (0, 0, i)),
                part,
                column,
                pl.BlockSpec((1, BLOCK), lambda i, *_: (0, i)),
                pl.BlockSpec((length, 1), lambda i, *_: (0, 0)),
            ],
            out_specs=(part, whole, whole, column),
            scratch_shapes=[
                pltpu.VMEM((heads, length, HEAD), LOW),
                pltpu.VMEM((heads, length, HEAD), LOW),
                pltpu.VMEM((cols, length), FULL),
                pltpu.VMEM((cols, length), FULL),
                pltpu.VMEM((cols, BLOCK), FULL),
            ],
        ),
        compiler_params=pltpu.CompilerParams(vmem_limit_bytes=62 * 2**20),
        cost_estimate=pl.CostEstimate(
            flops=8 * 5 * length * length * cols,
            bytes_accessed=8 * cols * length * 2,
            transcendentals=heads * length * length // 3,
        ),
    )(lo, hi, q, k, v, o, go, logs, raw, factor, segq, segk)


def remote(src, dst, sems, index, device):
    return pltpu.make_async_remote_copy(
        src_ref=src,
        dst_ref=dst,
        send_sem=sems[0].at[index],
        recv_sem=sems[1].at[index],
        device_id=device,
        device_id_type=pl.DeviceIdType.MESH,
    )


def greet(peers):
    barrier = pltpu.get_barrier_semaphore()
    for peer in peers:
        pl.semaphore_signal(barrier, inc=1, device_id=peer, device_id_type=pl.DeviceIdType.MESH)
    pl.semaphore_wait(barrier, len(peers))


def head_kernel(
    n_dp, n_pair, gain_ref, factor_ref, tokens_hbm, cot_hbm, block_hbm, slab_hbm,
    q_hbm, k_hbm, v_hbm, raw_hbm, normed_hbm, qkv_hbm, slabs_hbm, cot_out, inverse_ref,
    tokens, others, block, cs_recv, remote_block, pass_on, qkv, turned, normed, q, k, v, raw,
    send_sems, recv_sems, local_sems,
):
    r, s = lax.axis_index("row"), lax.axis_index("cs")
    j, d = lax.axis_index("cp"), lax.axis_index("dp")
    n_col = 2 * n_pair
    subs, width, piece = tokens.shape[1:]
    here = subs * piece
    share = cs_recv.shape[0]
    cols = q.shape[0]
    c_first = (s * n_pair + j) ^ (r * n_pair)
    near = r == s
    sems = (send_sems, recv_sems)
    counter, local_counter = iter(range(1000)), iter(range(1000))
    sent, stored = [], []

    def send(src, dst, device):
        copy = remote(src, dst, sems, next(counter), device)
        copy.start()
        sent.append(copy)
        return copy

    def move(src, dst):
        copy = pltpu.make_async_copy(src, dst, local_sems.at[next(local_counter)])
        copy.start()
        return copy

    def store(src, dst):
        stored.append(move(src, dst))

    def columns(u):
        return pl.ds(u * piece, piece)

    own_tokens = [move(tokens_hbm.at[:, columns(u)], tokens.at[0, u]) for u in range(subs)]
    own_block = move(block_hbm, block)
    store(slab_hbm, slabs_hbm.at[c_first])
    sibling_id = {"row": 1 - r}
    dp_ids = [{"dp": d ^ k} for k in range(1, n_dp)]
    col_ids = [{"cs": s ^ (k // n_pair), "cp": j ^ (k % n_pair)} for k in range(1, n_col)]
    greet([sibling_id] + dp_ids + col_ids)

    cs_copy = send(block_hbm.at[d], cs_recv, {"cs": 1 - s})
    other_copies = {}
    for u in range(subs):
        other_copies[0, u] = send(tokens_hbm.at[:, columns(u)], others.at[0, u], sibling_id)
    pair_copies = {}
    for u in range(subs):
        for m in range(1, n_pair):
            pair_copies[m, u] = send(
                tokens_hbm.at[:, columns(u)], tokens.at[m, u], {"cp": j ^ m}
            )

    cot_copy = send(cot_hbm, cot_out, sibling_id)

    def norm(m, u):
        own, other = tokens[m, u].astype(FULL), others[m, u].astype(FULL)
        squares = jnp.sum(own * own, axis=0, keepdims=True)
        squares = squares + jnp.sum(other * other, axis=0, keepdims=True)
        inverse = lax.rsqrt(squares / D + EPSILON)
        at = pl.ds(pl.multiple_of((j ^ m) * here + u * piece, 128), piece)
        normed[:width, at] = (own * inverse * gain_ref[:width]).astype(LOW)
        normed[width:, at] = (other * inverse * gain_ref[width:]).astype(LOW)
        store(normed.at[:, at], normed_hbm.at[:, at])
        if m == 0:
            inverse_ref[:, columns(u)] = inverse

    def project(m, u):
        at = pl.ds(pl.multiple_of((j ^ m) * here + u * piece, 128), piece)
        for part, out in ((0, None), (1, k), (2, v)):
            value = jnp.dot(
                turned[part * cols:(part + 1) * cols, :], normed[:, at],
                preferred_element_type=FULL,
            )
            if part == 0:
                raw[:, at] = value
                q[:, at] = (value * factor_ref[...]).astype(LOW)
            else:
                out[:, at] = value.astype(LOW)
        for src, dst in ((q, q_hbm), (k, k_hbm), (v, v_hbm), (raw, raw_hbm)):
            store(src.at[:, at], dst.at[:, at])

    for u in range(subs):
        own_tokens[u].wait()
        other_copies[0, u].wait_recv()
        norm(0, u)
    own_block.wait()

    cs_copy.wait_recv()
    dp_copies = [send(cs_recv, remote_block.at[d], peer) for peer in dp_ids]
    slab_copies = [send(slab_hbm, slabs_hbm.at[c_first], peer) for peer in col_ids]
    remote_block[d] = cs_recv[...]
    for u in range(subs - 1):
        for m in range(1, n_pair):
            pair_copies[m, u].wait_recv()
            other_copies[m, u] = send(tokens.at[m, u], others.at[m, u], sibling_id)
    cross_copies = []
    for m in range(n_dp):
        owner = d ^ m
        if m:
            dp_copies[m - 1].wait_recv()
        mine, its = block[owner], remote_block[owner]
        at = pl.multiple_of(owner * share, 32)
        qkv[pl.ds(at, share)] = jnp.where(near, mine, its)
        pass_on[owner] = jnp.where(near, its, mine)
        cross_copies.append(
            send(pass_on.at[owner], qkv.at[pl.ds(width + at, share)], sibling_id)
        )
    u = subs - 1
    for m in range(1, n_pair):
        pair_copies[m, u].wait_recv()
        other_copies[m, u] = send(tokens.at[m, u], others.at[m, u], sibling_id)
    turned[:, :width] = qkv[:width].T
    for copy in cross_copies:
        copy.wait_recv()
    turned[:, width:] = qkv[width:].T
    store(qkv, qkv_hbm)

    for u in range(subs):
        project(0, u)
    for u in range(subs):
        for m in range(1, n_pair):
            other_copies[m, u].wait_recv()
            norm(m, u)
            project(m, u)

    for copy in stored:
        copy.wait()
    for copy in slab_copies + [cot_copy]:
        copy.wait_recv()
    for copy in sent:
        copy.wait_send()


def head(n_dp, n_pair, gain, factor, tokens, cotangent, block, slab):
    width, here = tokens.shape
    wide = block.shape[1]
    cols = wide // 3
    share = width // n_dp
    length = n_pair * here
    n_col = 2 * n_pair
    subs = 2
    piece = here // subs
    count = subs * n_pair * 2 + 2 * n_dp + n_col + 6
    moves = 3 + subs + 5 * subs * n_pair + 4
    hbm = pl.BlockSpec(memory_space=pl.ANY)
    vmem = pl.BlockSpec(memory_space=pltpu.VMEM)
    V = pltpu.VMEM
    shape = jax.ShapeDtypeStruct((cols, length), LOW)
    return pl.pallas_call(
        functools.partial(head_kernel, n_dp, n_pair),
        out_shape=(
            shape,
            shape,
            shape,
            jax.ShapeDtypeStruct((cols, length), FULL),
            jax.ShapeDtypeStruct((2 * width, length), LOW),
            jax.ShapeDtypeStruct((2 * width, wide), LOW),
            jax.ShapeDtypeStruct((n_col,) + slab.shape, LOW),
            jax.ShapeDtypeStruct((width, here), LOW),
            jax.ShapeDtypeStruct((1, here), FULL),
        ),
        in_specs=[vmem] * 2 + [hbm] * 4,
        out_specs=(hbm,) * 8 + (vmem,),
        scratch_shapes=[
            V((n_pair, subs, width, piece), LOW),
            V((n_pair, subs, width, piece), LOW),
            V((n_dp, share, wide), LOW),
            V((share, wide), LOW),
            V((n_dp, share, wide), LOW),
            V((n_dp, share, wide), LOW),
            V((2 * width, wide), LOW),
            V((wide, 2 * width), LOW),
            V((2 * width, length), LOW),
            V((cols, length), LOW),
            V((cols, length), LOW),
            V((cols, length), LOW),
            V((cols, length), FULL),
            pltpu.SemaphoreType.DMA((count,)),
            pltpu.SemaphoreType.DMA((count,)),
            pltpu.SemaphoreType.DMA((moves,)),
        ],
        compiler_params=pltpu.CompilerParams(
            collective_id=2, has_side_effects=True, vmem_limit_bytes=60 * 2**20
        ),
        cost_estimate=pl.CostEstimate(
            flops=4 * wide * width * length, bytes_accessed=2**25, transcendentals=0
        ),
    )(gain, factor, tokens, cotangent, block.reshape(n_dp, share, wide), slab)


def middle_kernel(n_dp, n_pair, unit, gain_ref, att_hbm, tokens_hbm, cot_hbm, cot_other, *refs):
    n_col = 2 * n_pair
    slab_hbms, refs = refs[:n_dp], refs[n_dp:]
    down_hbms, refs = refs[:n_col - 1], refs[n_col - 1:]
    result_hbm, middle_hbm, out_hbm, refs = refs[0], refs[1], refs[2], refs[3:]
    grads_hbms, refs = refs[:n_dp], refs[n_dp:]
    down_outs, refs = refs[:n_col], refs[n_col:]
    (
        gain_out, tokens, cot, slab, out_w, up_w, down_w, out_t, up_t, down_t, out_half, up_half,
        down_half, att, scaled, normed, active, grad_hidden, branch, middle, grad, result, grad_att,
        grads, down_grads, square_send, square_recv, inner_send, inner_recv, inverse, narrow,
        send_sems, recv_sems, local_sems,
    ) = refs
    r, s = lax.axis_index("row"), lax.axis_index("cs")
    j, d = lax.axis_index("cp"), lax.axis_index("dp")
    width, here = tokens.shape
    pieces, _, piece = square_send.shape
    cols = att_hbm.shape[0]
    half = n_col * unit // 2
    rows_q = slab_hbms[0].shape[1]
    rows_g = grads_hbms[0].shape[1]
    c_first = (s * n_pair + j) ^ (r * n_pair)
    sems = (send_sems, recv_sems)
    counter, local_counter = iter(range(1000)), iter(range(1000))
    sent, stored = [], []

    def send(src, dst, device):
        copy = remote(src, dst, sems, next(counter), device)
        copy.start()
        sent.append(copy)
        return copy

    def move(src, dst):
        copy = pltpu.make_async_copy(src, dst, local_sems.at[next(local_counter)])
        copy.start()
        return copy

    def columns(u):
        return pl.ds(u * piece, piece)

    def span(u):
        return slice(u * piece, (u + 1) * piece)

    def down_rows(owner):
        return pl.ds(pl.multiple_of(owner * unit, 16), unit)

    own_rows, other_rows = pl.ds(0, width), pl.ds(width, width)
    weight_loads = [
        move(slab_hbms[m], slab.at[:, pl.ds(pl.multiple_of((d ^ m) * rows_q, 16), rows_q)])
        for m in range(n_dp)
    ] + [
        move(down_hbms[max(m - 1, 0)], down_w.at[down_rows(c_first ^ m)])
        for m in range(n_col)
        if m != 1
    ]
    att_loads = [
        move(
            att_hbm.at[:, pl.ds(pl.multiple_of(j * here + u * piece, 128), piece)],
            att.at[pl.ds(pl.multiple_of(j * cols, 16), cols), columns(u)],
        )
        for u in range(pieces)
    ]
    token_load = move(tokens_hbm, tokens)
    cot_loads = [move(cot_hbm, cot.at[own_rows]), move(cot_other, cot.at[other_rows])]
    sibling_id = {"row": 1 - r}
    pair_ids = [{"cp": j ^ m} for m in range(1, n_pair)]
    greet([sibling_id] + pair_ids)

    att_copies = {}
    for u in range(pieces):
        for m in range(1, n_pair):
            att_copies[u, m] = send(
                att_hbm.at[:, pl.ds(pl.multiple_of((j ^ m) * here + u * piece, 128), piece)],
                att.at[pl.ds(pl.multiple_of(j * cols, 16), cols), columns(u)],
                pair_ids[m - 1],
            )
        if u == 1:
            down_copy = send(down_hbms[0], down_w.at[down_rows(c_first)], pair_ids[0])

    for copy in weight_loads:
        copy.wait()
    for m in range(n_col):
        at = slice(m * unit, (m + 1) * unit)
        out_w[at] = slab[m, :unit]
        up_w[at] = slab[m, unit:2 * unit]
    cross_copies = []

    def cross(whole, part):
        cross_copies.append(send(whole.at[pl.ds(half, half)], part.at[:, other_rows], sibling_id))
        part[:, :width] = whole[:half]

    cross(up_w, up_half)
    cross(out_w, out_half)
    out_t[...] = out_w[...].T
    narrow[...] = jnp.zeros_like(narrow)

    copies = {}

    def exchange(name, u, ref):
        copies[name, u] = send(
            ref.at[own_rows, columns(u)], ref.at[other_rows, columns(u)], sibling_id
        )

    def share_heads(u):
        att_loads[u].wait()
        for m in range(1, n_pair):
            att_copies[u, m].wait_recv()
        exchange("att", u, att)

    def first_branch(u):
        if u == 0:
            token_load.wait()
        copies["att", u].wait_recv()
        value = tokens[:, span(u)].astype(FULL) + jnp.dot(
            out_t[...], att[:, span(u)], preferred_element_type=FULL
        )
        scaled[:width, span(u)] = (value * gain_ref[...]).astype(LOW)
        exchange("scaled", u, scaled)
        square_send[u] = jnp.sum(value * value, axis=0, keepdims=True)
        copies["square", u] = send(square_send.at[u], square_recv.at[u], sibling_id)
        middle[:, span(u)] = value

    def hidden_units(u):
        if u == 0:
            for copy in cot_loads:
                copy.wait()
            for copy in cross_copies:
                copy.wait_recv()
            up_t[...] = up_w[...].T
            down_t[...] = down_w[...].T
        grad_active = jnp.dot(down_half[...], cot[:, span(u)], preferred_element_type=FULL)
        copies["scaled", u].wait_recv()
        copies["square", u].wait_recv()
        scale = lax.rsqrt((square_send[u] + square_recv[u]) / D + EPSILON)
        inverse[u] = scale
        hidden = scale * jnp.dot(up_half[...], scaled[:, span(u)], preferred_element_type=FULL)
        sigmoid = jax.nn.sigmoid(hidden)
        value = (grad_active * sigmoid * (1.0 + hidden * (1.0 - sigmoid))).astype(LOW)
        grad_hidden[:half, span(u)] = value
        exchange("grad_hidden", u, grad_hidden)
        active[:half, span(u)] = (hidden * sigmoid).astype(LOW)
        exchange("active", u, active)
        inner_send[u] = jnp.sum(value.astype(FULL) * hidden, axis=0, keepdims=True)
        copies["inner", u] = send(inner_send.at[u], inner_recv.at[u], sibling_id)
        normed[:, span(u)] = (middle[:, span(u)] * scale * gain_ref[...]).astype(LOW)

    def second_branch(u):
        copies["grad_hidden", u].wait_recv()
        copies["inner", u].wait_recv()
        scale = inverse[u]
        inner = scale * scale * ((inner_send[u] + inner_recv[u]) / D)
        back = jnp.dot(up_t[...], grad_hidden[:, span(u)], preferred_element_type=FULL)
        value = (
            cot[:width, span(u)].astype(FULL)
            + scale * (back * gain_ref[...])
            - middle[:, span(u)] * inner
        )
        branch[:width, span(u)] = value.astype(LOW)
        exchange("branch", u, branch)
        grad[:, span(u)] = value
        stored.append(move(grad.at[:, columns(u)], middle_hbm.at[:, columns(u)]))
        product = back * middle[:, span(u)] * scale
        total = narrow[...]
        for v in range(piece // 128):
            total = total + product[:, v * 128:(v + 1) * 128]
        narrow[...] = total
        copies["active", u].wait_recv()
        result[:, span(u)] = middle[:, span(u)] + jnp.dot(
            down_t[...], active[:, span(u)], preferred_element_type=FULL
        )
        stored.append(move(result.at[:, columns(u)], result_hbm.at[:, columns(u)]))

    def heads_back(u):
        copies["branch", u].wait_recv()
        grad_att[:, span(u)] = jnp.dot(
            out_half[...], branch[:, span(u)], preferred_element_type=FULL
        ).astype(LOW)
        target = pl.ds(pl.multiple_of(j * here + u * piece, 128), piece)
        for m in range(n_pair):
            source = grad_att.at[
                pl.ds(pl.multiple_of((j ^ m) * cols, 16), cols), columns(u)
            ]
            if m:
                copies["out", u, m] = send(source, out_hbm.at[:, target], pair_ids[m - 1])
            else:
                stored.append(move(source, out_hbm.at[:, target]))

    stages = (share_heads, first_branch, hidden_units, second_branch, heads_back)
    for t in range(pieces + len(stages) - 1):
        for number in reversed(range(len(stages))):
            if 0 <= t - number < pieces:
                stages[number](t - number)
        if t == 1:
            down_copy.wait_recv()
            cross(down_w, down_half)

    def product(left, right, target, first):
        turned = right[:width].T
        for n in range(n_col):
            target[n, first:first + unit] = jnp.dot(
                left[n * unit:(n + 1) * unit], turned, preferred_element_type=FULL
            ).astype(LOW)

    product(active, cot, down_grads, 0)
    for m in range(n_col):
        stored.append(move(down_grads.at[c_first ^ m], down_outs[m]))
    if grads.shape[1] > 2 * unit:
        grads[...] = jnp.zeros_like(grads)
    product(grad_hidden, normed, grads, unit)
    product(att, branch, grads, 0)
    for m in range(n_dp):
        at = pl.ds(pl.multiple_of((d ^ m) * rows_g, 16), rows_g)
        stored.append(move(grads.at[:, at], grads_hbms[m]))
    gain_out[...] = jnp.sum(narrow[...].T, axis=0, keepdims=True)

    for u in range(pieces):
        for m in range(1, n_pair):
            copies["out", u, m].wait_recv()
    for copy in stored:
        copy.wait()
    for copy in sent:
        copy.wait_send()


def middle_part(n_dp, n_pair, gain, attended, tokens, cotangent, cot_other, slabs, downs):
    width, here = tokens.shape
    n_col = 2 * n_pair
    cols, length = attended.shape
    unit = downs[0].shape[0]
    half = n_col * unit // 2
    rows_q = slabs[0].shape[1]
    rows_g = quarter_rows(2 * unit, n_dp)
    pieces = max(2, here // 256)
    piece = here // pieces
    count = 2 * pieces * (n_pair - 1) + 7 * pieces + 8
    moves = 2 * n_dp + 2 * n_col + 4 * pieces + 4
    hbm = pl.BlockSpec(memory_space=pl.ANY)
    vmem = pl.BlockSpec(memory_space=pltpu.VMEM)
    V = pltpu.VMEM
    S = jax.ShapeDtypeStruct
    weight = V((2 * half, width), LOW)
    weight_t = V((width, 2 * half), LOW)
    both = V((2 * width, here), LOW)
    whole = V((width, here), FULL)
    row = V((pieces, 1, piece), FULL)
    out = pl.pallas_call(
        functools.partial(middle_kernel, n_dp, n_pair, unit),
        out_shape=(
            S((width, here), FULL),
            S((width, here), FULL),
            S((cols, length), LOW),
        )
        + (S((n_col, rows_g, width), LOW),) * n_dp
        + (S((unit, width), LOW),) * n_col
        + (S((1, width), FULL),),
        in_specs=[vmem] + [hbm] * (3 + n_dp + n_col),
        out_specs=(hbm,) * (3 + n_dp + n_col) + (vmem,),
        scratch_shapes=[
            V((width, here), LOW),
            both,
            V((n_col, n_dp * rows_q, width), LOW),
            weight,
            weight,
            weight,
            weight_t,
            weight_t,
            weight_t,
            V((half, 2 * width), LOW),
            V((half, 2 * width), LOW),
            V((half, 2 * width), LOW),
            both,
            both,
            V((width, here), LOW),
            V((2 * half, here), LOW),
            V((2 * half, here), LOW),
            both,
            whole,
            whole,
            whole,
            V((width, here), LOW),
            V((n_col, n_dp * rows_g, width), LOW),
            V((n_col, unit, width), LOW),
            row,
            row,
            row,
            row,
            row,
            V((width, 128), FULL),
            pltpu.SemaphoreType.DMA((count,)),
            pltpu.SemaphoreType.DMA((count,)),
            pltpu.SemaphoreType.DMA((moves,)),
        ],
        compiler_params=pltpu.CompilerParams(
            collective_id=3, has_side_effects=True, vmem_limit_bytes=62 * 2**20
        ),
        cost_estimate=pl.CostEstimate(
            flops=18 * 2 * half * width * here, bytes_accessed=2**25, transcendentals=0
        ),
    )(gain, attended, tokens, cotangent, cot_other, *slabs, *downs)
    return out[0], out[1], out[2], out[3:3 + n_dp], out[3 + n_dp:-1], out[-1]


def quarter_rows(rows, n_dp):
    return -(-rows // (16 * n_dp)) * 16


def tail_kernel(
    n_dp, n_pair, gain_ref, inverse_ref, sums_ref, qkv_hbm, dq_hbm, dk_hbm, dv_hbm, normed_hbm,
    tokens_hbm, middle_hbm, *refs,
):
    n_col = 2 * n_pair
    grads_hbms, refs = refs[:n_dp], refs[n_dp:]
    down_hbms, refs = refs[:n_col], refs[n_col:]
    (
        result_hbm, qkv_out, grads_out, down_out, sums_out,
        qkv, dproj, normed, tokens, middle, result, row_send, row_recv, own, pair_send, pair_recv,
        dp_send, dp_recv, dp_own, cross_send, cross_recv, cs_send, cs_recv, final, grads_parts,
        grads_send, grads_recv, grads_final, down_parts, down_send, down_recv, down_final,
        inner_send, inner_recv, sums_send, sums_recv, last_sums, send_sems, recv_sems, local_sems,
    ) = refs
    r, s = lax.axis_index("row"), lax.axis_index("cs")
    j, d = lax.axis_index("cp"), lax.axis_index("dp")
    width, here = tokens.shape
    cols = dq_hbm.shape[0]
    unit = down_parts.shape[1]
    share = width // n_dp
    part = share // 2
    rows_d = down_final.shape[0]
    subs = row_send.shape[1]
    piece = here // subs
    c_first = (s * n_pair + j) ^ (r * n_pair)
    near = r == s
    sems = (send_sems, recv_sems)
    counter, local_counter = iter(range(1000)), iter(range(1000))
    sent, stored = [], []

    def send(src, dst, device):
        copy = remote(src, dst, sems, next(counter), device)
        copy.start()
        sent.append(copy)
        return copy

    def move(src, dst):
        copy = pltpu.make_async_copy(src, dst, local_sems.at[next(local_counter)])
        copy.start()
        return copy

    early = [
        move(dq_hbm, dproj.at[pl.ds(0, cols)]),
        move(dk_hbm, dproj.at[pl.ds(cols, cols)]),
        move(dv_hbm, dproj.at[pl.ds(2 * cols, cols)]),
        move(normed_hbm, normed),
    ]
    load_qkv = move(qkv_hbm, qkv)
    load_down = [move(down_hbms[k], down_parts.at[k]) for k in range(n_col) if k != 1]
    load_grads = [move(grads_hbms[k], grads_parts.at[k]) for k in range(n_dp)]
    late = [move(tokens_hbm, tokens), move(middle_hbm, middle)]

    sibling_id = {"row": 1 - r}
    cs_id = {"cs": 1 - s}
    dp_ids = [{"dp": d ^ k} for k in range(1, n_dp)]
    col_ids = [{"cs": s ^ (k // n_pair), "cp": j ^ (k % n_pair)} for k in range(1, n_col)]
    greet([sibling_id] + dp_ids + col_ids)

    down_copy = send(down_hbms[1], down_parts.at[1], col_ids[0])

    def quarter(half, owner):
        at = pl.ds(pl.multiple_of(half * width + owner * share, 32), share)
        return mm(normed[at, :], dproj[...], 1, 1)

    def rows_of(half, chunk, u):
        at = pl.ds(pl.multiple_of(chunk * here + u * piece, 128), piece)
        return jnp.dot(
            qkv[half * width:(half + 1) * width, :], dproj[:, at], preferred_element_type=FULL
        )

    dp_copies = {}

    def send_part(k, p):
        rows = pl.ds(p * part, part)
        dp_copies[k, p] = send(
            dp_send.at[k - 1, :, rows], dp_recv.at[k - 1, :, rows], dp_ids[k - 1]
        )

    def quarters(k):
        for half in range(2):
            dp_send[k - 1, half] = quarter(half, d ^ k).astype(LOW)
        send_part(k, 0)

    row_copies, pair_copies = {}, []
    for copy in early:
        copy.wait()
    quarters(1)
    load_qkv.wait()
    for k in range(1, n_pair):
        for u in range(subs):
            row_send[k, u] = rows_of(1, j ^ k, u).astype(LOW)
            row_copies[k, u] = send(row_send.at[k, u], row_recv.at[k, u], sibling_id)
    for k in range(1, n_pair):
        for u in range(subs):
            value = rows_of(0, j ^ k, u)
            row_copies[k, u].wait_recv()
            pair_send[k - 1, u] = (value + row_recv[k, u].astype(FULL)).astype(LOW)
            pair_copies.append(
                send(pair_send.at[k - 1, u], pair_recv.at[k - 1, u], {"cp": j ^ k})
            )
    for k in range(2, n_dp):
        quarters(k)
    for copy in load_down:
        copy.wait()
    down_copy.wait_recv()
    value = down_parts[0].astype(FULL)
    for k in range(1, n_col):
        value = value + down_parts[k].astype(FULL)
    if down_send.shape[0] > unit:
        down_send[...] = jnp.zeros_like(down_send)
    down_send[:unit] = value.astype(LOW)

    def down_rows(owner):
        return pl.ds(pl.multiple_of(owner * rows_d, 16), rows_d)

    down_copies = [
        send(down_send.at[down_rows(d ^ k)], down_recv.at[k - 1], dp_ids[k - 1])
        for k in range(1, n_dp)
    ]
    for k in range(1, n_dp):
        send_part(k, 1)
    for half in range(2):
        dp_own[half] = quarter(half, d)

    for u in range(subs):
        row_send[0, u] = rows_of(1, j, u).astype(LOW)
        row_copies[0, u] = send(row_send.at[0, u], row_recv.at[0, u], sibling_id)
    for u in range(subs):
        own[u] = rows_of(0, j, u)

    cs_copies = []

    def reduce_part(p):
        rows = slice(p * part, (p + 1) * part)
        for k in range(1, n_dp):
            dp_copies[k, p].wait_recv()

        def total(half):
            value = dp_own[half, rows]
            for k in range(1, n_dp):
                value = value + dp_recv[k - 1, half, rows].astype(FULL)
            return value

        cross_send[p] = total(1).astype(LOW)
        cross_copy = send(cross_send.at[p], cross_recv.at[p], sibling_id)
        kept = total(0)
        cross_copy.wait_recv()
        crossed = cross_recv[p].astype(FULL)
        cs_send[p] = jnp.where(near, crossed, kept).astype(LOW)
        cs_copies.append(send(cs_send.at[p], cs_recv.at[p], cs_id))
        dp_own[0, rows] = jnp.where(near, kept, crossed)

    reduce_part(0)

    for copy in load_grads:
        copy.wait()

    def summed(place_at):
        value = grads_parts[0, place_at].astype(FULL)
        for k in range(1, n_dp):
            value = value + grads_parts[k, place_at].astype(FULL)
        return value

    grads_copies = []
    for k in range(1, n_col):
        grads_send[k - 1] = summed(c_first ^ k).astype(LOW)
        grads_copies.append(send(grads_send.at[k - 1], grads_recv.at[k - 1], col_ids[k - 1]))

    value = down_send[down_rows(d)].astype(FULL)
    for k in range(1, n_dp):
        down_copies[k - 1].wait_recv()
        value = value + down_recv[k - 1].astype(FULL)
    down_final[...] = value.astype(LOW)
    out_copies = [send(down_final, down_out.at[d], peer) for peer in dp_ids]
    stored.append(move(down_final, down_out.at[d]))
    reduce_part(1)

    for copy in late:
        copy.wait()
    for copy in pair_copies:
        copy.wait_recv()
    inverse = inverse_ref[...]
    for u in range(subs):
        row_copies[0, u].wait_recv()
        at = slice(u * piece, (u + 1) * piece)
        value = own[u] + row_recv[0, u].astype(FULL)
        for k in range(1, n_pair):
            value = value + pair_recv[k - 1, u].astype(FULL)
        own[u] = value
        inner_send[:, at] = jnp.sum(
            value * gain_ref[...] * tokens[:, at].astype(FULL), axis=0, keepdims=True
        )
    inner_copy = send(inner_send, inner_recv, sibling_id)

    def finish_part(p):
        cs_copies[p].wait_recv()
        rows = slice(p * part, (p + 1) * part)
        final[p] = (dp_own[0, rows] + cs_recv[p].astype(FULL)).astype(LOW)
        target = qkv_out.at[d, pl.ds(p * part, part)]
        out_copies.extend([send(final.at[p], target, peer) for peer in dp_ids])
        stored.append(move(final.at[p], target))

    finish_part(0)
    narrow = jnp.zeros((width, 128), FULL)
    for u in range(subs):
        at = slice(u * piece, (u + 1) * piece)
        wide = own[u] * tokens[:, at].astype(FULL) * inverse[:, at]
        for v in range(piece // 128):
            narrow = narrow + wide[:, v * 128:(v + 1) * 128]
    gain_part = jnp.sum(narrow.T, axis=0, keepdims=True)
    sums_send[0] = jnp.concatenate([gain_part, sums_ref[1:]], 0)
    sums_copies = {}

    def send_sums(step, peers):
        for k, peer in enumerate(peers):
            sums_copies[step, k] = send(sums_send.at[step], sums_recv.at[step, k], peer)

    def add_sums(step, members):
        value = sums_send[step]
        for k in range(members - 1):
            sums_copies[step, k].wait_recv()
            value = value + sums_recv[step, k]
        sums_send[step + 1] = value

    send_sums(0, dp_ids)
    inner_copy.wait_recv()
    inner = (inner_send[...] + inner_recv[...]) / D
    for u in range(subs):
        at = slice(u * piece, (u + 1) * piece)
        result[:, at] = (
            middle[:, at]
            + inverse[:, at] * (own[u] * gain_ref[...])
            - tokens[:, at].astype(FULL)
            * (inverse[:, at] * inverse[:, at] * inverse[:, at] * inner[:, at])
        )
    stored.append(move(result, result_hbm))
    add_sums(0, n_dp)
    send_sums(1, col_ids)
    finish_part(1)

    value = summed(c_first)
    for k in range(1, n_col):
        grads_copies[k - 1].wait_recv()
        value = value + grads_recv[k - 1].astype(FULL)
    grads_final[...] = value.astype(LOW)
    out_copies += [send(grads_final, grads_out.at[d], peer) for peer in dp_ids]
    stored.append(move(grads_final, grads_out.at[d]))

    add_sums(1, n_col)
    sums_copy = send(sums_send.at[2], last_sums, sibling_id)
    sums_copy.wait_recv()
    sums_out[0] = sums_send[2]
    sums_out[1] = last_sums[...]
    for copy in out_copies:
        copy.wait_recv()
    for copy in stored:
        copy.wait()
    for copy in sent:
        copy.wait_send()


def tail(n_dp, n_pair, gain, inverse, sums, qkv, dq, dk, dv, normed, tokens, middle, grads, downs):
    width, here = tokens.shape
    length = normed.shape[1]
    cols = dq.shape[0]
    unit = downs[0].shape[0]
    rows_d = quarter_rows(unit, n_dp)
    share = width // n_dp
    subs = 2
    piece = here // subs
    n_col = 2 * n_pair
    part = grads[0].shape[1:]
    wide = 3 * cols
    count = 2 * n_pair * subs + 8 * n_dp + 2 * n_col + 12
    moves = 13 + n_dp + n_col
    hbm = pl.BlockSpec(memory_space=pl.ANY)
    vmem = pl.BlockSpec(memory_space=pltpu.VMEM)
    V = pltpu.VMEM
    halves = V((2, share // 2, wide), LOW)
    return pl.pallas_call(
        functools.partial(tail_kernel, n_dp, n_pair),
        out_shape=(
            jax.ShapeDtypeStruct((width, here), FULL),
            jax.ShapeDtypeStruct((n_dp, share, wide), LOW),
            jax.ShapeDtypeStruct((n_dp,) + part, LOW),
            jax.ShapeDtypeStruct((n_dp, rows_d, width), LOW),
            jax.ShapeDtypeStruct((2,) + sums.shape, FULL),
        ),
        in_specs=[vmem] * 3 + [hbm] * (7 + n_dp + n_col),
        out_specs=(hbm,) * 4 + (vmem,),
        scratch_shapes=[
            V((2 * width, wide), LOW),
            V((wide, length), LOW),
            V((2 * width, length), LOW),
            V((width, here), LOW),
            V((width, here), FULL),
            V((width, here), FULL),
            V((n_pair, subs, width, piece), LOW),
            V((n_pair, subs, width, piece), LOW),
            V((subs, width, piece), FULL),
            V((n_pair - 1, subs, width, piece), LOW),
            V((n_pair - 1, subs, width, piece), LOW),
            V((n_dp - 1, 2, share, wide), LOW),
            V((n_dp - 1, 2, share, wide), LOW),
            V((2, share, wide), FULL),
            halves,
            halves,
            halves,
            halves,
            halves,
            V((n_dp, n_col) + part, LOW),
            V((n_col - 1,) + part, LOW),
            V((n_col - 1,) + part, LOW),
            V(part, LOW),
            V((n_col, unit, width), LOW),
            V((n_dp * rows_d, width), LOW),
            V((n_dp - 1, rows_d, width), LOW),
            V((rows_d, width), LOW),
            V((1, here), FULL),
            V((1, here), FULL),
            V((3,) + sums.shape, FULL),
            V((2, max(n_dp, n_col) - 1) + sums.shape, FULL),
            V(sums.shape, FULL),
            pltpu.SemaphoreType.DMA((count,)),
            pltpu.SemaphoreType.DMA((count,)),
            pltpu.SemaphoreType.DMA((moves,)),
        ],
        compiler_params=pltpu.CompilerParams(
            collective_id=1, has_side_effects=True, vmem_limit_bytes=62 * 2**20
        ),
        cost_estimate=pl.CostEstimate(
            flops=8 * wide * width * length, bytes_accessed=2**25, transcendentals=0
        ),
    )(gain, inverse, sums, qkv, dq, dk, dv, normed, tokens, middle, *grads, *downs)


def on_device(
    tokens,
    segment_ids,
    padding_mask,
    w_qkv,
    w_out,
    w_up,
    w_down,
    gain_attn,
    gain_mlp,
    scale_raw,
    cotangent,
):
    width, here = tokens.shape
    r, s = lax.axis_index("row"), lax.axis_index("cs")
    j, d = lax.axis_index("cp"), lax.axis_index("dp")
    n_pair, n_dp, n_col = lax.axis_size("cp"), lax.axis_size("dp"), lax.axis_size(COLS)
    c = s * n_pair + j
    head_cols = w_qkv.shape[0] // (3 * width)
    heads = head_cols // HEAD
    near = r == s

    segments = jnp.where(s == r, segment_ids[0], sibling(segment_ids)[0])
    padding = jnp.where(s == r, padding_mask[0], sibling(padding_mask)[0])
    length = segments.shape[0]
    firsts = segments[::BLOCK]
    starts = jnp.sum((segments[None, :] < firsts[:, None]).astype(jnp.int32), axis=1)
    filled = (jnp.sum(padding) + BLOCK - 1) // BLOCK
    blocks = jnp.arange(length // BLOCK, dtype=jnp.int32)
    lo = starts // BLOCK
    hi = jnp.minimum(blocks, filled)
    segq = segments[None, :]
    segk = jnp.where(padding == 1, segments, -1)[:, None]

    def halves(vector):
        whole = vector.reshape(2, width)
        own = lax.dynamic_index_in_dim(whole, r, 0, keepdims=False)
        other = lax.dynamic_index_in_dim(whole, 1 - r, 0, keepdims=False)
        return own[:, None], other[:, None]

    gain_one, gain_one_other = halves(gain_attn)
    gain_two, _ = halves(gain_mlp)
    factor = (LOG_TWO_E / math.sqrt(HEAD) * jnp.log1p(jnp.exp(scale_raw)))[:, None]

    block = w_qkv.reshape(width, 3 * head_cols)
    unit = w_up.shape[0] // width
    slab = jnp.concatenate([w_out.reshape(-1, width), w_up.reshape(width, -1).T], 0)
    slab_rows = quarter_rows(2 * unit, n_dp)
    slab = jnp.pad(slab, ((0, n_dp * slab_rows - 2 * unit), (0, 0)))
    slab = cut(slab, d, n_dp, 0)
    down = w_down.reshape(-1, width)
    (
        queries, key_heads, values, query_raw, normed_one, qkv, slabs, cot_other, inverse_one,
    ) = head(
        n_dp, n_pair, jnp.concatenate([gain_one, gain_one_other], 0), jnp.tile(factor, (heads, 1)),
        tokens, cotangent, block, slab,
    )
    slabs = gather(slabs, "dp")
    downs = [down] + [
        lax.ppermute(down, COLS, [(i, i ^ k) for i in range(n_col)]) for k in range(2, n_col)
    ]
    attended, logs = attention_forward(queries, key_heads, values, segq, segk, lo, hi)
    result, grad_middle, grad_attended, grads, down_grads, gain_two_part = middle_part(
        n_dp, n_pair, gain_two, attended, tokens, cotangent, cot_other, slabs, downs
    )
    received = [grads[0]] + [shift(grads[k], "dp", k) for k in range(1, n_dp)]
    down_received = list(down_grads[:2]) + [
        lax.ppermute(down_grads[k], COLS, [(i, i ^ k) for i in range(n_col)])
        for k in range(2, n_col)
    ]

    dq, dk, dv, scale_part = attention_backward(
        queries, key_heads, values, attended, grad_attended, logs, query_raw, factor,
        segq, segk, lo, hi,
    )
    scale_part = (
        scale_part[:, 0] * (LOG_TWO_E / math.sqrt(HEAD)) * jax.nn.sigmoid(scale_raw)
    )
    sums = jnp.concatenate(
        [
            jnp.zeros((1, width), FULL),
            gain_two_part,
            jnp.pad(scale_part, (0, width - HEAD))[None],
            jnp.zeros((5, width), FULL),
        ]
    )
    grad_tokens, grad_qkv, final, final_down, sums = tail(
        n_dp, n_pair, gain_one, inverse_one, sums, qkv, dq, dk, dv, normed_one, tokens,
        grad_middle, received, down_received,
    )
    grad_qkv = grad_qkv.astype(FULL)
    final = final.reshape(-1, width)
    final = [final[i * unit:(i + 1) * unit].astype(FULL) for i in range(2)]
    final.append(final_down.reshape(-1, width)[:unit].astype(FULL))
    own, other = sums[0], sums[1]
    first = r == 0
    gains = jnp.concatenate(
        [jnp.where(first, own[:2], other[:2]), jnp.where(first, other[:2], own[:2])], 1
    )
    scale_total = (own[2] + other[2])[:HEAD]
    return (
        result,
        grad_tokens,
        grad_qkv.reshape(-1),
        final[0].reshape(-1),
        final[1].T.reshape(-1),
        final[2].reshape(-1),
        gains[0],
        gains[1],
        scale_total,
    )


def solution(mesh):
    n_dp, n_row, n_col = (mesh.shape[name] for name in ("dp", "row", "col"))
    split = Mesh(
        np.asarray(mesh.devices).reshape(n_dp, n_row, n_row, n_col // n_row),
        ("dp", "row", "cs", "cp"),
    )
    rows = P("row", ("dp", "cs", "cp"))
    ids = P(("dp", "row"), None)
    blocks = P(("row", "cs", "cp"))
    return jax.shard_map(
        on_device,
        mesh=split,
        in_specs=(rows, ids, ids, blocks, blocks, blocks, blocks, P(), P(), P(), rows),
        out_specs=(rows, rows, blocks, blocks, blocks, blocks, P(), P(), P()),
        check_vma=False,
    )
```

```python
import functools
import math

import jax
import jax.numpy as jnp
import numpy as np
from jax import lax
from jax.experimental import pallas as pl
from jax.experimental.pallas import tpu as pltpu
from jax.sharding import Mesh, PartitionSpec as P

D = 1280
HEAD = 80
EPSILON = 1e-06
LOG_TWO_E = 1.442695041
BLOCK = 256
LOW = jnp.bfloat16
FULL = jnp.float32
COLS = ("cs", "cp")


def mm(left, right, left_axis, right_axis):
    return lax.dot_general(
        left, right, (((left_axis,), (right_axis,)), ((), ())), preferred_element_type=FULL
    )


def shift(x, axis, k):
    n = lax.axis_size(axis)
    return lax.ppermute(x, axis, [(i, i ^ k) for i in range(n)])


def sibling(x):
    return shift(x, "row", 1)


def cut(x, index, count, axis):
    step = x.shape[axis] // count
    return lax.dynamic_slice_in_dim(x, index * step, step, axis)


def gather(x, axis):
    return [x] + [shift(x, axis, k) for k in range(1, lax.axis_size(axis))]


def diag_mask(segq, segk):
    size = segk.shape[0], segq.shape[1]
    ki = lax.broadcasted_iota(jnp.int32, size, 0)
    qi = lax.broadcasted_iota(jnp.int32, size, 1)
    return ((segk == segq) & (ki <= qi)) | (ki == qi)


def column(row):
    return jnp.broadcast_to(row, (8, row.shape[1])).T[:, :1]


def rows_of(h):
    return slice(h * HEAD, (h + 1) * HEAD)


def forward_kernel(heads, lo_ref, hi_ref, q_ref, k_ref, v_ref, segq_ref, segk_ref, o_ref, log_ref, ks, segks):
    i = pl.program_id(0)

    @pl.when(i == 0)
    def _():
        for h in range(heads):
            ks[h] = k_ref[h * HEAD:(h + 1) * HEAD, :].T
        segks[...] = column(segk_ref[...])

    segq = segq_ref[...]

    def visit(kb, carry, diagonal):
        at = pl.ds(pl.multiple_of(kb * BLOCK, BLOCK), BLOCK)
        segk = segks[at, :]
        mask = diag_mask(segq, segk) if diagonal else segk == segq
        scores = [
            jnp.dot(ks[h, at, :], q_ref[rows_of(h), :], preferred_element_type=FULL)
            for h in range(heads)
        ]
        peaks, totals, weights = [], [], []
        for h in range(heads):
            s = jnp.where(mask, scores[h], -1e30)
            peak = jnp.max(s, axis=0, keepdims=True)
            if not diagonal:
                peak = jnp.maximum(carry[h][0], peak)
            p = jnp.exp(s - peak)
            peaks.append(peak)
            totals.append(jnp.sum(p, axis=0, keepdims=True))
            weights.append(p.astype(LOW))
        out = []
        for h in range(heads):
            new = jnp.dot(v_ref[rows_of(h), at], weights[h], preferred_element_type=FULL)
            total = totals[h]
            if not diagonal:
                m, l, acc = carry[h]
                keep = jnp.exp(m - peaks[h])
                total = l * keep + total
                new = acc * keep + new
            out.append((peaks[h], total, new))
        return tuple(out)

    carry = visit(i, None, True)
    carry = lax.fori_loop(lo_ref[i], hi_ref[i], lambda kb, c: visit(kb, c, False), carry)
    for h in range(heads):
        m, l, acc = carry[h]
        o_ref[h * HEAD:(h + 1) * HEAD, :] = (acc / l).astype(LOW)
        log_ref[h] = m + jnp.log(l)


def attention_forward(q, k, v, segq, segk, lo, hi):
    cols, length = q.shape
    heads = cols // HEAD
    steps = length // BLOCK
    whole = pl.BlockSpec((cols, length), lambda i, *_: (0, 0))
    part = pl.BlockSpec((cols, BLOCK), lambda i, *_: (0, i))
    return pl.pallas_call(
        functools.partial(forward_kernel, heads),
        out_shape=(
            jax.ShapeDtypeStruct((cols, length), LOW),
            jax.ShapeDtypeStruct((heads, 1, length), FULL),
        ),
        grid_spec=pltpu.PrefetchScalarGridSpec(
            num_scalar_prefetch=2,
            grid=(steps,),
            in_specs=[
                part,
                whole,
                whole,
                pl.BlockSpec((1, BLOCK), lambda i, *_: (0, i)),
                pl.BlockSpec((1, length), lambda i, *_: (0, 0)),
            ],
            out_specs=(part, pl.BlockSpec((heads, 1, BLOCK), lambda i, *_: (0, 0, i))),
            scratch_shapes=[pltpu.VMEM((heads, length, HEAD), LOW), pltpu.VMEM((length, 1), FULL)],
        ),
        compiler_params=pltpu.CompilerParams(vmem_limit_bytes=62 * 2**20),
        cost_estimate=pl.CostEstimate(
            flops=8 * 2 * length * length * cols,
            bytes_accessed=4 * cols * length * 2,
            transcendentals=heads * length * length // 3,
        ),
    )(lo, hi, q, k, v, segq, segk)


def backward_kernel(
    heads, lo_ref, hi_ref, q_ref, k_ref, v_ref, o_ref, go_ref, log_ref, raw_ref, factor_ref,
    segq_ref, segk_ref, dq_ref, dk_ref, dv_ref, scale_ref, ks, vs, qs, gs, dks, dvs, dqs, segks,
):
    i = pl.program_id(0)

    @pl.when(i == 0)
    def _():
        for h in range(heads):
            ks[h] = k_ref[h * HEAD:(h + 1) * HEAD, :].T
            vs[h] = v_ref[h * HEAD:(h + 1) * HEAD, :].T
        segks[...] = column(segk_ref[...])
        scale_ref[...] = jnp.zeros_like(scale_ref)

    segq = segq_ref[...]
    inner = [
        jnp.sum(
            o_ref[h * HEAD:(h + 1) * HEAD, :].astype(FULL)
            * go_ref[h * HEAD:(h + 1) * HEAD, :].astype(FULL),
            axis=0,
            keepdims=True,
        )
        for h in range(heads)
    ]

    for h in range(heads):
        qs[h] = q_ref[rows_of(h), :].T
        gs[h] = go_ref[rows_of(h), :].T

    def visit(kb, diagonal):
        at = pl.ds(pl.multiple_of(kb * BLOCK, BLOCK), BLOCK)
        segk = segks[at, :]
        mask = diag_mask(segq, segk) if diagonal else segk == segq
        scores = [
            jnp.dot(ks[h, at, :], q_ref[rows_of(h), :], preferred_element_type=FULL)
            for h in range(heads)
        ]
        dps = [
            jnp.dot(vs[h, at, :], go_ref[rows_of(h), :], preferred_element_type=FULL)
            for h in range(heads)
        ]
        ps, dss = [], []
        for h in range(heads):
            p = jnp.where(mask, jnp.exp(scores[h] - log_ref[h]), 0.0)
            dss.append((p * (dps[h] - inner[h])).astype(LOW))
            ps.append(p.astype(LOW))
        for h in range(heads):
            new_v = jnp.dot(ps[h], gs[h], preferred_element_type=FULL)
            new_k = jnp.dot(dss[h], qs[h], preferred_element_type=FULL)
            new_q = jnp.dot(k_ref[rows_of(h), at], dss[h], preferred_element_type=FULL)
            if diagonal:
                dvs[h, at, :], dks[h, at, :], dqs[rows_of(h), :] = new_v, new_k, new_q
            else:
                dvs[h, at, :] += new_v
                dks[h, at, :] += new_k
                dqs[rows_of(h), :] += new_q

    visit(i, True)

    @pl.loop(lo_ref[i], hi_ref[i])
    def _(kb):
        visit(kb, False)

    factor = column(factor_ref[...])
    part = jnp.zeros((HEAD, 1), FULL)
    for h in range(heads):
        rows = slice(h * HEAD, (h + 1) * HEAD)
        dq = dqs[rows, :]
        part = part + jnp.sum(dq * raw_ref[rows, :], axis=1, keepdims=True)
        dq_ref[rows, :] = (dq * factor).astype(LOW)
    scale_ref[...] += part

    @pl.when(i == pl.num_programs(0) - 1)
    def _():
        for h in range(heads):
            dk_ref[rows_of(h), :] = dks[h].astype(LOW).T
            dv_ref[rows_of(h), :] = dvs[h].astype(LOW).T


def attention_backward(q, k, v, o, go, logs, raw, factor, segq, segk, lo, hi):
    cols, length = q.shape
    heads = cols // HEAD
    steps = length // BLOCK
    whole = pl.BlockSpec((cols, length), lambda i, *_: (0, 0))
    part = pl.BlockSpec((cols, BLOCK), lambda i, *_: (0, i))
    total = pl.BlockSpec((HEAD, 1), lambda i, *_: (0, 0))
    shape = jax.ShapeDtypeStruct((cols, length), LOW)
    return pl.pallas_call(
        functools.partial(backward_kernel, heads),
        out_shape=(shape, shape, shape, jax.ShapeDtypeStruct((HEAD, 1), FULL)),
        grid_spec=pltpu.PrefetchScalarGridSpec(
            num_scalar_prefetch=2,
            grid=(steps,),
            in_specs=[
                part,
                whole,
                whole,
                part,
                part,
                pl.BlockSpec((heads, 1, BLOCK), lambda i, *_: (0, 0, i)),
                part,
                pl.BlockSpec((1, HEAD), lambda i, *_: (0, 0)),
                pl.BlockSpec((1, BLOCK), lambda i, *_: (0, i)),
                pl.BlockSpec((1, length), lambda i, *_: (0, 0)),
            ],
            out_specs=(part, whole, whole, total),
            scratch_shapes=[
                pltpu.VMEM((heads, length, HEAD), LOW),
                pltpu.VMEM((heads, length, HEAD), LOW),
                pltpu.VMEM((heads, BLOCK, HEAD), LOW),
                pltpu.VMEM((heads, BLOCK, HEAD), LOW),
                pltpu.VMEM((heads, length, HEAD), FULL),
                pltpu.VMEM((heads, length, HEAD), FULL),
                pltpu.VMEM((cols, BLOCK), FULL),
                pltpu.VMEM((length, 1), FULL),
            ],
        ),
        compiler_params=pltpu.CompilerParams(vmem_limit_bytes=62 * 2**20),
        cost_estimate=pl.CostEstimate(
            flops=8 * 5 * length * length * cols,
            bytes_accessed=8 * cols * length * 2,
            transcendentals=heads * length * length // 3,
        ),
    )(lo, hi, q, k, v, o, go, logs, raw, factor, segq, segk)


def remote(src, dst, sems, index, device):
    return pltpu.make_async_remote_copy(
        src_ref=src,
        dst_ref=dst,
        send_sem=sems[0].at[index],
        recv_sem=sems[1].at[index],
        device_id=device,
        device_id_type=pl.DeviceIdType.MESH,
    )


def greet(peers):
    barrier = pltpu.get_barrier_semaphore()
    for peer in peers:
        pl.semaphore_signal(barrier, inc=1, device_id=peer, device_id_type=pl.DeviceIdType.MESH)
    pl.semaphore_wait(barrier, len(peers))


def head_kernel(
    n_dp, n_pair, gain_ref, factor_ref, tokens_hbm, cot_hbm, block_hbm, slab_hbm, down_hbm,
    q_hbm, k_hbm, v_hbm, raw_hbm, normed_hbm, qkv_hbm, slabs_hbm, cot_out, down_out, inverse_ref,
    tokens, others, block, cs_recv, remote_block, pass_on, qkv, turned, normed, q, k, v, raw,
    send_sems, recv_sems, local_sems,
):
    r, s = lax.axis_index("row"), lax.axis_index("cs")
    j, d = lax.axis_index("cp"), lax.axis_index("dp")
    n_col = 2 * n_pair
    subs, width, piece = tokens.shape[1:]
    here = subs * piece
    share = cs_recv.shape[0]
    cols = q.shape[0]
    c_first = (s * n_pair + j) ^ (r * n_pair)
    near = r == s
    sems = (send_sems, recv_sems)
    counter, local_counter = iter(range(1000)), iter(range(1000))
    sent, stored = [], []

    def send(src, dst, device):
        copy = remote(src, dst, sems, next(counter), device)
        copy.start()
        sent.append(copy)
        return copy

    def move(src, dst):
        copy = pltpu.make_async_copy(src, dst, local_sems.at[next(local_counter)])
        copy.start()
        return copy

    def store(src, dst):
        stored.append(move(src, dst))

    def columns(u):
        return pl.ds(u * piece, piece)

    own_tokens = [move(tokens_hbm.at[:, columns(u)], tokens.at[0, u]) for u in range(subs)]
    own_block = move(block_hbm, block)
    store(slab_hbm, slabs_hbm.at[c_first])
    sibling_id = {"row": 1 - r}
    dp_ids = [{"dp": d ^ k} for k in range(1, n_dp)]
    col_ids = [{"cs": s ^ (k // n_pair), "cp": j ^ (k % n_pair)} for k in range(1, n_col)]
    greet([sibling_id] + dp_ids + col_ids)

    cs_copy = send(block_hbm.at[d], cs_recv, {"cs": 1 - s})
    down_copy = send(down_hbm.at[d], down_out.at[d], col_ids[0])
    other_copies = {}
    for u in range(subs):
        other_copies[0, u] = send(tokens_hbm.at[:, columns(u)], others.at[0, u], sibling_id)
    pair_copies = {}
    for u in range(subs):
        for m in range(1, n_pair):
            pair_copies[m, u] = send(
                tokens_hbm.at[:, columns(u)], tokens.at[m, u], {"cp": j ^ m}
            )

    cot_copy = send(cot_hbm, cot_out, sibling_id)
    gain_own = column(gain_ref[pl.ds(r, 1), :])
    gain_other = column(gain_ref[pl.ds(1 - r, 1), :])
    factor = column(factor_ref[...])

    def norm(m, u):
        own, other = tokens[m, u].astype(FULL), others[m, u].astype(FULL)
        squares = jnp.sum(own * own, axis=0, keepdims=True)
        squares = squares + jnp.sum(other * other, axis=0, keepdims=True)
        inverse = lax.rsqrt(squares / D + EPSILON)
        at = pl.ds(pl.multiple_of((j ^ m) * here + u * piece, 128), piece)
        normed[:width, at] = (own * inverse * gain_own).astype(LOW)
        normed[width:, at] = (other * inverse * gain_other).astype(LOW)
        store(normed.at[:, at], normed_hbm.at[:, at])
        if m == 0:
            inverse_ref[:, columns(u)] = inverse

    def project(m, u):
        at = pl.ds(pl.multiple_of((j ^ m) * here + u * piece, 128), piece)
        for part, out in ((0, None), (1, k), (2, v)):
            value = jnp.dot(
                turned[part * cols:(part + 1) * cols, :], normed[:, at],
                preferred_element_type=FULL,
            )
            if part == 0:
                raw[:, at] = value
                q[:, at] = (value * factor).astype(LOW)
            else:
                out[:, at] = value.astype(LOW)
        for src, dst in ((q, q_hbm), (k, k_hbm), (v, v_hbm), (raw, raw_hbm)):
            store(src.at[:, at], dst.at[:, at])

    for u in range(subs):
        own_tokens[u].wait()
        other_copies[0, u].wait_recv()
        norm(0, u)
    own_block.wait()
    down_copy.wait_recv()
    down_copies = [send(down_out.at[d], down_out.at[d], peer) for peer in dp_ids]

    cs_copy.wait_recv()
    dp_copies = [send(cs_recv, remote_block.at[d], peer) for peer in dp_ids]
    slab_copies = [send(slab_hbm, slabs_hbm.at[c_first], peer) for peer in col_ids]
    remote_block[d] = cs_recv[...]
    for u in range(subs - 1):
        for m in range(1, n_pair):
            pair_copies[m, u].wait_recv()
            other_copies[m, u] = send(tokens.at[m, u], others.at[m, u], sibling_id)
    cross_copies = []
    for m in range(n_dp):
        owner = d ^ m
        if m:
            dp_copies[m - 1].wait_recv()
        mine, its = block[owner], remote_block[owner]
        at = pl.multiple_of(owner * share, 32)
        qkv[pl.ds(at, share)] = jnp.where(near, mine, its)
        pass_on[owner] = jnp.where(near, its, mine)
        cross_copies.append(
            send(pass_on.at[owner], qkv.at[pl.ds(width + at, share)], sibling_id)
        )
    u = subs - 1
    for m in range(1, n_pair):
        pair_copies[m, u].wait_recv()
        other_copies[m, u] = send(tokens.at[m, u], others.at[m, u], sibling_id)
    turned[:, :width] = qkv[:width].T
    for copy in cross_copies:
        copy.wait_recv()
    turned[:, width:] = qkv[width:].T
    store(qkv, qkv_hbm)

    for u in range(subs):
        project(0, u)
    for u in range(subs):
        for m in range(1, n_pair):
            other_copies[m, u].wait_recv()
            norm(m, u)
            project(m, u)

    for copy in stored:
        copy.wait()
    for copy in slab_copies + down_copies + [cot_copy]:
        copy.wait_recv()
    for copy in sent:
        copy.wait_send()


def head(n_dp, n_pair, gain, factor, tokens, cotangent, block, slab, down):
    width, here = tokens.shape
    wide = block.shape[1]
    cols = wide // 3
    share = width // n_dp
    length = n_pair * here
    n_col = 2 * n_pair
    subs = 2
    piece = here // subs
    count = subs * n_pair * 2 + 3 * n_dp + n_col + 6
    moves = 3 + subs + 5 * subs * n_pair + 4
    hbm = pl.BlockSpec(memory_space=pl.ANY)
    vmem = pl.BlockSpec(memory_space=pltpu.VMEM)
    V = pltpu.VMEM
    shape = jax.ShapeDtypeStruct((cols, length), LOW)
    return pl.pallas_call(
        functools.partial(head_kernel, n_dp, n_pair),
        out_shape=(
            shape,
            shape,
            shape,
            jax.ShapeDtypeStruct((cols, length), FULL),
            jax.ShapeDtypeStruct((2 * width, length), LOW),
            jax.ShapeDtypeStruct((2 * width, wide), LOW),
            jax.ShapeDtypeStruct((n_col,) + slab.shape, LOW),
            jax.ShapeDtypeStruct((width, here), LOW),
            jax.ShapeDtypeStruct(down.shape, LOW),
            jax.ShapeDtypeStruct((1, here), FULL),
        ),
        in_specs=[vmem] * 2 + [hbm] * 5,
        out_specs=(hbm,) * 9 + (vmem,),
        scratch_shapes=[
            V((n_pair, subs, width, piece), LOW),
            V((n_pair, subs, width, piece), LOW),
            V((n_dp, share, wide), LOW),
            V((share, wide), LOW),
            V((n_dp, share, wide), LOW),
            V((n_dp, share, wide), LOW),
            V((2 * width, wide), LOW),
            V((wide, 2 * width), LOW),
            V((2 * width, length), LOW),
            V((cols, length), LOW),
            V((cols, length), LOW),
            V((cols, length), LOW),
            V((cols, length), FULL),
            pltpu.SemaphoreType.DMA((count,)),
            pltpu.SemaphoreType.DMA((count,)),
            pltpu.SemaphoreType.DMA((moves,)),
        ],
        compiler_params=pltpu.CompilerParams(
            collective_id=2, has_side_effects=True, vmem_limit_bytes=60 * 2**20
        ),
        cost_estimate=pl.CostEstimate(
            flops=4 * wide * width * length, bytes_accessed=2**25, transcendentals=0
        ),
    )(gain, factor, tokens, cotangent, block.reshape(n_dp, share, wide), slab, down)


def middle_kernel(n_dp, n_pair, unit, gain_ref, att_hbm, tokens_hbm, cot_hbm, cot_other, *refs):
    n_col = 2 * n_pair
    slab_hbms, refs = refs[:n_dp], refs[n_dp:]
    down_hbms, refs = refs[:n_col], refs[n_col:]
    result_hbm, middle_hbm, out_hbm, refs = refs[0], refs[1], refs[2], refs[3:]
    grads_hbms, refs = refs[:n_dp], refs[n_dp:]
    down_outs, refs = refs[:n_col], refs[n_col:]
    (
        gain_out, tokens, cot, slab, out_w, up_w, down_w, out_t, up_t, down_t, out_half, up_half,
        down_half, att, scaled, normed, active, grad_hidden, branch, middle, grad, result, grad_att,
        grads, down_grads, square_send, square_recv, inner_send, inner_recv, inverse, narrow,
        send_sems, recv_sems, local_sems,
    ) = refs
    r, s = lax.axis_index("row"), lax.axis_index("cs")
    j, d = lax.axis_index("cp"), lax.axis_index("dp")
    width, here = tokens.shape
    pieces, _, piece = square_send.shape
    cols = att_hbm.shape[0]
    half = n_col * unit // 2
    rows_q = slab_hbms[0].shape[1]
    rows_g = grads_hbms[0].shape[1]
    c_first = (s * n_pair + j) ^ (r * n_pair)
    sems = (send_sems, recv_sems)
    gain = column(gain_ref[pl.ds(r, 1), :])
    counter, local_counter = iter(range(1000)), iter(range(1000))
    sent, stored = [], []

    def send(src, dst, device):
        copy = remote(src, dst, sems, next(counter), device)
        copy.start()
        sent.append(copy)
        return copy

    def move(src, dst):
        copy = pltpu.make_async_copy(src, dst, local_sems.at[next(local_counter)])
        copy.start()
        return copy

    def columns(u):
        return pl.ds(u * piece, piece)

    def span(u):
        return slice(u * piece, (u + 1) * piece)

    def down_rows(owner):
        return pl.ds(pl.multiple_of(owner * unit, 16), unit)

    own_rows, other_rows = pl.ds(0, width), pl.ds(width, width)
    weight_loads = [
        move(slab_hbms[m], slab.at[:, pl.ds(pl.multiple_of((d ^ m) * rows_q, 16), rows_q)])
        for m in range(n_dp)
    ] + [
        move(down_hbms[m], down_w.at[down_rows(c_first ^ m)])
        for m in range(n_col)
    ]
    att_loads = [
        move(
            att_hbm.at[:, pl.ds(pl.multiple_of(j * here + u * piece, 128), piece)],
            att.at[pl.ds(pl.multiple_of(j * cols, 16), cols), columns(u)],
        )
        for u in range(pieces)
    ]
    token_load = move(tokens_hbm, tokens)
    cot_loads = [move(cot_hbm, cot.at[own_rows]), move(cot_other, cot.at[other_rows])]
    sibling_id = {"row": 1 - r}
    pair_ids = [{"cp": j ^ m} for m in range(1, n_pair)]
    greet([sibling_id] + pair_ids)

    att_copies = {}
    for u in range(pieces):
        for m in range(1, n_pair):
            att_copies[u, m] = send(
                att_hbm.at[:, pl.ds(pl.multiple_of((j ^ m) * here + u * piece, 128), piece)],
                att.at[pl.ds(pl.multiple_of(j * cols, 16), cols), columns(u)],
                pair_ids[m - 1],
            )

    for copy in weight_loads:
        copy.wait()
    for m in range(n_col):
        at = slice(m * unit, (m + 1) * unit)
        out_w[at] = slab[m, :unit]
        up_w[at] = slab[m, unit:2 * unit]
    cross_copies = []

    def cross(whole, part):
        cross_copies.append(send(whole.at[pl.ds(half, half)], part.at[:, other_rows], sibling_id))
        part[:, :width] = whole[:half]

    cross(up_w, up_half)
    cross(down_w, down_half)
    cross(out_w, out_half)
    out_t[...] = out_w[...].T
    narrow[...] = jnp.zeros_like(narrow)

    copies = {}

    def exchange(name, u, ref):
        copies[name, u] = send(
            ref.at[own_rows, columns(u)], ref.at[other_rows, columns(u)], sibling_id
        )

    def share_heads(u):
        att_loads[u].wait()
        for m in range(1, n_pair):
            att_copies[u, m].wait_recv()
        exchange("att", u, att)

    def first_branch(u):
        if u == 0:
            token_load.wait()
        copies["att", u].wait_recv()
        value = tokens[:, span(u)].astype(FULL) + jnp.dot(
            out_t[...], att[:, span(u)], preferred_element_type=FULL
        )
        scaled[:width, span(u)] = (value * gain).astype(LOW)
        exchange("scaled", u, scaled)
        square_send[u] = jnp.sum(value * value, axis=0, keepdims=True)
        copies["square", u] = send(square_send.at[u], square_recv.at[u], sibling_id)
        middle[:, span(u)] = value

    def hidden_units(u):
        if u == 0:
            for copy in cot_loads:
                copy.wait()
            for copy in cross_copies:
                copy.wait_recv()
            up_t[...] = up_w[...].T
            down_t[...] = down_w[...].T
        grad_active = jnp.dot(down_half[...], cot[:, span(u)], preferred_element_type=FULL)
        copies["scaled", u].wait_recv()
        copies["square", u].wait_recv()
        scale = lax.rsqrt((square_send[u] + square_recv[u]) / D + EPSILON)
        inverse[u] = scale
        hidden = scale * jnp.dot(up_half[...], scaled[:, span(u)], preferred_element_type=FULL)
        sigmoid = jax.nn.sigmoid(hidden)
        value = (grad_active * sigmoid * (1.0 + hidden * (1.0 - sigmoid))).astype(LOW)
        grad_hidden[:half, span(u)] = value
        exchange("grad_hidden", u, grad_hidden)
        active[:half, span(u)] = (hidden * sigmoid).astype(LOW)
        exchange("active", u, active)
        inner_send[u] = jnp.sum(value.astype(FULL) * hidden, axis=0, keepdims=True)
        copies["inner", u] = send(inner_send.at[u], inner_recv.at[u], sibling_id)
        normed[:, span(u)] = (middle[:, span(u)] * scale * gain).astype(LOW)

    def second_branch(u):
        copies["grad_hidden", u].wait_recv()
        copies["inner", u].wait_recv()
        scale = inverse[u]
        inner = scale * scale * ((inner_send[u] + inner_recv[u]) / D)
        back = jnp.dot(up_t[...], grad_hidden[:, span(u)], preferred_element_type=FULL)
        value = (
            cot[:width, span(u)].astype(FULL)
            + scale * (back * gain)
            - middle[:, span(u)] * inner
        )
        branch[:width, span(u)] = value.astype(LOW)
        exchange("branch", u, branch)
        grad[:, span(u)] = value
        stored.append(move(grad.at[:, columns(u)], middle_hbm.at[:, columns(u)]))
        product = back * middle[:, span(u)] * scale
        total = narrow[...]
        for v in range(piece // 128):
            total = total + product[:, v * 128:(v + 1) * 128]
        narrow[...] = total
        copies["active", u].wait_recv()
        result[:, span(u)] = middle[:, span(u)] + jnp.dot(
            down_t[...], active[:, span(u)], preferred_element_type=FULL
        )
        stored.append(move(result.at[:, columns(u)], result_hbm.at[:, columns(u)]))

    def heads_back(u):
        copies["branch", u].wait_recv()
        grad_att[:, span(u)] = jnp.dot(
            out_half[...], branch[:, span(u)], preferred_element_type=FULL
        ).astype(LOW)
        target = pl.ds(pl.multiple_of(j * here + u * piece, 128), piece)
        for m in range(n_pair):
            source = grad_att.at[
                pl.ds(pl.multiple_of((j ^ m) * cols, 16), cols), columns(u)
            ]
            if m:
                copies["out", u, m] = send(source, out_hbm.at[:, target], pair_ids[m - 1])
            else:
                stored.append(move(source, out_hbm.at[:, target]))

    stages = (share_heads, first_branch, hidden_units, second_branch, heads_back)
    for t in range(pieces + len(stages) - 1):
        for number in reversed(range(len(stages))):
            if 0 <= t - number < pieces:
                stages[number](t - number)

    def product(left, right, target, first):
        turned = right[:width].T
        for n in range(n_col):
            target[n, first:first + unit] = jnp.dot(
                left[n * unit:(n + 1) * unit], turned, preferred_element_type=FULL
            ).astype(LOW)

    product(active, cot, down_grads, 0)
    for m in range(n_col):
        stored.append(move(down_grads.at[c_first ^ m], down_outs[m]))
    if grads.shape[1] > 2 * unit:
        grads[...] = jnp.zeros_like(grads)
    product(grad_hidden, normed, grads, unit)
    product(att, branch, grads, 0)
    for m in range(n_dp):
        at = pl.ds(pl.multiple_of((d ^ m) * rows_g, 16), rows_g)
        stored.append(move(grads.at[:, at], grads_hbms[m]))
    gain_out[...] = jnp.sum(narrow[...].T, axis=0, keepdims=True)

    for u in range(pieces):
        for m in range(1, n_pair):
            copies["out", u, m].wait_recv()
    for copy in stored:
        copy.wait()
    for copy in sent:
        copy.wait_send()


def middle_part(n_dp, n_pair, gain, attended, tokens, cotangent, cot_other, slabs, downs):
    width, here = tokens.shape
    n_col = 2 * n_pair
    cols, length = attended.shape
    unit = downs[0].shape[0]
    half = n_col * unit // 2
    rows_q = slabs[0].shape[1]
    rows_g = quarter_rows(2 * unit, n_dp)
    pieces = max(2, here // 256)
    piece = here // pieces
    count = 2 * pieces * (n_pair - 1) + 7 * pieces + 8
    moves = 2 * n_dp + 2 * n_col + 4 * pieces + 4
    hbm = pl.BlockSpec(memory_space=pl.ANY)
    vmem = pl.BlockSpec(memory_space=pltpu.VMEM)
    V = pltpu.VMEM
    S = jax.ShapeDtypeStruct
    weight = V((2 * half, width), LOW)
    weight_t = V((width, 2 * half), LOW)
    both = V((2 * width, here), LOW)
    whole = V((width, here), FULL)
    row = V((pieces, 1, piece), FULL)
    out = pl.pallas_call(
        functools.partial(middle_kernel, n_dp, n_pair, unit),
        out_shape=(
            S((width, here), FULL),
            S((width, here), FULL),
            S((cols, length), LOW),
        )
        + (S((n_col, rows_g, width), LOW),) * n_dp
        + (S((unit, width), LOW),) * n_col
        + (S((1, width), FULL),),
        in_specs=[vmem] + [hbm] * (4 + n_dp + n_col),
        out_specs=(hbm,) * (3 + n_dp + n_col) + (vmem,),
        scratch_shapes=[
            V((width, here), LOW),
            both,
            V((n_col, n_dp * rows_q, width), LOW),
            weight,
            weight,
            weight,
            weight_t,
            weight_t,
            weight_t,
            V((half, 2 * width), LOW),
            V((half, 2 * width), LOW),
            V((half, 2 * width), LOW),
            both,
            both,
            V((width, here), LOW),
            V((2 * half, here), LOW),
            V((2 * half, here), LOW),
            both,
            whole,
            whole,
            whole,
            V((width, here), LOW),
            V((n_col, n_dp * rows_g, width), LOW),
            V((n_col, unit, width), LOW),
            row,
            row,
            row,
            row,
            row,
            V((width, 128), FULL),
            pltpu.SemaphoreType.DMA((count,)),
            pltpu.SemaphoreType.DMA((count,)),
            pltpu.SemaphoreType.DMA((moves,)),
        ],
        compiler_params=pltpu.CompilerParams(
            collective_id=3, has_side_effects=True, vmem_limit_bytes=62 * 2**20
        ),
        cost_estimate=pl.CostEstimate(
            flops=18 * 2 * half * width * here, bytes_accessed=2**25, transcendentals=0
        ),
    )(gain, attended, tokens, cotangent, cot_other, *slabs, *downs)
    return out[0], out[1], out[2], out[3:3 + n_dp], out[3 + n_dp:-1], out[-1]


def quarter_rows(rows, n_dp):
    return -(-rows // (16 * n_dp)) * 16


def tail_kernel(
    n_dp, n_pair, gain_ref, inverse_ref, sums_ref, qkv_hbm, dq_hbm, dk_hbm, dv_hbm, normed_hbm,
    tokens_hbm, middle_hbm, *refs,
):
    n_col = 2 * n_pair
    grads_hbms, refs = refs[:n_dp], refs[n_dp:]
    down_hbms, refs = refs[:n_col], refs[n_col:]
    (
        result_hbm, qkv_out, grads_out, down_out, sums_out,
        qkv, dproj, normed, tokens, middle, result, row_send, row_recv, own, pair_send, pair_recv,
        dp_send, dp_recv, dp_own, cross_send, cross_recv, cs_send, cs_recv, final, grads_parts,
        grads_send, grads_recv, grads_final, down_parts, down_send, down_recv, down_final,
        inner_send, inner_recv, sums_send, sums_recv, last_sums, send_sems, recv_sems, local_sems,
    ) = refs
    r, s = lax.axis_index("row"), lax.axis_index("cs")
    j, d = lax.axis_index("cp"), lax.axis_index("dp")
    width, here = tokens.shape
    cols = dq_hbm.shape[0]
    unit = down_parts.shape[1]
    share = width // n_dp
    part = share // 2
    rows_d = down_final.shape[0]
    subs = row_send.shape[1]
    piece = here // subs
    c_first = (s * n_pair + j) ^ (r * n_pair)
    near = r == s
    sems = (send_sems, recv_sems)
    gain = column(gain_ref[pl.ds(r, 1), :])
    counter, local_counter = iter(range(1000)), iter(range(1000))
    sent, stored = [], []

    def send(src, dst, device):
        copy = remote(src, dst, sems, next(counter), device)
        copy.start()
        sent.append(copy)
        return copy

    def move(src, dst):
        copy = pltpu.make_async_copy(src, dst, local_sems.at[next(local_counter)])
        copy.start()
        return copy

    early = [
        move(dq_hbm, dproj.at[pl.ds(0, cols)]),
        move(dk_hbm, dproj.at[pl.ds(cols, cols)]),
        move(dv_hbm, dproj.at[pl.ds(2 * cols, cols)]),
        move(normed_hbm, normed),
    ]
    load_qkv = move(qkv_hbm, qkv)
    load_down = [move(down_hbms[k], down_parts.at[k]) for k in range(n_col) if k != 1]
    load_grads = [move(grads_hbms[k], grads_parts.at[k]) for k in range(n_dp)]
    late = [move(tokens_hbm, tokens), move(middle_hbm, middle)]

    sibling_id = {"row": 1 - r}
    cs_id = {"cs": 1 - s}
    dp_ids = [{"dp": d ^ k} for k in range(1, n_dp)]
    col_ids = [{"cs": s ^ (k // n_pair), "cp": j ^ (k % n_pair)} for k in range(1, n_col)]
    greet([sibling_id] + dp_ids + col_ids)

    down_copy = send(down_hbms[1], down_parts.at[1], col_ids[0])

    def quarter(half, owner):
        at = pl.ds(pl.multiple_of(half * width + owner * share, 32), share)
        return mm(normed[at, :], dproj[...], 1, 1)

    def rows_of(half, chunk, u):
        at = pl.ds(pl.multiple_of(chunk * here + u * piece, 128), piece)
        return jnp.dot(
            qkv[half * width:(half + 1) * width, :], dproj[:, at], preferred_element_type=FULL
        )

    dp_copies = {}

    def send_part(k, p):
        rows = pl.ds(p * part, part)
        dp_copies[k, p] = send(
            dp_send.at[k - 1, :, rows], dp_recv.at[k - 1, :, rows], dp_ids[k - 1]
        )

    def quarters(k):
        for half in range(2):
            dp_send[k - 1, half] = quarter(half, d ^ k).astype(LOW)
        send_part(k, 0)

    row_copies, pair_copies = {}, []
    for copy in early:
        copy.wait()
    quarters(1)
    load_qkv.wait()
    for k in range(1, n_pair):
        for u in range(subs):
            row_send[k, u] = rows_of(1, j ^ k, u).astype(LOW)
            row_copies[k, u] = send(row_send.at[k, u], row_recv.at[k, u], sibling_id)
    for k in range(1, n_pair):
        for u in range(subs):
            value = rows_of(0, j ^ k, u)
            row_copies[k, u].wait_recv()
            pair_send[k - 1, u] = (value + row_recv[k, u].astype(FULL)).astype(LOW)
            pair_copies.append(
                send(pair_send.at[k - 1, u], pair_recv.at[k - 1, u], {"cp": j ^ k})
            )
    for k in range(2, n_dp):
        quarters(k)
    for copy in load_down:
        copy.wait()
    down_copy.wait_recv()
    value = down_parts[0].astype(FULL)
    for k in range(1, n_col):
        value = value + down_parts[k].astype(FULL)
    if down_send.shape[0] > unit:
        down_send[...] = jnp.zeros_like(down_send)
    down_send[:unit] = value.astype(LOW)

    def down_rows(owner):
        return pl.ds(pl.multiple_of(owner * rows_d, 16), rows_d)

    down_copies = [
        send(down_send.at[down_rows(d ^ k)], down_recv.at[k - 1], dp_ids[k - 1])
        for k in range(1, n_dp)
    ]
    for k in range(1, n_dp):
        send_part(k, 1)
    for half in range(2):
        dp_own[half] = quarter(half, d)

    for u in range(subs):
        row_send[0, u] = rows_of(1, j, u).astype(LOW)
        row_copies[0, u] = send(row_send.at[0, u], row_recv.at[0, u], sibling_id)
    for u in range(subs):
        own[u] = rows_of(0, j, u)

    cs_copies = []

    def reduce_part(p):
        rows = slice(p * part, (p + 1) * part)
        for k in range(1, n_dp):
            dp_copies[k, p].wait_recv()

        def total(half):
            value = dp_own[half, rows]
            for k in range(1, n_dp):
                value = value + dp_recv[k - 1, half, rows].astype(FULL)
            return value

        cross_send[p] = total(1).astype(LOW)
        cross_copy = send(cross_send.at[p], cross_recv.at[p], sibling_id)
        kept = total(0)
        cross_copy.wait_recv()
        crossed = cross_recv[p].astype(FULL)
        cs_send[p] = jnp.where(near, crossed, kept).astype(LOW)
        cs_copies.append(send(cs_send.at[p], cs_recv.at[p], cs_id))
        dp_own[0, rows] = jnp.where(near, kept, crossed)

    reduce_part(0)

    for copy in load_grads:
        copy.wait()

    def summed(place_at):
        value = grads_parts[0, place_at].astype(FULL)
        for k in range(1, n_dp):
            value = value + grads_parts[k, place_at].astype(FULL)
        return value

    grads_copies = []
    for k in range(1, n_col):
        grads_send[k - 1] = summed(c_first ^ k).astype(LOW)
        grads_copies.append(send(grads_send.at[k - 1], grads_recv.at[k - 1], col_ids[k - 1]))

    value = down_send[down_rows(d)].astype(FULL)
    for k in range(1, n_dp):
        down_copies[k - 1].wait_recv()
        value = value + down_recv[k - 1].astype(FULL)
    down_final[...] = value.astype(LOW)
    out_copies = [send(down_final, down_out.at[d], peer) for peer in dp_ids]
    stored.append(move(down_final, down_out.at[d]))
    reduce_part(1)

    for copy in late:
        copy.wait()
    for copy in pair_copies:
        copy.wait_recv()
    inverse = inverse_ref[...]
    for u in range(subs):
        row_copies[0, u].wait_recv()
        at = slice(u * piece, (u + 1) * piece)
        value = own[u] + row_recv[0, u].astype(FULL)
        for k in range(1, n_pair):
            value = value + pair_recv[k - 1, u].astype(FULL)
        own[u] = value
        inner_send[:, at] = jnp.sum(
            value * gain * tokens[:, at].astype(FULL), axis=0, keepdims=True
        )
    inner_copy = send(inner_send, inner_recv, sibling_id)

    def finish_part(p):
        cs_copies[p].wait_recv()
        rows = slice(p * part, (p + 1) * part)
        final[p] = (dp_own[0, rows] + cs_recv[p].astype(FULL)).astype(LOW)
        target = qkv_out.at[d, pl.ds(p * part, part)]
        out_copies.extend([send(final.at[p], target, peer) for peer in dp_ids])
        stored.append(move(final.at[p], target))

    finish_part(0)
    narrow = jnp.zeros((width, 128), FULL)
    for u in range(subs):
        at = slice(u * piece, (u + 1) * piece)
        wide = own[u] * tokens[:, at].astype(FULL) * inverse[:, at]
        for v in range(piece // 128):
            narrow = narrow + wide[:, v * 128:(v + 1) * 128]
    gain_part = jnp.sum(narrow.T, axis=0, keepdims=True)
    sums_send[0] = jnp.concatenate([gain_part, sums_ref[1:]], 0)
    sums_copies = {}

    def send_sums(step, peers):
        for k, peer in enumerate(peers):
            sums_copies[step, k] = send(sums_send.at[step], sums_recv.at[step, k], peer)

    def add_sums(step, members):
        value = sums_send[step]
        for k in range(members - 1):
            sums_copies[step, k].wait_recv()
            value = value + sums_recv[step, k]
        sums_send[step + 1] = value

    send_sums(0, dp_ids)
    inner_copy.wait_recv()
    inner = (inner_send[...] + inner_recv[...]) / D
    for u in range(subs):
        at = slice(u * piece, (u + 1) * piece)
        result[:, at] = (
            middle[:, at]
            + inverse[:, at] * (own[u] * gain)
            - tokens[:, at].astype(FULL)
            * (inverse[:, at] * inverse[:, at] * inverse[:, at] * inner[:, at])
        )
    stored.append(move(result, result_hbm))
    add_sums(0, n_dp)
    send_sums(1, col_ids)
    finish_part(1)

    value = summed(c_first)
    for k in range(1, n_col):
        grads_copies[k - 1].wait_recv()
        value = value + grads_recv[k - 1].astype(FULL)
    grads_final[...] = value.astype(LOW)
    out_copies += [send(grads_final, grads_out.at[d], peer) for peer in dp_ids]
    stored.append(move(grads_final, grads_out.at[d]))

    add_sums(1, n_col)
    sums_copy = send(sums_send.at[2], last_sums, sibling_id)
    sums_copy.wait_recv()
    sums_out[0] = sums_send[2]
    sums_out[1] = last_sums[...]
    for copy in out_copies:
        copy.wait_recv()
    for copy in stored:
        copy.wait()
    for copy in sent:
        copy.wait_send()


def tail(n_dp, n_pair, gain, inverse, sums, qkv, dq, dk, dv, normed, tokens, middle, grads, downs):
    width, here = tokens.shape
    length = normed.shape[1]
    cols = dq.shape[0]
    unit = downs[0].shape[0]
    rows_d = quarter_rows(unit, n_dp)
    share = width // n_dp
    subs = 2
    piece = here // subs
    n_col = 2 * n_pair
    part = grads[0].shape[1:]
    wide = 3 * cols
    count = 2 * n_pair * subs + 8 * n_dp + 2 * n_col + 12
    moves = 13 + n_dp + n_col
    hbm = pl.BlockSpec(memory_space=pl.ANY)
    vmem = pl.BlockSpec(memory_space=pltpu.VMEM)
    V = pltpu.VMEM
    halves = V((2, share // 2, wide), LOW)
    return pl.pallas_call(
        functools.partial(tail_kernel, n_dp, n_pair),
        out_shape=(
            jax.ShapeDtypeStruct((width, here), FULL),
            jax.ShapeDtypeStruct((n_dp, share, wide), LOW),
            jax.ShapeDtypeStruct((n_dp,) + part, LOW),
            jax.ShapeDtypeStruct((n_dp, rows_d, width), LOW),
            jax.ShapeDtypeStruct((2,) + sums.shape, FULL),
        ),
        in_specs=[vmem] * 3 + [hbm] * (7 + n_dp + n_col),
        out_specs=(hbm,) * 4 + (vmem,),
        scratch_shapes=[
            V((2 * width, wide), LOW),
            V((wide, length), LOW),
            V((2 * width, length), LOW),
            V((width, here), LOW),
            V((width, here), FULL),
            V((width, here), FULL),
            V((n_pair, subs, width, piece), LOW),
            V((n_pair, subs, width, piece), LOW),
            V((subs, width, piece), FULL),
            V((n_pair - 1, subs, width, piece), LOW),
            V((n_pair - 1, subs, width, piece), LOW),
            V((n_dp - 1, 2, share, wide), LOW),
            V((n_dp - 1, 2, share, wide), LOW),
            V((2, share, wide), FULL),
            halves,
            halves,
            halves,
            halves,
            halves,
            V((n_dp, n_col) + part, LOW),
            V((n_col - 1,) + part, LOW),
            V((n_col - 1,) + part, LOW),
            V(part, LOW),
            V((n_col, unit, width), LOW),
            V((n_dp * rows_d, width), LOW),
            V((n_dp - 1, rows_d, width), LOW),
            V((rows_d, width), LOW),
            V((1, here), FULL),
            V((1, here), FULL),
            V((3,) + sums.shape, FULL),
            V((2, max(n_dp, n_col) - 1) + sums.shape, FULL),
            V(sums.shape, FULL),
            pltpu.SemaphoreType.DMA((count,)),
            pltpu.SemaphoreType.DMA((count,)),
            pltpu.SemaphoreType.DMA((moves,)),
        ],
        compiler_params=pltpu.CompilerParams(
            collective_id=1, has_side_effects=True, vmem_limit_bytes=62 * 2**20
        ),
        cost_estimate=pl.CostEstimate(
            flops=8 * wide * width * length, bytes_accessed=2**25, transcendentals=0
        ),
    )(gain, inverse, sums, qkv, dq, dk, dv, normed, tokens, middle, *grads, *downs)


def on_device(
    tokens,
    segment_ids,
    padding_mask,
    w_qkv,
    w_out,
    w_up,
    w_down,
    gain_attn,
    gain_mlp,
    scale_raw,
    cotangent,
):
    width, here = tokens.shape
    r, s = lax.axis_index("row"), lax.axis_index("cs")
    j, d = lax.axis_index("cp"), lax.axis_index("dp")
    n_pair, n_dp, n_col = lax.axis_size("cp"), lax.axis_size("dp"), lax.axis_size(COLS)
    c = s * n_pair + j
    head_cols = w_qkv.shape[0] // (3 * width)
    heads = head_cols // HEAD
    near = r == s

    segments = jnp.where(s == r, segment_ids[0], sibling(segment_ids)[0])
    padding = jnp.where(s == r, padding_mask[0], sibling(padding_mask)[0])
    length = segments.shape[0]
    firsts = segments[::BLOCK]
    starts = jnp.sum((segments[None, :] < firsts[:, None]).astype(jnp.int32), axis=1)
    filled = (jnp.sum(padding) + BLOCK - 1) // BLOCK
    blocks = jnp.arange(length // BLOCK, dtype=jnp.int32)
    lo = starts // BLOCK
    hi = jnp.minimum(blocks, filled)
    segq = segments[None, :].astype(FULL)
    segk = jnp.where(padding == 1, segments, -1)[None, :].astype(FULL)

    gain_one, gain_two = gain_attn.reshape(2, width), gain_mlp.reshape(2, width)
    factor = (LOG_TWO_E / math.sqrt(HEAD) * jnp.log1p(jnp.exp(scale_raw)))[None, :]

    block = w_qkv.reshape(width, 3 * head_cols)
    unit = w_up.shape[0] // width
    slab = jnp.concatenate([w_out.reshape(-1, width), w_up.reshape(width, -1).T], 0)
    slab_rows = quarter_rows(2 * unit, n_dp)
    slab = jnp.pad(slab, ((0, n_dp * slab_rows - 2 * unit), (0, 0)))
    slab = cut(slab, d, n_dp, 0)
    down = w_down.reshape(-1, width)
    down_rows = quarter_rows(unit, n_dp)
    down_quarters = jnp.pad(down, ((0, n_dp * down_rows - unit), (0, 0)))
    down_quarters = down_quarters.reshape(n_dp, down_rows, width)
    (
        queries, key_heads, values, query_raw, normed_one, qkv, slabs, cot_other, down_pair,
        inverse_one,
    ) = head(
        n_dp, n_pair, gain_one, jnp.tile(factor, (1, heads)),
        tokens, cotangent, block, slab, down_quarters,
    )
    slabs = gather(slabs, "dp")
    downs = [down, down_pair.reshape(-1, width)[:unit]] + [
        lax.ppermute(down, COLS, [(i, i ^ k) for i in range(n_col)]) for k in range(2, n_col)
    ]
    attended, logs = attention_forward(queries, key_heads, values, segq, segk, lo, hi)
    result, grad_middle, grad_attended, grads, down_grads, gain_two_part = middle_part(
        n_dp, n_pair, gain_two, attended, tokens, cotangent, cot_other, slabs, downs
    )
    received = [grads[0]] + [shift(grads[k], "dp", k) for k in range(1, n_dp)]
    down_received = list(down_grads[:2]) + [
        lax.ppermute(down_grads[k], COLS, [(i, i ^ k) for i in range(n_col)])
        for k in range(2, n_col)
    ]

    dq, dk, dv, scale_part = attention_backward(
        queries, key_heads, values, attended, grad_attended, logs, query_raw, factor,
        segq, segk, lo, hi,
    )
    scale_part = (
        scale_part[:, 0] * (LOG_TWO_E / math.sqrt(HEAD)) * jax.nn.sigmoid(scale_raw)
    )
    sums = jnp.concatenate(
        [
            jnp.zeros((1, width), FULL),
            gain_two_part,
            jnp.pad(scale_part, (0, width - HEAD))[None],
            jnp.zeros((5, width), FULL),
        ]
    )
    grad_tokens, grad_qkv, final, final_down, sums = tail(
        n_dp, n_pair, gain_one, inverse_one, sums, qkv, dq, dk, dv, normed_one, tokens,
        grad_middle, received, down_received,
    )
    grad_qkv = grad_qkv.astype(FULL)
    final = final.reshape(-1, width)
    final = [final[i * unit:(i + 1) * unit].astype(FULL) for i in range(2)]
    final.append(final_down.reshape(-1, width)[:unit].astype(FULL))
    own, other = sums[0], sums[1]
    first = r == 0
    gains = jnp.concatenate(
        [jnp.where(first, own[:2], other[:2]), jnp.where(first, other[:2], own[:2])], 1
    )
    scale_total = (own[2] + other[2])[:HEAD]
    return (
        result,
        grad_tokens,
        grad_qkv.reshape(-1),
        final[0].reshape(-1),
        final[1].T.reshape(-1),
        final[2].reshape(-1),
        gains[0],
        gains[1],
        scale_total,
    )


def solution(mesh):
    n_dp, n_row, n_col = (mesh.shape[name] for name in ("dp", "row", "col"))
    split = Mesh(
        np.asarray(mesh.devices).reshape(n_dp, n_row, n_row, n_col // n_row),
        ("dp", "row", "cs", "cp"),
    )
    rows = P("row", ("dp", "cs", "cp"))
    ids = P(("dp", "row"), None)
    blocks = P(("row", "cs", "cp"))
    return jax.shard_map(
        on_device,
        mesh=split,
        in_specs=(rows, ids, ids, blocks, blocks, blocks, blocks, P(), P(), P(), rows),
        out_specs=(rows, rows, blocks, blocks, blocks, blocks, P(), P(), P()),
        check_vma=False,
    )
```

```python
import functools
import math

import jax
import jax.numpy as jnp
import numpy as np
from jax import lax
from jax.experimental import pallas as pl
from jax.experimental.pallas import tpu as pltpu
from jax.sharding import Mesh, PartitionSpec as P

D = 1280
HEAD = 80
EPSILON = 1e-06
LOG_TWO_E = 1.442695041
BLOCK = 256
LOW = jnp.bfloat16
FULL = jnp.float32
COLS = ("cs", "cp")


def mm(left, right, left_axis, right_axis):
    return lax.dot_general(
        left, right, (((left_axis,), (right_axis,)), ((), ())), preferred_element_type=FULL
    )


def shift(x, axis, k):
    n = lax.axis_size(axis)
    return lax.ppermute(x, axis, [(i, i ^ k) for i in range(n)])


def sibling(x):
    return shift(x, "row", 1)


def cut(x, index, count, axis):
    step = x.shape[axis] // count
    return lax.dynamic_slice_in_dim(x, index * step, step, axis)


def gather(x, axis):
    return [x] + [shift(x, axis, k) for k in range(1, lax.axis_size(axis))]


def diag_mask(segq, segk):
    size = segk.shape[0], segq.shape[1]
    ki = lax.broadcasted_iota(jnp.int32, size, 0)
    qi = lax.broadcasted_iota(jnp.int32, size, 1)
    return ((segk == segq) & (ki <= qi)) | (ki == qi)


def column(row):
    return jnp.broadcast_to(row, (8, row.shape[1])).T[:, :1]


def rows_of(h):
    return slice(h * HEAD, (h + 1) * HEAD)


def forward_kernel(heads, lo_ref, hi_ref, q_ref, k_ref, v_ref, segq_ref, segk_ref, o_ref, log_ref, ks, segks):
    i = pl.program_id(0)

    @pl.when(i == 0)
    def _():
        for h in range(heads):
            ks[h] = k_ref[h * HEAD:(h + 1) * HEAD, :].T
        segks[...] = column(segk_ref[...])

    segq = segq_ref[...]

    def visit(kb, carry, diagonal):
        at = pl.ds(pl.multiple_of(kb * BLOCK, BLOCK), BLOCK)
        segk = segks[at, :]
        mask = diag_mask(segq, segk) if diagonal else segk == segq
        scores = [
            jnp.dot(ks[h, at, :], q_ref[rows_of(h), :], preferred_element_type=FULL)
            for h in range(heads)
        ]
        peaks, totals, weights = [], [], []
        for h in range(heads):
            s = jnp.where(mask, scores[h], -1e30)
            peak = jnp.max(s, axis=0, keepdims=True)
            if not diagonal:
                peak = jnp.maximum(carry[h][0], peak)
            p = jnp.exp(s - peak)
            peaks.append(peak)
            totals.append(jnp.sum(p, axis=0, keepdims=True))
            weights.append(p.astype(LOW))
        out = []
        for h in range(heads):
            new = jnp.dot(v_ref[rows_of(h), at], weights[h], preferred_element_type=FULL)
            total = totals[h]
            if not diagonal:
                m, l, acc = carry[h]
                keep = jnp.exp(m - peaks[h])
                total = l * keep + total
                new = acc * keep + new
            out.append((peaks[h], total, new))
        return tuple(out)

    carry = visit(i, None, True)
    carry = lax.fori_loop(lo_ref[i], hi_ref[i], lambda kb, c: visit(kb, c, False), carry)
    for h in range(heads):
        m, l, acc = carry[h]
        o_ref[h * HEAD:(h + 1) * HEAD, :] = (acc / l).astype(LOW)
        log_ref[h] = m + jnp.log(l)


def attention_forward(q, k, v, segq, segk, lo, hi):
    cols, length = q.shape
    heads = cols // HEAD
    steps = length // BLOCK
    whole = pl.BlockSpec((cols, length), lambda i, *_: (0, 0))
    part = pl.BlockSpec((cols, BLOCK), lambda i, *_: (0, i))
    return pl.pallas_call(
        functools.partial(forward_kernel, heads),
        out_shape=(
            jax.ShapeDtypeStruct((cols, length), LOW),
            jax.ShapeDtypeStruct((heads, 1, length), FULL),
        ),
        grid_spec=pltpu.PrefetchScalarGridSpec(
            num_scalar_prefetch=2,
            grid=(steps,),
            in_specs=[
                part,
                whole,
                whole,
                pl.BlockSpec((1, BLOCK), lambda i, *_: (0, i)),
                pl.BlockSpec((1, length), lambda i, *_: (0, 0)),
            ],
            out_specs=(part, pl.BlockSpec((heads, 1, BLOCK), lambda i, *_: (0, 0, i))),
            scratch_shapes=[pltpu.VMEM((heads, length, HEAD), LOW), pltpu.VMEM((length, 1), FULL)],
        ),
        compiler_params=pltpu.CompilerParams(vmem_limit_bytes=62 * 2**20),
        cost_estimate=pl.CostEstimate(
            flops=8 * 2 * length * length * cols,
            bytes_accessed=4 * cols * length * 2,
            transcendentals=heads * length * length // 3,
        ),
    )(lo, hi, q, k, v, segq, segk)


def backward_kernel(
    heads, lo_ref, hi_ref, q_ref, k_ref, v_ref, o_ref, go_ref, log_ref, raw_ref, factor_ref,
    segq_ref, segk_ref, dq_ref, dk_ref, dv_ref, scale_ref, ks, vs, qs, gs, dks, dvs, dqs, segks,
):
    i = pl.program_id(0)

    @pl.when(i == 0)
    def _():
        for h in range(heads):
            ks[h] = k_ref[h * HEAD:(h + 1) * HEAD, :].T
            vs[h] = v_ref[h * HEAD:(h + 1) * HEAD, :].T
        segks[...] = column(segk_ref[...])
        scale_ref[...] = jnp.zeros_like(scale_ref)

    segq = segq_ref[...]
    inner = [
        jnp.sum(
            o_ref[h * HEAD:(h + 1) * HEAD, :].astype(FULL)
            * go_ref[h * HEAD:(h + 1) * HEAD, :].astype(FULL),
            axis=0,
            keepdims=True,
        )
        for h in range(heads)
    ]

    for h in range(heads):
        qs[h] = q_ref[rows_of(h), :].T
        gs[h] = go_ref[rows_of(h), :].T

    def visit(kb, diagonal):
        at = pl.ds(pl.multiple_of(kb * BLOCK, BLOCK), BLOCK)
        segk = segks[at, :]
        mask = diag_mask(segq, segk) if diagonal else segk == segq
        scores = [
            jnp.dot(ks[h, at, :], q_ref[rows_of(h), :], preferred_element_type=FULL)
            for h in range(heads)
        ]
        dps = [
            jnp.dot(vs[h, at, :], go_ref[rows_of(h), :], preferred_element_type=FULL)
            for h in range(heads)
        ]
        ps, dss = [], []
        for h in range(heads):
            p = jnp.where(mask, jnp.exp(scores[h] - log_ref[h]), 0.0)
            dss.append((p * (dps[h] - inner[h])).astype(LOW))
            ps.append(p.astype(LOW))
        for h in range(heads):
            new_v = jnp.dot(ps[h], gs[h], preferred_element_type=FULL)
            new_k = jnp.dot(dss[h], qs[h], preferred_element_type=FULL)
            new_q = jnp.dot(k_ref[rows_of(h), at], dss[h], preferred_element_type=FULL)
            if diagonal:
                dvs[h, at, :], dks[h, at, :], dqs[rows_of(h), :] = new_v, new_k, new_q
            else:
                dvs[h, at, :] += new_v
                dks[h, at, :] += new_k
                dqs[rows_of(h), :] += new_q

    visit(i, True)

    @pl.loop(lo_ref[i], hi_ref[i])
    def _(kb):
        visit(kb, False)

    factor = column(factor_ref[...])
    part = jnp.zeros((HEAD, 1), FULL)
    for h in range(heads):
        rows = slice(h * HEAD, (h + 1) * HEAD)
        dq = dqs[rows, :]
        part = part + jnp.sum(dq * raw_ref[rows, :], axis=1, keepdims=True)
        dq_ref[rows, :] = (dq * factor).astype(LOW)
    scale_ref[...] += part

    @pl.when(i == pl.num_programs(0) - 1)
    def _():
        for h in range(heads):
            dk_ref[rows_of(h), :] = dks[h].astype(LOW).T
            dv_ref[rows_of(h), :] = dvs[h].astype(LOW).T


def attention_backward(q, k, v, o, go, logs, raw, factor, segq, segk, lo, hi):
    cols, length = q.shape
    heads = cols // HEAD
    steps = length // BLOCK
    whole = pl.BlockSpec((cols, length), lambda i, *_: (0, 0))
    part = pl.BlockSpec((cols, BLOCK), lambda i, *_: (0, i))
    total = pl.BlockSpec((HEAD, 1), lambda i, *_: (0, 0))
    shape = jax.ShapeDtypeStruct((cols, length), LOW)
    return pl.pallas_call(
        functools.partial(backward_kernel, heads),
        out_shape=(shape, shape, shape, jax.ShapeDtypeStruct((HEAD, 1), FULL)),
        grid_spec=pltpu.PrefetchScalarGridSpec(
            num_scalar_prefetch=2,
            grid=(steps,),
            in_specs=[
                part,
                whole,
                whole,
                part,
                part,
                pl.BlockSpec((heads, 1, BLOCK), lambda i, *_: (0, 0, i)),
                part,
                pl.BlockSpec((1, HEAD), lambda i, *_: (0, 0)),
                pl.BlockSpec((1, BLOCK), lambda i, *_: (0, i)),
                pl.BlockSpec((1, length), lambda i, *_: (0, 0)),
            ],
            out_specs=(part, whole, whole, total),
            scratch_shapes=[
                pltpu.VMEM((heads, length, HEAD), LOW),
                pltpu.VMEM((heads, length, HEAD), LOW),
                pltpu.VMEM((heads, BLOCK, HEAD), LOW),
                pltpu.VMEM((heads, BLOCK, HEAD), LOW),
                pltpu.VMEM((heads, length, HEAD), FULL),
                pltpu.VMEM((heads, length, HEAD), FULL),
                pltpu.VMEM((cols, BLOCK), FULL),
                pltpu.VMEM((length, 1), FULL),
            ],
        ),
        compiler_params=pltpu.CompilerParams(vmem_limit_bytes=62 * 2**20),
        cost_estimate=pl.CostEstimate(
            flops=8 * 5 * length * length * cols,
            bytes_accessed=8 * cols * length * 2,
            transcendentals=heads * length * length // 3,
        ),
    )(lo, hi, q, k, v, o, go, logs, raw, factor, segq, segk)


def remote(src, dst, sems, index, device):
    return pltpu.make_async_remote_copy(
        src_ref=src,
        dst_ref=dst,
        send_sem=sems[0].at[index],
        recv_sem=sems[1].at[index],
        device_id=device,
        device_id_type=pl.DeviceIdType.MESH,
    )


def greet(peers):
    barrier = pltpu.get_barrier_semaphore()
    for peer in peers:
        pl.semaphore_signal(barrier, inc=1, device_id=peer, device_id_type=pl.DeviceIdType.MESH)
    pl.semaphore_wait(barrier, len(peers))


def head_kernel(
    n_dp, n_pair, gain_ref, factor_ref, tokens_hbm, cot_hbm, block_hbm, out_hbm, up_hbm,
    down_hbm, q_hbm, k_hbm, v_hbm, raw_hbm, normed_hbm, qkv_hbm, out_all, ups_hbm, cot_out, down_out,
    inverse_ref,
    tokens, others, block, cs_recv, remote_block, pass_on, qkv, turned, normed, q, k, v, raw,
    send_sems, recv_sems, local_sems,
):
    r, s = lax.axis_index("row"), lax.axis_index("cs")
    j, d = lax.axis_index("cp"), lax.axis_index("dp")
    n_col = 2 * n_pair
    subs, width, piece = tokens.shape[1:]
    here = subs * piece
    share = cs_recv.shape[0]
    cols = q.shape[0]
    c_first = (s * n_pair + j) ^ (r * n_pair)
    near = r == s
    sems = (send_sems, recv_sems)
    counter, local_counter = iter(range(1000)), iter(range(1000))
    sent, stored = [], []

    def send(src, dst, device):
        copy = remote(src, dst, sems, next(counter), device)
        copy.start()
        sent.append(copy)
        return copy

    def move(src, dst):
        copy = pltpu.make_async_copy(src, dst, local_sems.at[next(local_counter)])
        copy.start()
        return copy

    def store(src, dst):
        stored.append(move(src, dst))

    def columns(u):
        return pl.ds(u * piece, piece)

    own_tokens = [move(tokens_hbm.at[:, columns(u)], tokens.at[0, u]) for u in range(subs)]
    own_block = move(block_hbm, block)
    own_out = move(out_hbm, out_all.at[d, c_first])
    store(up_hbm, ups_hbm.at[c_first])
    sibling_id = {"row": 1 - r}
    dp_ids = [{"dp": d ^ k} for k in range(1, n_dp)]
    col_ids = [{"cs": s ^ (k // n_pair), "cp": j ^ (k % n_pair)} for k in range(1, n_col)]
    greet([sibling_id] + dp_ids + col_ids)

    cs_copy = send(block_hbm.at[d], cs_recv, {"cs": 1 - s})
    down_copy = send(down_hbm.at[d], down_out.at[d], col_ids[0])
    out_copies = [send(out_hbm, out_all.at[d, c_first], peer) for peer in col_ids]
    other_copies = {}
    for u in range(subs):
        other_copies[0, u] = send(tokens_hbm.at[:, columns(u)], others.at[0, u], sibling_id)
    pair_copies = {}

    def send_pairs(u):
        for m in range(1, n_pair):
            pair_copies[m, u] = send(
                tokens_hbm.at[:, columns(u)], tokens.at[m, u], {"cp": j ^ m}
            )

    send_pairs(0)

    cot_copy = send(cot_hbm, cot_out, sibling_id)
    gain_own = column(gain_ref[pl.ds(r, 1), :])
    gain_other = column(gain_ref[pl.ds(1 - r, 1), :])
    factor = column(factor_ref[...])

    def norm(m, u):
        own, other = tokens[m, u].astype(FULL), others[m, u].astype(FULL)
        squares = jnp.sum(own * own, axis=0, keepdims=True)
        squares = squares + jnp.sum(other * other, axis=0, keepdims=True)
        inverse = lax.rsqrt(squares / D + EPSILON)
        at = pl.ds(pl.multiple_of((j ^ m) * here + u * piece, 128), piece)
        normed[:width, at] = (own * inverse * gain_own).astype(LOW)
        normed[width:, at] = (other * inverse * gain_other).astype(LOW)
        store(normed.at[:, at], normed_hbm.at[:, at])
        if m == 0:
            inverse_ref[:, columns(u)] = inverse

    def project(m, u):
        at = pl.ds(pl.multiple_of((j ^ m) * here + u * piece, 128), piece)
        for part, out in ((0, None), (1, k), (2, v)):
            value = jnp.dot(
                turned[part * cols:(part + 1) * cols, :], normed[:, at],
                preferred_element_type=FULL,
            )
            if part == 0:
                raw[:, at] = value
                q[:, at] = (value * factor).astype(LOW)
            else:
                out[:, at] = value.astype(LOW)
        for src, dst in ((q, q_hbm), (k, k_hbm), (v, v_hbm), (raw, raw_hbm)):
            store(src.at[:, at], dst.at[:, at])

    for u in range(subs):
        own_tokens[u].wait()
        other_copies[0, u].wait_recv()
        norm(0, u)
    own_block.wait()
    down_copy.wait_recv()
    down_copies = [send(down_out.at[d], down_out.at[d], peer) for peer in dp_ids]

    cs_copy.wait_recv()
    send_pairs(1)
    dp_copies = [send(cs_recv, remote_block.at[d], peer) for peer in dp_ids]
    late_copies = [send(up_hbm, ups_hbm.at[c_first], peer) for peer in col_ids]
    remote_block[d] = cs_recv[...]
    for u in range(subs - 1):
        for m in range(1, n_pair):
            pair_copies[m, u].wait_recv()
            other_copies[m, u] = send(tokens.at[m, u], others.at[m, u], sibling_id)
    own_out.wait()
    for copy in out_copies:
        copy.wait_recv()
    late_copies += [send(out_all.at[d], out_all.at[d], peer) for peer in dp_ids]
    cross_copies = []
    for m in range(n_dp):
        owner = d ^ m
        if m:
            dp_copies[m - 1].wait_recv()
        mine, its = block[owner], remote_block[owner]
        at = pl.multiple_of(owner * share, 32)
        qkv[pl.ds(at, share)] = jnp.where(near, mine, its)
        pass_on[owner] = jnp.where(near, its, mine)
        cross_copies.append(
            send(pass_on.at[owner], qkv.at[pl.ds(width + at, share)], sibling_id)
        )
    u = subs - 1
    for m in range(1, n_pair):
        pair_copies[m, u].wait_recv()
        other_copies[m, u] = send(tokens.at[m, u], others.at[m, u], sibling_id)
    turned[:, :width] = qkv[:width].T
    for copy in cross_copies:
        copy.wait_recv()
    turned[:, width:] = qkv[width:].T
    store(qkv, qkv_hbm)

    for u in range(subs):
        project(0, u)
    for u in range(subs):
        for m in range(1, n_pair):
            other_copies[m, u].wait_recv()
            norm(m, u)
            project(m, u)

    for copy in stored:
        copy.wait()
    for copy in late_copies + down_copies + [cot_copy]:
        copy.wait_recv()
    for copy in sent:
        copy.wait_send()


def head(n_dp, n_pair, gain, factor, tokens, cotangent, block, out, up, down):
    width, here = tokens.shape
    wide = block.shape[1]
    cols = wide // 3
    share = width // n_dp
    length = n_pair * here
    n_col = 2 * n_pair
    subs = 2
    piece = here // subs
    count = subs * n_pair * 2 + 4 * n_dp + 2 * n_col + 6
    moves = 4 + subs + 5 * subs * n_pair + 4
    hbm = pl.BlockSpec(memory_space=pl.ANY)
    vmem = pl.BlockSpec(memory_space=pltpu.VMEM)
    V = pltpu.VMEM
    shape = jax.ShapeDtypeStruct((cols, length), LOW)
    return pl.pallas_call(
        functools.partial(head_kernel, n_dp, n_pair),
        out_shape=(
            shape,
            shape,
            shape,
            jax.ShapeDtypeStruct((cols, length), FULL),
            jax.ShapeDtypeStruct((2 * width, length), LOW),
            jax.ShapeDtypeStruct((2 * width, wide), LOW),
            jax.ShapeDtypeStruct((n_dp, n_col) + out.shape, LOW),
            jax.ShapeDtypeStruct((n_col,) + up.shape, LOW),
            jax.ShapeDtypeStruct((width, here), LOW),
            jax.ShapeDtypeStruct(down.shape, LOW),
            jax.ShapeDtypeStruct((1, here), FULL),
        ),
        in_specs=[vmem] * 2 + [hbm] * 6,
        out_specs=(hbm,) * 10 + (vmem,),
        scratch_shapes=[
            V((n_pair, subs, width, piece), LOW),
            V((n_pair, subs, width, piece), LOW),
            V((n_dp, share, wide), LOW),
            V((share, wide), LOW),
            V((n_dp, share, wide), LOW),
            V((n_dp, share, wide), LOW),
            V((2 * width, wide), LOW),
            V((wide, 2 * width), LOW),
            V((2 * width, length), LOW),
            V((cols, length), LOW),
            V((cols, length), LOW),
            V((cols, length), LOW),
            V((cols, length), FULL),
            pltpu.SemaphoreType.DMA((count,)),
            pltpu.SemaphoreType.DMA((count,)),
            pltpu.SemaphoreType.DMA((moves,)),
        ],
        compiler_params=pltpu.CompilerParams(
            collective_id=2, has_side_effects=True, vmem_limit_bytes=60 * 2**20
        ),
        cost_estimate=pl.CostEstimate(
            flops=4 * wide * width * length, bytes_accessed=2**25, transcendentals=0
        ),
    )(gain, factor, tokens, cotangent, block.reshape(n_dp, share, wide), out, up, down)


def middle_kernel(n_dp, n_pair, unit, gain_ref, att_hbm, tokens_hbm, cot_hbm, cot_other, out_all, *refs):
    n_col = 2 * n_pair
    up_hbms, refs = refs[:n_dp], refs[n_dp:]
    down_hbms, refs = refs[:n_col], refs[n_col:]
    result_hbm, middle_hbm, out_hbm, refs = refs[0], refs[1], refs[2], refs[3:]
    grads_hbms, refs = refs[:n_dp], refs[n_dp:]
    down_outs, refs = refs[:n_col], refs[n_col:]
    (
        gain_out, tokens, cot, out_slab, up_slab, out_w, up_w, down_w, out_t, up_t, down_t, out_half, up_half,
        down_half, att, scaled, normed, active, grad_hidden, branch, middle, grad, result, grad_att,
        grads, down_grads, square_send, square_recv, inner_send, inner_recv, inverse, narrow,
        send_sems, recv_sems, local_sems,
    ) = refs
    r, s = lax.axis_index("row"), lax.axis_index("cs")
    j, d = lax.axis_index("cp"), lax.axis_index("dp")
    width, here = tokens.shape
    pieces, _, piece = square_send.shape
    cols = att_hbm.shape[0]
    half = n_col * unit // 2
    rows_q = up_hbms[0].shape[1]
    rows_g = grads_hbms[0].shape[1]
    c_first = (s * n_pair + j) ^ (r * n_pair)
    sems = (send_sems, recv_sems)
    gain = column(gain_ref[pl.ds(r, 1), :])
    counter, local_counter = iter(range(1000)), iter(range(1000))
    sent, stored = [], []

    def send(src, dst, device):
        copy = remote(src, dst, sems, next(counter), device)
        copy.start()
        sent.append(copy)
        return copy

    def move(src, dst):
        copy = pltpu.make_async_copy(src, dst, local_sems.at[next(local_counter)])
        copy.start()
        return copy

    def columns(u):
        return pl.ds(u * piece, piece)

    def span(u):
        return slice(u * piece, (u + 1) * piece)

    def down_rows(owner):
        return pl.ds(pl.multiple_of(owner * unit, 16), unit)

    own_rows, other_rows = pl.ds(0, width), pl.ds(width, width)
    weight_loads = [
        move(out_all.at[m], out_slab.at[:, pl.ds(m * rows_q, rows_q)]) for m in range(n_dp)
    ] + [
        move(up_hbms[m], up_slab.at[:, pl.ds(pl.multiple_of((d ^ m) * rows_q, 16), rows_q)])
        for m in range(n_dp)
    ] + [
        move(down_hbms[m], down_w.at[down_rows(c_first ^ m)])
        for m in range(n_col)
    ]
    att_loads = [
        move(
            att_hbm.at[:, pl.ds(pl.multiple_of(j * here + u * piece, 128), piece)],
            att.at[pl.ds(pl.multiple_of(j * cols, 16), cols), columns(u)],
        )
        for u in range(pieces)
    ]
    token_load = move(tokens_hbm, tokens)
    cot_loads = [move(cot_hbm, cot.at[own_rows]), move(cot_other, cot.at[other_rows])]
    sibling_id = {"row": 1 - r}
    pair_ids = [{"cp": j ^ m} for m in range(1, n_pair)]
    greet([sibling_id] + pair_ids)

    att_copies = {}
    for u in range(pieces):
        for m in range(1, n_pair):
            att_copies[u, m] = send(
                att_hbm.at[:, pl.ds(pl.multiple_of((j ^ m) * here + u * piece, 128), piece)],
                att.at[pl.ds(pl.multiple_of(j * cols, 16), cols), columns(u)],
                pair_ids[m - 1],
            )

    for copy in weight_loads:
        copy.wait()
    for m in range(n_col):
        at = slice(m * unit, (m + 1) * unit)
        out_w[at] = out_slab[m, :unit]
        up_w[at] = up_slab[m, :unit]
    cross_copies = []

    def cross(whole, part):
        cross_copies.append(send(whole.at[pl.ds(half, half)], part.at[:, other_rows], sibling_id))
        part[:, :width] = whole[:half]

    cross(up_w, up_half)
    cross(down_w, down_half)
    cross(out_w, out_half)
    out_t[...] = out_w[...].T
    narrow[...] = jnp.zeros_like(narrow)

    copies = {}

    def exchange(name, u, ref):
        copies[name, u] = send(
            ref.at[own_rows, columns(u)], ref.at[other_rows, columns(u)], sibling_id
        )

    def share_heads(u):
        att_loads[u].wait()
        for m in range(1, n_pair):
            att_copies[u, m].wait_recv()
        exchange("att", u, att)

    def first_branch(u):
        if u == 0:
            token_load.wait()
        copies["att", u].wait_recv()
        value = tokens[:, span(u)].astype(FULL) + jnp.dot(
            out_t[...], att[:, span(u)], preferred_element_type=FULL
        )
        scaled[:width, span(u)] = (value * gain).astype(LOW)
        exchange("scaled", u, scaled)
        square_send[u] = jnp.sum(value * value, axis=0, keepdims=True)
        copies["square", u] = send(square_send.at[u], square_recv.at[u], sibling_id)
        middle[:, span(u)] = value

    def hidden_units(u):
        if u == 0:
            for copy in cot_loads:
                copy.wait()
            for copy in cross_copies:
                copy.wait_recv()
            up_t[...] = up_w[...].T
            down_t[...] = down_w[...].T
        grad_active = jnp.dot(down_half[...], cot[:, span(u)], preferred_element_type=FULL)
        copies["scaled", u].wait_recv()
        copies["square", u].wait_recv()
        scale = lax.rsqrt((square_send[u] + square_recv[u]) / D + EPSILON)
        inverse[u] = scale
        hidden = scale * jnp.dot(up_half[...], scaled[:, span(u)], preferred_element_type=FULL)
        sigmoid = jax.nn.sigmoid(hidden)
        value = (grad_active * sigmoid * (1.0 + hidden * (1.0 - sigmoid))).astype(LOW)
        grad_hidden[:half, span(u)] = value
        exchange("grad_hidden", u, grad_hidden)
        active[:half, span(u)] = (hidden * sigmoid).astype(LOW)
        exchange("active", u, active)
        inner_send[u] = jnp.sum(value.astype(FULL) * hidden, axis=0, keepdims=True)
        copies["inner", u] = send(inner_send.at[u], inner_recv.at[u], sibling_id)
        normed[:, span(u)] = (middle[:, span(u)] * scale * gain).astype(LOW)

    def second_branch(u):
        copies["grad_hidden", u].wait_recv()
        copies["inner", u].wait_recv()
        scale = inverse[u]
        inner = scale * scale * ((inner_send[u] + inner_recv[u]) / D)
        back = jnp.dot(up_t[...], grad_hidden[:, span(u)], preferred_element_type=FULL)
        value = (
            cot[:width, span(u)].astype(FULL)
            + scale * (back * gain)
            - middle[:, span(u)] * inner
        )
        branch[:width, span(u)] = value.astype(LOW)
        exchange("branch", u, branch)
        grad[:, span(u)] = value
        stored.append(move(grad.at[:, columns(u)], middle_hbm.at[:, columns(u)]))
        product = back * middle[:, span(u)] * scale
        total = narrow[...]
        for v in range(piece // 128):
            total = total + product[:, v * 128:(v + 1) * 128]
        narrow[...] = total
        copies["active", u].wait_recv()
        result[:, span(u)] = middle[:, span(u)] + jnp.dot(
            down_t[...], active[:, span(u)], preferred_element_type=FULL
        )
        stored.append(move(result.at[:, columns(u)], result_hbm.at[:, columns(u)]))

    def heads_back(u):
        copies["branch", u].wait_recv()
        grad_att[:, span(u)] = jnp.dot(
            out_half[...], branch[:, span(u)], preferred_element_type=FULL
        ).astype(LOW)
        target = pl.ds(pl.multiple_of(j * here + u * piece, 128), piece)
        for m in range(n_pair):
            source = grad_att.at[
                pl.ds(pl.multiple_of((j ^ m) * cols, 16), cols), columns(u)
            ]
            if m:
                copies["out", u, m] = send(source, out_hbm.at[:, target], pair_ids[m - 1])
            else:
                stored.append(move(source, out_hbm.at[:, target]))

    stages = (share_heads, first_branch, hidden_units, second_branch, heads_back)
    for t in range(pieces + len(stages) - 1):
        for number in reversed(range(len(stages))):
            if 0 <= t - number < pieces:
                stages[number](t - number)

    def product(left, right, target, first):
        turned = right[:width].T
        for n in range(n_col):
            target[n, first:first + unit] = jnp.dot(
                left[n * unit:(n + 1) * unit], turned, preferred_element_type=FULL
            ).astype(LOW)

    product(active, cot, down_grads, 0)
    for m in range(n_col):
        stored.append(move(down_grads.at[c_first ^ m], down_outs[m]))
    if grads.shape[1] > 2 * unit:
        grads[...] = jnp.zeros_like(grads)
    product(grad_hidden, normed, grads, unit)
    product(att, branch, grads, 0)
    for m in range(n_dp):
        at = pl.ds(pl.multiple_of((d ^ m) * rows_g, 16), rows_g)
        stored.append(move(grads.at[:, at], grads_hbms[m]))
    gain_out[...] = jnp.sum(narrow[...].T, axis=0, keepdims=True)

    for u in range(pieces):
        for m in range(1, n_pair):
            copies["out", u, m].wait_recv()
    for copy in stored:
        copy.wait()
    for copy in sent:
        copy.wait_send()


def middle_part(n_dp, n_pair, gain, attended, tokens, cotangent, cot_other, out_all, ups, downs):
    width, here = tokens.shape
    n_col = 2 * n_pair
    cols, length = attended.shape
    unit = downs[0].shape[0]
    half = n_col * unit // 2
    rows_q = ups[0].shape[1]
    rows_g = quarter_rows(2 * unit, n_dp)
    pieces = max(2, here // 256)
    piece = here // pieces
    count = 2 * pieces * (n_pair - 1) + 7 * pieces + 8
    moves = 3 * n_dp + 2 * n_col + 4 * pieces + 4
    hbm = pl.BlockSpec(memory_space=pl.ANY)
    vmem = pl.BlockSpec(memory_space=pltpu.VMEM)
    V = pltpu.VMEM
    S = jax.ShapeDtypeStruct
    weight = V((2 * half, width), LOW)
    weight_t = V((width, 2 * half), LOW)
    both = V((2 * width, here), LOW)
    whole = V((width, here), FULL)
    row = V((pieces, 1, piece), FULL)
    out = pl.pallas_call(
        functools.partial(middle_kernel, n_dp, n_pair, unit),
        out_shape=(
            S((width, here), FULL),
            S((width, here), FULL),
            S((cols, length), LOW),
        )
        + (S((n_col, rows_g, width), LOW),) * n_dp
        + (S((unit, width), LOW),) * n_col
        + (S((1, width), FULL),),
        in_specs=[vmem] + [hbm] * (5 + n_dp + n_col),
        out_specs=(hbm,) * (3 + n_dp + n_col) + (vmem,),
        scratch_shapes=[
            V((width, here), LOW),
            both,
            V((n_col, n_dp * rows_q, width), LOW),
            V((n_col, n_dp * rows_q, width), LOW),
            weight,
            weight,
            weight,
            weight_t,
            weight_t,
            weight_t,
            V((half, 2 * width), LOW),
            V((half, 2 * width), LOW),
            V((half, 2 * width), LOW),
            both,
            both,
            V((width, here), LOW),
            V((2 * half, here), LOW),
            V((2 * half, here), LOW),
            both,
            whole,
            whole,
            whole,
            V((width, here), LOW),
            V((n_col, n_dp * rows_g, width), LOW),
            V((n_col, unit, width), LOW),
            row,
            row,
            row,
            row,
            row,
            V((width, 128), FULL),
            pltpu.SemaphoreType.DMA((count,)),
            pltpu.SemaphoreType.DMA((count,)),
            pltpu.SemaphoreType.DMA((moves,)),
        ],
        compiler_params=pltpu.CompilerParams(
            collective_id=3, has_side_effects=True, vmem_limit_bytes=62 * 2**20
        ),
        cost_estimate=pl.CostEstimate(
            flops=18 * 2 * half * width * here, bytes_accessed=2**25, transcendentals=0
        ),
    )(gain, attended, tokens, cotangent, cot_other, out_all, *ups, *downs)
    return out[0], out[1], out[2], out[3:3 + n_dp], out[3 + n_dp:-1], out[-1]


def quarter_rows(rows, n_dp):
    return -(-rows // (16 * n_dp)) * 16


def tail_kernel(
    n_dp, n_pair, gain_ref, inverse_ref, sums_ref, qkv_hbm, dq_hbm, dk_hbm, dv_hbm, normed_hbm,
    tokens_hbm, middle_hbm, *refs,
):
    n_col = 2 * n_pair
    grads_hbms, refs = refs[:n_dp], refs[n_dp:]
    down_hbms, refs = refs[:n_col], refs[n_col:]
    (
        result_hbm, qkv_out, grads_out, down_out, sums_out,
        qkv, dproj, normed, tokens, middle, result, row_send, row_recv, own, pair_send, pair_recv,
        dp_send, dp_recv, dp_own, cross_send, cross_recv, cs_send, cs_recv, final, grads_parts,
        grads_send, grads_recv, grads_final, down_parts, down_send, down_recv, down_final,
        inner_send, inner_recv, sums_send, sums_recv, last_sums, send_sems, recv_sems, local_sems,
    ) = refs
    r, s = lax.axis_index("row"), lax.axis_index("cs")
    j, d = lax.axis_index("cp"), lax.axis_index("dp")
    width, here = tokens.shape
    cols = dq_hbm.shape[0]
    unit = down_parts.shape[1]
    share = width // n_dp
    part = share // 2
    rows_d = down_final.shape[0]
    subs = row_send.shape[1]
    piece = here // subs
    c_first = (s * n_pair + j) ^ (r * n_pair)
    near = r == s
    sems = (send_sems, recv_sems)
    gain = column(gain_ref[pl.ds(r, 1), :])
    counter, local_counter = iter(range(1000)), iter(range(1000))
    sent, stored = [], []

    def send(src, dst, device):
        copy = remote(src, dst, sems, next(counter), device)
        copy.start()
        sent.append(copy)
        return copy

    def move(src, dst):
        copy = pltpu.make_async_copy(src, dst, local_sems.at[next(local_counter)])
        copy.start()
        return copy

    load_grads = [move(grads_hbms[k], grads_parts.at[k]) for k in range(n_dp)]
    early = [
        move(dq_hbm, dproj.at[pl.ds(0, cols)]),
        move(dk_hbm, dproj.at[pl.ds(cols, cols)]),
        move(dv_hbm, dproj.at[pl.ds(2 * cols, cols)]),
        move(normed_hbm, normed),
    ]
    load_qkv = move(qkv_hbm, qkv)
    load_down = [move(down_hbms[k], down_parts.at[k]) for k in range(n_col) if k != 1]
    late = [move(tokens_hbm, tokens), move(middle_hbm, middle)]

    sibling_id = {"row": 1 - r}
    cs_id = {"cs": 1 - s}
    dp_ids = [{"dp": d ^ k} for k in range(1, n_dp)]
    col_ids = [{"cs": s ^ (k // n_pair), "cp": j ^ (k % n_pair)} for k in range(1, n_col)]
    greet([sibling_id] + dp_ids + col_ids)


    for copy in load_grads:
        copy.wait()

    def summed(place_at):
        value = grads_parts[0, place_at].astype(FULL)
        for k in range(1, n_dp):
            value = value + grads_parts[k, place_at].astype(FULL)
        return value

    grads_copies = []
    for k in range(1, n_col):
        grads_send[k - 1] = summed(c_first ^ k).astype(LOW)
        grads_copies.append(send(grads_send.at[k - 1], grads_recv.at[k - 1], col_ids[k - 1]))
    down_copy = send(down_hbms[1], down_parts.at[1], col_ids[0])

    def quarter(half, owner):
        at = pl.ds(pl.multiple_of(half * width + owner * share, 32), share)
        return mm(normed[at, :], dproj[...], 1, 1)

    def rows_of(half, chunk, u):
        at = pl.ds(pl.multiple_of(chunk * here + u * piece, 128), piece)
        return jnp.dot(
            qkv[half * width:(half + 1) * width, :], dproj[:, at], preferred_element_type=FULL
        )

    dp_copies = {}

    def send_part(k, p):
        rows = pl.ds(p * part, part)
        dp_copies[k, p] = send(
            dp_send.at[k - 1, :, rows], dp_recv.at[k - 1, :, rows], dp_ids[k - 1]
        )

    def quarters(k):
        for half in range(2):
            dp_send[k - 1, half] = quarter(half, d ^ k).astype(LOW)
        send_part(k, 0)

    row_copies, pair_copies = {}, []
    for copy in early:
        copy.wait()
    for k in reversed(range(1, n_dp)):
        quarters(k)
    for k in reversed(range(1, n_dp)):
        send_part(k, 1)
    load_qkv.wait()
    for k in range(1, n_pair):
        for u in range(subs):
            row_send[k, u] = rows_of(1, j ^ k, u).astype(LOW)
            row_copies[k, u] = send(row_send.at[k, u], row_recv.at[k, u], sibling_id)
    for k in range(1, n_pair):
        for u in range(subs):
            value = rows_of(0, j ^ k, u)
            row_copies[k, u].wait_recv()
            pair_send[k - 1, u] = (value + row_recv[k, u].astype(FULL)).astype(LOW)
            pair_copies.append(
                send(pair_send.at[k - 1, u], pair_recv.at[k - 1, u], {"cp": j ^ k})
            )
    for copy in load_down:
        copy.wait()
    down_copy.wait_recv()
    value = down_parts[0].astype(FULL)
    for k in range(1, n_col):
        value = value + down_parts[k].astype(FULL)
    if down_send.shape[0] > unit:
        down_send[...] = jnp.zeros_like(down_send)
    down_send[:unit] = value.astype(LOW)

    def down_rows(owner):
        return pl.ds(pl.multiple_of(owner * rows_d, 16), rows_d)

    down_copies = [
        send(down_send.at[down_rows(d ^ k)], down_recv.at[k - 1], dp_ids[k - 1])
        for k in range(1, n_dp)
    ]
    for half in range(2):
        dp_own[half] = quarter(half, d)

    for u in range(subs):
        row_send[0, u] = rows_of(1, j, u).astype(LOW)
        row_copies[0, u] = send(row_send.at[0, u], row_recv.at[0, u], sibling_id)
    for u in range(subs):
        own[u] = rows_of(0, j, u)

    cs_copies = []

    def reduce_part(p):
        rows = slice(p * part, (p + 1) * part)
        for k in range(1, n_dp):
            dp_copies[k, p].wait_recv()

        def total(half):
            value = dp_own[half, rows]
            for k in range(1, n_dp):
                value = value + dp_recv[k - 1, half, rows].astype(FULL)
            return value

        cross_send[p] = total(1).astype(LOW)
        cross_copy = send(cross_send.at[p], cross_recv.at[p], sibling_id)
        kept = total(0)
        cross_copy.wait_recv()
        crossed = cross_recv[p].astype(FULL)
        cs_send[p] = jnp.where(near, crossed, kept).astype(LOW)
        cs_copies.append(send(cs_send.at[p], cs_recv.at[p], cs_id))
        dp_own[0, rows] = jnp.where(near, kept, crossed)

    reduce_part(0)

    reduce_part(1)

    value = down_send[down_rows(d)].astype(FULL)
    for k in range(1, n_dp):
        down_copies[k - 1].wait_recv()
        value = value + down_recv[k - 1].astype(FULL)
    down_final[...] = value.astype(LOW)
    out_copies = [send(down_final, down_out.at[d], peer) for peer in dp_ids]
    stored.append(move(down_final, down_out.at[d]))

    value = summed(c_first)
    for k in range(1, n_col):
        grads_copies[k - 1].wait_recv()
        value = value + grads_recv[k - 1].astype(FULL)
    grads_final[...] = value.astype(LOW)
    out_copies += [send(grads_final, grads_out.at[d], peer) for peer in dp_ids]
    stored.append(move(grads_final, grads_out.at[d]))

    for copy in late:
        copy.wait()
    for copy in pair_copies:
        copy.wait_recv()
    inverse = inverse_ref[...]
    for u in range(subs):
        row_copies[0, u].wait_recv()
        at = slice(u * piece, (u + 1) * piece)
        value = own[u] + row_recv[0, u].astype(FULL)
        for k in range(1, n_pair):
            value = value + pair_recv[k - 1, u].astype(FULL)
        own[u] = value
        inner_send[:, at] = jnp.sum(
            value * gain * tokens[:, at].astype(FULL), axis=0, keepdims=True
        )
    inner_copy = send(inner_send, inner_recv, sibling_id)

    def finish_part(p):
        cs_copies[p].wait_recv()
        rows = slice(p * part, (p + 1) * part)
        final[p] = (dp_own[0, rows] + cs_recv[p].astype(FULL)).astype(LOW)
        target = qkv_out.at[d, pl.ds(p * part, part)]
        out_copies.extend([send(final.at[p], target, peer) for peer in dp_ids])
        stored.append(move(final.at[p], target))

    finish_part(0)
    narrow = jnp.zeros((width, 128), FULL)
    for u in range(subs):
        at = slice(u * piece, (u + 1) * piece)
        wide = own[u] * tokens[:, at].astype(FULL) * inverse[:, at]
        for v in range(piece // 128):
            narrow = narrow + wide[:, v * 128:(v + 1) * 128]
    gain_part = jnp.sum(narrow.T, axis=0, keepdims=True)
    sums_send[0] = jnp.concatenate([gain_part, sums_ref[1:]], 0)
    sums_copies = {}

    def send_sums(step, peers):
        for k, peer in enumerate(peers):
            sums_copies[step, k] = send(sums_send.at[step], sums_recv.at[step, k], peer)

    def add_sums(step, members):
        value = sums_send[step]
        for k in range(members - 1):
            sums_copies[step, k].wait_recv()
            value = value + sums_recv[step, k]
        sums_send[step + 1] = value

    send_sums(0, dp_ids)
    inner_copy.wait_recv()
    inner = (inner_send[...] + inner_recv[...]) / D
    for u in range(subs):
        at = slice(u * piece, (u + 1) * piece)
        result[:, at] = (
            middle[:, at]
            + inverse[:, at] * (own[u] * gain)
            - tokens[:, at].astype(FULL)
            * (inverse[:, at] * inverse[:, at] * inverse[:, at] * inner[:, at])
        )
    stored.append(move(result, result_hbm))
    add_sums(0, n_dp)
    send_sums(1, col_ids)
    finish_part(1)

    add_sums(1, n_col)
    sums_copy = send(sums_send.at[2], last_sums, sibling_id)
    sums_copy.wait_recv()
    sums_out[0] = sums_send[2]
    sums_out[1] = last_sums[...]
    for copy in out_copies:
        copy.wait_recv()
    for copy in stored:
        copy.wait()
    for copy in sent:
        copy.wait_send()


def tail(n_dp, n_pair, gain, inverse, sums, qkv, dq, dk, dv, normed, tokens, middle, grads, downs):
    width, here = tokens.shape
    length = normed.shape[1]
    cols = dq.shape[0]
    unit = downs[0].shape[0]
    rows_d = quarter_rows(unit, n_dp)
    share = width // n_dp
    subs = 2
    piece = here // subs
    n_col = 2 * n_pair
    part = grads[0].shape[1:]
    wide = 3 * cols
    count = 2 * n_pair * subs + 8 * n_dp + 2 * n_col + 12
    moves = 13 + n_dp + n_col
    hbm = pl.BlockSpec(memory_space=pl.ANY)
    vmem = pl.BlockSpec(memory_space=pltpu.VMEM)
    V = pltpu.VMEM
    halves = V((2, share // 2, wide), LOW)
    return pl.pallas_call(
        functools.partial(tail_kernel, n_dp, n_pair),
        out_shape=(
            jax.ShapeDtypeStruct((width, here), FULL),
            jax.ShapeDtypeStruct((n_dp, share, wide), LOW),
            jax.ShapeDtypeStruct((n_dp,) + part, LOW),
            jax.ShapeDtypeStruct((n_dp, rows_d, width), LOW),
            jax.ShapeDtypeStruct((2,) + sums.shape, FULL),
        ),
        in_specs=[vmem] * 3 + [hbm] * (7 + n_dp + n_col),
        out_specs=(hbm,) * 4 + (vmem,),
        scratch_shapes=[
            V((2 * width, wide), LOW),
            V((wide, length), LOW),
            V((2 * width, length), LOW),
            V((width, here), LOW),
            V((width, here), FULL),
            V((width, here), FULL),
            V((n_pair, subs, width, piece), LOW),
            V((n_pair, subs, width, piece), LOW),
            V((subs, width, piece), FULL),
            V((n_pair - 1, subs, width, piece), LOW),
            V((n_pair - 1, subs, width, piece), LOW),
            V((n_dp - 1, 2, share, wide), LOW),
            V((n_dp - 1, 2, share, wide), LOW),
            V((2, share, wide), FULL),
            halves,
            halves,
            halves,
            halves,
            halves,
            V((n_dp, n_col) + part, LOW),
            V((n_col - 1,) + part, LOW),
            V((n_col - 1,) + part, LOW),
            V(part, LOW),
            V((n_col, unit, width), LOW),
            V((n_dp * rows_d, width), LOW),
            V((n_dp - 1, rows_d, width), LOW),
            V((rows_d, width), LOW),
            V((1, here), FULL),
            V((1, here), FULL),
            V((3,) + sums.shape, FULL),
            V((2, max(n_dp, n_col) - 1) + sums.shape, FULL),
            V(sums.shape, FULL),
            pltpu.SemaphoreType.DMA((count,)),
            pltpu.SemaphoreType.DMA((count,)),
            pltpu.SemaphoreType.DMA((moves,)),
        ],
        compiler_params=pltpu.CompilerParams(
            collective_id=1, has_side_effects=True, vmem_limit_bytes=62 * 2**20
        ),
        cost_estimate=pl.CostEstimate(
            flops=8 * wide * width * length, bytes_accessed=2**25, transcendentals=0
        ),
    )(gain, inverse, sums, qkv, dq, dk, dv, normed, tokens, middle, *grads, *downs)


def on_device(
    tokens,
    segment_ids,
    padding_mask,
    w_qkv,
    w_out,
    w_up,
    w_down,
    gain_attn,
    gain_mlp,
    scale_raw,
    cotangent,
):
    width, here = tokens.shape
    r, s = lax.axis_index("row"), lax.axis_index("cs")
    j, d = lax.axis_index("cp"), lax.axis_index("dp")
    n_pair, n_dp, n_col = lax.axis_size("cp"), lax.axis_size("dp"), lax.axis_size(COLS)
    c = s * n_pair + j
    head_cols = w_qkv.shape[0] // (3 * width)
    heads = head_cols // HEAD
    near = r == s

    segments = jnp.where(s == r, segment_ids[0], sibling(segment_ids)[0])
    padding = jnp.where(s == r, padding_mask[0], sibling(padding_mask)[0])
    length = segments.shape[0]
    firsts = segments[::BLOCK]
    starts = jnp.sum((segments[None, :] < firsts[:, None]).astype(jnp.int32), axis=1)
    filled = (jnp.sum(padding) + BLOCK - 1) // BLOCK
    blocks = jnp.arange(length // BLOCK, dtype=jnp.int32)
    lo = starts // BLOCK
    hi = jnp.minimum(blocks, filled)
    segq = segments[None, :].astype(FULL)
    segk = jnp.where(padding == 1, segments, -1)[None, :].astype(FULL)

    gain_one, gain_two = gain_attn.reshape(2, width), gain_mlp.reshape(2, width)
    factor = (LOG_TWO_E / math.sqrt(HEAD) * jnp.log1p(jnp.exp(scale_raw)))[None, :]

    block = w_qkv.reshape(width, 3 * head_cols)
    down = w_down.reshape(-1, width)
    unit = down.shape[0]
    part_rows = quarter_rows(unit, n_dp)

    def quarters(matrix):
        padded = jnp.pad(matrix, ((0, n_dp * part_rows - unit), (0, 0)))
        return padded.reshape(n_dp, part_rows, width)

    out = lax.dynamic_index_in_dim(quarters(w_out.reshape(-1, width)), d, 0, keepdims=False)
    up = lax.dynamic_index_in_dim(quarters(w_up.reshape(width, -1).T), d, 0, keepdims=False)
    (
        queries, key_heads, values, query_raw, normed_one, qkv, out_all, ups, cot_other, down_pair,
        inverse_one,
    ) = head(
        n_dp, n_pair, gain_one, jnp.tile(factor, (1, heads)), tokens, cotangent, block, out, up,
        quarters(down),
    )
    ups = gather(ups, "dp")
    downs = [down, down_pair.reshape(-1, width)[:unit]] + [
        lax.ppermute(down, COLS, [(i, i ^ k) for i in range(n_col)]) for k in range(2, n_col)
    ]
    attended, logs = attention_forward(queries, key_heads, values, segq, segk, lo, hi)
    result, grad_middle, grad_attended, grads, down_grads, gain_two_part = middle_part(
        n_dp, n_pair, gain_two, attended, tokens, cotangent, cot_other, out_all, ups, downs
    )
    received = [grads[0]] + [shift(grads[k], "dp", k) for k in range(1, n_dp)]
    down_received = list(down_grads[:2]) + [
        lax.ppermute(down_grads[k], COLS, [(i, i ^ k) for i in range(n_col)])
        for k in range(2, n_col)
    ]

    dq, dk, dv, scale_part = attention_backward(
        queries, key_heads, values, attended, grad_attended, logs, query_raw, factor,
        segq, segk, lo, hi,
    )
    scale_part = (
        scale_part[:, 0] * (LOG_TWO_E / math.sqrt(HEAD)) * jax.nn.sigmoid(scale_raw)
    )
    sums = jnp.concatenate(
        [
            jnp.zeros((1, width), FULL),
            gain_two_part,
            jnp.pad(scale_part, (0, width - HEAD))[None],
            jnp.zeros((5, width), FULL),
        ]
    )
    grad_tokens, grad_qkv, final, final_down, sums = tail(
        n_dp, n_pair, gain_one, inverse_one, sums, qkv, dq, dk, dv, normed_one, tokens,
        grad_middle, received, down_received,
    )
    grad_qkv = grad_qkv.astype(FULL)
    final = final.reshape(-1, width)
    final = [final[i * unit:(i + 1) * unit].astype(FULL) for i in range(2)]
    final.append(final_down.reshape(-1, width)[:unit].astype(FULL))
    own, other = sums[0], sums[1]
    first = r == 0
    gains = jnp.concatenate(
        [jnp.where(first, own[:2], other[:2]), jnp.where(first, other[:2], own[:2])], 1
    )
    scale_total = (own[2] + other[2])[:HEAD]
    return (
        result,
        grad_tokens,
        grad_qkv.reshape(-1),
        final[0].reshape(-1),
        final[1].T.reshape(-1),
        final[2].reshape(-1),
        gains[0],
        gains[1],
        scale_total,
    )


def solution(mesh):
    n_dp, n_row, n_col = (mesh.shape[name] for name in ("dp", "row", "col"))
    split = Mesh(
        np.asarray(mesh.devices).reshape(n_dp, n_row, n_row, n_col // n_row),
        ("dp", "row", "cs", "cp"),
    )
    rows = P("row", ("dp", "cs", "cp"))
    ids = P(("dp", "row"), None)
    blocks = P(("row", "cs", "cp"))
    return jax.shard_map(
        on_device,
        mesh=split,
        in_specs=(rows, ids, ids, blocks, blocks, blocks, blocks, P(), P(), P(), rows),
        out_specs=(rows, rows, blocks, blocks, blocks, blocks, P(), P(), P()),
        check_vma=False,
    )
```

```python
import functools
import math

import jax
import jax.numpy as jnp
import numpy as np
from jax import lax
from jax.experimental import pallas as pl
from jax.experimental.pallas import tpu as pltpu
from jax.sharding import Mesh, PartitionSpec as P

D = 1280
HEAD = 80
EPSILON = 1e-06
LOG_TWO_E = 1.442695041
BLOCK = 256
LOW = jnp.bfloat16
FULL = jnp.float32
COLS = ("cs", "cp")


def mm(left, right, left_axis, right_axis):
    return lax.dot_general(
        left, right, (((left_axis,), (right_axis,)), ((), ())), preferred_element_type=FULL
    )


def shift(x, axis, k):
    n = lax.axis_size(axis)
    return lax.ppermute(x, axis, [(i, i ^ k) for i in range(n)])


def sibling(x):
    return shift(x, "row", 1)


def cut(x, index, count, axis):
    step = x.shape[axis] // count
    return lax.dynamic_slice_in_dim(x, index * step, step, axis)


def gather(x, axis):
    return [x] + [shift(x, axis, k) for k in range(1, lax.axis_size(axis))]


def diag_mask(segq, segk):
    size = segk.shape[0], segq.shape[1]
    ki = lax.broadcasted_iota(jnp.int32, size, 0)
    qi = lax.broadcasted_iota(jnp.int32, size, 1)
    return ((segk == segq) & (ki <= qi)) | (ki == qi)


def half_row(ref, which):
    size = ref.shape[1] // 2
    return jnp.where(which == 0, ref[:, :size], ref[:, size:])


def column(row):
    return jnp.broadcast_to(row, (8, row.shape[1])).T[:, :1]


def rows_of(h):
    return slice(h * HEAD, (h + 1) * HEAD)


def forward_kernel(heads, lo_ref, hi_ref, q_ref, k_ref, v_ref, segq_ref, segk_ref, o_ref, log_ref, ks, segks):
    i = pl.program_id(0)

    @pl.when(i == 0)
    def _():
        for h in range(heads):
            ks[h] = k_ref[h * HEAD:(h + 1) * HEAD, :].T
        segks[...] = column(jnp.where(segk_ref[1:] == 1, segk_ref[:1], -1).astype(FULL))

    segq = segq_ref[:1].astype(FULL)

    def visit(kb, carry, diagonal):
        at = pl.ds(pl.multiple_of(kb * BLOCK, BLOCK), BLOCK)
        segk = segks[at, :]
        mask = diag_mask(segq, segk) if diagonal else segk == segq
        scores = [
            jnp.dot(ks[h, at, :], q_ref[rows_of(h), :], preferred_element_type=FULL)
            for h in range(heads)
        ]
        peaks, totals, weights = [], [], []
        for h in range(heads):
            s = jnp.where(mask, scores[h], -1e30)
            peak = jnp.max(s, axis=0, keepdims=True)
            if not diagonal:
                peak = jnp.maximum(carry[h][0], peak)
            p = jnp.exp(s - peak)
            peaks.append(peak)
            totals.append(jnp.sum(p, axis=0, keepdims=True))
            weights.append(p.astype(LOW))
        out = []
        for h in range(heads):
            new = jnp.dot(v_ref[rows_of(h), at], weights[h], preferred_element_type=FULL)
            total = totals[h]
            if not diagonal:
                m, l, acc = carry[h]
                keep = jnp.exp(m - peaks[h])
                total = l * keep + total
                new = acc * keep + new
            out.append((peaks[h], total, new))
        return tuple(out)

    carry = visit(i, None, True)
    carry = lax.fori_loop(lo_ref[i], hi_ref[i], lambda kb, c: visit(kb, c, False), carry)
    for h in range(heads):
        m, l, acc = carry[h]
        o_ref[h * HEAD:(h + 1) * HEAD, :] = (acc / l).astype(LOW)
        log_ref[h] = m + jnp.log(l)


def attention_forward(q, k, v, segq, segk, lo, hi):
    cols, length = q.shape
    heads = cols // HEAD
    steps = length // BLOCK
    whole = pl.BlockSpec((cols, length), lambda i, *_: (0, 0))
    part = pl.BlockSpec((cols, BLOCK), lambda i, *_: (0, i))
    return pl.pallas_call(
        functools.partial(forward_kernel, heads),
        out_shape=(
            jax.ShapeDtypeStruct((cols, length), LOW),
            jax.ShapeDtypeStruct((heads, 1, length), FULL),
        ),
        grid_spec=pltpu.PrefetchScalarGridSpec(
            num_scalar_prefetch=2,
            grid=(steps,),
            in_specs=[
                part,
                whole,
                whole,
                pl.BlockSpec((2, BLOCK), lambda i, *_: (0, i)),
                pl.BlockSpec((2, length), lambda i, *_: (0, 0)),
            ],
            out_specs=(part, pl.BlockSpec((heads, 1, BLOCK), lambda i, *_: (0, 0, i))),
            scratch_shapes=[pltpu.VMEM((heads, length, HEAD), LOW), pltpu.VMEM((length, 1), FULL)],
        ),
        compiler_params=pltpu.CompilerParams(vmem_limit_bytes=62 * 2**20),
        cost_estimate=pl.CostEstimate(
            flops=8 * 2 * length * length * cols,
            bytes_accessed=4 * cols * length * 2,
            transcendentals=heads * length * length // 3,
        ),
    )(lo, hi, q, k, v, segq, segk)


def backward_kernel(
    heads, lo_ref, hi_ref, q_ref, k_ref, v_ref, o_ref, go_ref, log_ref, raw_ref, factor_ref,
    segq_ref, segk_ref, dq_ref, dk_ref, dv_ref, scale_ref, ks, vs, qs, gs, dks, dvs, dqs, segks,
):
    i = pl.program_id(0)

    @pl.when(i == 0)
    def _():
        for h in range(heads):
            ks[h] = k_ref[h * HEAD:(h + 1) * HEAD, :].T
            vs[h] = v_ref[h * HEAD:(h + 1) * HEAD, :].T
        segks[...] = column(jnp.where(segk_ref[1:] == 1, segk_ref[:1], -1).astype(FULL))
        scale_ref[...] = jnp.zeros_like(scale_ref)

    segq = segq_ref[:1].astype(FULL)
    inner = [
        jnp.sum(
            o_ref[h * HEAD:(h + 1) * HEAD, :].astype(FULL)
            * go_ref[h * HEAD:(h + 1) * HEAD, :].astype(FULL),
            axis=0,
            keepdims=True,
        )
        for h in range(heads)
    ]

    for h in range(heads):
        qs[h] = q_ref[rows_of(h), :].T
        gs[h] = go_ref[rows_of(h), :].T

    def visit(kb, diagonal):
        at = pl.ds(pl.multiple_of(kb * BLOCK, BLOCK), BLOCK)
        segk = segks[at, :]
        mask = diag_mask(segq, segk) if diagonal else segk == segq
        scores = [
            jnp.dot(ks[h, at, :], q_ref[rows_of(h), :], preferred_element_type=FULL)
            for h in range(heads)
        ]
        dps = [
            jnp.dot(vs[h, at, :], go_ref[rows_of(h), :], preferred_element_type=FULL)
            for h in range(heads)
        ]
        ps, dss = [], []
        for h in range(heads):
            p = jnp.where(mask, jnp.exp(scores[h] - log_ref[h]), 0.0)
            dss.append((p * (dps[h] - inner[h])).astype(LOW))
            ps.append(p.astype(LOW))
        for h in range(heads):
            new_v = jnp.dot(ps[h], gs[h], preferred_element_type=FULL)
            new_k = jnp.dot(dss[h], qs[h], preferred_element_type=FULL)
            new_q = jnp.dot(k_ref[rows_of(h), at], dss[h], preferred_element_type=FULL)
            if diagonal:
                dvs[h, at, :], dks[h, at, :], dqs[rows_of(h), :] = new_v, new_k, new_q
            else:
                dvs[h, at, :] += new_v
                dks[h, at, :] += new_k
                dqs[rows_of(h), :] += new_q

    visit(i, True)

    @pl.loop(lo_ref[i], hi_ref[i])
    def _(kb):
        visit(kb, False)

    factor = column(factor_ref[...])
    part = jnp.zeros((HEAD, 1), FULL)
    for h in range(heads):
        rows = slice(h * HEAD, (h + 1) * HEAD)
        dq = dqs[rows, :]
        part = part + jnp.sum(dq * raw_ref[rows, :], axis=1, keepdims=True)
        dq_ref[rows, :] = (dq * factor).astype(LOW)
    scale_ref[...] += part

    @pl.when(i == pl.num_programs(0) - 1)
    def _():
        for h in range(heads):
            dk_ref[rows_of(h), :] = dks[h].astype(LOW).T
            dv_ref[rows_of(h), :] = dvs[h].astype(LOW).T


def attention_backward(q, k, v, o, go, logs, raw, factor, segq, segk, lo, hi):
    cols, length = q.shape
    heads = cols // HEAD
    steps = length // BLOCK
    whole = pl.BlockSpec((cols, length), lambda i, *_: (0, 0))
    part = pl.BlockSpec((cols, BLOCK), lambda i, *_: (0, i))
    total = pl.BlockSpec((HEAD, 1), lambda i, *_: (0, 0))
    shape = jax.ShapeDtypeStruct((cols, length), LOW)
    return pl.pallas_call(
        functools.partial(backward_kernel, heads),
        out_shape=(shape, shape, shape, jax.ShapeDtypeStruct((HEAD, 1), FULL)),
        grid_spec=pltpu.PrefetchScalarGridSpec(
            num_scalar_prefetch=2,
            grid=(steps,),
            in_specs=[
                part,
                whole,
                whole,
                part,
                part,
                pl.BlockSpec((heads, 1, BLOCK), lambda i, *_: (0, 0, i)),
                part,
                pl.BlockSpec((1, HEAD), lambda i, *_: (0, 0)),
                pl.BlockSpec((2, BLOCK), lambda i, *_: (0, i)),
                pl.BlockSpec((2, length), lambda i, *_: (0, 0)),
            ],
            out_specs=(part, whole, whole, total),
            scratch_shapes=[
                pltpu.VMEM((heads, length, HEAD), LOW),
                pltpu.VMEM((heads, length, HEAD), LOW),
                pltpu.VMEM((heads, BLOCK, HEAD), LOW),
                pltpu.VMEM((heads, BLOCK, HEAD), LOW),
                pltpu.VMEM((heads, length, HEAD), FULL),
                pltpu.VMEM((heads, length, HEAD), FULL),
                pltpu.VMEM((cols, BLOCK), FULL),
                pltpu.VMEM((length, 1), FULL),
            ],
        ),
        compiler_params=pltpu.CompilerParams(vmem_limit_bytes=62 * 2**20),
        cost_estimate=pl.CostEstimate(
            flops=8 * 5 * length * length * cols,
            bytes_accessed=8 * cols * length * 2,
            transcendentals=heads * length * length // 3,
        ),
    )(lo, hi, q, k, v, o, go, logs, raw, factor, segq, segk)


def remote(src, dst, sems, index, device):
    return pltpu.make_async_remote_copy(
        src_ref=src,
        dst_ref=dst,
        send_sem=sems[0].at[index],
        recv_sem=sems[1].at[index],
        device_id=device,
        device_id_type=pl.DeviceIdType.MESH,
    )


def greet(peers):
    barrier = pltpu.get_barrier_semaphore()
    for peer in peers:
        pl.semaphore_signal(barrier, inc=1, device_id=peer, device_id_type=pl.DeviceIdType.MESH)
    pl.semaphore_wait(barrier, len(peers))


def head_kernel(
    n_dp, n_pair, gain_ref, factor_ref, tokens_hbm, cot_hbm, block_hbm, out_hbm, up_hbm,
    down_hbm, q_hbm, k_hbm, v_hbm, raw_hbm, normed_hbm, qkv_hbm, out_all, ups_hbm, cot_out, down_out,
    inverse_ref,
    tokens, others, block, cs_recv, remote_block, pass_on, qkv, turned, normed, q, k, v, raw,
    send_sems, recv_sems, local_sems,
):
    r, s = lax.axis_index("row"), lax.axis_index("cs")
    j, d = lax.axis_index("cp"), lax.axis_index("dp")
    n_col = 2 * n_pair
    subs, width, piece = tokens.shape[1:]
    here = subs * piece
    share = cs_recv.shape[0]
    cols = q.shape[0]
    c_first = (s * n_pair + j) ^ (r * n_pair)
    near = r == s
    sems = (send_sems, recv_sems)
    counter, local_counter = iter(range(1000)), iter(range(1000))
    sent, stored = [], []

    def send(src, dst, device):
        copy = remote(src, dst, sems, next(counter), device)
        copy.start()
        sent.append(copy)
        return copy

    def move(src, dst):
        copy = pltpu.make_async_copy(src, dst, local_sems.at[next(local_counter)])
        copy.start()
        return copy

    def store(src, dst):
        stored.append(move(src, dst))

    def columns(u):
        return pl.ds(u * piece, piece)

    own_tokens = [move(tokens_hbm.at[:, columns(u)], tokens.at[0, u]) for u in range(subs)]
    own_block = move(block_hbm, block)
    own_out = move(out_hbm, out_all.at[d, c_first])
    store(up_hbm, ups_hbm.at[c_first])
    sibling_id = {"row": 1 - r}
    dp_ids = [{"dp": d ^ k} for k in range(1, n_dp)]
    col_ids = [{"cs": s ^ (k // n_pair), "cp": j ^ (k % n_pair)} for k in range(1, n_col)]
    greet([sibling_id] + dp_ids + col_ids)

    cs_copy = send(block_hbm.at[d], cs_recv, {"cs": 1 - s})
    down_ids = [col_ids[0], col_ids[n_pair]]
    down_copies = [
        send(down_hbm.at[d], down_out.at[m, d], peer) for m, peer in enumerate(down_ids)
    ]
    out_copies = [send(out_hbm, out_all.at[d, c_first], peer) for peer in col_ids]
    other_copies = {}
    for u in range(subs):
        other_copies[0, u] = send(tokens_hbm.at[:, columns(u)], others.at[0, u], sibling_id)
    pair_copies = {}

    def send_pairs(u):
        for m in range(1, n_pair):
            pair_copies[m, u] = send(
                tokens_hbm.at[:, columns(u)], tokens.at[m, u], {"cp": j ^ m}
            )

    send_pairs(0)

    cot_copy = send(cot_hbm, cot_out, sibling_id)
    gain_own = column(half_row(gain_ref, r))
    gain_other = column(half_row(gain_ref, 1 - r))
    factor = jnp.concatenate([column(factor_ref[...])] * (cols // HEAD), 0)

    def norm(m, u):
        own, other = tokens[m, u].astype(FULL), others[m, u].astype(FULL)
        squares = jnp.sum(own * own, axis=0, keepdims=True)
        squares = squares + jnp.sum(other * other, axis=0, keepdims=True)
        inverse = lax.rsqrt(squares / D + EPSILON)
        at = pl.ds(pl.multiple_of((j ^ m) * here + u * piece, 128), piece)
        normed[:width, at] = (own * inverse * gain_own).astype(LOW)
        normed[width:, at] = (other * inverse * gain_other).astype(LOW)
        store(normed.at[:, at], normed_hbm.at[:, at])
        if m == 0:
            inverse_ref[:, columns(u)] = inverse

    def project(m, u):
        at = pl.ds(pl.multiple_of((j ^ m) * here + u * piece, 128), piece)
        for part, out in ((0, None), (1, k), (2, v)):
            value = jnp.dot(
                turned[part * cols:(part + 1) * cols, :], normed[:, at],
                preferred_element_type=FULL,
            )
            if part == 0:
                raw[:, at] = value
                q[:, at] = (value * factor).astype(LOW)
            else:
                out[:, at] = value.astype(LOW)
        for src, dst in ((q, q_hbm), (k, k_hbm), (v, v_hbm), (raw, raw_hbm)):
            store(src.at[:, at], dst.at[:, at])

    for u in range(subs):
        own_tokens[u].wait()
        other_copies[0, u].wait_recv()
        norm(0, u)
    own_block.wait()

    cs_copy.wait_recv()
    send_pairs(1)
    dp_copies = [send(cs_recv, remote_block.at[d], peer) for peer in dp_ids]
    for copy in down_copies:
        copy.wait_recv()
    down_copies = [send(down_out.at[:, d], down_out.at[:, d], peer) for peer in dp_ids]
    late_copies = [send(up_hbm, ups_hbm.at[c_first], peer) for peer in col_ids]
    remote_block[d] = cs_recv[...]
    for u in range(subs - 1):
        for m in range(1, n_pair):
            pair_copies[m, u].wait_recv()
            other_copies[m, u] = send(tokens.at[m, u], others.at[m, u], sibling_id)
    own_out.wait()
    for copy in out_copies:
        copy.wait_recv()
    late_copies += [send(out_all.at[d], out_all.at[d], peer) for peer in dp_ids]
    cross_copies = []
    for m in range(n_dp):
        owner = d ^ m
        if m:
            dp_copies[m - 1].wait_recv()
        mine, its = block[owner], remote_block[owner]
        at = pl.multiple_of(owner * share, 32)
        qkv[pl.ds(at, share)] = jnp.where(near, mine, its)
        pass_on[owner] = jnp.where(near, its, mine)
        cross_copies.append(
            send(pass_on.at[owner], qkv.at[pl.ds(width + at, share)], sibling_id)
        )
    u = subs - 1
    for m in range(1, n_pair):
        pair_copies[m, u].wait_recv()
        other_copies[m, u] = send(tokens.at[m, u], others.at[m, u], sibling_id)
    turned[:, :width] = qkv[:width].T
    for copy in cross_copies:
        copy.wait_recv()
    turned[:, width:] = qkv[width:].T
    store(qkv, qkv_hbm)

    for u in range(subs):
        project(0, u)
    for u in range(subs):
        for m in range(1, n_pair):
            other_copies[m, u].wait_recv()
            norm(m, u)
            project(m, u)

    for copy in stored:
        copy.wait()
    for copy in late_copies + down_copies + [cot_copy]:
        copy.wait_recv()
    for copy in sent:
        copy.wait_send()


def head(n_dp, n_pair, gain, factor, tokens, cotangent, block, out, up, down):
    width, here = tokens.shape
    wide = block.shape[1]
    cols = wide // 3
    share = width // n_dp
    length = n_pair * here
    n_col = 2 * n_pair
    subs = 2
    piece = here // subs
    count = subs * n_pair * 2 + 4 * n_dp + 2 * n_col + 7
    moves = 4 + subs + 5 * subs * n_pair + 4
    hbm = pl.BlockSpec(memory_space=pl.ANY)
    vmem = pl.BlockSpec(memory_space=pltpu.VMEM)
    V = pltpu.VMEM
    shape = jax.ShapeDtypeStruct((cols, length), LOW)
    return pl.pallas_call(
        functools.partial(head_kernel, n_dp, n_pair),
        out_shape=(
            shape,
            shape,
            shape,
            jax.ShapeDtypeStruct((cols, length), FULL),
            jax.ShapeDtypeStruct((2 * width, length), LOW),
            jax.ShapeDtypeStruct((2 * width, wide), LOW),
            jax.ShapeDtypeStruct((n_dp, n_col) + out.shape, LOW),
            jax.ShapeDtypeStruct((n_col,) + up.shape, LOW),
            jax.ShapeDtypeStruct((width, here), LOW),
            jax.ShapeDtypeStruct((2,) + down.shape, LOW),
            jax.ShapeDtypeStruct((1, here), FULL),
        ),
        in_specs=[vmem] * 2 + [hbm] * 6,
        out_specs=(hbm,) * 10 + (vmem,),
        scratch_shapes=[
            V((n_pair, subs, width, piece), LOW),
            V((n_pair, subs, width, piece), LOW),
            V((n_dp, share, wide), LOW),
            V((share, wide), LOW),
            V((n_dp, share, wide), LOW),
            V((n_dp, share, wide), LOW),
            V((2 * width, wide), LOW),
            V((wide, 2 * width), LOW),
            V((2 * width, length), LOW),
            V((cols, length), LOW),
            V((cols, length), LOW),
            V((cols, length), LOW),
            V((cols, length), FULL),
            pltpu.SemaphoreType.DMA((count,)),
            pltpu.SemaphoreType.DMA((count,)),
            pltpu.SemaphoreType.DMA((moves,)),
        ],
        compiler_params=pltpu.CompilerParams(
            collective_id=2, has_side_effects=True, vmem_limit_bytes=60 * 2**20
        ),
        cost_estimate=pl.CostEstimate(
            flops=4 * wide * width * length, bytes_accessed=2**25, transcendentals=0
        ),
    )(gain, factor, tokens, cotangent, block.reshape(n_dp, share, wide), out, up, down)


def middle_kernel(n_dp, n_pair, unit, gain_ref, att_hbm, tokens_hbm, cot_hbm, cot_other, out_all, *refs):
    n_col = 2 * n_pair
    up_hbms, refs = refs[:n_dp], refs[n_dp:]
    down_hbms, refs = refs[:n_col], refs[n_col:]
    result_hbm, middle_hbm, out_hbm, refs = refs[0], refs[1], refs[2], refs[3:]
    grads_hbms, refs = refs[:n_dp], refs[n_dp:]
    down_outs, refs = refs[:n_col], refs[n_col:]
    (
        gain_out, tokens, cot, out_slab, up_slab, out_w, up_w, down_w, out_t, up_t, down_t, out_half, up_half,
        down_half, att, scaled, normed, active, grad_hidden, branch, middle, grad, result, grad_att,
        grads, down_grads, square_send, square_recv, inner_send, inner_recv, inverse, narrow,
        send_sems, recv_sems, local_sems,
    ) = refs
    r, s = lax.axis_index("row"), lax.axis_index("cs")
    j, d = lax.axis_index("cp"), lax.axis_index("dp")
    width, here = tokens.shape
    pieces, _, piece = square_send.shape
    cols = att_hbm.shape[0]
    half = n_col * unit // 2
    rows_q = up_hbms[0].shape[1]
    rows_g = grads_hbms[0].shape[1]
    c_first = (s * n_pair + j) ^ (r * n_pair)
    sems = (send_sems, recv_sems)
    gain = column(half_row(gain_ref, r))
    counter, local_counter = iter(range(1000)), iter(range(1000))
    sent, stored = [], []

    def send(src, dst, device):
        copy = remote(src, dst, sems, next(counter), device)
        copy.start()
        sent.append(copy)
        return copy

    def move(src, dst):
        copy = pltpu.make_async_copy(src, dst, local_sems.at[next(local_counter)])
        copy.start()
        return copy

    def columns(u):
        return pl.ds(u * piece, piece)

    def span(u):
        return slice(u * piece, (u + 1) * piece)

    def down_rows(owner):
        return pl.ds(pl.multiple_of(owner * unit, 16), unit)

    own_rows, other_rows = pl.ds(0, width), pl.ds(width, width)
    weight_loads = [
        move(out_all.at[m], out_slab.at[:, pl.ds(m * rows_q, rows_q)]) for m in range(n_dp)
    ] + [
        move(up_hbms[m], up_slab.at[:, pl.ds(pl.multiple_of((d ^ m) * rows_q, 16), rows_q)])
        for m in range(n_dp)
    ] + [
        move(down_hbms[m], down_w.at[down_rows(c_first ^ m)])
        for m in range(n_col)
    ]
    att_loads = [
        move(
            att_hbm.at[:, pl.ds(pl.multiple_of(j * here + u * piece, 128), piece)],
            att.at[pl.ds(pl.multiple_of(j * cols, 16), cols), columns(u)],
        )
        for u in range(pieces)
    ]
    token_load = move(tokens_hbm, tokens)
    cot_loads = [move(cot_hbm, cot.at[own_rows]), move(cot_other, cot.at[other_rows])]
    sibling_id = {"row": 1 - r}
    pair_ids = [{"cp": j ^ m} for m in range(1, n_pair)]
    greet([sibling_id] + pair_ids)

    att_copies = {}
    for u in range(pieces):
        for m in range(1, n_pair):
            att_copies[u, m] = send(
                att_hbm.at[:, pl.ds(pl.multiple_of((j ^ m) * here + u * piece, 128), piece)],
                att.at[pl.ds(pl.multiple_of(j * cols, 16), cols), columns(u)],
                pair_ids[m - 1],
            )

    for copy in weight_loads:
        copy.wait()
    for m in range(n_col):
        at = slice(m * unit, (m + 1) * unit)
        out_w[at] = out_slab[m, :unit]
        up_w[at] = up_slab[m, :unit]
    cross_copies = []

    def cross(whole, part):
        cross_copies.append(send(whole.at[pl.ds(half, half)], part.at[:, other_rows], sibling_id))
        part[:, :width] = whole[:half]

    cross(up_w, up_half)
    cross(down_w, down_half)
    cross(out_w, out_half)
    out_t[...] = out_w[...].T
    narrow[...] = jnp.zeros_like(narrow)

    copies = {}

    def exchange(name, u, ref):
        copies[name, u] = send(
            ref.at[own_rows, columns(u)], ref.at[other_rows, columns(u)], sibling_id
        )

    def share_heads(u):
        att_loads[u].wait()
        for m in range(1, n_pair):
            att_copies[u, m].wait_recv()
        exchange("att", u, att)

    def first_branch(u):
        if u == 0:
            token_load.wait()
        copies["att", u].wait_recv()
        value = tokens[:, span(u)].astype(FULL) + jnp.dot(
            out_t[...], att[:, span(u)], preferred_element_type=FULL
        )
        scaled[:width, span(u)] = (value * gain).astype(LOW)
        exchange("scaled", u, scaled)
        square_send[u] = jnp.sum(value * value, axis=0, keepdims=True)
        copies["square", u] = send(square_send.at[u], square_recv.at[u], sibling_id)
        middle[:, span(u)] = value

    def hidden_units(u):
        if u == 0:
            for copy in cot_loads:
                copy.wait()
            for copy in cross_copies:
                copy.wait_recv()
            up_t[...] = up_w[...].T
            down_t[...] = down_w[...].T
        grad_active = jnp.dot(down_half[...], cot[:, span(u)], preferred_element_type=FULL)
        copies["scaled", u].wait_recv()
        copies["square", u].wait_recv()
        scale = lax.rsqrt((square_send[u] + square_recv[u]) / D + EPSILON)
        inverse[u] = scale
        hidden = scale * jnp.dot(up_half[...], scaled[:, span(u)], preferred_element_type=FULL)
        sigmoid = jax.nn.sigmoid(hidden)
        value = (grad_active * sigmoid * (1.0 + hidden * (1.0 - sigmoid))).astype(LOW)
        grad_hidden[:half, span(u)] = value
        exchange("grad_hidden", u, grad_hidden)
        active[:half, span(u)] = (hidden * sigmoid).astype(LOW)
        exchange("active", u, active)
        inner_send[u] = jnp.sum(value.astype(FULL) * hidden, axis=0, keepdims=True)
        copies["inner", u] = send(inner_send.at[u], inner_recv.at[u], sibling_id)
        normed[:, span(u)] = (middle[:, span(u)] * scale * gain).astype(LOW)

    def second_branch(u):
        copies["grad_hidden", u].wait_recv()
        copies["inner", u].wait_recv()
        scale = inverse[u]
        inner = scale * scale * ((inner_send[u] + inner_recv[u]) / D)
        back = jnp.dot(up_t[...], grad_hidden[:, span(u)], preferred_element_type=FULL)
        value = (
            cot[:width, span(u)].astype(FULL)
            + scale * (back * gain)
            - middle[:, span(u)] * inner
        )
        branch[:width, span(u)] = value.astype(LOW)
        exchange("branch", u, branch)
        grad[:, span(u)] = value
        stored.append(move(grad.at[:, columns(u)], middle_hbm.at[:, columns(u)]))
        product = back * middle[:, span(u)] * scale
        total = narrow[...]
        for v in range(piece // 128):
            total = total + product[:, v * 128:(v + 1) * 128]
        narrow[...] = total
        copies["active", u].wait_recv()
        result[:, span(u)] = middle[:, span(u)] + jnp.dot(
            down_t[...], active[:, span(u)], preferred_element_type=FULL
        )
        stored.append(move(result.at[:, columns(u)], result_hbm.at[:, columns(u)]))

    def heads_back(u):
        copies["branch", u].wait_recv()
        grad_att[:, span(u)] = jnp.dot(
            out_half[...], branch[:, span(u)], preferred_element_type=FULL
        ).astype(LOW)
        target = pl.ds(pl.multiple_of(j * here + u * piece, 128), piece)
        for m in range(n_pair):
            source = grad_att.at[
                pl.ds(pl.multiple_of((j ^ m) * cols, 16), cols), columns(u)
            ]
            if m:
                copies["out", u, m] = send(source, out_hbm.at[:, target], pair_ids[m - 1])
            else:
                stored.append(move(source, out_hbm.at[:, target]))

    stages = (share_heads, first_branch, hidden_units, second_branch, heads_back)
    turned = {}

    def product(name, first, left, right, target, at):
        if name not in turned:
            turned[name] = right[:width].T
        count = n_col // 2
        for n in range(0 if first else count, count if first else n_col):
            target[n, at:at + unit] = jnp.dot(
                left[n * unit:(n + 1) * unit], turned[name], preferred_element_type=FULL
            ).astype(LOW)

    if grads.shape[1] > 2 * unit:
        grads[...] = jnp.zeros_like(grads)
    for t in range(pieces + len(stages) - 1):
        for number in reversed(range(len(stages))):
            if 0 <= t - number < pieces:
                stages[number](t - number)
            if number == 4 and t == pieces + 2:
                product("down", True, active, cot, down_grads, 0)
        if t == pieces + 2:
            product("up", True, grad_hidden, normed, grads, unit)

    product("down", False, active, cot, down_grads, 0)
    for m in range(n_col):
        stored.append(move(down_grads.at[c_first ^ m], down_outs[m]))
    product("up", False, grad_hidden, normed, grads, unit)
    for first in (True, False):
        product("out", first, att, branch, grads, 0)
    for m in range(n_dp):
        at = pl.ds(pl.multiple_of((d ^ m) * rows_g, 16), rows_g)
        stored.append(move(grads.at[:, at], grads_hbms[m]))
    gain_out[...] = jnp.sum(narrow[...].T, axis=0, keepdims=True)

    for u in range(pieces):
        for m in range(1, n_pair):
            copies["out", u, m].wait_recv()
    for copy in stored:
        copy.wait()
    for copy in sent:
        copy.wait_send()


def middle_part(n_dp, n_pair, gain, attended, tokens, cotangent, cot_other, out_all, ups, downs):
    width, here = tokens.shape
    n_col = 2 * n_pair
    cols, length = attended.shape
    unit = downs[0].shape[0]
    half = n_col * unit // 2
    rows_q = ups[0].shape[1]
    rows_g = quarter_rows(2 * unit, n_dp)
    pieces = max(2, here // 256)
    piece = here // pieces
    count = 2 * pieces * (n_pair - 1) + 7 * pieces + 8
    moves = 3 * n_dp + 2 * n_col + 4 * pieces + 4
    hbm = pl.BlockSpec(memory_space=pl.ANY)
    vmem = pl.BlockSpec(memory_space=pltpu.VMEM)
    V = pltpu.VMEM
    S = jax.ShapeDtypeStruct
    weight = V((2 * half, width), LOW)
    weight_t = V((width, 2 * half), LOW)
    both = V((2 * width, here), LOW)
    whole = V((width, here), FULL)
    row = V((pieces, 1, piece), FULL)
    out = pl.pallas_call(
        functools.partial(middle_kernel, n_dp, n_pair, unit),
        out_shape=(
            S((width, here), FULL),
            S((width, here), FULL),
            S((cols, length), LOW),
        )
        + (S((n_col, rows_g, width), LOW),) * n_dp
        + (S((unit, width), LOW),) * n_col
        + (S((1, width), FULL),),
        in_specs=[vmem] + [hbm] * (5 + n_dp + n_col),
        out_specs=(hbm,) * (3 + n_dp + n_col) + (vmem,),
        scratch_shapes=[
            V((width, here), LOW),
            both,
            V((n_col, n_dp * rows_q, width), LOW),
            V((n_col, n_dp * rows_q, width), LOW),
            weight,
            weight,
            weight,
            weight_t,
            weight_t,
            weight_t,
            V((half, 2 * width), LOW),
            V((half, 2 * width), LOW),
            V((half, 2 * width), LOW),
            both,
            both,
            V((width, here), LOW),
            V((2 * half, here), LOW),
            V((2 * half, here), LOW),
            both,
            whole,
            whole,
            whole,
            V((width, here), LOW),
            V((n_col, n_dp * rows_g, width), LOW),
            V((n_col, unit, width), LOW),
            row,
            row,
            row,
            row,
            row,
            V((width, 128), FULL),
            pltpu.SemaphoreType.DMA((count,)),
            pltpu.SemaphoreType.DMA((count,)),
            pltpu.SemaphoreType.DMA((moves,)),
        ],
        compiler_params=pltpu.CompilerParams(
            collective_id=3, has_side_effects=True, vmem_limit_bytes=62 * 2**20
        ),
        cost_estimate=pl.CostEstimate(
            flops=18 * 2 * half * width * here, bytes_accessed=2**25, transcendentals=0
        ),
    )(gain, attended, tokens, cotangent, cot_other, out_all, *ups, *downs)
    return out[0], out[1], out[2], out[3:3 + n_dp], out[3 + n_dp:-1], out[-1]


def quarter_rows(rows, n_dp):
    return -(-rows // (16 * n_dp)) * 16


def tail_kernel(
    n_dp, n_pair, gain_ref, inverse_ref, sums_ref, qkv_hbm, dq_hbm, dk_hbm, dv_hbm, normed_hbm,
    tokens_hbm, middle_hbm, *refs,
):
    n_col = 2 * n_pair
    grads_hbms, refs = refs[:n_dp], refs[n_dp:]
    down_hbms, refs = refs[:n_col], refs[n_col:]
    (
        result_hbm, qkv_out, grads_out, down_out, sums_out,
        qkv, dproj, normed, tokens, middle, result, row_send, row_recv, own, pair_send, pair_recv,
        dp_send, dp_recv, dp_own, cross_send, cross_recv, cs_send, cs_recv, final, grads_parts,
        grads_send, grads_recv, grads_final, down_parts, down_send, down_recv, down_final,
        inner_send, inner_recv, sums_send, sums_recv, last_sums, send_sems, recv_sems, local_sems,
    ) = refs
    r, s = lax.axis_index("row"), lax.axis_index("cs")
    j, d = lax.axis_index("cp"), lax.axis_index("dp")
    width, here = tokens.shape
    cols = dq_hbm.shape[0]
    unit = down_parts.shape[1]
    share = width // n_dp
    part = share // 2
    rows_d = down_final.shape[0]
    subs = row_send.shape[1]
    piece = here // subs
    c_first = (s * n_pair + j) ^ (r * n_pair)
    near = r == s
    sems = (send_sems, recv_sems)
    gain = column(half_row(gain_ref, r))
    counter, local_counter = iter(range(1000)), iter(range(1000))
    sent, stored = [], []

    def send(src, dst, device):
        copy = remote(src, dst, sems, next(counter), device)
        copy.start()
        sent.append(copy)
        return copy

    def move(src, dst):
        copy = pltpu.make_async_copy(src, dst, local_sems.at[next(local_counter)])
        copy.start()
        return copy

    load_grads = [move(grads_hbms[k], grads_parts.at[k]) for k in range(n_dp)]
    early = [
        move(dq_hbm, dproj.at[pl.ds(0, cols)]),
        move(dk_hbm, dproj.at[pl.ds(cols, cols)]),
        move(dv_hbm, dproj.at[pl.ds(2 * cols, cols)]),
        move(normed_hbm, normed),
    ]
    load_qkv = move(qkv_hbm, qkv)
    load_down = [move(down_hbms[k], down_parts.at[k]) for k in range(n_col) if k != 1]
    late = [move(tokens_hbm, tokens), move(middle_hbm, middle)]

    sibling_id = {"row": 1 - r}
    cs_id = {"cs": 1 - s}
    dp_ids = [{"dp": d ^ k} for k in range(1, n_dp)]
    col_ids = [{"cs": s ^ (k // n_pair), "cp": j ^ (k % n_pair)} for k in range(1, n_col)]
    greet([sibling_id] + dp_ids + col_ids)


    for copy in load_grads:
        copy.wait()

    def summed(place_at):
        value = grads_parts[0, place_at].astype(FULL)
        for k in range(1, n_dp):
            value = value + grads_parts[k, place_at].astype(FULL)
        return value

    grads_copies = []
    for k in range(1, n_col):
        grads_send[k - 1] = summed(c_first ^ k).astype(LOW)
        grads_copies.append(send(grads_send.at[k - 1], grads_recv.at[k - 1], col_ids[k - 1]))
    down_copy = send(down_hbms[1], down_parts.at[1], col_ids[0])

    def quarter(half, owner):
        at = pl.ds(pl.multiple_of(half * width + owner * share, 32), share)
        return mm(normed[at, :], dproj[...], 1, 1)

    def rows_of(half, chunk, u):
        at = pl.ds(pl.multiple_of(chunk * here + u * piece, 128), piece)
        return jnp.dot(
            qkv[half * width:(half + 1) * width, :], dproj[:, at], preferred_element_type=FULL
        )

    dp_copies = {}

    def send_part(k, p):
        rows = pl.ds(p * part, part)
        dp_copies[k, p] = send(
            dp_send.at[k - 1, :, rows], dp_recv.at[k - 1, :, rows], dp_ids[k - 1]
        )

    def quarters(k):
        for half in range(2):
            dp_send[k - 1, half] = quarter(half, d ^ k).astype(LOW)
        send_part(k, 0)

    row_copies, pair_copies = {}, []
    for copy in early:
        copy.wait()
    for k in reversed(range(1, n_dp)):
        quarters(k)
    for k in reversed(range(1, n_dp)):
        send_part(k, 1)
    load_qkv.wait()
    for k in range(1, n_pair):
        for u in range(subs):
            row_send[k, u] = rows_of(1, j ^ k, u).astype(LOW)
            row_copies[k, u] = send(row_send.at[k, u], row_recv.at[k, u], sibling_id)
    for k in range(1, n_pair):
        for u in range(subs):
            value = rows_of(0, j ^ k, u)
            row_copies[k, u].wait_recv()
            pair_send[k - 1, u] = (value + row_recv[k, u].astype(FULL)).astype(LOW)
            pair_copies.append(
                send(pair_send.at[k - 1, u], pair_recv.at[k - 1, u], {"cp": j ^ k})
            )
    for copy in load_down:
        copy.wait()
    down_copy.wait_recv()
    value = down_parts[0].astype(FULL)
    for k in range(1, n_col):
        value = value + down_parts[k].astype(FULL)
    if down_send.shape[0] > unit:
        down_send[...] = jnp.zeros_like(down_send)
    down_send[:unit] = value.astype(LOW)

    def down_rows(owner):
        return pl.ds(pl.multiple_of(owner * rows_d, 16), rows_d)

    down_copies = [
        send(down_send.at[down_rows(d ^ k)], down_recv.at[k - 1], dp_ids[k - 1])
        for k in range(1, n_dp)
    ]
    for half in range(2):
        dp_own[half] = quarter(half, d)

    for u in range(subs):
        row_send[0, u] = rows_of(1, j, u).astype(LOW)
        row_copies[0, u] = send(row_send.at[0, u], row_recv.at[0, u], sibling_id)
    for u in range(subs):
        own[u] = rows_of(0, j, u)

    cs_copies = []

    def reduce_part(p):
        rows = slice(p * part, (p + 1) * part)
        for k in range(1, n_dp):
            dp_copies[k, p].wait_recv()

        def total(half):
            value = dp_own[half, rows]
            for k in range(1, n_dp):
                value = value + dp_recv[k - 1, half, rows].astype(FULL)
            return value

        cross_send[p] = total(1).astype(LOW)
        cross_copy = send(cross_send.at[p], cross_recv.at[p], sibling_id)
        kept = total(0)
        cross_copy.wait_recv()
        crossed = cross_recv[p].astype(FULL)
        cs_send[p] = jnp.where(near, crossed, kept).astype(LOW)
        cs_copies.append(send(cs_send.at[p], cs_recv.at[p], cs_id))
        dp_own[0, rows] = jnp.where(near, kept, crossed)

    reduce_part(0)

    reduce_part(1)

    value = down_send[down_rows(d)].astype(FULL)
    for k in range(1, n_dp):
        down_copies[k - 1].wait_recv()
        value = value + down_recv[k - 1].astype(FULL)
    down_final[...] = value.astype(LOW)
    out_copies = [send(down_final, down_out.at[d], peer) for peer in dp_ids]
    stored.append(move(down_final, down_out.at[d]))

    value = summed(c_first)
    for k in range(1, n_col):
        grads_copies[k - 1].wait_recv()
        value = value + grads_recv[k - 1].astype(FULL)
    grads_final[...] = value.astype(LOW)
    out_copies += [send(grads_final, grads_out.at[d], peer) for peer in dp_ids]
    stored.append(move(grads_final, grads_out.at[d]))

    for copy in late:
        copy.wait()
    for copy in pair_copies:
        copy.wait_recv()
    inverse = inverse_ref[...]
    for u in range(subs):
        row_copies[0, u].wait_recv()
        at = slice(u * piece, (u + 1) * piece)
        value = own[u] + row_recv[0, u].astype(FULL)
        for k in range(1, n_pair):
            value = value + pair_recv[k - 1, u].astype(FULL)
        own[u] = value
        inner_send[:, at] = jnp.sum(
            value * gain * tokens[:, at].astype(FULL), axis=0, keepdims=True
        )
    inner_copy = send(inner_send, inner_recv, sibling_id)

    def finish_part(p):
        cs_copies[p].wait_recv()
        rows = slice(p * part, (p + 1) * part)
        final[p] = (dp_own[0, rows] + cs_recv[p].astype(FULL)).astype(LOW)
        target = qkv_out.at[d, pl.ds(p * part, part)]
        out_copies.extend([send(final.at[p], target, peer) for peer in dp_ids])
        stored.append(move(final.at[p], target))

    finish_part(0)
    narrow = jnp.zeros((width, 128), FULL)
    for u in range(subs):
        at = slice(u * piece, (u + 1) * piece)
        wide = own[u] * tokens[:, at].astype(FULL) * inverse[:, at]
        for v in range(piece // 128):
            narrow = narrow + wide[:, v * 128:(v + 1) * 128]
    gain_part = jnp.sum(narrow.T, axis=0, keepdims=True)
    sums_send[0] = jnp.concatenate([gain_part, sums_ref[1:]], 0)
    sums_copies = {}

    def send_sums(step, peers):
        for k, peer in enumerate(peers):
            sums_copies[step, k] = send(sums_send.at[step], sums_recv.at[step, k], peer)

    def add_sums(step, members):
        value = sums_send[step]
        for k in range(members - 1):
            sums_copies[step, k].wait_recv()
            value = value + sums_recv[step, k]
        sums_send[step + 1] = value

    send_sums(0, dp_ids)
    inner_copy.wait_recv()
    inner = (inner_send[...] + inner_recv[...]) / D
    for u in range(subs):
        at = slice(u * piece, (u + 1) * piece)
        result[:, at] = (
            middle[:, at]
            + inverse[:, at] * (own[u] * gain)
            - tokens[:, at].astype(FULL)
            * (inverse[:, at] * inverse[:, at] * inverse[:, at] * inner[:, at])
        )
    stored.append(move(result, result_hbm))
    add_sums(0, n_dp)
    send_sums(1, col_ids)
    finish_part(1)

    add_sums(1, n_col)
    sums_copy = send(sums_send.at[2], last_sums, sibling_id)
    sums_copy.wait_recv()
    sums_out[0] = sums_send[2]
    sums_out[1] = last_sums[...]
    for copy in out_copies:
        copy.wait_recv()
    for copy in stored:
        copy.wait()
    for copy in sent:
        copy.wait_send()


def tail(n_dp, n_pair, gain, inverse, sums, qkv, dq, dk, dv, normed, tokens, middle, grads, downs):
    width, here = tokens.shape
    length = normed.shape[1]
    cols = dq.shape[0]
    unit = downs[0].shape[0]
    rows_d = quarter_rows(unit, n_dp)
    share = width // n_dp
    subs = 2
    piece = here // subs
    n_col = 2 * n_pair
    part = grads[0].shape[1:]
    wide = 3 * cols
    count = 2 * n_pair * subs + 8 * n_dp + 2 * n_col + 12
    moves = 13 + n_dp + n_col
    hbm = pl.BlockSpec(memory_space=pl.ANY)
    vmem = pl.BlockSpec(memory_space=pltpu.VMEM)
    V = pltpu.VMEM
    halves = V((2, share // 2, wide), LOW)
    return pl.pallas_call(
        functools.partial(tail_kernel, n_dp, n_pair),
        out_shape=(
            jax.ShapeDtypeStruct((width, here), FULL),
            jax.ShapeDtypeStruct((n_dp, share, wide), LOW),
            jax.ShapeDtypeStruct((n_dp,) + part, LOW),
            jax.ShapeDtypeStruct((n_dp, rows_d, width), LOW),
            jax.ShapeDtypeStruct((2,) + sums.shape, FULL),
        ),
        in_specs=[vmem] * 3 + [hbm] * (7 + n_dp + n_col),
        out_specs=(hbm,) * 4 + (vmem,),
        scratch_shapes=[
            V((2 * width, wide), LOW),
            V((wide, length), LOW),
            V((2 * width, length), LOW),
            V((width, here), LOW),
            V((width, here), FULL),
            V((width, here), FULL),
            V((n_pair, subs, width, piece), LOW),
            V((n_pair, subs, width, piece), LOW),
            V((subs, width, piece), FULL),
            V((n_pair - 1, subs, width, piece), LOW),
            V((n_pair - 1, subs, width, piece), LOW),
            V((n_dp - 1, 2, share, wide), LOW),
            V((n_dp - 1, 2, share, wide), LOW),
            V((2, share, wide), FULL),
            halves,
            halves,
            halves,
            halves,
            halves,
            V((n_dp, n_col) + part, LOW),
            V((n_col - 1,) + part, LOW),
            V((n_col - 1,) + part, LOW),
            V(part, LOW),
            V((n_col, unit, width), LOW),
            V((n_dp * rows_d, width), LOW),
            V((n_dp - 1, rows_d, width), LOW),
            V((rows_d, width), LOW),
            V((1, here), FULL),
            V((1, here), FULL),
            V((3,) + sums.shape, FULL),
            V((2, max(n_dp, n_col) - 1) + sums.shape, FULL),
            V(sums.shape, FULL),
            pltpu.SemaphoreType.DMA((count,)),
            pltpu.SemaphoreType.DMA((count,)),
            pltpu.SemaphoreType.DMA((moves,)),
        ],
        compiler_params=pltpu.CompilerParams(
            collective_id=1, has_side_effects=True, vmem_limit_bytes=62 * 2**20
        ),
        cost_estimate=pl.CostEstimate(
            flops=8 * wide * width * length, bytes_accessed=2**25, transcendentals=0
        ),
    )(gain, inverse, sums, qkv, dq, dk, dv, normed, tokens, middle, *grads, *downs)


def on_device(
    tokens,
    segment_ids,
    padding_mask,
    w_qkv,
    w_out,
    w_up,
    w_down,
    gain_attn,
    gain_mlp,
    scale_raw,
    cotangent,
):
    width, here = tokens.shape
    r, s = lax.axis_index("row"), lax.axis_index("cs")
    j, d = lax.axis_index("cp"), lax.axis_index("dp")
    n_pair, n_dp, n_col = lax.axis_size("cp"), lax.axis_size("dp"), lax.axis_size(COLS)
    c = s * n_pair + j
    head_cols = w_qkv.shape[0] // (3 * width)
    heads = head_cols // HEAD
    near = r == s

    ids = jnp.concatenate([segment_ids, padding_mask], 0)
    ids = jnp.where(s == r, ids, sibling(ids))
    segments, padding = ids[0], ids[1]
    length = segments.shape[0]
    firsts = segments[::BLOCK]
    starts = jnp.sum((segments[None, :] < firsts[:, None]).astype(jnp.int32), axis=1)
    filled = (jnp.sum(padding) + BLOCK - 1) // BLOCK
    blocks = jnp.arange(length // BLOCK, dtype=jnp.int32)
    lo = starts // BLOCK
    hi = jnp.minimum(blocks, filled)
    gain_one, gain_two = gain_attn[None, :], gain_mlp[None, :]
    factor = (LOG_TWO_E / math.sqrt(HEAD) * jnp.log1p(jnp.exp(scale_raw)))[None, :]

    block = w_qkv.reshape(width, 3 * head_cols)
    down = w_down.reshape(-1, width)
    unit = down.shape[0]
    part_rows = quarter_rows(unit, n_dp)

    def quarters(matrix):
        padded = jnp.pad(matrix, ((0, n_dp * part_rows - unit), (0, 0)))
        return padded.reshape(n_dp, part_rows, width)

    out = lax.dynamic_index_in_dim(quarters(w_out.reshape(-1, width)), d, 0, keepdims=False)
    up = lax.dynamic_index_in_dim(quarters(w_up.reshape(width, -1).T), d, 0, keepdims=False)
    (
        queries, key_heads, values, query_raw, normed_one, qkv, out_all, ups, cot_other, down_pair,
        inverse_one,
    ) = head(
        n_dp, n_pair, gain_one, factor, tokens, cotangent, block, out, up,
        quarters(down),
    )
    ups = gather(ups, "dp")
    downs = {0: down}
    for m, k in enumerate((1, n_pair + 1)):
        downs[k] = down_pair[m].reshape(-1, width)[:unit]
    for k in range(n_col):
        if k not in downs:
            downs[k] = lax.ppermute(down, COLS, [(i, i ^ k) for i in range(n_col)])
    downs = [downs[k] for k in range(n_col)]
    attended, logs = attention_forward(queries, key_heads, values, ids, ids, lo, hi)
    result, grad_middle, grad_attended, grads, down_grads, gain_two_part = middle_part(
        n_dp, n_pair, gain_two, attended, tokens, cotangent, cot_other, out_all, ups, downs
    )
    received = [grads[0]] + [shift(grads[k], "dp", k) for k in range(1, n_dp)]
    down_received = list(down_grads[:2]) + [
        lax.ppermute(down_grads[k], COLS, [(i, i ^ k) for i in range(n_col)])
        for k in range(2, n_col)
    ]

    dq, dk, dv, scale_part = attention_backward(
        queries, key_heads, values, attended, grad_attended, logs, query_raw, factor,
        ids, ids, lo, hi,
    )
    scale_part = (
        scale_part[:, 0] * (LOG_TWO_E / math.sqrt(HEAD)) * jax.nn.sigmoid(scale_raw)
    )
    sums = jnp.concatenate(
        [
            jnp.zeros((1, width), FULL),
            gain_two_part,
            jnp.pad(scale_part, (0, width - HEAD))[None],
            jnp.zeros((5, width), FULL),
        ]
    )
    grad_tokens, grad_qkv, final, final_down, sums = tail(
        n_dp, n_pair, gain_one, inverse_one, sums, qkv, dq, dk, dv, normed_one, tokens,
        grad_middle, received, down_received,
    )
    grad_qkv = grad_qkv.astype(FULL)
    final = final.reshape(-1, width)
    final = [final[i * unit:(i + 1) * unit].astype(FULL) for i in range(2)]
    final.append(final_down.reshape(-1, width)[:unit].astype(FULL))
    own, other = sums[0], sums[1]
    first = r == 0
    gains = jnp.concatenate(
        [jnp.where(first, own[:2], other[:2]), jnp.where(first, other[:2], own[:2])], 1
    )
    scale_total = (own[2] + other[2])[:HEAD]
    return (
        result,
        grad_tokens,
        grad_qkv.reshape(-1),
        final[0].reshape(-1),
        final[1].T.reshape(-1),
        final[2].reshape(-1),
        gains[0],
        gains[1],
        scale_total,
    )


def solution(mesh):
    n_dp, n_row, n_col = (mesh.shape[name] for name in ("dp", "row", "col"))
    split = Mesh(
        np.asarray(mesh.devices).reshape(n_dp, n_row, n_row, n_col // n_row),
        ("dp", "row", "cs", "cp"),
    )
    rows = P("row", ("dp", "cs", "cp"))
    ids = P(("dp", "row"), None)
    blocks = P(("row", "cs", "cp"))
    return jax.shard_map(
        on_device,
        mesh=split,
        in_specs=(rows, ids, ids, blocks, blocks, blocks, blocks, P(), P(), P(), rows),
        out_specs=(rows, rows, blocks, blocks, blocks, blocks, P(), P(), P()),
        check_vma=False,
    )
```

```python
import functools
import math

import jax
import jax.numpy as jnp
import numpy as np
from jax import lax
from jax.experimental import pallas as pl
from jax.experimental.pallas import tpu as pltpu
from jax.sharding import Mesh, PartitionSpec as P

D = 1280
HEAD = 80
EPSILON = 1e-06
LOG_TWO_E = 1.442695041
BLOCK = 256
LOW = jnp.bfloat16
FULL = jnp.float32
COLS = ("cs", "cp")


def mm(left, right, left_axis, right_axis):
    return lax.dot_general(
        left, right, (((left_axis,), (right_axis,)), ((), ())), preferred_element_type=FULL
    )


def shift(x, axis, k):
    n = lax.axis_size(axis)
    return lax.ppermute(x, axis, [(i, i ^ k) for i in range(n)])


def sibling(x):
    return shift(x, "row", 1)


def cut(x, index, count, axis):
    step = x.shape[axis] // count
    return lax.dynamic_slice_in_dim(x, index * step, step, axis)


def gather(x, axis):
    return [x] + [shift(x, axis, k) for k in range(1, lax.axis_size(axis))]


def diag_mask(segq, segk):
    size = segk.shape[0], segq.shape[1]
    ki = lax.broadcasted_iota(jnp.int32, size, 0)
    qi = lax.broadcasted_iota(jnp.int32, size, 1)
    return ((segk == segq) & (ki <= qi)) | (ki == qi)


def half_row(ref, which):
    size = ref.shape[1] // 2
    return jnp.where(which == 0, ref[:, :size], ref[:, size:])


def column(row):
    return jnp.broadcast_to(row, (8, row.shape[1])).T[:, :1]


def rows_of(h):
    return slice(h * HEAD, (h + 1) * HEAD)


def forward_kernel(heads, lo_ref, hi_ref, q_ref, k_ref, v_ref, segq_ref, segk_ref, o_ref, log_ref, ks, segks):
    i = pl.program_id(0)

    @pl.when(i == 0)
    def _():
        for h in range(heads):
            ks[h] = k_ref[h * HEAD:(h + 1) * HEAD, :].T
        segks[...] = column(jnp.where(segk_ref[1:] == 1, segk_ref[:1], -1).astype(FULL))

    segq = segq_ref[:1].astype(FULL)

    def visit(kb, carry, diagonal):
        at = pl.ds(pl.multiple_of(kb * BLOCK, BLOCK), BLOCK)
        segk = segks[at, :]
        mask = diag_mask(segq, segk) if diagonal else segk == segq
        scores = [
            jnp.dot(ks[h, at, :], q_ref[rows_of(h), :], preferred_element_type=FULL)
            for h in range(heads)
        ]
        peaks, totals, weights = [], [], []
        for h in range(heads):
            s = jnp.where(mask, scores[h], -1e30)
            peak = jnp.max(s, axis=0, keepdims=True)
            if not diagonal:
                peak = jnp.maximum(carry[h][0], peak)
            p = jnp.exp(s - peak)
            peaks.append(peak)
            totals.append(jnp.sum(p, axis=0, keepdims=True))
            weights.append(p.astype(LOW))
        out = []
        for h in range(heads):
            new = jnp.dot(v_ref[rows_of(h), at], weights[h], preferred_element_type=FULL)
            total = totals[h]
            if not diagonal:
                m, l, acc = carry[h]
                keep = jnp.exp(m - peaks[h])
                total = l * keep + total
                new = acc * keep + new
            out.append((peaks[h], total, new))
        return tuple(out)

    carry = visit(i, None, True)
    carry = lax.fori_loop(lo_ref[i], hi_ref[i], lambda kb, c: visit(kb, c, False), carry)
    for h in range(heads):
        m, l, acc = carry[h]
        o_ref[h * HEAD:(h + 1) * HEAD, :] = (acc / l).astype(LOW)
        log_ref[h] = m + jnp.log(l)


def attention_forward(q, k, v, segq, segk, lo, hi):
    cols, length = q.shape
    heads = cols // HEAD
    steps = length // BLOCK
    whole = pl.BlockSpec((cols, length), lambda i, *_: (0, 0))
    part = pl.BlockSpec((cols, BLOCK), lambda i, *_: (0, i))
    return pl.pallas_call(
        functools.partial(forward_kernel, heads),
        out_shape=(
            jax.ShapeDtypeStruct((cols, length), LOW),
            jax.ShapeDtypeStruct((heads, 1, length), FULL),
        ),
        grid_spec=pltpu.PrefetchScalarGridSpec(
            num_scalar_prefetch=2,
            grid=(steps,),
            in_specs=[
                part,
                whole,
                whole,
                pl.BlockSpec((2, BLOCK), lambda i, *_: (0, i)),
                pl.BlockSpec((2, length), lambda i, *_: (0, 0)),
            ],
            out_specs=(part, pl.BlockSpec((heads, 1, BLOCK), lambda i, *_: (0, 0, i))),
            scratch_shapes=[pltpu.VMEM((heads, length, HEAD), LOW), pltpu.VMEM((length, 1), FULL)],
        ),
        compiler_params=pltpu.CompilerParams(vmem_limit_bytes=62 * 2**20),
        cost_estimate=pl.CostEstimate(
            flops=8 * 2 * length * length * cols,
            bytes_accessed=4 * cols * length * 2,
            transcendentals=heads * length * length // 3,
        ),
    )(lo, hi, q, k, v, segq, segk)


def backward_kernel(
    heads, lo_ref, hi_ref, q_ref, k_ref, v_ref, o_ref, go_ref, log_ref, raw_ref, factor_ref,
    segq_ref, segk_ref, dq_ref, dk_ref, dv_ref, scale_ref, ks, vs, qs, gs, dks, dvs, dqs, segks,
):
    i = pl.program_id(0)

    @pl.when(i == 0)
    def _():
        for h in range(heads):
            ks[h] = k_ref[h * HEAD:(h + 1) * HEAD, :].T
            vs[h] = v_ref[h * HEAD:(h + 1) * HEAD, :].T
        segks[...] = column(jnp.where(segk_ref[1:] == 1, segk_ref[:1], -1).astype(FULL))
        scale_ref[...] = jnp.zeros_like(scale_ref)

    segq = segq_ref[:1].astype(FULL)
    inner = [
        jnp.sum(
            o_ref[h * HEAD:(h + 1) * HEAD, :].astype(FULL)
            * go_ref[h * HEAD:(h + 1) * HEAD, :].astype(FULL),
            axis=0,
            keepdims=True,
        )
        for h in range(heads)
    ]

    for h in range(heads):
        qs[h] = q_ref[rows_of(h), :].T
        gs[h] = go_ref[rows_of(h), :].T

    def visit(kb, diagonal):
        at = pl.ds(pl.multiple_of(kb * BLOCK, BLOCK), BLOCK)
        segk = segks[at, :]
        mask = diag_mask(segq, segk) if diagonal else segk == segq
        scores = [
            jnp.dot(ks[h, at, :], q_ref[rows_of(h), :], preferred_element_type=FULL)
            for h in range(heads)
        ]
        dps = [
            jnp.dot(vs[h, at, :], go_ref[rows_of(h), :], preferred_element_type=FULL)
            for h in range(heads)
        ]
        ps, dss = [], []
        for h in range(heads):
            p = jnp.where(mask, jnp.exp(scores[h] - log_ref[h]), 0.0)
            dss.append((p * (dps[h] - inner[h])).astype(LOW))
            ps.append(p.astype(LOW))
        for h in range(heads):
            new_v = jnp.dot(ps[h], gs[h], preferred_element_type=FULL)
            new_k = jnp.dot(dss[h], qs[h], preferred_element_type=FULL)
            new_q = jnp.dot(k_ref[rows_of(h), at], dss[h], preferred_element_type=FULL)
            if diagonal:
                dvs[h, at, :], dks[h, at, :], dqs[rows_of(h), :] = new_v, new_k, new_q
            else:
                dvs[h, at, :] += new_v
                dks[h, at, :] += new_k
                dqs[rows_of(h), :] += new_q

    visit(i, True)

    @pl.loop(lo_ref[i], hi_ref[i])
    def _(kb):
        visit(kb, False)

    factor = column(factor_ref[...])
    part = jnp.zeros((HEAD, 1), FULL)
    for h in range(heads):
        rows = slice(h * HEAD, (h + 1) * HEAD)
        dq = dqs[rows, :]
        part = part + jnp.sum(dq * raw_ref[rows, :], axis=1, keepdims=True)
        dq_ref[rows, :] = (dq * factor).astype(LOW)
    scale_ref[...] += part

    @pl.when(i == pl.num_programs(0) - 1)
    def _():
        for h in range(heads):
            dk_ref[rows_of(h), :] = dks[h].astype(LOW).T
            dv_ref[rows_of(h), :] = dvs[h].astype(LOW).T


def attention_backward(q, k, v, o, go, logs, raw, factor, segq, segk, lo, hi):
    cols, length = q.shape
    heads = cols // HEAD
    steps = length // BLOCK
    whole = pl.BlockSpec((cols, length), lambda i, *_: (0, 0))
    part = pl.BlockSpec((cols, BLOCK), lambda i, *_: (0, i))
    total = pl.BlockSpec((HEAD, 1), lambda i, *_: (0, 0))
    shape = jax.ShapeDtypeStruct((cols, length), LOW)
    return pl.pallas_call(
        functools.partial(backward_kernel, heads),
        out_shape=(shape, shape, shape, jax.ShapeDtypeStruct((HEAD, 1), FULL)),
        grid_spec=pltpu.PrefetchScalarGridSpec(
            num_scalar_prefetch=2,
            grid=(steps,),
            in_specs=[
                part,
                whole,
                whole,
                part,
                part,
                pl.BlockSpec((heads, 1, BLOCK), lambda i, *_: (0, 0, i)),
                part,
                pl.BlockSpec((1, HEAD), lambda i, *_: (0, 0)),
                pl.BlockSpec((2, BLOCK), lambda i, *_: (0, i)),
                pl.BlockSpec((2, length), lambda i, *_: (0, 0)),
            ],
            out_specs=(part, whole, whole, total),
            scratch_shapes=[
                pltpu.VMEM((heads, length, HEAD), LOW),
                pltpu.VMEM((heads, length, HEAD), LOW),
                pltpu.VMEM((heads, BLOCK, HEAD), LOW),
                pltpu.VMEM((heads, BLOCK, HEAD), LOW),
                pltpu.VMEM((heads, length, HEAD), FULL),
                pltpu.VMEM((heads, length, HEAD), FULL),
                pltpu.VMEM((cols, BLOCK), FULL),
                pltpu.VMEM((length, 1), FULL),
            ],
        ),
        compiler_params=pltpu.CompilerParams(vmem_limit_bytes=62 * 2**20),
        cost_estimate=pl.CostEstimate(
            flops=8 * 5 * length * length * cols,
            bytes_accessed=8 * cols * length * 2,
            transcendentals=heads * length * length // 3,
        ),
    )(lo, hi, q, k, v, o, go, logs, raw, factor, segq, segk)


def remote(src, dst, sems, index, device):
    return pltpu.make_async_remote_copy(
        src_ref=src,
        dst_ref=dst,
        send_sem=sems[0].at[index],
        recv_sem=sems[1].at[index],
        device_id=device,
        device_id_type=pl.DeviceIdType.MESH,
    )


def greet(peers):
    barrier = pltpu.get_barrier_semaphore()
    for peer in peers:
        pl.semaphore_signal(barrier, inc=1, device_id=peer, device_id_type=pl.DeviceIdType.MESH)
    pl.semaphore_wait(barrier, len(peers))


def head_kernel(
    n_dp, n_pair, gain_ref, factor_ref, tokens_hbm, cot_hbm, block_hbm, out_hbm, up_hbm,
    down_hbm, q_hbm, k_hbm, v_hbm, raw_hbm, normed_hbm, qkv_hbm, out_all, ups_hbm, cot_out, inverse_ref,
    tokens, others, block, cs_recv, remote_block, pass_on, qkv, turned, normed, q, k, v, raw,
    send_sems, recv_sems, local_sems,
):
    r, s = lax.axis_index("row"), lax.axis_index("cs")
    j, d = lax.axis_index("cp"), lax.axis_index("dp")
    n_col = 2 * n_pair
    subs, width, piece = tokens.shape[1:]
    here = subs * piece
    share = cs_recv.shape[0]
    cols = q.shape[0]
    c_first = (s * n_pair + j) ^ (r * n_pair)
    near = r == s
    sems = (send_sems, recv_sems)
    counter, local_counter = iter(range(1000)), iter(range(1000))
    sent, stored = [], []

    def send(src, dst, device):
        copy = remote(src, dst, sems, next(counter), device)
        copy.start()
        sent.append(copy)
        return copy

    def move(src, dst):
        copy = pltpu.make_async_copy(src, dst, local_sems.at[next(local_counter)])
        copy.start()
        return copy

    def store(src, dst):
        stored.append(move(src, dst))

    def columns(u):
        return pl.ds(u * piece, piece)

    own_tokens = [move(tokens_hbm.at[:, columns(u)], tokens.at[0, u]) for u in range(subs)]
    own_block = move(block_hbm, block)
    own_out = move(out_hbm, out_all.at[d, c_first])
    store(up_hbm, ups_hbm.at[c_first])
    sibling_id = {"row": 1 - r}
    dp_ids = [{"dp": d ^ k} for k in range(1, n_dp)]
    col_ids = [{"cs": s ^ (k // n_pair), "cp": j ^ (k % n_pair)} for k in range(1, n_col)]
    greet([sibling_id] + dp_ids + col_ids)

    cs_copy = send(block_hbm.at[d], cs_recv, {"cs": 1 - s})
    down_ids = [col_ids[0], col_ids[n_pair]]
    down_copies = [
        send(down_hbm.at[d], ups_hbm.at[n_col + m], peer) for m, peer in enumerate(down_ids)
    ]
    out_copies = [send(out_hbm, out_all.at[d, c_first], peer) for peer in col_ids]
    other_copies = {}
    for u in range(subs):
        other_copies[0, u] = send(tokens_hbm.at[:, columns(u)], others.at[0, u], sibling_id)
    pair_copies = {}

    def send_pairs(u):
        for m in range(1, n_pair):
            pair_copies[m, u] = send(
                tokens_hbm.at[:, columns(u)], tokens.at[m, u], {"cp": j ^ m}
            )

    send_pairs(0)

    cot_copy = send(cot_hbm, cot_out, sibling_id)
    gain_own = column(half_row(gain_ref, r))
    gain_other = column(half_row(gain_ref, 1 - r))
    factor = jnp.concatenate([column(factor_ref[...])] * (cols // HEAD), 0)

    def norm(m, u):
        own, other = tokens[m, u].astype(FULL), others[m, u].astype(FULL)
        squares = jnp.sum(own * own, axis=0, keepdims=True)
        squares = squares + jnp.sum(other * other, axis=0, keepdims=True)
        inverse = lax.rsqrt(squares / D + EPSILON)
        at = pl.ds(pl.multiple_of((j ^ m) * here + u * piece, 128), piece)
        normed[:width, at] = (own * inverse * gain_own).astype(LOW)
        normed[width:, at] = (other * inverse * gain_other).astype(LOW)
        store(normed.at[:, at], normed_hbm.at[:, at])
        if m == 0:
            inverse_ref[:, columns(u)] = inverse

    def project(m, u):
        at = pl.ds(pl.multiple_of((j ^ m) * here + u * piece, 128), piece)
        for part, out in ((0, None), (1, k), (2, v)):
            value = jnp.dot(
                turned[part * cols:(part + 1) * cols, :], normed[:, at],
                preferred_element_type=FULL,
            )
            if part == 0:
                raw[:, at] = value
                q[:, at] = (value * factor).astype(LOW)
            else:
                out[:, at] = value.astype(LOW)
        for src, dst in ((q, q_hbm), (k, k_hbm), (v, v_hbm), (raw, raw_hbm)):
            store(src.at[:, at], dst.at[:, at])

    for u in range(subs):
        own_tokens[u].wait()
        other_copies[0, u].wait_recv()
        norm(0, u)
    own_block.wait()

    cs_copy.wait_recv()
    send_pairs(1)
    dp_copies = [send(cs_recv, remote_block.at[d], peer) for peer in dp_ids]
    own_out.wait()
    for copy in out_copies:
        copy.wait_recv()
    late_copies = [send(out_all.at[d], out_all.at[d], peer) for peer in dp_ids]
    remote_block[d] = cs_recv[...]
    for u in range(subs - 1):
        for m in range(1, n_pair):
            pair_copies[m, u].wait_recv()
            other_copies[m, u] = send(tokens.at[m, u], others.at[m, u], sibling_id)
    cross_copies = []
    for m in range(n_dp):
        owner = d ^ m
        if m:
            dp_copies[m - 1].wait_recv()
        mine, its = block[owner], remote_block[owner]
        at = pl.multiple_of(owner * share, 32)
        qkv[pl.ds(at, share)] = jnp.where(near, mine, its)
        pass_on[owner] = jnp.where(near, its, mine)
        cross_copies.append(
            send(pass_on.at[owner], qkv.at[pl.ds(width + at, share)], sibling_id)
        )
    u = subs - 1
    for m in range(1, n_pair):
        pair_copies[m, u].wait_recv()
        other_copies[m, u] = send(tokens.at[m, u], others.at[m, u], sibling_id)
    late_copies += [send(up_hbm, ups_hbm.at[c_first], peer) for peer in col_ids]
    turned[:, :width] = qkv[:width].T
    for copy in cross_copies:
        copy.wait_recv()
    turned[:, width:] = qkv[width:].T
    store(qkv, qkv_hbm)

    for u in range(subs):
        project(0, u)
    for u in range(subs):
        for m in range(1, n_pair):
            other_copies[m, u].wait_recv()
            norm(m, u)
            project(m, u)

    for copy in stored:
        copy.wait()
    for copy in late_copies + down_copies + [cot_copy]:
        copy.wait_recv()
    for copy in sent:
        copy.wait_send()


def head(n_dp, n_pair, gain, factor, tokens, cotangent, block, out, up, down):
    width, here = tokens.shape
    wide = block.shape[1]
    cols = wide // 3
    share = width // n_dp
    length = n_pair * here
    n_col = 2 * n_pair
    subs = 2
    piece = here // subs
    count = subs * n_pair * 2 + 4 * n_dp + 2 * n_col + 7
    moves = 4 + subs + 5 * subs * n_pair + 4
    hbm = pl.BlockSpec(memory_space=pl.ANY)
    vmem = pl.BlockSpec(memory_space=pltpu.VMEM)
    V = pltpu.VMEM
    shape = jax.ShapeDtypeStruct((cols, length), LOW)
    return pl.pallas_call(
        functools.partial(head_kernel, n_dp, n_pair),
        out_shape=(
            shape,
            shape,
            shape,
            jax.ShapeDtypeStruct((cols, length), FULL),
            jax.ShapeDtypeStruct((2 * width, length), LOW),
            jax.ShapeDtypeStruct((2 * width, wide), LOW),
            jax.ShapeDtypeStruct((n_dp, n_col) + out.shape, LOW),
            jax.ShapeDtypeStruct((n_col + 2,) + up.shape, LOW),
            jax.ShapeDtypeStruct((width, here), LOW),
            jax.ShapeDtypeStruct((1, here), FULL),
        ),
        in_specs=[vmem] * 2 + [hbm] * 6,
        out_specs=(hbm,) * 9 + (vmem,),
        scratch_shapes=[
            V((n_pair, subs, width, piece), LOW),
            V((n_pair, subs, width, piece), LOW),
            V((n_dp, share, wide), LOW),
            V((share, wide), LOW),
            V((n_dp, share, wide), LOW),
            V((n_dp, share, wide), LOW),
            V((2 * width, wide), LOW),
            V((wide, 2 * width), LOW),
            V((2 * width, length), LOW),
            V((cols, length), LOW),
            V((cols, length), LOW),
            V((cols, length), LOW),
            V((cols, length), FULL),
            pltpu.SemaphoreType.DMA((count,)),
            pltpu.SemaphoreType.DMA((count,)),
            pltpu.SemaphoreType.DMA((moves,)),
        ],
        compiler_params=pltpu.CompilerParams(
            collective_id=2, has_side_effects=True, vmem_limit_bytes=60 * 2**20
        ),
        cost_estimate=pl.CostEstimate(
            flops=4 * wide * width * length, bytes_accessed=2**25, transcendentals=0
        ),
    )(gain, factor, tokens, cotangent, block.reshape(n_dp, share, wide), out, up, down)


def middle_kernel(n_dp, n_pair, unit, gain_ref, att_hbm, tokens_hbm, cot_hbm, cot_other, out_all, *refs):
    n_col = 2 * n_pair
    up_hbms, refs = refs[:n_dp], refs[n_dp:]
    down_hbms, refs = refs[:n_col - 2], refs[n_col - 2:]
    result_hbm, middle_hbm, out_hbm, refs = refs[0], refs[1], refs[2], refs[3:]
    grads_hbms, refs = refs[:n_dp], refs[n_dp:]
    down_outs, refs = refs[:n_col], refs[n_col:]
    (
        gain_out, tokens, cot, out_slab, up_slab, down_slab, out_w, up_w, down_w, out_t, up_t, down_t, out_half, up_half,
        down_half, att, scaled, normed, active, grad_hidden, branch, middle, grad, result, grad_att,
        grads, down_grads, square_send, square_recv, inner_send, inner_recv, inverse, narrow,
        send_sems, recv_sems, local_sems,
    ) = refs
    r, s = lax.axis_index("row"), lax.axis_index("cs")
    j, d = lax.axis_index("cp"), lax.axis_index("dp")
    width, here = tokens.shape
    pieces, _, piece = square_send.shape
    cols = att_hbm.shape[0]
    half = n_col * unit // 2
    rows_q = up_hbms[0].shape[1]
    rows_g = grads_hbms[0].shape[1]
    c_first = (s * n_pair + j) ^ (r * n_pair)
    sems = (send_sems, recv_sems)
    gain = column(half_row(gain_ref, r))
    counter, local_counter = iter(range(1000)), iter(range(1000))
    sent, stored = [], []

    def send(src, dst, device):
        copy = remote(src, dst, sems, next(counter), device)
        copy.start()
        sent.append(copy)
        return copy

    def move(src, dst):
        copy = pltpu.make_async_copy(src, dst, local_sems.at[next(local_counter)])
        copy.start()
        return copy

    def columns(u):
        return pl.ds(u * piece, piece)

    def span(u):
        return slice(u * piece, (u + 1) * piece)

    def down_rows(owner):
        return pl.ds(pl.multiple_of(owner * unit, 16), unit)

    def quarter_of(owner):
        return pl.ds(pl.multiple_of(owner * rows_q, 16), rows_q)

    quartered = (1, n_pair + 1)
    own_rows, other_rows = pl.ds(0, width), pl.ds(width, width)
    weight_loads = [
        move(out_all.at[m], out_slab.at[:, pl.ds(m * rows_q, rows_q)]) for m in range(n_dp)
    ] + [
        move(up_hbms[m].at[pl.ds(first, size)], target.at[:, quarter_of(d ^ m)])
        for m in range(n_dp)
        for first, size, target in ((0, n_col, up_slab), (n_col, 2, down_slab))
    ] + [
        move(ref, down_w.at[down_rows(c_first ^ m)])
        for m, ref in zip([m for m in range(n_col) if m not in quartered], down_hbms)
    ]
    att_loads = [
        move(
            att_hbm.at[:, pl.ds(pl.multiple_of(j * here + u * piece, 128), piece)],
            att.at[pl.ds(pl.multiple_of(j * cols, 16), cols), columns(u)],
        )
        for u in range(pieces)
    ]
    token_load = move(tokens_hbm, tokens)
    cot_loads = [move(cot_hbm, cot.at[own_rows]), move(cot_other, cot.at[other_rows])]
    sibling_id = {"row": 1 - r}
    pair_ids = [{"cp": j ^ m} for m in range(1, n_pair)]
    greet([sibling_id] + pair_ids)

    att_copies = {}
    for u in range(pieces):
        for m in range(1, n_pair):
            att_copies[u, m] = send(
                att_hbm.at[:, pl.ds(pl.multiple_of((j ^ m) * here + u * piece, 128), piece)],
                att.at[pl.ds(pl.multiple_of(j * cols, 16), cols), columns(u)],
                pair_ids[m - 1],
            )

    for copy in weight_loads:
        copy.wait()
    for m in range(n_col):
        at = slice(m * unit, (m + 1) * unit)
        out_w[at] = out_slab[m, :unit]
        up_w[at] = up_slab[m, :unit]
    for m, k in enumerate(quartered):
        down_w[down_rows(c_first ^ k)] = down_slab[m, :unit]
    cross_copies = []

    def cross(whole, part):
        cross_copies.append(send(whole.at[pl.ds(half, half)], part.at[:, other_rows], sibling_id))
        part[:, :width] = whole[:half]

    cross(up_w, up_half)
    cross(down_w, down_half)
    cross(out_w, out_half)
    out_t[...] = out_w[...].T
    narrow[...] = jnp.zeros_like(narrow)

    copies = {}

    def exchange(name, u, ref):
        copies[name, u] = send(
            ref.at[own_rows, columns(u)], ref.at[other_rows, columns(u)], sibling_id
        )

    def share_heads(u):
        att_loads[u].wait()
        for m in range(1, n_pair):
            att_copies[u, m].wait_recv()
        exchange("att", u, att)

    def first_branch(u):
        if u == 0:
            token_load.wait()
        copies["att", u].wait_recv()
        value = tokens[:, span(u)].astype(FULL) + jnp.dot(
            out_t[...], att[:, span(u)], preferred_element_type=FULL
        )
        scaled[:width, span(u)] = (value * gain).astype(LOW)
        exchange("scaled", u, scaled)
        square_send[u] = jnp.sum(value * value, axis=0, keepdims=True)
        copies["square", u] = send(square_send.at[u], square_recv.at[u], sibling_id)
        middle[:, span(u)] = value

    def hidden_units(u):
        if u == 0:
            for copy in cot_loads:
                copy.wait()
            for copy in cross_copies:
                copy.wait_recv()
            up_t[...] = up_w[...].T
            down_t[...] = down_w[...].T
        grad_active = jnp.dot(down_half[...], cot[:, span(u)], preferred_element_type=FULL)
        copies["scaled", u].wait_recv()
        copies["square", u].wait_recv()
        scale = lax.rsqrt((square_send[u] + square_recv[u]) / D + EPSILON)
        inverse[u] = scale
        hidden = scale * jnp.dot(up_half[...], scaled[:, span(u)], preferred_element_type=FULL)
        sigmoid = jax.nn.sigmoid(hidden)
        value = (grad_active * sigmoid * (1.0 + hidden * (1.0 - sigmoid))).astype(LOW)
        grad_hidden[:half, span(u)] = value
        exchange("grad_hidden", u, grad_hidden)
        active[:half, span(u)] = (hidden * sigmoid).astype(LOW)
        exchange("active", u, active)
        inner_send[u] = jnp.sum(value.astype(FULL) * hidden, axis=0, keepdims=True)
        copies["inner", u] = send(inner_send.at[u], inner_recv.at[u], sibling_id)
        normed[:, span(u)] = (middle[:, span(u)] * scale * gain).astype(LOW)

    def second_branch(u):
        copies["grad_hidden", u].wait_recv()
        copies["inner", u].wait_recv()
        scale = inverse[u]
        inner = scale * scale * ((inner_send[u] + inner_recv[u]) / D)
        back = jnp.dot(up_t[...], grad_hidden[:, span(u)], preferred_element_type=FULL)
        value = (
            cot[:width, span(u)].astype(FULL)
            + scale * (back * gain)
            - middle[:, span(u)] * inner
        )
        branch[:width, span(u)] = value.astype(LOW)
        exchange("branch", u, branch)
        grad[:, span(u)] = value
        stored.append(move(grad.at[:, columns(u)], middle_hbm.at[:, columns(u)]))
        product = back * middle[:, span(u)] * scale
        total = narrow[...]
        for v in range(piece // 128):
            total = total + product[:, v * 128:(v + 1) * 128]
        narrow[...] = total
        copies["active", u].wait_recv()
        result[:, span(u)] = middle[:, span(u)] + jnp.dot(
            down_t[...], active[:, span(u)], preferred_element_type=FULL
        )
        stored.append(move(result.at[:, columns(u)], result_hbm.at[:, columns(u)]))

    def heads_back(u):
        copies["branch", u].wait_recv()
        grad_att[:, span(u)] = jnp.dot(
            out_half[...], branch[:, span(u)], preferred_element_type=FULL
        ).astype(LOW)
        target = pl.ds(pl.multiple_of(j * here + u * piece, 128), piece)
        for m in range(n_pair):
            source = grad_att.at[
                pl.ds(pl.multiple_of((j ^ m) * cols, 16), cols), columns(u)
            ]
            if m:
                copies["out", u, m] = send(source, out_hbm.at[:, target], pair_ids[m - 1])
            else:
                stored.append(move(source, out_hbm.at[:, target]))

    stages = (share_heads, first_branch, hidden_units, second_branch, heads_back)
    turned = {}

    def product(name, first, left, right, target, at):
        if name not in turned:
            turned[name] = right[:width].T
        count = n_col // 2
        for n in range(0 if first else count, count if first else n_col):
            target[n, at:at + unit] = jnp.dot(
                left[n * unit:(n + 1) * unit], turned[name], preferred_element_type=FULL
            ).astype(LOW)

    if grads.shape[1] > 2 * unit:
        grads[...] = jnp.zeros_like(grads)
    for t in range(pieces + len(stages) - 1):
        for number in reversed(range(len(stages))):
            if 0 <= t - number < pieces:
                stages[number](t - number)
            if number == 4 and t == pieces + 2:
                product("down", True, active, cot, down_grads, 0)
        if t == pieces + 2:
            product("up", True, grad_hidden, normed, grads, unit)

    product("down", False, active, cot, down_grads, 0)
    for m in range(n_col):
        stored.append(move(down_grads.at[c_first ^ m], down_outs[m]))
    product("up", False, grad_hidden, normed, grads, unit)
    for first in (True, False):
        product("out", first, att, branch, grads, 0)
    for m in range(n_dp):
        at = pl.ds(pl.multiple_of((d ^ m) * rows_g, 16), rows_g)
        stored.append(move(grads.at[:, at], grads_hbms[m]))
    gain_out[...] = jnp.sum(narrow[...].T, axis=0, keepdims=True)

    for u in range(pieces):
        for m in range(1, n_pair):
            copies["out", u, m].wait_recv()
    for copy in stored:
        copy.wait()
    for copy in sent:
        copy.wait_send()


def middle_part(n_dp, n_pair, gain, attended, tokens, cotangent, cot_other, out_all, ups, downs):
    width, here = tokens.shape
    n_col = 2 * n_pair
    cols, length = attended.shape
    unit = downs[0].shape[0]
    half = n_col * unit // 2
    rows_q = ups[0].shape[1]
    rows_g = quarter_rows(2 * unit, n_dp)
    pieces = max(2, here // 256)
    piece = here // pieces
    count = 2 * pieces * (n_pair - 1) + 7 * pieces + 8
    moves = 4 * n_dp + 2 * n_col + 4 * pieces + 4
    hbm = pl.BlockSpec(memory_space=pl.ANY)
    vmem = pl.BlockSpec(memory_space=pltpu.VMEM)
    V = pltpu.VMEM
    S = jax.ShapeDtypeStruct
    weight = V((2 * half, width), LOW)
    weight_t = V((width, 2 * half), LOW)
    both = V((2 * width, here), LOW)
    whole = V((width, here), FULL)
    row = V((pieces, 1, piece), FULL)
    out = pl.pallas_call(
        functools.partial(middle_kernel, n_dp, n_pair, unit),
        out_shape=(
            S((width, here), FULL),
            S((width, here), FULL),
            S((cols, length), LOW),
        )
        + (S((n_col, rows_g, width), LOW),) * n_dp
        + (S((unit, width), LOW),) * n_col
        + (S((1, width), FULL),),
        in_specs=[vmem] + [hbm] * (3 + n_dp + n_col),
        out_specs=(hbm,) * (3 + n_dp + n_col) + (vmem,),
        scratch_shapes=[
            V((width, here), LOW),
            both,
            V((n_col, n_dp * rows_q, width), LOW),
            V((n_col, n_dp * rows_q, width), LOW),
            V((2, n_dp * rows_q, width), LOW),
            weight,
            weight,
            weight,
            weight_t,
            weight_t,
            weight_t,
            V((half, 2 * width), LOW),
            V((half, 2 * width), LOW),
            V((half, 2 * width), LOW),
            both,
            both,
            V((width, here), LOW),
            V((2 * half, here), LOW),
            V((2 * half, here), LOW),
            both,
            whole,
            whole,
            whole,
            V((width, here), LOW),
            V((n_col, n_dp * rows_g, width), LOW),
            V((n_col, unit, width), LOW),
            row,
            row,
            row,
            row,
            row,
            V((width, 128), FULL),
            pltpu.SemaphoreType.DMA((count,)),
            pltpu.SemaphoreType.DMA((count,)),
            pltpu.SemaphoreType.DMA((moves,)),
        ],
        compiler_params=pltpu.CompilerParams(
            collective_id=3, has_side_effects=True, vmem_limit_bytes=62 * 2**20
        ),
        cost_estimate=pl.CostEstimate(
            flops=18 * 2 * half * width * here, bytes_accessed=2**25, transcendentals=0
        ),
    )(gain, attended, tokens, cotangent, cot_other, out_all, *ups, *downs)
    return out[0], out[1], out[2], out[3:3 + n_dp], out[3 + n_dp:-1], out[-1]


def quarter_rows(rows, n_dp):
    return -(-rows // (16 * n_dp)) * 16


def tail_kernel(
    n_dp, n_pair, gain_ref, inverse_ref, sums_ref, qkv_hbm, dq_hbm, dk_hbm, dv_hbm, normed_hbm,
    tokens_hbm, middle_hbm, *refs,
):
    n_col = 2 * n_pair
    grads_hbms, refs = refs[:n_dp], refs[n_dp:]
    down_hbms, refs = refs[:n_col], refs[n_col:]
    (
        result_hbm, qkv_out, grads_out, down_out, sums_out,
        qkv, dproj, normed, tokens, middle, result, row_send, row_recv, own, pair_send, pair_recv,
        dp_send, dp_recv, dp_own, cross_send, cross_recv, cs_send, cs_recv, final, grads_parts,
        grads_send, grads_recv, grads_final, down_parts, down_send, down_recv, down_final,
        inner_send, inner_recv, sums_send, sums_recv, last_sums, send_sems, recv_sems, local_sems,
    ) = refs
    r, s = lax.axis_index("row"), lax.axis_index("cs")
    j, d = lax.axis_index("cp"), lax.axis_index("dp")
    width, here = tokens.shape
    cols = dq_hbm.shape[0]
    unit = down_parts.shape[1]
    share = width // n_dp
    part = share // 2
    rows_d = down_final.shape[0]
    subs = row_send.shape[1]
    piece = here // subs
    c_first = (s * n_pair + j) ^ (r * n_pair)
    near = r == s
    sems = (send_sems, recv_sems)
    gain = column(half_row(gain_ref, r))
    counter, local_counter = iter(range(1000)), iter(range(1000))
    sent, stored = [], []

    def send(src, dst, device):
        copy = remote(src, dst, sems, next(counter), device)
        copy.start()
        sent.append(copy)
        return copy

    def move(src, dst):
        copy = pltpu.make_async_copy(src, dst, local_sems.at[next(local_counter)])
        copy.start()
        return copy

    load_grads = [move(grads_hbms[k], grads_parts.at[k]) for k in range(n_dp)]
    early = [
        move(dq_hbm, dproj.at[pl.ds(0, cols)]),
        move(dk_hbm, dproj.at[pl.ds(cols, cols)]),
        move(dv_hbm, dproj.at[pl.ds(2 * cols, cols)]),
        move(normed_hbm, normed),
    ]
    load_qkv = move(qkv_hbm, qkv)
    load_down = [move(down_hbms[k], down_parts.at[k]) for k in range(n_col) if k != 1]
    late = [move(tokens_hbm, tokens), move(middle_hbm, middle)]

    sibling_id = {"row": 1 - r}
    cs_id = {"cs": 1 - s}
    dp_ids = [{"dp": d ^ k} for k in range(1, n_dp)]
    col_ids = [{"cs": s ^ (k // n_pair), "cp": j ^ (k % n_pair)} for k in range(1, n_col)]
    greet([sibling_id] + dp_ids + col_ids)


    for copy in load_grads:
        copy.wait()

    def summed(place_at):
        value = grads_parts[0, place_at].astype(FULL)
        for k in range(1, n_dp):
            value = value + grads_parts[k, place_at].astype(FULL)
        return value

    grads_copies = []
    for k in range(1, n_col):
        grads_send[k - 1] = summed(c_first ^ k).astype(LOW)
        grads_copies.append(send(grads_send.at[k - 1], grads_recv.at[k - 1], col_ids[k - 1]))
    down_copy = send(down_hbms[1], down_parts.at[1], col_ids[0])

    def quarter(half, owner):
        at = pl.ds(pl.multiple_of(half * width + owner * share, 32), share)
        return mm(normed[at, :], dproj[...], 1, 1)

    def rows_of(half, chunk, u):
        at = pl.ds(pl.multiple_of(chunk * here + u * piece, 128), piece)
        return jnp.dot(
            qkv[half * width:(half + 1) * width, :], dproj[:, at], preferred_element_type=FULL
        )

    dp_copies = {}

    def send_part(k, p):
        rows = pl.ds(p * part, part)
        dp_copies[k, p] = send(
            dp_send.at[k - 1, :, rows], dp_recv.at[k - 1, :, rows], dp_ids[k - 1]
        )

    def quarters(k):
        for half in range(2):
            dp_send[k - 1, half] = quarter(half, d ^ k).astype(LOW)
        send_part(k, 0)

    row_copies, pair_copies = {}, []
    for copy in early:
        copy.wait()
    for k in reversed(range(1, n_dp)):
        quarters(k)
    for k in reversed(range(1, n_dp)):
        send_part(k, 1)
    load_qkv.wait()
    for k in range(1, n_pair):
        for u in range(subs):
            row_send[k, u] = rows_of(1, j ^ k, u).astype(LOW)
            row_copies[k, u] = send(row_send.at[k, u], row_recv.at[k, u], sibling_id)
    for k in range(1, n_pair):
        for u in range(subs):
            value = rows_of(0, j ^ k, u)
            row_copies[k, u].wait_recv()
            pair_send[k - 1, u] = (value + row_recv[k, u].astype(FULL)).astype(LOW)
            pair_copies.append(
                send(pair_send.at[k - 1, u], pair_recv.at[k - 1, u], {"cp": j ^ k})
            )
    for copy in load_down:
        copy.wait()
    down_copy.wait_recv()
    value = down_parts[0].astype(FULL)
    for k in range(1, n_col):
        value = value + down_parts[k].astype(FULL)
    if down_send.shape[0] > unit:
        down_send[...] = jnp.zeros_like(down_send)
    down_send[:unit] = value.astype(LOW)

    def down_rows(owner):
        return pl.ds(pl.multiple_of(owner * rows_d, 16), rows_d)

    down_copies = [
        send(down_send.at[down_rows(d ^ k)], down_recv.at[k - 1], dp_ids[k - 1])
        for k in range(1, n_dp)
    ]
    for half in range(2):
        dp_own[half] = quarter(half, d)

    for u in range(subs):
        row_send[0, u] = rows_of(1, j, u).astype(LOW)
        row_copies[0, u] = send(row_send.at[0, u], row_recv.at[0, u], sibling_id)
    for u in range(subs):
        own[u] = rows_of(0, j, u)

    cs_copies = []

    def reduce_part(p):
        rows = slice(p * part, (p + 1) * part)
        for k in range(1, n_dp):
            dp_copies[k, p].wait_recv()

        def total(half):
            value = dp_own[half, rows]
            for k in range(1, n_dp):
                value = value + dp_recv[k - 1, half, rows].astype(FULL)
            return value

        cross_send[p] = total(1).astype(LOW)
        cross_copy = send(cross_send.at[p], cross_recv.at[p], sibling_id)
        kept = total(0)
        cross_copy.wait_recv()
        crossed = cross_recv[p].astype(FULL)
        cs_send[p] = jnp.where(near, crossed, kept).astype(LOW)
        cs_copies.append(send(cs_send.at[p], cs_recv.at[p], cs_id))
        dp_own[0, rows] = jnp.where(near, kept, crossed)

    reduce_part(0)

    reduce_part(1)

    value = down_send[down_rows(d)].astype(FULL)
    for k in range(1, n_dp):
        down_copies[k - 1].wait_recv()
        value = value + down_recv[k - 1].astype(FULL)
    down_final[...] = value.astype(LOW)
    out_copies = [send(down_final, down_out.at[d], peer) for peer in dp_ids]
    stored.append(move(down_final, down_out.at[d]))

    value = summed(c_first)
    for k in range(1, n_col):
        grads_copies[k - 1].wait_recv()
        value = value + grads_recv[k - 1].astype(FULL)
    grads_final[...] = value.astype(LOW)
    out_copies += [send(grads_final, grads_out.at[d], peer) for peer in dp_ids]
    stored.append(move(grads_final, grads_out.at[d]))

    for copy in late:
        copy.wait()
    for copy in pair_copies:
        copy.wait_recv()
    inverse = inverse_ref[...]
    for u in range(subs):
        row_copies[0, u].wait_recv()
        at = slice(u * piece, (u + 1) * piece)
        value = own[u] + row_recv[0, u].astype(FULL)
        for k in range(1, n_pair):
            value = value + pair_recv[k - 1, u].astype(FULL)
        own[u] = value
        inner_send[:, at] = jnp.sum(
            value * gain * tokens[:, at].astype(FULL), axis=0, keepdims=True
        )
    inner_copy = send(inner_send, inner_recv, sibling_id)

    def finish_part(p):
        cs_copies[p].wait_recv()
        rows = slice(p * part, (p + 1) * part)
        final[p] = (dp_own[0, rows] + cs_recv[p].astype(FULL)).astype(LOW)
        target = qkv_out.at[d, pl.ds(p * part, part)]
        out_copies.extend([send(final.at[p], target, peer) for peer in dp_ids])
        stored.append(move(final.at[p], target))

    finish_part(0)
    narrow = jnp.zeros((width, 128), FULL)
    for u in range(subs):
        at = slice(u * piece, (u + 1) * piece)
        wide = own[u] * tokens[:, at].astype(FULL) * inverse[:, at]
        for v in range(piece // 128):
            narrow = narrow + wide[:, v * 128:(v + 1) * 128]
    gain_part = jnp.sum(narrow.T, axis=0, keepdims=True)
    sums_send[0] = jnp.concatenate([gain_part, sums_ref[1:]], 0)
    sums_copies = {}

    def send_sums(step, peers):
        for k, peer in enumerate(peers):
            sums_copies[step, k] = send(sums_send.at[step], sums_recv.at[step, k], peer)

    def add_sums(step, members):
        value = sums_send[step]
        for k in range(members - 1):
            sums_copies[step, k].wait_recv()
            value = value + sums_recv[step, k]
        sums_send[step + 1] = value

    send_sums(0, dp_ids)
    inner_copy.wait_recv()
    inner = (inner_send[...] + inner_recv[...]) / D
    for u in range(subs):
        at = slice(u * piece, (u + 1) * piece)
        result[:, at] = (
            middle[:, at]
            + inverse[:, at] * (own[u] * gain)
            - tokens[:, at].astype(FULL)
            * (inverse[:, at] * inverse[:, at] * inverse[:, at] * inner[:, at])
        )
    stored.append(move(result, result_hbm))
    add_sums(0, n_dp)
    send_sums(1, col_ids)
    finish_part(1)

    add_sums(1, n_col)
    sums_copy = send(sums_send.at[2], last_sums, sibling_id)
    sums_copy.wait_recv()
    sums_out[0] = sums_send[2]
    sums_out[1] = last_sums[...]
    for copy in out_copies:
        copy.wait_recv()
    for copy in stored:
        copy.wait()
    for copy in sent:
        copy.wait_send()


def tail(n_dp, n_pair, gain, inverse, sums, qkv, dq, dk, dv, normed, tokens, middle, grads, downs):
    width, here = tokens.shape
    length = normed.shape[1]
    cols = dq.shape[0]
    unit = downs[0].shape[0]
    rows_d = quarter_rows(unit, n_dp)
    share = width // n_dp
    subs = 2
    piece = here // subs
    n_col = 2 * n_pair
    part = grads[0].shape[1:]
    wide = 3 * cols
    count = 2 * n_pair * subs + 8 * n_dp + 2 * n_col + 12
    moves = 13 + n_dp + n_col
    hbm = pl.BlockSpec(memory_space=pl.ANY)
    vmem = pl.BlockSpec(memory_space=pltpu.VMEM)
    V = pltpu.VMEM
    halves = V((2, share // 2, wide), LOW)
    return pl.pallas_call(
        functools.partial(tail_kernel, n_dp, n_pair),
        out_shape=(
            jax.ShapeDtypeStruct((width, here), FULL),
            jax.ShapeDtypeStruct((n_dp, share, wide), LOW),
            jax.ShapeDtypeStruct((n_dp,) + part, LOW),
            jax.ShapeDtypeStruct((n_dp, rows_d, width), LOW),
            jax.ShapeDtypeStruct((2,) + sums.shape, FULL),
        ),
        in_specs=[vmem] * 3 + [hbm] * (7 + n_dp + n_col),
        out_specs=(hbm,) * 4 + (vmem,),
        scratch_shapes=[
            V((2 * width, wide), LOW),
            V((wide, length), LOW),
            V((2 * width, length), LOW),
            V((width, here), LOW),
            V((width, here), FULL),
            V((width, here), FULL),
            V((n_pair, subs, width, piece), LOW),
            V((n_pair, subs, width, piece), LOW),
            V((subs, width, piece), FULL),
            V((n_pair - 1, subs, width, piece), LOW),
            V((n_pair - 1, subs, width, piece), LOW),
            V((n_dp - 1, 2, share, wide), LOW),
            V((n_dp - 1, 2, share, wide), LOW),
            V((2, share, wide), FULL),
            halves,
            halves,
            halves,
            halves,
            halves,
            V((n_dp, n_col) + part, LOW),
            V((n_col - 1,) + part, LOW),
            V((n_col - 1,) + part, LOW),
            V(part, LOW),
            V((n_col, unit, width), LOW),
            V((n_dp * rows_d, width), LOW),
            V((n_dp - 1, rows_d, width), LOW),
            V((rows_d, width), LOW),
            V((1, here), FULL),
            V((1, here), FULL),
            V((3,) + sums.shape, FULL),
            V((2, max(n_dp, n_col) - 1) + sums.shape, FULL),
            V(sums.shape, FULL),
            pltpu.SemaphoreType.DMA((count,)),
            pltpu.SemaphoreType.DMA((count,)),
            pltpu.SemaphoreType.DMA((moves,)),
        ],
        compiler_params=pltpu.CompilerParams(
            collective_id=1, has_side_effects=True, vmem_limit_bytes=62 * 2**20
        ),
        cost_estimate=pl.CostEstimate(
            flops=8 * wide * width * length, bytes_accessed=2**25, transcendentals=0
        ),
    )(gain, inverse, sums, qkv, dq, dk, dv, normed, tokens, middle, *grads, *downs)


def on_device(
    tokens,
    segment_ids,
    padding_mask,
    w_qkv,
    w_out,
    w_up,
    w_down,
    gain_attn,
    gain_mlp,
    scale_raw,
    cotangent,
):
    width, here = tokens.shape
    r, s = lax.axis_index("row"), lax.axis_index("cs")
    j, d = lax.axis_index("cp"), lax.axis_index("dp")
    n_pair, n_dp, n_col = lax.axis_size("cp"), lax.axis_size("dp"), lax.axis_size(COLS)
    c = s * n_pair + j
    head_cols = w_qkv.shape[0] // (3 * width)
    heads = head_cols // HEAD
    near = r == s

    ids = jnp.concatenate([segment_ids, padding_mask], 0)
    ids = jnp.where(s == r, ids, sibling(ids))
    segments, padding = ids[0], ids[1]
    length = segments.shape[0]
    firsts = segments[::BLOCK]
    starts = jnp.sum((segments[None, :] < firsts[:, None]).astype(jnp.int32), axis=1)
    filled = (jnp.sum(padding) + BLOCK - 1) // BLOCK
    blocks = jnp.arange(length // BLOCK, dtype=jnp.int32)
    lo = starts // BLOCK
    hi = jnp.minimum(blocks, filled)
    gain_one, gain_two = gain_attn[None, :], gain_mlp[None, :]
    factor = (LOG_TWO_E / math.sqrt(HEAD) * jnp.log1p(jnp.exp(scale_raw)))[None, :]

    block = w_qkv.reshape(width, 3 * head_cols)
    down = w_down.reshape(-1, width)
    unit = down.shape[0]
    part_rows = quarter_rows(unit, n_dp)

    def quarters(matrix):
        padded = jnp.pad(matrix, ((0, n_dp * part_rows - unit), (0, 0)))
        return padded.reshape(n_dp, part_rows, width)

    out = lax.dynamic_index_in_dim(quarters(w_out.reshape(-1, width)), d, 0, keepdims=False)
    up = lax.dynamic_index_in_dim(quarters(w_up.reshape(width, -1).T), d, 0, keepdims=False)
    (
        queries, key_heads, values, query_raw, normed_one, qkv, out_all, ups, cot_other,
        inverse_one,
    ) = head(
        n_dp, n_pair, gain_one, factor, tokens, cotangent, block, out, up,
        quarters(down),
    )
    ups = gather(ups, "dp")
    downs = [down] + [
        lax.ppermute(down, COLS, [(i, i ^ k) for i in range(n_col)])
        for k in range(2, n_col)
        if k != n_pair + 1
    ]
    attended, logs = attention_forward(queries, key_heads, values, ids, ids, lo, hi)
    result, grad_middle, grad_attended, grads, down_grads, gain_two_part = middle_part(
        n_dp, n_pair, gain_two, attended, tokens, cotangent, cot_other, out_all, ups, downs
    )
    received = [grads[0]] + [shift(grads[k], "dp", k) for k in range(1, n_dp)]
    down_received = list(down_grads[:2]) + [
        lax.ppermute(down_grads[k], COLS, [(i, i ^ k) for i in range(n_col)])
        for k in range(2, n_col)
    ]

    dq, dk, dv, scale_part = attention_backward(
        queries, key_heads, values, attended, grad_attended, logs, query_raw, factor,
        ids, ids, lo, hi,
    )
    scale_part = (
        scale_part[:, 0] * (LOG_TWO_E / math.sqrt(HEAD)) * jax.nn.sigmoid(scale_raw)
    )
    sums = jnp.concatenate(
        [
            jnp.zeros((1, width), FULL),
            gain_two_part,
            jnp.pad(scale_part, (0, width - HEAD))[None],
            jnp.zeros((5, width), FULL),
        ]
    )
    grad_tokens, grad_qkv, final, final_down, sums = tail(
        n_dp, n_pair, gain_one, inverse_one, sums, qkv, dq, dk, dv, normed_one, tokens,
        grad_middle, received, down_received,
    )
    grad_qkv = grad_qkv.astype(FULL)
    final = final.reshape(-1, width)
    final = [final[i * unit:(i + 1) * unit].astype(FULL) for i in range(2)]
    final.append(final_down.reshape(-1, width)[:unit].astype(FULL))
    own, other = sums[0], sums[1]
    first = r == 0
    gains = jnp.concatenate(
        [jnp.where(first, own[:2], other[:2]), jnp.where(first, other[:2], own[:2])], 1
    )
    scale_total = (own[2] + other[2])[:HEAD]
    return (
        result,
        grad_tokens,
        grad_qkv.reshape(-1),
        final[0].reshape(-1),
        final[1].T.reshape(-1),
        final[2].reshape(-1),
        gains[0],
        gains[1],
        scale_total,
    )


def solution(mesh):
    n_dp, n_row, n_col = (mesh.shape[name] for name in ("dp", "row", "col"))
    split = Mesh(
        np.asarray(mesh.devices).reshape(n_dp, n_row, n_row, n_col // n_row),
        ("dp", "row", "cs", "cp"),
    )
    rows = P("row", ("dp", "cs", "cp"))
    ids = P(("dp", "row"), None)
    blocks = P(("row", "cs", "cp"))
    return jax.shard_map(
        on_device,
        mesh=split,
        in_specs=(rows, ids, ids, blocks, blocks, blocks, blocks, P(), P(), P(), rows),
        out_specs=(rows, rows, blocks, blocks, blocks, blocks, P(), P(), P()),
        check_vma=False,
    )
```

```python
import functools
import math

import jax
import jax.numpy as jnp
import numpy as np
from jax import lax
from jax.experimental import pallas as pl
from jax.experimental.pallas import tpu as pltpu
from jax.sharding import Mesh, PartitionSpec as P

D = 1280
HEAD = 80
EPSILON = 1e-06
LOG_TWO_E = 1.442695041
BLOCK = 256
LOW = jnp.bfloat16
FULL = jnp.float32
COLS = ("cs", "cp")


def mm(left, right, left_axis, right_axis):
    return lax.dot_general(
        left, right, (((left_axis,), (right_axis,)), ((), ())), preferred_element_type=FULL
    )


def shift(x, axis, k):
    n = lax.axis_size(axis)
    return lax.ppermute(x, axis, [(i, i ^ k) for i in range(n)])


def sibling(x):
    return shift(x, "row", 1)


def cut(x, index, count, axis):
    step = x.shape[axis] // count
    return lax.dynamic_slice_in_dim(x, index * step, step, axis)


def gather(x, axis):
    return [x] + [shift(x, axis, k) for k in range(1, lax.axis_size(axis))]


def diag_mask(segq, segk):
    size = segk.shape[0], segq.shape[1]
    ki = lax.broadcasted_iota(jnp.int32, size, 0)
    qi = lax.broadcasted_iota(jnp.int32, size, 1)
    return ((segk == segq) & (ki <= qi)) | (ki == qi)


def half_row(ref, number, which):
    size = ref.shape[1] // 2
    row = slice(number, number + 1)
    return jnp.where(which == 0, ref[row, :size], ref[row, size:])


def column(row):
    return jnp.broadcast_to(row, (8, row.shape[1])).T[:, :1]


def rows_of(h):
    return slice(h * HEAD, (h + 1) * HEAD)


def forward_kernel(heads, lo_ref, hi_ref, q_ref, k_ref, v_ref, segq_ref, segk_ref, o_ref, log_ref, ks, segks):
    i = pl.program_id(0)

    here = pl.ds(pl.multiple_of(i * BLOCK, BLOCK), BLOCK)
    for h in range(heads):
        ks[h, here, :] = k_ref[rows_of(h), here].T
    segks[here, :] = column(jnp.where(segk_ref[1:, here] == 1, segk_ref[:1, here], -1).astype(FULL))
    segq = segq_ref[:1].astype(FULL)

    def visit(kb, carry, diagonal):
        at = pl.ds(pl.multiple_of(kb * BLOCK, BLOCK), BLOCK)
        segk = segks[at, :]
        mask = diag_mask(segq, segk) if diagonal else segk == segq
        scores = [
            jnp.dot(ks[h, at, :], q_ref[rows_of(h), :], preferred_element_type=FULL)
            for h in range(heads)
        ]
        peaks, totals, weights = [], [], []
        for h in range(heads):
            s = jnp.where(mask, scores[h], -1e30)
            peak = jnp.max(s, axis=0, keepdims=True)
            if not diagonal:
                peak = jnp.maximum(carry[h][0], peak)
            p = jnp.exp(s - peak)
            peaks.append(peak)
            totals.append(jnp.sum(p, axis=0, keepdims=True))
            weights.append(p.astype(LOW))
        out = []
        for h in range(heads):
            new = jnp.dot(v_ref[rows_of(h), at], weights[h], preferred_element_type=FULL)
            total = totals[h]
            if not diagonal:
                m, l, acc = carry[h]
                keep = jnp.exp(m - peaks[h])
                total = l * keep + total
                new = acc * keep + new
            out.append((peaks[h], total, new))
        return tuple(out)

    carry = visit(i, None, True)
    carry = lax.fori_loop(lo_ref[i], hi_ref[i], lambda kb, c: visit(kb, c, False), carry)
    for h in range(heads):
        m, l, acc = carry[h]
        o_ref[h * HEAD:(h + 1) * HEAD, :] = (acc / l).astype(LOW)
        log_ref[h] = m + jnp.log(l)


def attention_forward(q, k, v, segq, segk, lo, hi):
    cols, length = q.shape
    heads = cols // HEAD
    steps = length // BLOCK
    whole = pl.BlockSpec((cols, length), lambda i, *_: (0, 0))
    part = pl.BlockSpec((cols, BLOCK), lambda i, *_: (0, i))
    return pl.pallas_call(
        functools.partial(forward_kernel, heads),
        out_shape=(
            jax.ShapeDtypeStruct((cols, length), LOW),
            jax.ShapeDtypeStruct((heads, 1, length), FULL),
        ),
        grid_spec=pltpu.PrefetchScalarGridSpec(
            num_scalar_prefetch=2,
            grid=(steps,),
            in_specs=[
                part,
                whole,
                whole,
                pl.BlockSpec((2, BLOCK), lambda i, *_: (0, i)),
                pl.BlockSpec((2, length), lambda i, *_: (0, 0)),
            ],
            out_specs=(part, pl.BlockSpec((heads, 1, BLOCK), lambda i, *_: (0, 0, i))),
            scratch_shapes=[pltpu.VMEM((heads, length, HEAD), LOW), pltpu.VMEM((length, 1), FULL)],
        ),
        compiler_params=pltpu.CompilerParams(vmem_limit_bytes=62 * 2**20),
        cost_estimate=pl.CostEstimate(
            flops=8 * 2 * length * length * cols,
            bytes_accessed=4 * cols * length * 2,
            transcendentals=heads * length * length // 3,
        ),
    )(lo, hi, q, k, v, segq, segk)


def backward_kernel(
    heads, lo_ref, hi_ref, q_ref, k_ref, v_ref, o_ref, go_ref, log_ref, raw_ref, factor_ref, gain_ref,
    segq_ref, segk_ref, dq_ref, dk_ref, dv_ref, sums_ref, ks, vs, qs, gs, dks, dvs, dqs, segks, total,
):
    i = pl.program_id(0)

    @pl.when(i == 0)
    def _():
        sums_ref[...] = jnp.zeros_like(sums_ref)
        total[...] = jnp.zeros_like(total)

    here = pl.ds(pl.multiple_of(i * BLOCK, BLOCK), BLOCK)
    for h in range(heads):
        ks[h, here, :] = k_ref[rows_of(h), here].T
        vs[h, here, :] = v_ref[rows_of(h), here].T
    segks[here, :] = column(jnp.where(segk_ref[1:, here] == 1, segk_ref[:1, here], -1).astype(FULL))
    segq = segq_ref[:1].astype(FULL)
    inner = [
        jnp.sum(
            o_ref[h * HEAD:(h + 1) * HEAD, :].astype(FULL)
            * go_ref[h * HEAD:(h + 1) * HEAD, :].astype(FULL),
            axis=0,
            keepdims=True,
        )
        for h in range(heads)
    ]

    for h in range(heads):
        qs[h] = q_ref[rows_of(h), :].T
        gs[h] = go_ref[rows_of(h), :].T

    def visit(kb, diagonal):
        at = pl.ds(pl.multiple_of(kb * BLOCK, BLOCK), BLOCK)
        segk = segks[at, :]
        mask = diag_mask(segq, segk) if diagonal else segk == segq
        scores = [
            jnp.dot(ks[h, at, :], q_ref[rows_of(h), :], preferred_element_type=FULL)
            for h in range(heads)
        ]
        dps = [
            jnp.dot(vs[h, at, :], go_ref[rows_of(h), :], preferred_element_type=FULL)
            for h in range(heads)
        ]
        ps, dss = [], []
        for h in range(heads):
            p = jnp.where(mask, jnp.exp(scores[h] - log_ref[h]), 0.0)
            dss.append((p * (dps[h] - inner[h])).astype(LOW))
            ps.append(p.astype(LOW))
        for h in range(heads):
            new_v = jnp.dot(ps[h], gs[h], preferred_element_type=FULL)
            new_k = jnp.dot(dss[h], qs[h], preferred_element_type=FULL)
            new_q = jnp.dot(k_ref[rows_of(h), at], dss[h], preferred_element_type=FULL)
            if diagonal:
                dvs[h, at, :], dks[h, at, :], dqs[rows_of(h), :] = new_v, new_k, new_q
            else:
                dvs[h, at, :] += new_v
                dks[h, at, :] += new_k
                dqs[rows_of(h), :] += new_q

    visit(i, True)

    @pl.loop(lo_ref[i], hi_ref[i])
    def _(kb):
        visit(kb, False)

    factor = column(factor_ref[:1])
    part = jnp.zeros((HEAD, 1), FULL)
    for h in range(heads):
        rows = slice(h * HEAD, (h + 1) * HEAD)
        dq = dqs[rows, :]
        part = part + jnp.sum(dq * raw_ref[rows, :], axis=1, keepdims=True)
        dq_ref[rows, :] = (dq * factor).astype(LOW)
    total[...] += part

    @pl.when(i == pl.num_programs(0) - 1)
    def _():
        for h in range(heads):
            dk_ref[rows_of(h), :] = dks[h].astype(LOW).T
            dv_ref[rows_of(h), :] = dvs[h].astype(LOW).T
        sums_ref[1:2, :] = gain_ref[...]
        row = jnp.broadcast_to(total[...], (HEAD, 128)).T[:1]
        sums_ref[2:3, :HEAD] = row * factor_ref[1:]


def attention_backward(q, k, v, o, go, logs, raw, factor, gain_part, segq, segk, lo, hi):
    cols, length = q.shape
    heads = cols // HEAD
    steps = length // BLOCK
    whole = pl.BlockSpec((cols, length), lambda i, *_: (0, 0))
    part = pl.BlockSpec((cols, BLOCK), lambda i, *_: (0, i))
    width = gain_part.shape[1]
    total = pl.BlockSpec((8, width), lambda i, *_: (0, 0))
    shape = jax.ShapeDtypeStruct((cols, length), LOW)
    return pl.pallas_call(
        functools.partial(backward_kernel, heads),
        out_shape=(shape, shape, shape, jax.ShapeDtypeStruct((8, width), FULL)),
        grid_spec=pltpu.PrefetchScalarGridSpec(
            num_scalar_prefetch=2,
            grid=(steps,),
            in_specs=[
                part,
                whole,
                whole,
                part,
                part,
                pl.BlockSpec((heads, 1, BLOCK), lambda i, *_: (0, 0, i)),
                part,
                pl.BlockSpec((2, HEAD), lambda i, *_: (0, 0)),
                pl.BlockSpec((1, width), lambda i, *_: (0, 0)),
                pl.BlockSpec((2, BLOCK), lambda i, *_: (0, i)),
                pl.BlockSpec((2, length), lambda i, *_: (0, 0)),
            ],
            out_specs=(part, whole, whole, total),
            scratch_shapes=[
                pltpu.VMEM((heads, length, HEAD), LOW),
                pltpu.VMEM((heads, length, HEAD), LOW),
                pltpu.VMEM((heads, BLOCK, HEAD), LOW),
                pltpu.VMEM((heads, BLOCK, HEAD), LOW),
                pltpu.VMEM((heads, length, HEAD), FULL),
                pltpu.VMEM((heads, length, HEAD), FULL),
                pltpu.VMEM((cols, BLOCK), FULL),
                pltpu.VMEM((length, 1), FULL),
                pltpu.VMEM((HEAD, 1), FULL),
            ],
        ),
        compiler_params=pltpu.CompilerParams(vmem_limit_bytes=62 * 2**20),
        cost_estimate=pl.CostEstimate(
            flops=8 * 5 * length * length * cols,
            bytes_accessed=8 * cols * length * 2,
            transcendentals=heads * length * length // 3,
        ),
    )(lo, hi, q, k, v, o, go, logs, raw, factor, gain_part, segq, segk)


def remote(src, dst, sems, index, device):
    return pltpu.make_async_remote_copy(
        src_ref=src,
        dst_ref=dst,
        send_sem=sems[0].at[index],
        recv_sem=sems[1].at[index],
        device_id=device,
        device_id_type=pl.DeviceIdType.MESH,
    )


def greet(peers):
    barrier = pltpu.get_barrier_semaphore()
    for peer in peers:
        pl.semaphore_signal(barrier, inc=1, device_id=peer, device_id_type=pl.DeviceIdType.MESH)
    pl.semaphore_wait(barrier, len(peers))


def head_kernel(
    n_dp, n_pair, gain_ref, factor_ref, tokens_hbm, cot_hbm, block_hbm, out_hbm, up_hbm,
    down_hbm, q_hbm, k_hbm, v_hbm, raw_hbm, normed_hbm, qkv_hbm, out_all, ups_hbm, cot_out, inverse_ref,
    tokens, others, block, cs_recv, remote_block, pass_on, qkv, turned, normed, q, k, v, raw,
    send_sems, recv_sems, local_sems,
):
    r, s = lax.axis_index("row"), lax.axis_index("cs")
    j, d = lax.axis_index("cp"), lax.axis_index("dp")
    n_col = 2 * n_pair
    subs, width, piece = tokens.shape[1:]
    here = subs * piece
    share = cs_recv.shape[0]
    cols = q.shape[0]
    c_first = (s * n_pair + j) ^ (r * n_pair)
    near = r == s
    sems = (send_sems, recv_sems)
    counter, local_counter = iter(range(1000)), iter(range(1000))
    sent, stored = [], []

    def send(src, dst, device):
        copy = remote(src, dst, sems, next(counter), device)
        copy.start()
        sent.append(copy)
        return copy

    def move(src, dst):
        copy = pltpu.make_async_copy(src, dst, local_sems.at[next(local_counter)])
        copy.start()
        return copy

    def store(src, dst):
        stored.append(move(src, dst))

    def columns(u):
        return pl.ds(u * piece, piece)

    own_tokens = [move(tokens_hbm.at[:, columns(u)], tokens.at[0, u]) for u in range(subs)]
    own_block = move(block_hbm, block)
    own_out = move(out_hbm, out_all.at[d, c_first])
    store(up_hbm, ups_hbm.at[c_first])
    sibling_id = {"row": 1 - r}
    dp_ids = [{"dp": d ^ k} for k in range(1, n_dp)]
    col_ids = [{"cs": s ^ (k // n_pair), "cp": j ^ (k % n_pair)} for k in range(1, n_col)]
    greet([sibling_id] + dp_ids + col_ids)

    cs_copy = send(block_hbm.at[d], cs_recv, {"cs": 1 - s})
    down_ids = [col_ids[0], col_ids[n_pair]]
    down_copies = [
        send(down_hbm.at[d], ups_hbm.at[n_col + m], peer) for m, peer in enumerate(down_ids)
    ]
    out_copies = [send(out_hbm, out_all.at[d, c_first], peer) for peer in col_ids]
    other_copies = {}
    for u in range(subs):
        other_copies[0, u] = send(tokens_hbm.at[:, columns(u)], others.at[0, u], sibling_id)
    pair_copies = {}

    def send_pairs(u):
        for m in range(1, n_pair):
            pair_copies[m, u] = send(
                tokens_hbm.at[:, columns(u)], tokens.at[m, u], {"cp": j ^ m}
            )

    send_pairs(0)

    cot_copy = send(cot_hbm, cot_out, sibling_id)
    gain_own = column(half_row(gain_ref, 0, r))
    gain_other = column(half_row(gain_ref, 0, 1 - r))
    factor = jnp.concatenate([column(factor_ref[:1])] * (cols // HEAD), 0)

    def norm(m, u):
        own, other = tokens[m, u].astype(FULL), others[m, u].astype(FULL)
        squares = jnp.sum(own * own, axis=0, keepdims=True)
        squares = squares + jnp.sum(other * other, axis=0, keepdims=True)
        inverse = lax.rsqrt(squares / D + EPSILON)
        at = pl.ds(pl.multiple_of((j ^ m) * here + u * piece, 128), piece)
        normed[:width, at] = (own * inverse * gain_own).astype(LOW)
        normed[width:, at] = (other * inverse * gain_other).astype(LOW)
        store(normed.at[:, at], normed_hbm.at[:, at])
        if m == 0:
            inverse_ref[:, columns(u)] = inverse

    def project(m, u):
        at = pl.ds(pl.multiple_of((j ^ m) * here + u * piece, 128), piece)
        for part, out in ((0, None), (1, k), (2, v)):
            value = jnp.dot(
                turned[part * cols:(part + 1) * cols, :], normed[:, at],
                preferred_element_type=FULL,
            )
            if part == 0:
                raw[:, at] = value
                q[:, at] = (value * factor).astype(LOW)
            else:
                out[:, at] = value.astype(LOW)
        for src, dst in ((q, q_hbm), (k, k_hbm), (v, v_hbm), (raw, raw_hbm)):
            store(src.at[:, at], dst.at[:, at])

    for u in range(subs):
        own_tokens[u].wait()
        other_copies[0, u].wait_recv()
        norm(0, u)
    own_block.wait()

    cs_copy.wait_recv()
    send_pairs(1)
    dp_copies = [send(cs_recv, remote_block.at[d], peer) for peer in dp_ids]
    own_out.wait()
    for copy in out_copies:
        copy.wait_recv()
    late_copies = [send(out_all.at[d], out_all.at[d], peer) for peer in dp_ids]
    remote_block[d] = cs_recv[...]
    for u in range(subs - 1):
        for m in range(1, n_pair):
            pair_copies[m, u].wait_recv()
            other_copies[m, u] = send(tokens.at[m, u], others.at[m, u], sibling_id)
    cross_copies = []
    for m in range(n_dp):
        owner = d ^ m
        if m:
            dp_copies[m - 1].wait_recv()
        mine, its = block[owner], remote_block[owner]
        at = pl.multiple_of(owner * share, 32)
        qkv[pl.ds(at, share)] = jnp.where(near, mine, its)
        pass_on[owner] = jnp.where(near, its, mine)
        cross_copies.append(
            send(pass_on.at[owner], qkv.at[pl.ds(width + at, share)], sibling_id)
        )
    u = subs - 1
    for m in range(1, n_pair):
        pair_copies[m, u].wait_recv()
        other_copies[m, u] = send(tokens.at[m, u], others.at[m, u], sibling_id)
    late_copies += [send(up_hbm, ups_hbm.at[c_first], peer) for peer in col_ids]
    turned[:, :width] = qkv[:width].T
    for copy in cross_copies:
        copy.wait_recv()
    turned[:, width:] = qkv[width:].T
    store(qkv, qkv_hbm)

    for u in range(subs):
        project(0, u)
    for u in range(subs):
        for m in range(1, n_pair):
            other_copies[m, u].wait_recv()
            norm(m, u)
            project(m, u)

    for copy in stored:
        copy.wait()
    for copy in late_copies + down_copies + [cot_copy]:
        copy.wait_recv()
    for copy in sent:
        copy.wait_send()


def head(n_dp, n_pair, gain, factor, tokens, cotangent, block, out, up, down):
    width, here = tokens.shape
    wide = block.shape[1]
    cols = wide // 3
    share = width // n_dp
    length = n_pair * here
    n_col = 2 * n_pair
    subs = 2
    piece = here // subs
    count = subs * n_pair * 2 + 4 * n_dp + 2 * n_col + 7
    moves = 4 + subs + 5 * subs * n_pair + 4
    hbm = pl.BlockSpec(memory_space=pl.ANY)
    vmem = pl.BlockSpec(memory_space=pltpu.VMEM)
    V = pltpu.VMEM
    shape = jax.ShapeDtypeStruct((cols, length), LOW)
    return pl.pallas_call(
        functools.partial(head_kernel, n_dp, n_pair),
        out_shape=(
            shape,
            shape,
            shape,
            jax.ShapeDtypeStruct((cols, length), FULL),
            jax.ShapeDtypeStruct((2 * width, length), LOW),
            jax.ShapeDtypeStruct((2 * width, wide), LOW),
            jax.ShapeDtypeStruct((n_dp, n_col) + out.shape, LOW),
            jax.ShapeDtypeStruct((n_col + 2,) + up.shape, LOW),
            jax.ShapeDtypeStruct((width, here), LOW),
            jax.ShapeDtypeStruct((1, here), FULL),
        ),
        in_specs=[vmem] * 2 + [hbm] * 6,
        out_specs=(hbm,) * 9 + (vmem,),
        scratch_shapes=[
            V((n_pair, subs, width, piece), LOW),
            V((n_pair, subs, width, piece), LOW),
            V((n_dp, share, wide), LOW),
            V((share, wide), LOW),
            V((n_dp, share, wide), LOW),
            V((n_dp, share, wide), LOW),
            V((2 * width, wide), LOW),
            V((wide, 2 * width), LOW),
            V((2 * width, length), LOW),
            V((cols, length), LOW),
            V((cols, length), LOW),
            V((cols, length), LOW),
            V((cols, length), FULL),
            pltpu.SemaphoreType.DMA((count,)),
            pltpu.SemaphoreType.DMA((count,)),
            pltpu.SemaphoreType.DMA((moves,)),
        ],
        compiler_params=pltpu.CompilerParams(
            collective_id=2, has_side_effects=True, vmem_limit_bytes=60 * 2**20
        ),
        cost_estimate=pl.CostEstimate(
            flops=4 * wide * width * length, bytes_accessed=2**25, transcendentals=0
        ),
    )(gain, factor, tokens, cotangent, block.reshape(n_dp, share, wide), out, up, down)


def middle_kernel(n_dp, n_pair, unit, gain_ref, att_hbm, tokens_hbm, cot_hbm, cot_other, out_all, *refs):
    n_col = 2 * n_pair
    up_hbms, refs = refs[:n_dp], refs[n_dp:]
    down_hbms, refs = refs[:n_col - 2], refs[n_col - 2:]
    result_hbm, middle_hbm, out_hbm, refs = refs[0], refs[1], refs[2], refs[3:]
    grads_hbms, refs = refs[:n_dp], refs[n_dp:]
    down_outs, refs = refs[:n_col], refs[n_col:]
    (
        gain_out, tokens, cot, out_slab, up_slab, down_slab, out_w, up_w, down_w, out_t, up_t, down_t, out_half, up_half,
        down_half, att, scaled, normed, active, grad_hidden, branch, middle, grad, result, grad_att,
        grads, down_grads, square_send, square_recv, inner_send, inner_recv, inverse, narrow,
        send_sems, recv_sems, local_sems,
    ) = refs
    r, s = lax.axis_index("row"), lax.axis_index("cs")
    j, d = lax.axis_index("cp"), lax.axis_index("dp")
    width, here = tokens.shape
    pieces, _, piece = square_send.shape
    cols = att_hbm.shape[0]
    half = n_col * unit // 2
    rows_q = up_hbms[0].shape[1]
    rows_g = grads_hbms[0].shape[1]
    c_first = (s * n_pair + j) ^ (r * n_pair)
    sems = (send_sems, recv_sems)
    gain = column(half_row(gain_ref, 1, r))
    counter, local_counter = iter(range(1000)), iter(range(1000))
    sent, stored = [], []

    def send(src, dst, device):
        copy = remote(src, dst, sems, next(counter), device)
        copy.start()
        sent.append(copy)
        return copy

    def move(src, dst):
        copy = pltpu.make_async_copy(src, dst, local_sems.at[next(local_counter)])
        copy.start()
        return copy

    def columns(u):
        return pl.ds(u * piece, piece)

    def span(u):
        return slice(u * piece, (u + 1) * piece)

    def down_rows(owner):
        return pl.ds(pl.multiple_of(owner * unit, 16), unit)

    def quarter_of(owner):
        return pl.ds(pl.multiple_of(owner * rows_q, 16), rows_q)

    quartered = (1, n_pair + 1)
    own_rows, other_rows = pl.ds(0, width), pl.ds(width, width)
    weight_loads = [
        move(out_all.at[m], out_slab.at[:, pl.ds(m * rows_q, rows_q)]) for m in range(n_dp)
    ] + [
        move(up_hbms[m].at[pl.ds(first, size)], target.at[:, quarter_of(d ^ m)])
        for m in range(n_dp)
        for first, size, target in ((0, n_col, up_slab), (n_col, 2, down_slab))
    ] + [
        move(ref, down_w.at[down_rows(c_first ^ m)])
        for m, ref in zip([m for m in range(n_col) if m not in quartered], down_hbms)
    ]
    att_loads = [
        move(
            att_hbm.at[:, pl.ds(pl.multiple_of(j * here + u * piece, 128), piece)],
            att.at[pl.ds(pl.multiple_of(j * cols, 16), cols), columns(u)],
        )
        for u in range(pieces)
    ]
    token_load = move(tokens_hbm, tokens)
    cot_loads = [move(cot_hbm, cot.at[own_rows]), move(cot_other, cot.at[other_rows])]
    sibling_id = {"row": 1 - r}
    pair_ids = [{"cp": j ^ m} for m in range(1, n_pair)]
    greet([sibling_id] + pair_ids)

    att_copies = {}
    for u in range(pieces):
        for m in range(1, n_pair):
            att_copies[u, m] = send(
                att_hbm.at[:, pl.ds(pl.multiple_of((j ^ m) * here + u * piece, 128), piece)],
                att.at[pl.ds(pl.multiple_of(j * cols, 16), cols), columns(u)],
                pair_ids[m - 1],
            )

    for copy in weight_loads:
        copy.wait()
    for m in range(n_col):
        at = slice(m * unit, (m + 1) * unit)
        out_w[at] = out_slab[m, :unit]
        up_w[at] = up_slab[m, :unit]
    for m, k in enumerate(quartered):
        down_w[down_rows(c_first ^ k)] = down_slab[m, :unit]
    cross_copies = []

    def cross(whole, part):
        cross_copies.append(send(whole.at[pl.ds(half, half)], part.at[:, other_rows], sibling_id))
        part[:, :width] = whole[:half]

    cross(up_w, up_half)
    cross(down_w, down_half)
    cross(out_w, out_half)
    out_t[...] = out_w[...].T
    narrow[...] = jnp.zeros_like(narrow)

    copies = {}

    def exchange(name, u, ref):
        copies[name, u] = send(
            ref.at[own_rows, columns(u)], ref.at[other_rows, columns(u)], sibling_id
        )

    def share_heads(u):
        att_loads[u].wait()
        for m in range(1, n_pair):
            att_copies[u, m].wait_recv()
        exchange("att", u, att)

    def first_branch(u):
        if u == 0:
            token_load.wait()
        copies["att", u].wait_recv()
        value = tokens[:, span(u)].astype(FULL) + jnp.dot(
            out_t[...], att[:, span(u)], preferred_element_type=FULL
        )
        scaled[:width, span(u)] = (value * gain).astype(LOW)
        exchange("scaled", u, scaled)
        square_send[u] = jnp.sum(value * value, axis=0, keepdims=True)
        copies["square", u] = send(square_send.at[u], square_recv.at[u], sibling_id)
        middle[:, span(u)] = value

    def hidden_units(u):
        if u == 0:
            for copy in cot_loads:
                copy.wait()
            for copy in cross_copies:
                copy.wait_recv()
            up_t[...] = up_w[...].T
            down_t[...] = down_w[...].T
        grad_active = jnp.dot(down_half[...], cot[:, span(u)], preferred_element_type=FULL)
        copies["scaled", u].wait_recv()
        copies["square", u].wait_recv()
        scale = lax.rsqrt((square_send[u] + square_recv[u]) / D + EPSILON)
        inverse[u] = scale
        hidden = scale * jnp.dot(up_half[...], scaled[:, span(u)], preferred_element_type=FULL)
        sigmoid = jax.nn.sigmoid(hidden)
        value = (grad_active * sigmoid * (1.0 + hidden * (1.0 - sigmoid))).astype(LOW)
        grad_hidden[:half, span(u)] = value
        exchange("grad_hidden", u, grad_hidden)
        active[:half, span(u)] = (hidden * sigmoid).astype(LOW)
        exchange("active", u, active)
        inner_send[u] = jnp.sum(value.astype(FULL) * hidden, axis=0, keepdims=True)
        copies["inner", u] = send(inner_send.at[u], inner_recv.at[u], sibling_id)
        normed[:, span(u)] = (middle[:, span(u)] * scale * gain).astype(LOW)

    def second_branch(u):
        copies["grad_hidden", u].wait_recv()
        copies["inner", u].wait_recv()
        scale = inverse[u]
        inner = scale * scale * ((inner_send[u] + inner_recv[u]) / D)
        back = jnp.dot(up_t[...], grad_hidden[:, span(u)], preferred_element_type=FULL)
        value = (
            cot[:width, span(u)].astype(FULL)
            + scale * (back * gain)
            - middle[:, span(u)] * inner
        )
        branch[:width, span(u)] = value.astype(LOW)
        exchange("branch", u, branch)
        grad[:, span(u)] = value
        stored.append(move(grad.at[:, columns(u)], middle_hbm.at[:, columns(u)]))
        product = back * middle[:, span(u)] * scale
        total = narrow[...]
        for v in range(piece // 128):
            total = total + product[:, v * 128:(v + 1) * 128]
        narrow[...] = total
        copies["active", u].wait_recv()
        result[:, span(u)] = middle[:, span(u)] + jnp.dot(
            down_t[...], active[:, span(u)], preferred_element_type=FULL
        )
        stored.append(move(result.at[:, columns(u)], result_hbm.at[:, columns(u)]))

    def heads_back(u):
        copies["branch", u].wait_recv()
        grad_att[:, span(u)] = jnp.dot(
            out_half[...], branch[:, span(u)], preferred_element_type=FULL
        ).astype(LOW)
        target = pl.ds(pl.multiple_of(j * here + u * piece, 128), piece)
        for m in range(n_pair):
            source = grad_att.at[
                pl.ds(pl.multiple_of((j ^ m) * cols, 16), cols), columns(u)
            ]
            if m:
                copies["out", u, m] = send(source, out_hbm.at[:, target], pair_ids[m - 1])
            else:
                stored.append(move(source, out_hbm.at[:, target]))

    stages = (share_heads, first_branch, hidden_units, second_branch, heads_back)
    turned = {}

    def product(name, first, left, right, target, at):
        if name not in turned:
            turned[name] = right[:width].T
        count = n_col // 2
        for n in range(0 if first else count, count if first else n_col):
            target[n, at:at + unit] = jnp.dot(
                left[n * unit:(n + 1) * unit], turned[name], preferred_element_type=FULL
            ).astype(LOW)

    if grads.shape[1] > 2 * unit:
        grads[...] = jnp.zeros_like(grads)
    if down_grads.shape[1] > unit:
        down_grads[...] = jnp.zeros_like(down_grads)
    for t in range(pieces + len(stages) - 1):
        for number in reversed(range(len(stages))):
            if 0 <= t - number < pieces:
                stages[number](t - number)
            if number == 4 and t == pieces + 2:
                product("down", True, active, cot, down_grads, 0)
        if t == pieces + 2:
            product("up", True, grad_hidden, normed, grads, unit)

    product("down", False, active, cot, down_grads, 0)
    for m in range(n_col):
        stored.append(move(down_grads.at[c_first ^ m], down_outs[m]))
    product("up", False, grad_hidden, normed, grads, unit)
    for first in (True, False):
        product("out", first, att, branch, grads, 0)
    for m in range(n_dp):
        at = pl.ds(pl.multiple_of((d ^ m) * rows_g, 16), rows_g)
        stored.append(move(grads.at[:, at], grads_hbms[m]))
    gain_out[...] = jnp.sum(narrow[...].T, axis=0, keepdims=True)

    for u in range(pieces):
        for m in range(1, n_pair):
            copies["out", u, m].wait_recv()
    for copy in stored:
        copy.wait()
    for copy in sent:
        copy.wait_send()


def middle_part(n_dp, n_pair, gain, attended, tokens, cotangent, cot_other, out_all, ups, downs):
    width, here = tokens.shape
    n_col = 2 * n_pair
    cols, length = attended.shape
    unit = downs[0].shape[0]
    half = n_col * unit // 2
    rows_q = ups[0].shape[1]
    rows_g = quarter_rows(2 * unit, n_dp)
    pieces = max(2, here // 256)
    piece = here // pieces
    count = 2 * pieces * (n_pair - 1) + 7 * pieces + 8
    moves = 4 * n_dp + 2 * n_col + 4 * pieces + 4
    hbm = pl.BlockSpec(memory_space=pl.ANY)
    vmem = pl.BlockSpec(memory_space=pltpu.VMEM)
    V = pltpu.VMEM
    S = jax.ShapeDtypeStruct
    weight = V((2 * half, width), LOW)
    weight_t = V((width, 2 * half), LOW)
    both = V((2 * width, here), LOW)
    whole = V((width, here), FULL)
    row = V((pieces, 1, piece), FULL)
    out = pl.pallas_call(
        functools.partial(middle_kernel, n_dp, n_pair, unit),
        out_shape=(
            S((width, here), FULL),
            S((width, here), FULL),
            S((cols, length), LOW),
        )
        + (S((n_col, rows_g, width), LOW),) * n_dp
        + (S((n_dp * quarter_rows(unit, n_dp), width), LOW),) * n_col
        + (S((1, width), FULL),),
        in_specs=[vmem] + [hbm] * (3 + n_dp + n_col),
        out_specs=(hbm,) * (3 + n_dp + n_col) + (vmem,),
        scratch_shapes=[
            V((width, here), LOW),
            both,
            V((n_col, n_dp * rows_q, width), LOW),
            V((n_col, n_dp * rows_q, width), LOW),
            V((2, n_dp * rows_q, width), LOW),
            weight,
            weight,
            weight,
            weight_t,
            weight_t,
            weight_t,
            V((half, 2 * width), LOW),
            V((half, 2 * width), LOW),
            V((half, 2 * width), LOW),
            both,
            both,
            V((width, here), LOW),
            V((2 * half, here), LOW),
            V((2 * half, here), LOW),
            both,
            whole,
            whole,
            whole,
            V((width, here), LOW),
            V((n_col, n_dp * rows_g, width), LOW),
            V((n_col, n_dp * quarter_rows(unit, n_dp), width), LOW),
            row,
            row,
            row,
            row,
            row,
            V((width, 128), FULL),
            pltpu.SemaphoreType.DMA((count,)),
            pltpu.SemaphoreType.DMA((count,)),
            pltpu.SemaphoreType.DMA((moves,)),
        ],
        compiler_params=pltpu.CompilerParams(
            collective_id=3, has_side_effects=True, vmem_limit_bytes=62 * 2**20
        ),
        cost_estimate=pl.CostEstimate(
            flops=18 * 2 * half * width * here, bytes_accessed=2**25, transcendentals=0
        ),
    )(gain, attended, tokens, cotangent, cot_other, out_all, *ups, *downs)
    return out[0], out[1], out[2], out[3:3 + n_dp], out[3 + n_dp:-1], out[-1]


def quarter_rows(rows, n_dp):
    return -(-rows // (16 * n_dp)) * 16


def tail_kernel(
    n_dp, n_pair, gain_ref, inverse_ref, sums_ref, qkv_hbm, dq_hbm, dk_hbm, dv_hbm, normed_hbm,
    tokens_hbm, middle_hbm, *refs,
):
    n_col = 2 * n_pair
    grads_hbms, refs = refs[:n_dp], refs[n_dp:]
    down_hbms, refs = refs[:n_col], refs[n_col:]
    (
        result_hbm, qkv_out, grads_out, down_out, sums_out,
        qkv, dproj, normed, tokens, middle, result, row_send, row_recv, own, pair_send, pair_recv,
        dp_send, dp_recv, dp_own, cross_send, cross_recv, cs_send, cs_recv, final, grads_parts,
        grads_send, grads_recv, grads_final, down_parts, down_send, down_recv, down_final,
        far_own, far_recv, far_send, far_parts,
        inner_send, inner_recv, sums_send, sums_recv, last_sums, send_sems, recv_sems, local_sems,
    ) = refs
    r, s = lax.axis_index("row"), lax.axis_index("cs")
    j, d = lax.axis_index("cp"), lax.axis_index("dp")
    width, here = tokens.shape
    cols = dq_hbm.shape[0]
    quartered = (1, n_pair + 1)
    whole = [k for k in range(n_col) if k not in quartered]
    share = width // n_dp
    part = share // 2
    rows_d = down_final.shape[0]
    subs = row_send.shape[1]
    piece = here // subs
    c_first = (s * n_pair + j) ^ (r * n_pair)
    near = r == s
    sems = (send_sems, recv_sems)
    gain = column(half_row(gain_ref, 0, r))
    counter, local_counter = iter(range(1000)), iter(range(1000))
    sent, stored = [], []

    def send(src, dst, device):
        copy = remote(src, dst, sems, next(counter), device)
        copy.start()
        sent.append(copy)
        return copy

    def move(src, dst):
        copy = pltpu.make_async_copy(src, dst, local_sems.at[next(local_counter)])
        copy.start()
        return copy

    def down_rows(owner):
        return pl.ds(pl.multiple_of(owner * rows_d, 16), rows_d)

    load_grads = [move(grads_hbms[k], grads_parts.at[k]) for k in range(n_dp)]
    early = [
        move(dq_hbm, dproj.at[pl.ds(0, cols)]),
        move(dk_hbm, dproj.at[pl.ds(cols, cols)]),
        move(dv_hbm, dproj.at[pl.ds(2 * cols, cols)]),
        move(normed_hbm, normed),
    ]
    load_qkv = move(qkv_hbm, qkv)
    load_down = [move(down_hbms[k], down_parts.at[m]) for m, k in enumerate(whole)]
    load_far = [
        move(down_hbms[k].at[down_rows(d)], far_own.at[m]) for m, k in enumerate(quartered)
    ]
    late = [move(tokens_hbm, tokens), move(middle_hbm, middle)]

    sibling_id = {"row": 1 - r}
    cs_id = {"cs": 1 - s}
    dp_ids = [{"dp": d ^ k} for k in range(1, n_dp)]
    col_ids = [{"cs": s ^ (k // n_pair), "cp": j ^ (k % n_pair)} for k in range(1, n_col)]
    greet([sibling_id] + dp_ids + col_ids)


    for copy in load_grads:
        copy.wait()

    def summed(place_at):
        value = grads_parts[0, place_at].astype(FULL)
        for k in range(1, n_dp):
            value = value + grads_parts[k, place_at].astype(FULL)
        return value

    grads_copies = []
    for k in range(1, n_col):
        grads_send[k - 1] = summed(c_first ^ k).astype(LOW)
        grads_copies.append(send(grads_send.at[k - 1], grads_recv.at[k - 1], col_ids[k - 1]))
    far_copies = [
        send(down_hbms[k].at[down_rows(d ^ peer)], far_recv.at[peer - 1, m], dp_ids[peer - 1])
        for m, k in enumerate(quartered)
        for peer in range(1, n_dp)
    ]

    def quarter(half, owner):
        at = pl.ds(pl.multiple_of(half * width + owner * share, 32), share)
        return mm(normed[at, :], dproj[...], 1, 1)

    def rows_of(half, chunk, u):
        at = pl.ds(pl.multiple_of(chunk * here + u * piece, 128), piece)
        return jnp.dot(
            qkv[half * width:(half + 1) * width, :], dproj[:, at], preferred_element_type=FULL
        )

    dp_copies = {}

    def send_part(k, p):
        rows = pl.ds(p * part, part)
        dp_copies[k, p] = send(
            dp_send.at[k - 1, :, rows], dp_recv.at[k - 1, :, rows], dp_ids[k - 1]
        )

    def quarters(k):
        for half in range(2):
            dp_send[k - 1, half] = quarter(half, d ^ k).astype(LOW)
        send_part(k, 0)

    row_copies, pair_copies = {}, []
    for copy in early:
        copy.wait()
    for k in reversed(range(1, n_dp)):
        quarters(k)
    for k in reversed(range(1, n_dp)):
        send_part(k, 1)
    for copy in load_far:
        copy.wait()
    for copy in far_copies:
        copy.wait_recv()
    far_z = []
    for m, k in enumerate(quartered):
        value = far_own[m].astype(FULL)
        for peer in range(1, n_dp):
            value = value + far_recv[peer - 1, m].astype(FULL)
        far_send[m] = value.astype(LOW)
        far_z.append(send(far_send.at[m], far_parts.at[m], col_ids[k - 1]))
    load_qkv.wait()
    for k in range(1, n_pair):
        for u in range(subs):
            row_send[k, u] = rows_of(1, j ^ k, u).astype(LOW)
            row_copies[k, u] = send(row_send.at[k, u], row_recv.at[k, u], sibling_id)
    for k in range(1, n_pair):
        for u in range(subs):
            value = rows_of(0, j ^ k, u)
            row_copies[k, u].wait_recv()
            pair_send[k - 1, u] = (value + row_recv[k, u].astype(FULL)).astype(LOW)
            pair_copies.append(
                send(pair_send.at[k - 1, u], pair_recv.at[k - 1, u], {"cp": j ^ k})
            )
    for copy in load_down:
        copy.wait()
    value = down_parts[0].astype(FULL)
    for m in range(1, n_col - 2):
        value = value + down_parts[m].astype(FULL)
    down_send[...] = value.astype(LOW)

    down_copies = [
        send(down_send.at[down_rows(d ^ k)], down_recv.at[k - 1], dp_ids[k - 1])
        for k in range(1, n_dp)
    ]
    for half in range(2):
        dp_own[half] = quarter(half, d)

    for u in range(subs):
        row_send[0, u] = rows_of(1, j, u).astype(LOW)
        row_copies[0, u] = send(row_send.at[0, u], row_recv.at[0, u], sibling_id)
    for u in range(subs):
        own[u] = rows_of(0, j, u)

    cs_copies = []

    def reduce_part(p):
        rows = slice(p * part, (p + 1) * part)
        for k in range(1, n_dp):
            dp_copies[k, p].wait_recv()

        def total(half):
            value = dp_own[half, rows]
            for k in range(1, n_dp):
                value = value + dp_recv[k - 1, half, rows].astype(FULL)
            return value

        cross_send[p] = total(1).astype(LOW)
        cross_copy = send(cross_send.at[p], cross_recv.at[p], sibling_id)
        kept = total(0)
        cross_copy.wait_recv()
        crossed = cross_recv[p].astype(FULL)
        cs_send[p] = jnp.where(near, crossed, kept).astype(LOW)
        cs_copies.append(send(cs_send.at[p], cs_recv.at[p], cs_id))
        dp_own[0, rows] = jnp.where(near, kept, crossed)

    reduce_part(0)

    reduce_part(1)

    value = down_send[down_rows(d)].astype(FULL)
    for k in range(1, n_dp):
        down_copies[k - 1].wait_recv()
        value = value + down_recv[k - 1].astype(FULL)
    for m in range(2):
        far_z[m].wait_recv()
        value = value + far_parts[m].astype(FULL)
    down_final[...] = value.astype(LOW)
    out_copies = [send(down_final, down_out.at[d], peer) for peer in dp_ids]
    stored.append(move(down_final, down_out.at[d]))

    value = summed(c_first)
    for k in range(1, n_col):
        grads_copies[k - 1].wait_recv()
        value = value + grads_recv[k - 1].astype(FULL)
    grads_final[...] = value.astype(LOW)
    out_copies += [send(grads_final, grads_out.at[d], peer) for peer in dp_ids]
    stored.append(move(grads_final, grads_out.at[d]))

    for copy in late:
        copy.wait()
    for copy in pair_copies:
        copy.wait_recv()
    inverse = inverse_ref[...]
    for u in range(subs):
        row_copies[0, u].wait_recv()
        at = slice(u * piece, (u + 1) * piece)
        value = own[u] + row_recv[0, u].astype(FULL)
        for k in range(1, n_pair):
            value = value + pair_recv[k - 1, u].astype(FULL)
        own[u] = value
        inner_send[:, at] = jnp.sum(
            value * gain * tokens[:, at].astype(FULL), axis=0, keepdims=True
        )
    inner_copy = send(inner_send, inner_recv, sibling_id)

    def finish_part(p):
        cs_copies[p].wait_recv()
        rows = slice(p * part, (p + 1) * part)
        final[p] = (dp_own[0, rows] + cs_recv[p].astype(FULL)).astype(LOW)
        target = qkv_out.at[d, pl.ds(p * part, part)]
        out_copies.extend([send(final.at[p], target, peer) for peer in dp_ids])
        stored.append(move(final.at[p], target))

    finish_part(0)
    narrow = jnp.zeros((width, 128), FULL)
    for u in range(subs):
        at = slice(u * piece, (u + 1) * piece)
        wide = own[u] * tokens[:, at].astype(FULL) * inverse[:, at]
        for v in range(piece // 128):
            narrow = narrow + wide[:, v * 128:(v + 1) * 128]
    gain_part = jnp.sum(narrow.T, axis=0, keepdims=True)
    sums_send[0] = jnp.concatenate([gain_part, sums_ref[1:]], 0)
    sums_copies = {}

    def send_sums(step, peers):
        for k, peer in enumerate(peers):
            sums_copies[step, k] = send(sums_send.at[step], sums_recv.at[step, k], peer)

    def add_sums(step, members):
        value = sums_send[step]
        for k in range(members - 1):
            sums_copies[step, k].wait_recv()
            value = value + sums_recv[step, k]
        sums_send[step + 1] = value

    send_sums(0, dp_ids)
    inner_copy.wait_recv()
    inner = (inner_send[...] + inner_recv[...]) / D
    for u in range(subs):
        at = slice(u * piece, (u + 1) * piece)
        result[:, at] = (
            middle[:, at]
            + inverse[:, at] * (own[u] * gain)
            - tokens[:, at].astype(FULL)
            * (inverse[:, at] * inverse[:, at] * inverse[:, at] * inner[:, at])
        )
    stored.append(move(result, result_hbm))
    add_sums(0, n_dp)
    send_sums(1, col_ids)
    finish_part(1)

    add_sums(1, n_col)
    sums_copy = send(sums_send.at[2], last_sums, sibling_id)
    sums_copy.wait_recv()
    sums_out[0] = sums_send[2]
    sums_out[1] = last_sums[...]
    for copy in out_copies:
        copy.wait_recv()
    for copy in stored:
        copy.wait()
    for copy in sent:
        copy.wait_send()


def tail(n_dp, n_pair, gain, inverse, sums, qkv, dq, dk, dv, normed, tokens, middle, grads, downs):
    width, here = tokens.shape
    length = normed.shape[1]
    cols = dq.shape[0]
    unit = downs[0].shape[0]
    rows_d = unit // n_dp
    share = width // n_dp
    subs = 2
    piece = here // subs
    n_col = 2 * n_pair
    part = grads[0].shape[1:]
    wide = 3 * cols
    count = 2 * n_pair * subs + 10 * n_dp + 2 * n_col + 14
    moves = 15 + n_dp + n_col
    hbm = pl.BlockSpec(memory_space=pl.ANY)
    vmem = pl.BlockSpec(memory_space=pltpu.VMEM)
    V = pltpu.VMEM
    halves = V((2, share // 2, wide), LOW)
    return pl.pallas_call(
        functools.partial(tail_kernel, n_dp, n_pair),
        out_shape=(
            jax.ShapeDtypeStruct((width, here), FULL),
            jax.ShapeDtypeStruct((n_dp, share, wide), LOW),
            jax.ShapeDtypeStruct((n_dp,) + part, LOW),
            jax.ShapeDtypeStruct((n_dp, rows_d, width), LOW),
            jax.ShapeDtypeStruct((2,) + sums.shape, FULL),
        ),
        in_specs=[vmem] * 3 + [hbm] * (7 + n_dp + n_col),
        out_specs=(hbm,) * 4 + (vmem,),
        scratch_shapes=[
            V((2 * width, wide), LOW),
            V((wide, length), LOW),
            V((2 * width, length), LOW),
            V((width, here), LOW),
            V((width, here), FULL),
            V((width, here), FULL),
            V((n_pair, subs, width, piece), LOW),
            V((n_pair, subs, width, piece), LOW),
            V((subs, width, piece), FULL),
            V((n_pair - 1, subs, width, piece), LOW),
            V((n_pair - 1, subs, width, piece), LOW),
            V((n_dp - 1, 2, share, wide), LOW),
            V((n_dp - 1, 2, share, wide), LOW),
            V((2, share, wide), FULL),
            halves,
            halves,
            halves,
            halves,
            halves,
            V((n_dp, n_col) + part, LOW),
            V((n_col - 1,) + part, LOW),
            V((n_col - 1,) + part, LOW),
            V(part, LOW),
            V((n_col - 2, unit, width), LOW),
            V((n_dp * rows_d, width), LOW),
            V((n_dp - 1, rows_d, width), LOW),
            V((rows_d, width), LOW),
            V((2, rows_d, width), LOW),
            V((n_dp - 1, 2, rows_d, width), LOW),
            V((2, rows_d, width), LOW),
            V((2, rows_d, width), LOW),
            V((1, here), FULL),
            V((1, here), FULL),
            V((3,) + sums.shape, FULL),
            V((2, max(n_dp, n_col) - 1) + sums.shape, FULL),
            V(sums.shape, FULL),
            pltpu.SemaphoreType.DMA((count,)),
            pltpu.SemaphoreType.DMA((count,)),
            pltpu.SemaphoreType.DMA((moves,)),
        ],
        compiler_params=pltpu.CompilerParams(
            collective_id=1, has_side_effects=True, vmem_limit_bytes=62 * 2**20
        ),
        cost_estimate=pl.CostEstimate(
            flops=8 * wide * width * length, bytes_accessed=2**25, transcendentals=0
        ),
    )(gain, inverse, sums, qkv, dq, dk, dv, normed, tokens, middle, *grads, *downs)


def on_device(
    tokens,
    segment_ids,
    padding_mask,
    w_qkv,
    w_out,
    w_up,
    w_down,
    gain_attn,
    gain_mlp,
    scale_raw,
    cotangent,
):
    width, here = tokens.shape
    r, s = lax.axis_index("row"), lax.axis_index("cs")
    j, d = lax.axis_index("cp"), lax.axis_index("dp")
    n_pair, n_dp, n_col = lax.axis_size("cp"), lax.axis_size("dp"), lax.axis_size(COLS)
    c = s * n_pair + j
    head_cols = w_qkv.shape[0] // (3 * width)
    heads = head_cols // HEAD
    near = r == s

    ids = jnp.concatenate([segment_ids, padding_mask], 0)
    ids = jnp.where(s == r, ids, sibling(ids))
    segments, padding = ids[0], ids[1]
    length = segments.shape[0]
    firsts = segments[::BLOCK]
    starts = jnp.sum((segments[None, :] < firsts[:, None]).astype(jnp.int32), axis=1)
    filled = (jnp.sum(padding) + BLOCK - 1) // BLOCK
    blocks = jnp.arange(length // BLOCK, dtype=jnp.int32)
    lo = starts // BLOCK
    hi = jnp.minimum(blocks, filled)
    gains_in = jnp.stack([gain_attn, gain_mlp])
    factor = jnp.stack([jnp.log1p(jnp.exp(scale_raw)), jax.nn.sigmoid(scale_raw)])
    factor = LOG_TWO_E / math.sqrt(HEAD) * factor

    block = w_qkv.reshape(width, 3 * head_cols)
    down = w_down.reshape(-1, width)
    unit = down.shape[0]
    part_rows = quarter_rows(unit, n_dp)

    def quarters(matrix):
        padded = jnp.pad(matrix, ((0, n_dp * part_rows - unit), (0, 0)))
        return padded.reshape(n_dp, part_rows, width)

    out = lax.dynamic_index_in_dim(quarters(w_out.reshape(-1, width)), d, 0, keepdims=False)
    up = lax.dynamic_index_in_dim(quarters(w_up.reshape(width, -1).T), d, 0, keepdims=False)
    (
        queries, key_heads, values, query_raw, normed_one, qkv, out_all, ups, cot_other,
        inverse_one,
    ) = head(
        n_dp, n_pair, gains_in, factor, tokens, cotangent, block, out, up,
        quarters(down),
    )
    ups = gather(ups, "dp")
    downs = [down] + [
        lax.ppermute(down, COLS, [(i, i ^ k) for i in range(n_col)])
        for k in range(2, n_col)
        if k != n_pair + 1
    ]
    attended, logs = attention_forward(queries, key_heads, values, ids, ids, lo, hi)
    result, grad_middle, grad_attended, grads, down_grads, gain_two_part = middle_part(
        n_dp, n_pair, gains_in, attended, tokens, cotangent, cot_other, out_all, ups, downs
    )
    received = [grads[0]] + [shift(grads[k], "dp", k) for k in range(1, n_dp)]
    down_received = [
        down_grads[k]
        if k in (0, 1, n_pair + 1)
        else lax.ppermute(down_grads[k], COLS, [(i, i ^ k) for i in range(n_col)])
        for k in range(n_col)
    ]

    dq, dk, dv, sums = attention_backward(
        queries, key_heads, values, attended, grad_attended, logs, query_raw, factor, gain_two_part,
        ids, ids, lo, hi,
    )
    grad_tokens, grad_qkv, final, final_down, sums = tail(
        n_dp, n_pair, gains_in, inverse_one, sums, qkv, dq, dk, dv, normed_one, tokens,
        grad_middle, received, down_received,
    )
    grad_qkv = grad_qkv.astype(FULL)
    final = final.reshape(-1, width)
    final = [final[i * unit:(i + 1) * unit].astype(FULL) for i in range(2)]
    final.append(final_down.reshape(-1, width)[:unit].astype(FULL))
    own, other = sums[0], sums[1]
    first = r == 0
    gains = jnp.concatenate(
        [jnp.where(first, own[:2], other[:2]), jnp.where(first, other[:2], own[:2])], 1
    )
    scale_total = (own[2] + other[2])[:HEAD]
    return (
        result,
        grad_tokens,
        grad_qkv.reshape(-1),
        final[0].reshape(-1),
        final[1].T.reshape(-1),
        final[2].reshape(-1),
        gains[0],
        gains[1],
        scale_total,
    )


def solution(mesh):
    n_dp, n_row, n_col = (mesh.shape[name] for name in ("dp", "row", "col"))
    split = Mesh(
        np.asarray(mesh.devices).reshape(n_dp, n_row, n_row, n_col // n_row),
        ("dp", "row", "cs", "cp"),
    )
    rows = P("row", ("dp", "cs", "cp"))
    ids = P(("dp", "row"), None)
    blocks = P(("row", "cs", "cp"))
    return jax.shard_map(
        on_device,
        mesh=split,
        in_specs=(rows, ids, ids, blocks, blocks, blocks, blocks, P(), P(), P(), rows),
        out_specs=(rows, rows, blocks, blocks, blocks, blocks, P(), P(), P()),
        check_vma=False,
    )
```

```python
import functools
import math

import jax
import jax.numpy as jnp
import numpy as np
from jax import lax
from jax.experimental import pallas as pl
from jax.experimental.pallas import tpu as pltpu
from jax.sharding import Mesh, PartitionSpec as P

D = 1280
HEAD = 80
EPSILON = 1e-06
LOG_TWO_E = 1.442695041
BLOCK = 256
LOW = jnp.bfloat16
FULL = jnp.float32
COLS = ("cs", "cp")


def mm(left, right, left_axis, right_axis):
    return lax.dot_general(
        left, right, (((left_axis,), (right_axis,)), ((), ())), preferred_element_type=FULL
    )


def shift(x, axis, k):
    n = lax.axis_size(axis)
    return lax.ppermute(x, axis, [(i, i ^ k) for i in range(n)])


def sibling(x):
    return shift(x, "row", 1)


def cut(x, index, count, axis):
    step = x.shape[axis] // count
    return lax.dynamic_slice_in_dim(x, index * step, step, axis)


def gather(x, axis):
    return [x] + [shift(x, axis, k) for k in range(1, lax.axis_size(axis))]


def diag_mask(segq, segk):
    size = segk.shape[0], segq.shape[1]
    ki = lax.broadcasted_iota(jnp.int32, size, 0)
    qi = lax.broadcasted_iota(jnp.int32, size, 1)
    return ((segk == segq) & (ki <= qi)) | (ki == qi)


def half_row(ref, which):
    size = ref.shape[1] // 2
    return jnp.where(which == 0, ref[:, :size], ref[:, size:])


def column(row):
    return jnp.broadcast_to(row, (8, row.shape[1])).T[:, :1]


def rows_of(h):
    return slice(h * HEAD, (h + 1) * HEAD)


def forward_kernel(heads, lo_ref, hi_ref, q_ref, k_ref, v_ref, segq_ref, segk_ref, o_ref, log_ref, ks, segks):
    i = pl.program_id(0)

    here = pl.ds(pl.multiple_of(i * BLOCK, BLOCK), BLOCK)
    for h in range(heads):
        ks[h, here, :] = k_ref[rows_of(h), here].T
    segks[here, :] = column(jnp.where(segk_ref[1:, here] == 1, segk_ref[:1, here], -1).astype(FULL))
    segq = segq_ref[:1].astype(FULL)

    def visit(kb, carry, diagonal):
        at = pl.ds(pl.multiple_of(kb * BLOCK, BLOCK), BLOCK)
        segk = segks[at, :]
        mask = diag_mask(segq, segk) if diagonal else segk == segq
        scores = [
            jnp.dot(ks[h, at, :], q_ref[rows_of(h), :], preferred_element_type=FULL)
            for h in range(heads)
        ]
        peaks, totals, weights = [], [], []
        for h in range(heads):
            s = jnp.where(mask, scores[h], -1e30)
            peak = jnp.max(s, axis=0, keepdims=True)
            if not diagonal:
                peak = jnp.maximum(carry[h][0], peak)
            p = jnp.exp(s - peak)
            peaks.append(peak)
            totals.append(jnp.sum(p, axis=0, keepdims=True))
            weights.append(p.astype(LOW))
        out = []
        for h in range(heads):
            new = jnp.dot(v_ref[rows_of(h), at], weights[h], preferred_element_type=FULL)
            total = totals[h]
            if not diagonal:
                m, l, acc = carry[h]
                keep = jnp.exp(m - peaks[h])
                total = l * keep + total
                new = acc * keep + new
            out.append((peaks[h], total, new))
        return tuple(out)

    carry = visit(i, None, True)
    carry = lax.fori_loop(lo_ref[i], hi_ref[i], lambda kb, c: visit(kb, c, False), carry)
    for h in range(heads):
        m, l, acc = carry[h]
        o_ref[h * HEAD:(h + 1) * HEAD, :] = (acc / l).astype(LOW)
        log_ref[h] = m + jnp.log(l)


def attention_forward(q, k, v, segq, segk, lo, hi):
    cols, length = q.shape
    heads = cols // HEAD
    steps = length // BLOCK
    whole = pl.BlockSpec((cols, length), lambda i, *_: (0, 0))
    part = pl.BlockSpec((cols, BLOCK), lambda i, *_: (0, i))
    return pl.pallas_call(
        functools.partial(forward_kernel, heads),
        out_shape=(
            jax.ShapeDtypeStruct((cols, length), LOW),
            jax.ShapeDtypeStruct((heads, 1, length), FULL),
        ),
        grid_spec=pltpu.PrefetchScalarGridSpec(
            num_scalar_prefetch=2,
            grid=(steps,),
            in_specs=[
                part,
                whole,
                whole,
                pl.BlockSpec((2, BLOCK), lambda i, *_: (0, i)),
                pl.BlockSpec((2, length), lambda i, *_: (0, 0)),
            ],
            out_specs=(part, pl.BlockSpec((heads, 1, BLOCK), lambda i, *_: (0, 0, i))),
            scratch_shapes=[pltpu.VMEM((heads, length, HEAD), LOW), pltpu.VMEM((length, 1), FULL)],
        ),
        compiler_params=pltpu.CompilerParams(vmem_limit_bytes=62 * 2**20),
        cost_estimate=pl.CostEstimate(
            flops=8 * 2 * length * length * cols,
            bytes_accessed=4 * cols * length * 2,
            transcendentals=heads * length * length // 3,
        ),
    )(lo, hi, q, k, v, segq, segk)


def backward_kernel(
    heads, lo_ref, hi_ref, q_ref, k_ref, v_ref, o_ref, go_ref, log_ref, raw_ref, factor_ref, slope_ref,
    gain_ref, segq_ref, segk_ref, dq_ref, dk_ref, dv_ref, sums_ref, ks, vs, qs, gs, dks, dvs, dqs, segks, total,
):
    i = pl.program_id(0)

    @pl.when(i == 0)
    def _():
        sums_ref[...] = jnp.zeros_like(sums_ref)
        total[...] = jnp.zeros_like(total)

    here = pl.ds(pl.multiple_of(i * BLOCK, BLOCK), BLOCK)
    for h in range(heads):
        ks[h, here, :] = k_ref[rows_of(h), here].T
        vs[h, here, :] = v_ref[rows_of(h), here].T
    segks[here, :] = column(jnp.where(segk_ref[1:, here] == 1, segk_ref[:1, here], -1).astype(FULL))
    segq = segq_ref[:1].astype(FULL)
    inner = [
        jnp.sum(
            o_ref[h * HEAD:(h + 1) * HEAD, :].astype(FULL)
            * go_ref[h * HEAD:(h + 1) * HEAD, :].astype(FULL),
            axis=0,
            keepdims=True,
        )
        for h in range(heads)
    ]

    for h in range(heads):
        qs[h] = q_ref[rows_of(h), :].T
        gs[h] = go_ref[rows_of(h), :].T

    def visit(kb, diagonal):
        at = pl.ds(pl.multiple_of(kb * BLOCK, BLOCK), BLOCK)
        segk = segks[at, :]
        mask = diag_mask(segq, segk) if diagonal else segk == segq
        scores = [
            jnp.dot(ks[h, at, :], q_ref[rows_of(h), :], preferred_element_type=FULL)
            for h in range(heads)
        ]
        dps = [
            jnp.dot(vs[h, at, :], go_ref[rows_of(h), :], preferred_element_type=FULL)
            for h in range(heads)
        ]
        ps, dss = [], []
        for h in range(heads):
            p = jnp.where(mask, jnp.exp(scores[h] - log_ref[h]), 0.0)
            dss.append((p * (dps[h] - inner[h])).astype(LOW))
            ps.append(p.astype(LOW))
        for h in range(heads):
            new_v = jnp.dot(ps[h], gs[h], preferred_element_type=FULL)
            new_k = jnp.dot(dss[h], qs[h], preferred_element_type=FULL)
            new_q = jnp.dot(k_ref[rows_of(h), at], dss[h], preferred_element_type=FULL)
            if diagonal:
                dvs[h, at, :], dks[h, at, :], dqs[rows_of(h), :] = new_v, new_k, new_q
            else:
                dvs[h, at, :] += new_v
                dks[h, at, :] += new_k
                dqs[rows_of(h), :] += new_q

    visit(i, True)

    @pl.loop(lo_ref[i], hi_ref[i])
    def _(kb):
        visit(kb, False)

    factor = column(factor_ref[...])
    part = jnp.zeros((HEAD, 1), FULL)
    for h in range(heads):
        rows = slice(h * HEAD, (h + 1) * HEAD)
        dq = dqs[rows, :]
        part = part + jnp.sum(dq * raw_ref[rows, :], axis=1, keepdims=True)
        dq_ref[rows, :] = (dq * factor).astype(LOW)
    total[...] += part

    @pl.when(i == pl.num_programs(0) - 1)
    def _():
        for h in range(heads):
            dk_ref[rows_of(h), :] = dks[h].astype(LOW).T
            dv_ref[rows_of(h), :] = dvs[h].astype(LOW).T
        sums_ref[1:2, :] = gain_ref[...]
        row = jnp.broadcast_to(total[...], (HEAD, 128)).T[:1]
        sums_ref[2:3, :HEAD] = row * slope_ref[...]


def attention_backward(q, k, v, o, go, logs, raw, factor, slope, gain_part, segq, segk, lo, hi):
    cols, length = q.shape
    heads = cols // HEAD
    steps = length // BLOCK
    whole = pl.BlockSpec((cols, length), lambda i, *_: (0, 0))
    part = pl.BlockSpec((cols, BLOCK), lambda i, *_: (0, i))
    width = gain_part.shape[1]
    total = pl.BlockSpec((8, width), lambda i, *_: (0, 0))
    shape = jax.ShapeDtypeStruct((cols, length), LOW)
    return pl.pallas_call(
        functools.partial(backward_kernel, heads),
        out_shape=(shape, shape, shape, jax.ShapeDtypeStruct((8, width), FULL)),
        grid_spec=pltpu.PrefetchScalarGridSpec(
            num_scalar_prefetch=2,
            grid=(steps,),
            in_specs=[
                part,
                whole,
                whole,
                part,
                part,
                pl.BlockSpec((heads, 1, BLOCK), lambda i, *_: (0, 0, i)),
                part,
                pl.BlockSpec((1, HEAD), lambda i, *_: (0, 0)),
                pl.BlockSpec((1, HEAD), lambda i, *_: (0, 0)),
                pl.BlockSpec((1, width), lambda i, *_: (0, 0)),
                pl.BlockSpec((2, BLOCK), lambda i, *_: (0, i)),
                pl.BlockSpec((2, length), lambda i, *_: (0, 0)),
            ],
            out_specs=(part, whole, whole, total),
            scratch_shapes=[
                pltpu.VMEM((heads, length, HEAD), LOW),
                pltpu.VMEM((heads, length, HEAD), LOW),
                pltpu.VMEM((heads, BLOCK, HEAD), LOW),
                pltpu.VMEM((heads, BLOCK, HEAD), LOW),
                pltpu.VMEM((heads, length, HEAD), FULL),
                pltpu.VMEM((heads, length, HEAD), FULL),
                pltpu.VMEM((cols, BLOCK), FULL),
                pltpu.VMEM((length, 1), FULL),
                pltpu.VMEM((HEAD, 1), FULL),
            ],
        ),
        compiler_params=pltpu.CompilerParams(vmem_limit_bytes=62 * 2**20),
        cost_estimate=pl.CostEstimate(
            flops=8 * 5 * length * length * cols,
            bytes_accessed=8 * cols * length * 2,
            transcendentals=heads * length * length // 3,
        ),
    )(lo, hi, q, k, v, o, go, logs, raw, factor, slope, gain_part, segq, segk)


def remote(src, dst, sems, index, device):
    return pltpu.make_async_remote_copy(
        src_ref=src,
        dst_ref=dst,
        send_sem=sems[0].at[index],
        recv_sem=sems[1].at[index],
        device_id=device,
        device_id_type=pl.DeviceIdType.MESH,
    )


def greet(peers):
    barrier = pltpu.get_barrier_semaphore()
    for peer in peers:
        pl.semaphore_signal(barrier, inc=1, device_id=peer, device_id_type=pl.DeviceIdType.MESH)
    pl.semaphore_wait(barrier, len(peers))


def head_kernel(
    n_dp, n_pair, gain_ref, factor_ref, tokens_hbm, cot_hbm, block_hbm, out_hbm, up_hbm,
    down_hbm, q_hbm, k_hbm, v_hbm, raw_hbm, normed_hbm, qkv_hbm, out_all, ups_hbm, cot_out, inverse_ref,
    tokens, others, block, cs_recv, remote_block, pass_on, qkv, turned, normed, q, k, v, raw,
    send_sems, recv_sems, local_sems,
):
    r, s = lax.axis_index("row"), lax.axis_index("cs")
    j, d = lax.axis_index("cp"), lax.axis_index("dp")
    n_col = 2 * n_pair
    subs, width, piece = tokens.shape[1:]
    here = subs * piece
    share = cs_recv.shape[0]
    cols = q.shape[0]
    c_first = (s * n_pair + j) ^ (r * n_pair)
    near = r == s
    sems = (send_sems, recv_sems)
    counter, local_counter = iter(range(1000)), iter(range(1000))
    sent, stored = [], []

    def send(src, dst, device):
        copy = remote(src, dst, sems, next(counter), device)
        copy.start()
        sent.append(copy)
        return copy

    def move(src, dst):
        copy = pltpu.make_async_copy(src, dst, local_sems.at[next(local_counter)])
        copy.start()
        return copy

    def store(src, dst):
        stored.append(move(src, dst))

    def columns(u):
        return pl.ds(u * piece, piece)

    own_tokens = [move(tokens_hbm.at[:, columns(u)], tokens.at[0, u]) for u in range(subs)]
    own_block = move(block_hbm, block)
    own_out = move(out_hbm, out_all.at[d, c_first])
    store(up_hbm, ups_hbm.at[c_first])
    sibling_id = {"row": 1 - r}
    dp_ids = [{"dp": d ^ k} for k in range(1, n_dp)]
    col_ids = [{"cs": s ^ (k // n_pair), "cp": j ^ (k % n_pair)} for k in range(1, n_col)]
    greet([sibling_id] + dp_ids + col_ids)

    cs_copy = send(block_hbm.at[d], cs_recv, {"cs": 1 - s})
    down_ids = [col_ids[0], col_ids[n_pair]]
    down_copies = [
        send(down_hbm.at[d], ups_hbm.at[n_col + m], peer) for m, peer in enumerate(down_ids)
    ]
    out_copies = [send(out_hbm, out_all.at[d, c_first], peer) for peer in col_ids]
    other_copies = {}
    for u in range(subs):
        other_copies[0, u] = send(tokens_hbm.at[:, columns(u)], others.at[0, u], sibling_id)
    pair_copies = {}

    def send_pairs(u):
        for m in range(1, n_pair):
            pair_copies[m, u] = send(
                tokens_hbm.at[:, columns(u)], tokens.at[m, u], {"cp": j ^ m}
            )

    send_pairs(0)

    cot_copy = send(cot_hbm, cot_out, sibling_id)
    gain_own = column(half_row(gain_ref, r))
    gain_other = column(half_row(gain_ref, 1 - r))
    factor = jnp.concatenate([column(factor_ref[...])] * (cols // HEAD), 0)

    def norm(m, u):
        own, other = tokens[m, u].astype(FULL), others[m, u].astype(FULL)
        squares = jnp.sum(own * own, axis=0, keepdims=True)
        squares = squares + jnp.sum(other * other, axis=0, keepdims=True)
        inverse = lax.rsqrt(squares / D + EPSILON)
        at = pl.ds(pl.multiple_of((j ^ m) * here + u * piece, 128), piece)
        normed[:width, at] = (own * inverse * gain_own).astype(LOW)
        normed[width:, at] = (other * inverse * gain_other).astype(LOW)
        store(normed.at[:, at], normed_hbm.at[:, at])
        if m == 0:
            inverse_ref[:, columns(u)] = inverse

    def project(m, u):
        at = pl.ds(pl.multiple_of((j ^ m) * here + u * piece, 128), piece)
        for part, out in ((0, None), (1, k), (2, v)):
            value = jnp.dot(
                turned[part * cols:(part + 1) * cols, :], normed[:, at],
                preferred_element_type=FULL,
            )
            if part == 0:
                raw[:, at] = value
                q[:, at] = (value * factor).astype(LOW)
            else:
                out[:, at] = value.astype(LOW)
        for src, dst in ((q, q_hbm), (k, k_hbm), (v, v_hbm), (raw, raw_hbm)):
            store(src.at[:, at], dst.at[:, at])

    for u in range(subs):
        own_tokens[u].wait()
        other_copies[0, u].wait_recv()
        norm(0, u)
    own_block.wait()

    cs_copy.wait_recv()
    send_pairs(1)
    dp_copies = [send(cs_recv, remote_block.at[d], peer) for peer in dp_ids]
    own_out.wait()
    for copy in out_copies:
        copy.wait_recv()
    late_copies = [send(out_all.at[d], out_all.at[d], peer) for peer in dp_ids]
    remote_block[d] = cs_recv[...]
    for u in range(subs - 1):
        for m in range(1, n_pair):
            pair_copies[m, u].wait_recv()
            other_copies[m, u] = send(tokens.at[m, u], others.at[m, u], sibling_id)
    cross_copies = []
    for m in range(n_dp):
        owner = d ^ m
        if m:
            dp_copies[m - 1].wait_recv()
        mine, its = block[owner], remote_block[owner]
        at = pl.multiple_of(owner * share, 32)
        qkv[pl.ds(at, share)] = jnp.where(near, mine, its)
        pass_on[owner] = jnp.where(near, its, mine)
        cross_copies.append(
            send(pass_on.at[owner], qkv.at[pl.ds(width + at, share)], sibling_id)
        )
    u = subs - 1
    for m in range(1, n_pair):
        pair_copies[m, u].wait_recv()
        other_copies[m, u] = send(tokens.at[m, u], others.at[m, u], sibling_id)
    late_copies += [send(up_hbm, ups_hbm.at[c_first], peer) for peer in col_ids]
    turned[:, :width] = qkv[:width].T
    for copy in cross_copies:
        copy.wait_recv()
    turned[:, width:] = qkv[width:].T
    store(qkv, qkv_hbm)

    for u in range(subs):
        project(0, u)
    for u in range(subs):
        for m in range(1, n_pair):
            other_copies[m, u].wait_recv()
            norm(m, u)
            project(m, u)

    for copy in stored:
        copy.wait()
    for copy in late_copies + down_copies + [cot_copy]:
        copy.wait_recv()
    for copy in sent:
        copy.wait_send()


def head(n_dp, n_pair, gain, factor, tokens, cotangent, block, out, up, down):
    width, here = tokens.shape
    wide = block.shape[1]
    cols = wide // 3
    share = width // n_dp
    length = n_pair * here
    n_col = 2 * n_pair
    subs = 2
    piece = here // subs
    count = subs * n_pair * 2 + 4 * n_dp + 2 * n_col + 7
    moves = 4 + subs + 5 * subs * n_pair + 4
    hbm = pl.BlockSpec(memory_space=pl.ANY)
    vmem = pl.BlockSpec(memory_space=pltpu.VMEM)
    V = pltpu.VMEM
    shape = jax.ShapeDtypeStruct((cols, length), LOW)
    return pl.pallas_call(
        functools.partial(head_kernel, n_dp, n_pair),
        out_shape=(
            shape,
            shape,
            shape,
            jax.ShapeDtypeStruct((cols, length), FULL),
            jax.ShapeDtypeStruct((2 * width, length), LOW),
            jax.ShapeDtypeStruct((2 * width, wide), LOW),
            jax.ShapeDtypeStruct((n_dp, n_col) + out.shape, LOW),
            jax.ShapeDtypeStruct((n_col + 2,) + up.shape, LOW),
            jax.ShapeDtypeStruct((width, here), LOW),
            jax.ShapeDtypeStruct((1, here), FULL),
        ),
        in_specs=[vmem] * 2 + [hbm] * 6,
        out_specs=(hbm,) * 9 + (vmem,),
        scratch_shapes=[
            V((n_pair, subs, width, piece), LOW),
            V((n_pair, subs, width, piece), LOW),
            V((n_dp, share, wide), LOW),
            V((share, wide), LOW),
            V((n_dp, share, wide), LOW),
            V((n_dp, share, wide), LOW),
            V((2 * width, wide), LOW),
            V((wide, 2 * width), LOW),
            V((2 * width, length), LOW),
            V((cols, length), LOW),
            V((cols, length), LOW),
            V((cols, length), LOW),
            V((cols, length), FULL),
            pltpu.SemaphoreType.DMA((count,)),
            pltpu.SemaphoreType.DMA((count,)),
            pltpu.SemaphoreType.DMA((moves,)),
        ],
        compiler_params=pltpu.CompilerParams(
            collective_id=2, has_side_effects=True, vmem_limit_bytes=60 * 2**20
        ),
        cost_estimate=pl.CostEstimate(
            flops=4 * wide * width * length, bytes_accessed=2**25, transcendentals=0
        ),
    )(gain, factor, tokens, cotangent, block.reshape(n_dp, share, wide), out, up, down)


def middle_kernel(n_dp, n_pair, unit, gain_ref, att_hbm, tokens_hbm, cot_hbm, cot_other, out_all, *refs):
    n_col = 2 * n_pair
    up_hbms, refs = refs[:n_dp], refs[n_dp:]
    down_hbms, refs = refs[:n_col - 2], refs[n_col - 2:]
    result_hbm, middle_hbm, out_hbm, refs = refs[0], refs[1], refs[2], refs[3:]
    grads_hbms, refs = refs[:n_dp], refs[n_dp:]
    down_outs, refs = refs[:n_col], refs[n_col:]
    (
        gain_out, tokens, cot, out_slab, up_slab, down_slab, out_w, up_w, down_w, out_t, up_t, down_t, out_half, up_half,
        down_half, att, scaled, normed, active, grad_hidden, branch, middle, grad, result, grad_att,
        grads, down_grads, square_send, square_recv, inner_send, inner_recv, inverse, narrow,
        send_sems, recv_sems, local_sems,
    ) = refs
    r, s = lax.axis_index("row"), lax.axis_index("cs")
    j, d = lax.axis_index("cp"), lax.axis_index("dp")
    width, here = tokens.shape
    pieces, _, piece = square_send.shape
    cols = att_hbm.shape[0]
    half = n_col * unit // 2
    rows_q = up_hbms[0].shape[1]
    rows_g = grads_hbms[0].shape[1]
    c_first = (s * n_pair + j) ^ (r * n_pair)
    sems = (send_sems, recv_sems)
    gain = column(half_row(gain_ref, r))
    counter, local_counter = iter(range(1000)), iter(range(1000))
    sent, stored = [], []

    def send(src, dst, device):
        copy = remote(src, dst, sems, next(counter), device)
        copy.start()
        sent.append(copy)
        return copy

    def move(src, dst):
        copy = pltpu.make_async_copy(src, dst, local_sems.at[next(local_counter)])
        copy.start()
        return copy

    def columns(u):
        return pl.ds(u * piece, piece)

    def span(u):
        return slice(u * piece, (u + 1) * piece)

    def down_rows(owner):
        return pl.ds(pl.multiple_of(owner * unit, 16), unit)

    def quarter_of(owner):
        return pl.ds(pl.multiple_of(owner * rows_q, 16), rows_q)

    quartered = (1, n_pair + 1)
    own_rows, other_rows = pl.ds(0, width), pl.ds(width, width)
    weight_loads = [
        move(out_all.at[m], out_slab.at[:, pl.ds(m * rows_q, rows_q)]) for m in range(n_dp)
    ] + [
        move(up_hbms[m].at[pl.ds(first, size)], target.at[:, quarter_of(d ^ m)])
        for m in range(n_dp)
        for first, size, target in ((0, n_col, up_slab), (n_col, 2, down_slab))
    ] + [
        move(ref, down_w.at[down_rows(c_first ^ m)])
        for m, ref in zip([m for m in range(n_col) if m not in quartered], down_hbms)
    ]
    att_loads = [
        move(
            att_hbm.at[:, pl.ds(pl.multiple_of(j * here + u * piece, 128), piece)],
            att.at[pl.ds(pl.multiple_of(j * cols, 16), cols), columns(u)],
        )
        for u in range(pieces)
    ]
    token_load = move(tokens_hbm, tokens)
    cot_loads = [move(cot_hbm, cot.at[own_rows]), move(cot_other, cot.at[other_rows])]
    sibling_id = {"row": 1 - r}
    pair_ids = [{"cp": j ^ m} for m in range(1, n_pair)]
    greet([sibling_id] + pair_ids)

    att_copies = {}
    for u in range(pieces):
        for m in range(1, n_pair):
            att_copies[u, m] = send(
                att_hbm.at[:, pl.ds(pl.multiple_of((j ^ m) * here + u * piece, 128), piece)],
                att.at[pl.ds(pl.multiple_of(j * cols, 16), cols), columns(u)],
                pair_ids[m - 1],
            )

    for copy in weight_loads:
        copy.wait()
    for m in range(n_col):
        at = slice(m * unit, (m + 1) * unit)
        out_w[at] = out_slab[m, :unit]
        up_w[at] = up_slab[m, :unit]
    for m, k in enumerate(quartered):
        down_w[down_rows(c_first ^ k)] = down_slab[m, :unit]
    cross_copies = []

    def cross(whole, part):
        cross_copies.append(send(whole.at[pl.ds(half, half)], part.at[:, other_rows], sibling_id))
        part[:, :width] = whole[:half]

    cross(up_w, up_half)
    cross(down_w, down_half)
    cross(out_w, out_half)
    out_t[...] = out_w[...].T
    narrow[...] = jnp.zeros_like(narrow)

    copies = {}

    def exchange(name, u, ref):
        copies[name, u] = send(
            ref.at[own_rows, columns(u)], ref.at[other_rows, columns(u)], sibling_id
        )

    def share_heads(u):
        att_loads[u].wait()
        for m in range(1, n_pair):
            att_copies[u, m].wait_recv()
        exchange("att", u, att)

    def first_branch(u):
        if u == 0:
            token_load.wait()
        copies["att", u].wait_recv()
        value = tokens[:, span(u)].astype(FULL) + jnp.dot(
            out_t[...], att[:, span(u)], preferred_element_type=FULL
        )
        scaled[:width, span(u)] = (value * gain).astype(LOW)
        exchange("scaled", u, scaled)
        square_send[u] = jnp.sum(value * value, axis=0, keepdims=True)
        copies["square", u] = send(square_send.at[u], square_recv.at[u], sibling_id)
        middle[:, span(u)] = value

    def hidden_units(u):
        if u == 0:
            for copy in cot_loads:
                copy.wait()
            for copy in cross_copies:
                copy.wait_recv()
            up_t[...] = up_w[...].T
            down_t[...] = down_w[...].T
        grad_active = jnp.dot(down_half[...], cot[:, span(u)], preferred_element_type=FULL)
        copies["scaled", u].wait_recv()
        copies["square", u].wait_recv()
        scale = lax.rsqrt((square_send[u] + square_recv[u]) / D + EPSILON)
        inverse[u] = scale
        hidden = scale * jnp.dot(up_half[...], scaled[:, span(u)], preferred_element_type=FULL)
        sigmoid = jax.nn.sigmoid(hidden)
        value = (grad_active * sigmoid * (1.0 + hidden * (1.0 - sigmoid))).astype(LOW)
        grad_hidden[:half, span(u)] = value
        exchange("grad_hidden", u, grad_hidden)
        active[:half, span(u)] = (hidden * sigmoid).astype(LOW)
        exchange("active", u, active)
        inner_send[u] = jnp.sum(value.astype(FULL) * hidden, axis=0, keepdims=True)
        copies["inner", u] = send(inner_send.at[u], inner_recv.at[u], sibling_id)
        normed[:, span(u)] = (middle[:, span(u)] * scale * gain).astype(LOW)

    def second_branch(u):
        copies["grad_hidden", u].wait_recv()
        copies["inner", u].wait_recv()
        scale = inverse[u]
        inner = scale * scale * ((inner_send[u] + inner_recv[u]) / D)
        back = jnp.dot(up_t[...], grad_hidden[:, span(u)], preferred_element_type=FULL)
        value = (
            cot[:width, span(u)].astype(FULL)
            + scale * (back * gain)
            - middle[:, span(u)] * inner
        )
        branch[:width, span(u)] = value.astype(LOW)
        exchange("branch", u, branch)
        grad[:, span(u)] = value
        stored.append(move(grad.at[:, columns(u)], middle_hbm.at[:, columns(u)]))
        product = back * middle[:, span(u)] * scale
        total = narrow[...]
        for v in range(piece // 128):
            total = total + product[:, v * 128:(v + 1) * 128]
        narrow[...] = total
        copies["active", u].wait_recv()
        result[:, span(u)] = middle[:, span(u)] + jnp.dot(
            down_t[...], active[:, span(u)], preferred_element_type=FULL
        )
        stored.append(move(result.at[:, columns(u)], result_hbm.at[:, columns(u)]))

    def heads_back(u):
        copies["branch", u].wait_recv()
        grad_att[:, span(u)] = jnp.dot(
            out_half[...], branch[:, span(u)], preferred_element_type=FULL
        ).astype(LOW)
        target = pl.ds(pl.multiple_of(j * here + u * piece, 128), piece)
        for m in range(n_pair):
            source = grad_att.at[
                pl.ds(pl.multiple_of((j ^ m) * cols, 16), cols), columns(u)
            ]
            if m:
                copies["out", u, m] = send(source, out_hbm.at[:, target], pair_ids[m - 1])
            else:
                stored.append(move(source, out_hbm.at[:, target]))

    stages = (share_heads, first_branch, hidden_units, second_branch, heads_back)
    turned = {}

    def product(name, first, left, right, target, at):
        if name not in turned:
            turned[name] = right[:width].T
        count = n_col // 2
        for n in range(0 if first else count, count if first else n_col):
            target[n, at:at + unit] = jnp.dot(
                left[n * unit:(n + 1) * unit], turned[name], preferred_element_type=FULL
            ).astype(LOW)

    if grads.shape[1] > 2 * unit:
        grads[...] = jnp.zeros_like(grads)
    if down_grads.shape[1] > unit:
        down_grads[...] = jnp.zeros_like(down_grads)
    for t in range(pieces + len(stages) - 1):
        for number in reversed(range(len(stages))):
            if 0 <= t - number < pieces:
                stages[number](t - number)
            if number == 4 and t == pieces + 2:
                product("down", True, active, cot, down_grads, 0)
        if t == pieces + 2:
            product("up", True, grad_hidden, normed, grads, unit)

    product("down", False, active, cot, down_grads, 0)
    for m in range(n_col):
        stored.append(move(down_grads.at[c_first ^ m], down_outs[m]))
    product("up", False, grad_hidden, normed, grads, unit)
    for first in (True, False):
        product("out", first, att, branch, grads, 0)
    for m in range(n_dp):
        at = pl.ds(pl.multiple_of((d ^ m) * rows_g, 16), rows_g)
        stored.append(move(grads.at[:, at], grads_hbms[m]))
    gain_out[...] = jnp.sum(narrow[...].T, axis=0, keepdims=True)

    for u in range(pieces):
        for m in range(1, n_pair):
            copies["out", u, m].wait_recv()
    for copy in stored:
        copy.wait()
    for copy in sent:
        copy.wait_send()


def middle_part(n_dp, n_pair, gain, attended, tokens, cotangent, cot_other, out_all, ups, downs):
    width, here = tokens.shape
    n_col = 2 * n_pair
    cols, length = attended.shape
    unit = downs[0].shape[0]
    half = n_col * unit // 2
    rows_q = ups[0].shape[1]
    rows_g = quarter_rows(2 * unit, n_dp)
    pieces = max(2, here // 256)
    piece = here // pieces
    count = 2 * pieces * (n_pair - 1) + 7 * pieces + 8
    moves = 4 * n_dp + 2 * n_col + 4 * pieces + 4
    hbm = pl.BlockSpec(memory_space=pl.ANY)
    vmem = pl.BlockSpec(memory_space=pltpu.VMEM)
    V = pltpu.VMEM
    S = jax.ShapeDtypeStruct
    weight = V((2 * half, width), LOW)
    weight_t = V((width, 2 * half), LOW)
    both = V((2 * width, here), LOW)
    whole = V((width, here), FULL)
    row = V((pieces, 1, piece), FULL)
    out = pl.pallas_call(
        functools.partial(middle_kernel, n_dp, n_pair, unit),
        out_shape=(
            S((width, here), FULL),
            S((width, here), FULL),
            S((cols, length), LOW),
        )
        + (S((n_col, rows_g, width), LOW),) * n_dp
        + (S((n_dp * quarter_rows(unit, n_dp), width), LOW),) * n_col
        + (S((1, width), FULL),),
        in_specs=[vmem] + [hbm] * (3 + n_dp + n_col),
        out_specs=(hbm,) * (3 + n_dp + n_col) + (vmem,),
        scratch_shapes=[
            V((width, here), LOW),
            both,
            V((n_col, n_dp * rows_q, width), LOW),
            V((n_col, n_dp * rows_q, width), LOW),
            V((2, n_dp * rows_q, width), LOW),
            weight,
            weight,
            weight,
            weight_t,
            weight_t,
            weight_t,
            V((half, 2 * width), LOW),
            V((half, 2 * width), LOW),
            V((half, 2 * width), LOW),
            both,
            both,
            V((width, here), LOW),
            V((2 * half, here), LOW),
            V((2 * half, here), LOW),
            both,
            whole,
            whole,
            whole,
            V((width, here), LOW),
            V((n_col, n_dp * rows_g, width), LOW),
            V((n_col, n_dp * quarter_rows(unit, n_dp), width), LOW),
            row,
            row,
            row,
            row,
            row,
            V((width, 128), FULL),
            pltpu.SemaphoreType.DMA((count,)),
            pltpu.SemaphoreType.DMA((count,)),
            pltpu.SemaphoreType.DMA((moves,)),
        ],
        compiler_params=pltpu.CompilerParams(
            collective_id=3, has_side_effects=True, vmem_limit_bytes=62 * 2**20
        ),
        cost_estimate=pl.CostEstimate(
            flops=18 * 2 * half * width * here, bytes_accessed=2**25, transcendentals=0
        ),
    )(gain, attended, tokens, cotangent, cot_other, out_all, *ups, *downs)
    return out[0], out[1], out[2], out[3:3 + n_dp], out[3 + n_dp:-1], out[-1]


def quarter_rows(rows, n_dp):
    return -(-rows // (16 * n_dp)) * 16


def tail_kernel(
    n_dp, n_pair, gain_ref, inverse_ref, sums_ref, qkv_hbm, dq_hbm, dk_hbm, dv_hbm, normed_hbm,
    tokens_hbm, middle_hbm, *refs,
):
    n_col = 2 * n_pair
    grads_hbms, refs = refs[:n_dp], refs[n_dp:]
    down_hbms, refs = refs[:n_col], refs[n_col:]
    (
        result_hbm, qkv_out, grads_out, down_out, sums_out,
        qkv, dproj, normed, tokens, middle, result, row_send, row_recv, own, pair_send, pair_recv,
        dp_send, dp_recv, dp_own, cross_send, cross_recv, cs_send, cs_recv, final, grads_parts,
        grads_send, grads_recv, grads_final, down_parts, down_send, down_recv, down_final,
        far_own, far_recv, far_send, far_parts,
        inner_send, inner_recv, sums_send, sums_recv, last_sums, send_sems, recv_sems, local_sems,
    ) = refs
    r, s = lax.axis_index("row"), lax.axis_index("cs")
    j, d = lax.axis_index("cp"), lax.axis_index("dp")
    width, here = tokens.shape
    cols = dq_hbm.shape[0]
    quartered = (1, n_pair + 1)
    whole = [k for k in range(n_col) if k not in quartered]
    share = width // n_dp
    part = share // 2
    rows_d = down_final.shape[0]
    subs = row_send.shape[1]
    piece = here // subs
    c_first = (s * n_pair + j) ^ (r * n_pair)
    near = r == s
    sems = (send_sems, recv_sems)
    gain = column(half_row(gain_ref, r))
    counter, local_counter = iter(range(1000)), iter(range(1000))
    sent, stored = [], []

    def send(src, dst, device):
        copy = remote(src, dst, sems, next(counter), device)
        copy.start()
        sent.append(copy)
        return copy

    def move(src, dst):
        copy = pltpu.make_async_copy(src, dst, local_sems.at[next(local_counter)])
        copy.start()
        return copy

    def down_rows(owner):
        return pl.ds(pl.multiple_of(owner * rows_d, 16), rows_d)

    load_grads = [move(grads_hbms[k], grads_parts.at[k]) for k in range(n_dp)]
    early = [
        move(dq_hbm, dproj.at[pl.ds(0, cols)]),
        move(dk_hbm, dproj.at[pl.ds(cols, cols)]),
        move(dv_hbm, dproj.at[pl.ds(2 * cols, cols)]),
        move(normed_hbm, normed),
    ]
    load_qkv = move(qkv_hbm, qkv)
    load_down = [move(down_hbms[k], down_parts.at[m]) for m, k in enumerate(whole)]
    load_far = [
        move(down_hbms[k].at[down_rows(d)], far_own.at[m]) for m, k in enumerate(quartered)
    ]
    late = [move(tokens_hbm, tokens), move(middle_hbm, middle)]

    sibling_id = {"row": 1 - r}
    cs_id = {"cs": 1 - s}
    dp_ids = [{"dp": d ^ k} for k in range(1, n_dp)]
    col_ids = [{"cs": s ^ (k // n_pair), "cp": j ^ (k % n_pair)} for k in range(1, n_col)]
    greet([sibling_id] + dp_ids + col_ids)


    for copy in load_grads:
        copy.wait()

    def summed(place_at):
        value = grads_parts[0, place_at].astype(FULL)
        for k in range(1, n_dp):
            value = value + grads_parts[k, place_at].astype(FULL)
        return value

    grads_copies = []
    for k in range(1, n_col):
        grads_send[k - 1] = summed(c_first ^ k).astype(LOW)
        grads_copies.append(send(grads_send.at[k - 1], grads_recv.at[k - 1], col_ids[k - 1]))
    far_copies = [
        send(down_hbms[k].at[down_rows(d ^ peer)], far_recv.at[peer - 1, m], dp_ids[peer - 1])
        for m, k in enumerate(quartered)
        for peer in range(1, n_dp)
    ]

    def quarter(half, owner):
        at = pl.ds(pl.multiple_of(half * width + owner * share, 32), share)
        return mm(normed[at, :], dproj[...], 1, 1)

    def rows_of(half, chunk, u):
        at = pl.ds(pl.multiple_of(chunk * here + u * piece, 128), piece)
        return jnp.dot(
            qkv[half * width:(half + 1) * width, :], dproj[:, at], preferred_element_type=FULL
        )

    dp_copies = {}

    def send_part(k, p):
        rows = pl.ds(p * part, part)
        dp_copies[k, p] = send(
            dp_send.at[k - 1, :, rows], dp_recv.at[k - 1, :, rows], dp_ids[k - 1]
        )

    def quarters(k):
        for half in range(2):
            dp_send[k - 1, half] = quarter(half, d ^ k).astype(LOW)
        send_part(k, 0)

    row_copies, pair_copies = {}, []
    for copy in early:
        copy.wait()
    for k in reversed(range(1, n_dp)):
        quarters(k)
    for k in reversed(range(1, n_dp)):
        send_part(k, 1)
    for copy in load_far:
        copy.wait()
    for copy in far_copies:
        copy.wait_recv()
    far_z = []
    for m, k in enumerate(quartered):
        value = far_own[m].astype(FULL)
        for peer in range(1, n_dp):
            value = value + far_recv[peer - 1, m].astype(FULL)
        far_send[m] = value.astype(LOW)
        far_z.append(send(far_send.at[m], far_parts.at[m], col_ids[k - 1]))
    load_qkv.wait()
    for k in range(1, n_pair):
        for u in range(subs):
            row_send[k, u] = rows_of(1, j ^ k, u).astype(LOW)
            row_copies[k, u] = send(row_send.at[k, u], row_recv.at[k, u], sibling_id)
    for k in range(1, n_pair):
        for u in range(subs):
            value = rows_of(0, j ^ k, u)
            row_copies[k, u].wait_recv()
            pair_send[k - 1, u] = (value + row_recv[k, u].astype(FULL)).astype(LOW)
            pair_copies.append(
                send(pair_send.at[k - 1, u], pair_recv.at[k - 1, u], {"cp": j ^ k})
            )
    for copy in load_down:
        copy.wait()
    value = down_parts[0].astype(FULL)
    for m in range(1, n_col - 2):
        value = value + down_parts[m].astype(FULL)
    down_send[...] = value.astype(LOW)

    down_copies = [
        send(down_send.at[down_rows(d ^ k)], down_recv.at[k - 1], dp_ids[k - 1])
        for k in range(1, n_dp)
    ]
    for half in range(2):
        dp_own[half] = quarter(half, d)

    for u in range(subs):
        row_send[0, u] = rows_of(1, j, u).astype(LOW)
        row_copies[0, u] = send(row_send.at[0, u], row_recv.at[0, u], sibling_id)
    for u in range(subs):
        own[u] = rows_of(0, j, u)

    cs_copies = []

    def reduce_part(p):
        rows = slice(p * part, (p + 1) * part)
        for k in range(1, n_dp):
            dp_copies[k, p].wait_recv()

        def total(half):
            value = dp_own[half, rows]
            for k in range(1, n_dp):
                value = value + dp_recv[k - 1, half, rows].astype(FULL)
            return value

        cross_send[p] = total(1).astype(LOW)
        cross_copy = send(cross_send.at[p], cross_recv.at[p], sibling_id)
        kept = total(0)
        cross_copy.wait_recv()
        crossed = cross_recv[p].astype(FULL)
        cs_send[p] = jnp.where(near, crossed, kept).astype(LOW)
        cs_copies.append(send(cs_send.at[p], cs_recv.at[p], cs_id))
        dp_own[0, rows] = jnp.where(near, kept, crossed)

    reduce_part(0)

    reduce_part(1)

    value = down_send[down_rows(d)].astype(FULL)
    for k in range(1, n_dp):
        down_copies[k - 1].wait_recv()
        value = value + down_recv[k - 1].astype(FULL)
    for m in range(2):
        far_z[m].wait_recv()
        value = value + far_parts[m].astype(FULL)
    down_final[...] = value.astype(LOW)
    out_copies = [send(down_final, down_out.at[d], peer) for peer in dp_ids]
    stored.append(move(down_final, down_out.at[d]))

    value = summed(c_first)
    for k in range(1, n_col):
        grads_copies[k - 1].wait_recv()
        value = value + grads_recv[k - 1].astype(FULL)
    grads_final[...] = value.astype(LOW)
    out_copies += [send(grads_final, grads_out.at[d], peer) for peer in dp_ids]
    stored.append(move(grads_final, grads_out.at[d]))

    for copy in late:
        copy.wait()
    for copy in pair_copies:
        copy.wait_recv()
    inverse = inverse_ref[...]
    for u in range(subs):
        row_copies[0, u].wait_recv()
        at = slice(u * piece, (u + 1) * piece)
        value = own[u] + row_recv[0, u].astype(FULL)
        for k in range(1, n_pair):
            value = value + pair_recv[k - 1, u].astype(FULL)
        own[u] = value
        inner_send[:, at] = jnp.sum(
            value * gain * tokens[:, at].astype(FULL), axis=0, keepdims=True
        )
    inner_copy = send(inner_send, inner_recv, sibling_id)

    def finish_part(p):
        cs_copies[p].wait_recv()
        rows = slice(p * part, (p + 1) * part)
        final[p] = (dp_own[0, rows] + cs_recv[p].astype(FULL)).astype(LOW)
        target = qkv_out.at[d, pl.ds(p * part, part)]
        out_copies.extend([send(final.at[p], target, peer) for peer in dp_ids])
        stored.append(move(final.at[p], target))

    finish_part(0)
    narrow = jnp.zeros((width, 128), FULL)
    for u in range(subs):
        at = slice(u * piece, (u + 1) * piece)
        wide = own[u] * tokens[:, at].astype(FULL) * inverse[:, at]
        for v in range(piece // 128):
            narrow = narrow + wide[:, v * 128:(v + 1) * 128]
    gain_part = jnp.sum(narrow.T, axis=0, keepdims=True)
    sums_send[0] = jnp.concatenate([gain_part, sums_ref[1:]], 0)
    sums_copies = {}

    def send_sums(step, peers):
        for k, peer in enumerate(peers):
            sums_copies[step, k] = send(sums_send.at[step], sums_recv.at[step, k], peer)

    def add_sums(step, members):
        value = sums_send[step]
        for k in range(members - 1):
            sums_copies[step, k].wait_recv()
            value = value + sums_recv[step, k]
        sums_send[step + 1] = value

    send_sums(0, dp_ids)
    inner_copy.wait_recv()
    inner = (inner_send[...] + inner_recv[...]) / D
    for u in range(subs):
        at = slice(u * piece, (u + 1) * piece)
        result[:, at] = (
            middle[:, at]
            + inverse[:, at] * (own[u] * gain)
            - tokens[:, at].astype(FULL)
            * (inverse[:, at] * inverse[:, at] * inverse[:, at] * inner[:, at])
        )
    stored.append(move(result, result_hbm))
    add_sums(0, n_dp)
    send_sums(1, col_ids)
    finish_part(1)

    add_sums(1, n_col)
    sums_copy = send(sums_send.at[2], last_sums, sibling_id)
    sums_copy.wait_recv()
    sums_out[0] = sums_send[2]
    sums_out[1] = last_sums[...]
    for copy in out_copies:
        copy.wait_recv()
    for copy in stored:
        copy.wait()
    for copy in sent:
        copy.wait_send()


def tail(n_dp, n_pair, gain, inverse, sums, qkv, dq, dk, dv, normed, tokens, middle, grads, downs):
    width, here = tokens.shape
    length = normed.shape[1]
    cols = dq.shape[0]
    unit = downs[0].shape[0]
    rows_d = unit // n_dp
    share = width // n_dp
    subs = 2
    piece = here // subs
    n_col = 2 * n_pair
    part = grads[0].shape[1:]
    wide = 3 * cols
    count = 2 * n_pair * subs + 10 * n_dp + 2 * n_col + 14
    moves = 15 + n_dp + n_col
    hbm = pl.BlockSpec(memory_space=pl.ANY)
    vmem = pl.BlockSpec(memory_space=pltpu.VMEM)
    V = pltpu.VMEM
    halves = V((2, share // 2, wide), LOW)
    return pl.pallas_call(
        functools.partial(tail_kernel, n_dp, n_pair),
        out_shape=(
            jax.ShapeDtypeStruct((width, here), FULL),
            jax.ShapeDtypeStruct((n_dp, share, wide), LOW),
            jax.ShapeDtypeStruct((n_dp,) + part, LOW),
            jax.ShapeDtypeStruct((n_dp, rows_d, width), LOW),
            jax.ShapeDtypeStruct((2,) + sums.shape, FULL),
        ),
        in_specs=[vmem] * 3 + [hbm] * (7 + n_dp + n_col),
        out_specs=(hbm,) * 4 + (vmem,),
        scratch_shapes=[
            V((2 * width, wide), LOW),
            V((wide, length), LOW),
            V((2 * width, length), LOW),
            V((width, here), LOW),
            V((width, here), FULL),
            V((width, here), FULL),
            V((n_pair, subs, width, piece), LOW),
            V((n_pair, subs, width, piece), LOW),
            V((subs, width, piece), FULL),
            V((n_pair - 1, subs, width, piece), LOW),
            V((n_pair - 1, subs, width, piece), LOW),
            V((n_dp - 1, 2, share, wide), LOW),
            V((n_dp - 1, 2, share, wide), LOW),
            V((2, share, wide), FULL),
            halves,
            halves,
            halves,
            halves,
            halves,
            V((n_dp, n_col) + part, LOW),
            V((n_col - 1,) + part, LOW),
            V((n_col - 1,) + part, LOW),
            V(part, LOW),
            V((n_col - 2, unit, width), LOW),
            V((n_dp * rows_d, width), LOW),
            V((n_dp - 1, rows_d, width), LOW),
            V((rows_d, width), LOW),
            V((2, rows_d, width), LOW),
            V((n_dp - 1, 2, rows_d, width), LOW),
            V((2, rows_d, width), LOW),
            V((2, rows_d, width), LOW),
            V((1, here), FULL),
            V((1, here), FULL),
            V((3,) + sums.shape, FULL),
            V((2, max(n_dp, n_col) - 1) + sums.shape, FULL),
            V(sums.shape, FULL),
            pltpu.SemaphoreType.DMA((count,)),
            pltpu.SemaphoreType.DMA((count,)),
            pltpu.SemaphoreType.DMA((moves,)),
        ],
        compiler_params=pltpu.CompilerParams(
            collective_id=1, has_side_effects=True, vmem_limit_bytes=62 * 2**20
        ),
        cost_estimate=pl.CostEstimate(
            flops=8 * wide * width * length, bytes_accessed=2**25, transcendentals=0
        ),
    )(gain, inverse, sums, qkv, dq, dk, dv, normed, tokens, middle, *grads, *downs)


def on_device(
    tokens,
    segment_ids,
    padding_mask,
    w_qkv,
    w_out,
    w_up,
    w_down,
    gain_attn,
    gain_mlp,
    scale_raw,
    cotangent,
):
    width, here = tokens.shape
    r, s = lax.axis_index("row"), lax.axis_index("cs")
    j, d = lax.axis_index("cp"), lax.axis_index("dp")
    n_pair, n_dp, n_col = lax.axis_size("cp"), lax.axis_size("dp"), lax.axis_size(COLS)
    c = s * n_pair + j
    head_cols = w_qkv.shape[0] // (3 * width)
    heads = head_cols // HEAD
    near = r == s

    ids = jnp.concatenate([segment_ids, padding_mask], 0)
    ids = jnp.where(s == r, ids, sibling(ids))
    segments, padding = ids[0], ids[1]
    length = segments.shape[0]
    firsts = segments[::BLOCK]
    starts = jnp.sum((segments[None, :] < firsts[:, None]).astype(jnp.int32), axis=1)
    filled = (jnp.sum(padding) + BLOCK - 1) // BLOCK
    blocks = jnp.arange(length // BLOCK, dtype=jnp.int32)
    lo = starts // BLOCK
    hi = jnp.minimum(blocks, filled)
    gain_one, gain_two = gain_attn[None, :], gain_mlp[None, :]
    factor = (LOG_TWO_E / math.sqrt(HEAD) * jnp.log1p(jnp.exp(scale_raw)))[None, :]
    slope = (LOG_TWO_E / math.sqrt(HEAD) * jax.nn.sigmoid(scale_raw))[None, :]

    block = w_qkv.reshape(width, 3 * head_cols)
    down = w_down.reshape(-1, width)
    unit = down.shape[0]
    part_rows = quarter_rows(unit, n_dp)

    def quarters(matrix):
        padded = jnp.pad(matrix, ((0, n_dp * part_rows - unit), (0, 0)))
        return padded.reshape(n_dp, part_rows, width)

    out = lax.dynamic_index_in_dim(quarters(w_out.reshape(-1, width)), d, 0, keepdims=False)
    up = lax.dynamic_index_in_dim(quarters(w_up.reshape(width, -1).T), d, 0, keepdims=False)
    (
        queries, key_heads, values, query_raw, normed_one, qkv, out_all, ups, cot_other,
        inverse_one,
    ) = head(
        n_dp, n_pair, gain_one, factor, tokens, cotangent, block, out, up,
        quarters(down),
    )
    ups = gather(ups, "dp")
    downs = [down] + [
        lax.ppermute(down, COLS, [(i, i ^ k) for i in range(n_col)])
        for k in range(2, n_col)
        if k != n_pair + 1
    ]
    attended, logs = attention_forward(queries, key_heads, values, ids, ids, lo, hi)
    result, grad_middle, grad_attended, grads, down_grads, gain_two_part = middle_part(
        n_dp, n_pair, gain_two, attended, tokens, cotangent, cot_other, out_all, ups, downs
    )
    received = [grads[0]] + [shift(grads[k], "dp", k) for k in range(1, n_dp)]
    down_received = [
        down_grads[k]
        if k in (0, 1, n_pair + 1)
        else lax.ppermute(down_grads[k], COLS, [(i, i ^ k) for i in range(n_col)])
        for k in range(n_col)
    ]

    dq, dk, dv, sums = attention_backward(
        queries, key_heads, values, attended, grad_attended, logs, query_raw, factor, slope, gain_two_part,
        ids, ids, lo, hi,
    )
    grad_tokens, grad_qkv, final, final_down, sums = tail(
        n_dp, n_pair, gain_one, inverse_one, sums, qkv, dq, dk, dv, normed_one, tokens,
        grad_middle, received, down_received,
    )
    grad_qkv = grad_qkv.astype(FULL)
    final = final.reshape(-1, width)
    final = [final[i * unit:(i + 1) * unit].astype(FULL) for i in range(2)]
    final.append(final_down.reshape(-1, width)[:unit].astype(FULL))
    own, other = sums[0], sums[1]
    first = r == 0
    gains = jnp.concatenate(
        [jnp.where(first, own[:2], other[:2]), jnp.where(first, other[:2], own[:2])], 1
    )
    scale_total = (own[2] + other[2])[:HEAD]
    return (
        result,
        grad_tokens,
        grad_qkv.reshape(-1),
        final[0].reshape(-1),
        final[1].T.reshape(-1),
        final[2].reshape(-1),
        gains[0],
        gains[1],
        scale_total,
    )


def solution(mesh):
    n_dp, n_row, n_col = (mesh.shape[name] for name in ("dp", "row", "col"))
    split = Mesh(
        np.asarray(mesh.devices).reshape(n_dp, n_row, n_row, n_col // n_row),
        ("dp", "row", "cs", "cp"),
    )
    rows = P("row", ("dp", "cs", "cp"))
    ids = P(("dp", "row"), None)
    blocks = P(("row", "cs", "cp"))
    return jax.shard_map(
        on_device,
        mesh=split,
        in_specs=(rows, ids, ids, blocks, blocks, blocks, blocks, P(), P(), P(), rows),
        out_specs=(rows, rows, blocks, blocks, blocks, blocks, P(), P(), P()),
        check_vma=False,
    )
```

```python
import functools
import math

import jax
import jax.numpy as jnp
import numpy as np
from jax import lax
from jax.experimental import pallas as pl
from jax.experimental.pallas import tpu as pltpu
from jax.sharding import Mesh, PartitionSpec as P

D = 1280
HEAD = 80
EPSILON = 1e-06
LOG_TWO_E = 1.442695041
BLOCK = 256
LOW = jnp.bfloat16
FULL = jnp.float32
COLS = ("cs", "cp")


def mm(left, right, left_axis, right_axis):
    return lax.dot_general(
        left, right, (((left_axis,), (right_axis,)), ((), ())), preferred_element_type=FULL
    )


def shift(x, axis, k):
    n = lax.axis_size(axis)
    return lax.ppermute(x, axis, [(i, i ^ k) for i in range(n)])


def sibling(x):
    return shift(x, "row", 1)


def cut(x, index, count, axis):
    step = x.shape[axis] // count
    return lax.dynamic_slice_in_dim(x, index * step, step, axis)


def gather(x, axis):
    return [x] + [shift(x, axis, k) for k in range(1, lax.axis_size(axis))]


def diag_mask(segq, segk):
    size = segk.shape[0], segq.shape[1]
    ki = lax.broadcasted_iota(jnp.int32, size, 0)
    qi = lax.broadcasted_iota(jnp.int32, size, 1)
    return ((segk == segq) & (ki <= qi)) | (ki == qi)


def softplus_scale(row):
    return LOG_TWO_E / math.sqrt(HEAD) * jnp.log1p(jnp.exp(row))


def half_row(ref, which):
    size = ref.shape[1] // 2
    return jnp.where(which == 0, ref[:, :size], ref[:, size:])


def column(row):
    return jnp.broadcast_to(row, (8, row.shape[1])).T[:, :1]


def rows_of(h):
    return slice(h * HEAD, (h + 1) * HEAD)


def forward_kernel(heads, lo_ref, hi_ref, q_ref, k_ref, v_ref, segq_ref, segk_ref, o_ref, log_ref, ks, segks):
    i = pl.program_id(0)

    here = pl.ds(pl.multiple_of(i * BLOCK, BLOCK), BLOCK)
    for h in range(heads):
        ks[h, here, :] = k_ref[rows_of(h), here].T
    segks[here, :] = column(jnp.where(segk_ref[1:, here] == 1, segk_ref[:1, here], -1).astype(FULL))
    segq = segq_ref[:1].astype(FULL)

    def visit(kb, carry, diagonal):
        at = pl.ds(pl.multiple_of(kb * BLOCK, BLOCK), BLOCK)
        segk = segks[at, :]
        mask = diag_mask(segq, segk) if diagonal else segk == segq
        scores = [
            jnp.dot(ks[h, at, :], q_ref[rows_of(h), :], preferred_element_type=FULL)
            for h in range(heads)
        ]
        peaks, totals, weights = [], [], []
        for h in range(heads):
            s = jnp.where(mask, scores[h], -1e30)
            peak = jnp.max(s, axis=0, keepdims=True)
            if not diagonal:
                peak = jnp.maximum(carry[h][0], peak)
            p = jnp.exp(s - peak)
            peaks.append(peak)
            totals.append(jnp.sum(p, axis=0, keepdims=True))
            weights.append(p.astype(LOW))
        out = []
        for h in range(heads):
            new = jnp.dot(v_ref[rows_of(h), at], weights[h], preferred_element_type=FULL)
            total = totals[h]
            if not diagonal:
                m, l, acc = carry[h]
                keep = jnp.exp(m - peaks[h])
                total = l * keep + total
                new = acc * keep + new
            out.append((peaks[h], total, new))
        return tuple(out)

    carry = visit(i, None, True)
    carry = lax.fori_loop(lo_ref[i], hi_ref[i], lambda kb, c: visit(kb, c, False), carry)
    for h in range(heads):
        m, l, acc = carry[h]
        o_ref[h * HEAD:(h + 1) * HEAD, :] = (acc / l).astype(LOW)
        log_ref[h] = m + jnp.log(l)


def attention_forward(q, k, v, segq, segk, lo, hi):
    cols, length = q.shape
    heads = cols // HEAD
    steps = length // BLOCK
    whole = pl.BlockSpec((cols, length), lambda i, *_: (0, 0))
    part = pl.BlockSpec((cols, BLOCK), lambda i, *_: (0, i))
    return pl.pallas_call(
        functools.partial(forward_kernel, heads),
        out_shape=(
            jax.ShapeDtypeStruct((cols, length), LOW),
            jax.ShapeDtypeStruct((heads, 1, length), FULL),
        ),
        grid_spec=pltpu.PrefetchScalarGridSpec(
            num_scalar_prefetch=2,
            grid=(steps,),
            in_specs=[
                part,
                whole,
                whole,
                pl.BlockSpec((2, BLOCK), lambda i, *_: (0, i)),
                pl.BlockSpec((2, length), lambda i, *_: (0, 0)),
            ],
            out_specs=(part, pl.BlockSpec((heads, 1, BLOCK), lambda i, *_: (0, 0, i))),
            scratch_shapes=[pltpu.VMEM((heads, length, HEAD), LOW), pltpu.VMEM((length, 1), FULL)],
        ),
        compiler_params=pltpu.CompilerParams(vmem_limit_bytes=62 * 2**20),
        cost_estimate=pl.CostEstimate(
            flops=8 * 2 * length * length * cols,
            bytes_accessed=4 * cols * length * 2,
            transcendentals=heads * length * length // 3,
        ),
    )(lo, hi, q, k, v, segq, segk)


def backward_kernel(
    heads, lo_ref, hi_ref, q_ref, k_ref, v_ref, o_ref, go_ref, log_ref, raw_ref, scale_ref,
    gain_ref, segq_ref, segk_ref, dq_ref, dk_ref, dv_ref, sums_ref, ks, vs, qs, gs, dks, dvs, dqs, segks, total,
):
    i = pl.program_id(0)

    @pl.when(i == 0)
    def _():
        sums_ref[...] = jnp.zeros_like(sums_ref)
        total[...] = jnp.zeros_like(total)

    here = pl.ds(pl.multiple_of(i * BLOCK, BLOCK), BLOCK)
    for h in range(heads):
        ks[h, here, :] = k_ref[rows_of(h), here].T
        vs[h, here, :] = v_ref[rows_of(h), here].T
    segks[here, :] = column(jnp.where(segk_ref[1:, here] == 1, segk_ref[:1, here], -1).astype(FULL))
    segq = segq_ref[:1].astype(FULL)
    inner = [
        jnp.sum(
            o_ref[h * HEAD:(h + 1) * HEAD, :].astype(FULL)
            * go_ref[h * HEAD:(h + 1) * HEAD, :].astype(FULL),
            axis=0,
            keepdims=True,
        )
        for h in range(heads)
    ]

    for h in range(heads):
        qs[h] = q_ref[rows_of(h), :].T
        gs[h] = go_ref[rows_of(h), :].T

    def visit(kb, diagonal):
        at = pl.ds(pl.multiple_of(kb * BLOCK, BLOCK), BLOCK)
        segk = segks[at, :]
        mask = diag_mask(segq, segk) if diagonal else segk == segq
        scores = [
            jnp.dot(ks[h, at, :], q_ref[rows_of(h), :], preferred_element_type=FULL)
            for h in range(heads)
        ]
        dps = [
            jnp.dot(vs[h, at, :], go_ref[rows_of(h), :], preferred_element_type=FULL)
            for h in range(heads)
        ]
        ps, dss = [], []
        for h in range(heads):
            p = jnp.where(mask, jnp.exp(scores[h] - log_ref[h]), 0.0)
            dss.append((p * (dps[h] - inner[h])).astype(LOW))
            ps.append(p.astype(LOW))
        for h in range(heads):
            new_v = jnp.dot(ps[h], gs[h], preferred_element_type=FULL)
            new_k = jnp.dot(dss[h], qs[h], preferred_element_type=FULL)
            new_q = jnp.dot(k_ref[rows_of(h), at], dss[h], preferred_element_type=FULL)
            if diagonal:
                dvs[h, at, :], dks[h, at, :], dqs[rows_of(h), :] = new_v, new_k, new_q
            else:
                dvs[h, at, :] += new_v
                dks[h, at, :] += new_k
                dqs[rows_of(h), :] += new_q

    visit(i, True)

    @pl.loop(lo_ref[i], hi_ref[i])
    def _(kb):
        visit(kb, False)

    factor = column(softplus_scale(scale_ref[...]))
    part = jnp.zeros((HEAD, 1), FULL)
    for h in range(heads):
        rows = slice(h * HEAD, (h + 1) * HEAD)
        dq = dqs[rows, :]
        part = part + jnp.sum(dq * raw_ref[rows, :], axis=1, keepdims=True)
        dq_ref[rows, :] = (dq * factor).astype(LOW)
    total[...] += part

    @pl.when(i == pl.num_programs(0) - 1)
    def _():
        for h in range(heads):
            dk_ref[rows_of(h), :] = dks[h].astype(LOW).T
            dv_ref[rows_of(h), :] = dvs[h].astype(LOW).T
        sums_ref[1:2, :] = gain_ref[...]
        row = jnp.broadcast_to(total[...], (HEAD, 128)).T[:1]
        slope = LOG_TWO_E / math.sqrt(HEAD) * jax.nn.sigmoid(scale_ref[...])
        sums_ref[2:3, :HEAD] = row * slope


def attention_backward(q, k, v, o, go, logs, raw, scale, gain_part, segq, segk, lo, hi):
    cols, length = q.shape
    heads = cols // HEAD
    steps = length // BLOCK
    whole = pl.BlockSpec((cols, length), lambda i, *_: (0, 0))
    part = pl.BlockSpec((cols, BLOCK), lambda i, *_: (0, i))
    width = gain_part.shape[1]
    total = pl.BlockSpec((8, width), lambda i, *_: (0, 0))
    shape = jax.ShapeDtypeStruct((cols, length), LOW)
    return pl.pallas_call(
        functools.partial(backward_kernel, heads),
        out_shape=(shape, shape, shape, jax.ShapeDtypeStruct((8, width), FULL)),
        grid_spec=pltpu.PrefetchScalarGridSpec(
            num_scalar_prefetch=2,
            grid=(steps,),
            in_specs=[
                part,
                whole,
                whole,
                part,
                part,
                pl.BlockSpec((heads, 1, BLOCK), lambda i, *_: (0, 0, i)),
                part,
                pl.BlockSpec((1, HEAD), lambda i, *_: (0, 0)),
                pl.BlockSpec((1, width), lambda i, *_: (0, 0)),
                pl.BlockSpec((2, BLOCK), lambda i, *_: (0, i)),
                pl.BlockSpec((2, length), lambda i, *_: (0, 0)),
            ],
            out_specs=(part, whole, whole, total),
            scratch_shapes=[
                pltpu.VMEM((heads, length, HEAD), LOW),
                pltpu.VMEM((heads, length, HEAD), LOW),
                pltpu.VMEM((heads, BLOCK, HEAD), LOW),
                pltpu.VMEM((heads, BLOCK, HEAD), LOW),
                pltpu.VMEM((heads, length, HEAD), FULL),
                pltpu.VMEM((heads, length, HEAD), FULL),
                pltpu.VMEM((cols, BLOCK), FULL),
                pltpu.VMEM((length, 1), FULL),
                pltpu.VMEM((HEAD, 1), FULL),
            ],
        ),
        compiler_params=pltpu.CompilerParams(vmem_limit_bytes=62 * 2**20),
        cost_estimate=pl.CostEstimate(
            flops=8 * 5 * length * length * cols,
            bytes_accessed=8 * cols * length * 2,
            transcendentals=heads * length * length // 3,
        ),
    )(lo, hi, q, k, v, o, go, logs, raw, scale, gain_part, segq, segk)


def remote(src, dst, sems, index, device):
    return pltpu.make_async_remote_copy(
        src_ref=src,
        dst_ref=dst,
        send_sem=sems[0].at[index],
        recv_sem=sems[1].at[index],
        device_id=device,
        device_id_type=pl.DeviceIdType.MESH,
    )


def greet(peers):
    barrier = pltpu.get_barrier_semaphore()
    for peer in peers:
        pl.semaphore_signal(barrier, inc=1, device_id=peer, device_id_type=pl.DeviceIdType.MESH)
    pl.semaphore_wait(barrier, len(peers))


def head_kernel(
    n_dp, n_pair, gain_ref, raw_ref, tokens_hbm, cot_hbm, block_hbm, out_hbm, up_hbm,
    down_hbm, q_hbm, k_hbm, v_hbm, raw_hbm, normed_hbm, qkv_hbm, out_all, ups_hbm, cot_out, inverse_ref,
    tokens, others, block, cs_recv, remote_block, pass_on, qkv, turned, normed, q, k, v, raw,
    send_sems, recv_sems, local_sems,
):
    r, s = lax.axis_index("row"), lax.axis_index("cs")
    j, d = lax.axis_index("cp"), lax.axis_index("dp")
    n_col = 2 * n_pair
    subs, width, piece = tokens.shape[1:]
    here = subs * piece
    share = cs_recv.shape[0]
    cols = q.shape[0]
    c_first = (s * n_pair + j) ^ (r * n_pair)
    near = r == s
    sems = (send_sems, recv_sems)
    counter, local_counter = iter(range(1000)), iter(range(1000))
    sent, stored = [], []

    def send(src, dst, device):
        copy = remote(src, dst, sems, next(counter), device)
        copy.start()
        sent.append(copy)
        return copy

    def move(src, dst):
        copy = pltpu.make_async_copy(src, dst, local_sems.at[next(local_counter)])
        copy.start()
        return copy

    def store(src, dst):
        stored.append(move(src, dst))

    def columns(u):
        return pl.ds(u * piece, piece)

    own_tokens = [move(tokens_hbm.at[:, columns(u)], tokens.at[0, u]) for u in range(subs)]
    own_block = move(block_hbm, block)
    own_out = move(out_hbm, out_all.at[d, c_first])
    store(up_hbm, ups_hbm.at[c_first])
    sibling_id = {"row": 1 - r}
    dp_ids = [{"dp": d ^ k} for k in range(1, n_dp)]
    col_ids = [{"cs": s ^ (k // n_pair), "cp": j ^ (k % n_pair)} for k in range(1, n_col)]
    greet([sibling_id] + dp_ids + col_ids)

    cs_copy = send(block_hbm.at[d], cs_recv, {"cs": 1 - s})
    down_ids = [col_ids[0], col_ids[n_pair]]
    down_copies = [
        send(down_hbm.at[d], ups_hbm.at[n_col + m], peer) for m, peer in enumerate(down_ids)
    ]
    out_copies = [send(out_hbm, out_all.at[d, c_first], peer) for peer in col_ids]
    other_copies = {}
    for u in range(subs):
        other_copies[0, u] = send(tokens_hbm.at[:, columns(u)], others.at[0, u], sibling_id)
    pair_copies = {}

    def send_pairs(u):
        for m in range(1, n_pair):
            pair_copies[m, u] = send(
                tokens_hbm.at[:, columns(u)], tokens.at[m, u], {"cp": j ^ m}
            )

    send_pairs(0)

    cot_copy = send(cot_hbm, cot_out, sibling_id)
    gain_own = column(half_row(gain_ref, r))
    gain_other = column(half_row(gain_ref, 1 - r))
    factor = jnp.concatenate([column(softplus_scale(raw_ref[...]))] * (cols // HEAD), 0)

    def norm(m, u):
        own, other = tokens[m, u].astype(FULL), others[m, u].astype(FULL)
        squares = jnp.sum(own * own, axis=0, keepdims=True)
        squares = squares + jnp.sum(other * other, axis=0, keepdims=True)
        inverse = lax.rsqrt(squares / D + EPSILON)
        at = pl.ds(pl.multiple_of((j ^ m) * here + u * piece, 128), piece)
        normed[:width, at] = (own * inverse * gain_own).astype(LOW)
        normed[width:, at] = (other * inverse * gain_other).astype(LOW)
        store(normed.at[:, at], normed_hbm.at[:, at])
        if m == 0:
            inverse_ref[:, columns(u)] = inverse

    def project(m, u):
        at = pl.ds(pl.multiple_of((j ^ m) * here + u * piece, 128), piece)
        for part, out in ((0, None), (1, k), (2, v)):
            value = jnp.dot(
                turned[part * cols:(part + 1) * cols, :], normed[:, at],
                preferred_element_type=FULL,
            )
            if part == 0:
                raw[:, at] = value
                q[:, at] = (value * factor).astype(LOW)
            else:
                out[:, at] = value.astype(LOW)
        for src, dst in ((q, q_hbm), (k, k_hbm), (v, v_hbm), (raw, raw_hbm)):
            store(src.at[:, at], dst.at[:, at])

    for u in range(subs):
        own_tokens[u].wait()
        other_copies[0, u].wait_recv()
        norm(0, u)
    own_block.wait()

    cs_copy.wait_recv()
    send_pairs(1)
    dp_copies = [send(cs_recv, remote_block.at[d], peer) for peer in dp_ids]
    own_out.wait()
    for copy in out_copies:
        copy.wait_recv()
    late_copies = [send(out_all.at[d], out_all.at[d], peer) for peer in dp_ids]
    remote_block[d] = cs_recv[...]
    for u in range(subs - 1):
        for m in range(1, n_pair):
            pair_copies[m, u].wait_recv()
            other_copies[m, u] = send(tokens.at[m, u], others.at[m, u], sibling_id)
    cross_copies = []
    for m in range(n_dp):
        owner = d ^ m
        if m:
            dp_copies[m - 1].wait_recv()
        mine, its = block[owner], remote_block[owner]
        at = pl.multiple_of(owner * share, 32)
        qkv[pl.ds(at, share)] = jnp.where(near, mine, its)
        pass_on[owner] = jnp.where(near, its, mine)
        cross_copies.append(
            send(pass_on.at[owner], qkv.at[pl.ds(width + at, share)], sibling_id)
        )
    u = subs - 1
    for m in range(1, n_pair):
        pair_copies[m, u].wait_recv()
        other_copies[m, u] = send(tokens.at[m, u], others.at[m, u], sibling_id)
    late_copies += [send(up_hbm, ups_hbm.at[c_first], peer) for peer in col_ids]
    turned[:, :width] = qkv[:width].T
    for copy in cross_copies:
        copy.wait_recv()
    turned[:, width:] = qkv[width:].T
    store(qkv, qkv_hbm)

    for u in range(subs):
        project(0, u)
    for u in range(subs):
        for m in range(1, n_pair):
            other_copies[m, u].wait_recv()
            norm(m, u)
            project(m, u)

    for copy in stored:
        copy.wait()
    for copy in late_copies + down_copies + [cot_copy]:
        copy.wait_recv()
    for copy in sent:
        copy.wait_send()


def head(n_dp, n_pair, gain, scale, tokens, cotangent, block, out, up, down):
    width, here = tokens.shape
    wide = block.shape[1]
    cols = wide // 3
    share = width // n_dp
    length = n_pair * here
    n_col = 2 * n_pair
    subs = 2
    piece = here // subs
    count = subs * n_pair * 2 + 4 * n_dp + 2 * n_col + 7
    moves = 4 + subs + 5 * subs * n_pair + 4
    hbm = pl.BlockSpec(memory_space=pl.ANY)
    vmem = pl.BlockSpec(memory_space=pltpu.VMEM)
    V = pltpu.VMEM
    shape = jax.ShapeDtypeStruct((cols, length), LOW)
    return pl.pallas_call(
        functools.partial(head_kernel, n_dp, n_pair),
        out_shape=(
            shape,
            shape,
            shape,
            jax.ShapeDtypeStruct((cols, length), FULL),
            jax.ShapeDtypeStruct((2 * width, length), LOW),
            jax.ShapeDtypeStruct((2 * width, wide), LOW),
            jax.ShapeDtypeStruct((n_dp, n_col) + out.shape, LOW),
            jax.ShapeDtypeStruct((n_col + 2,) + up.shape, LOW),
            jax.ShapeDtypeStruct((width, here), LOW),
            jax.ShapeDtypeStruct((1, here), FULL),
        ),
        in_specs=[vmem] * 2 + [hbm] * 6,
        out_specs=(hbm,) * 9 + (vmem,),
        scratch_shapes=[
            V((n_pair, subs, width, piece), LOW),
            V((n_pair, subs, width, piece), LOW),
            V((n_dp, share, wide), LOW),
            V((share, wide), LOW),
            V((n_dp, share, wide), LOW),
            V((n_dp, share, wide), LOW),
            V((2 * width, wide), LOW),
            V((wide, 2 * width), LOW),
            V((2 * width, length), LOW),
            V((cols, length), LOW),
            V((cols, length), LOW),
            V((cols, length), LOW),
            V((cols, length), FULL),
            pltpu.SemaphoreType.DMA((count,)),
            pltpu.SemaphoreType.DMA((count,)),
            pltpu.SemaphoreType.DMA((moves,)),
        ],
        compiler_params=pltpu.CompilerParams(
            collective_id=2, has_side_effects=True, vmem_limit_bytes=60 * 2**20
        ),
        cost_estimate=pl.CostEstimate(
            flops=4 * wide * width * length, bytes_accessed=2**25, transcendentals=0
        ),
    )(gain, scale, tokens, cotangent, block.reshape(n_dp, share, wide), out, up, down)


def middle_kernel(n_dp, n_pair, unit, gain_ref, att_hbm, tokens_hbm, cot_hbm, cot_other, out_all, *refs):
    n_col = 2 * n_pair
    up_hbms, refs = refs[:n_dp], refs[n_dp:]
    down_hbms, refs = refs[:n_col - 2], refs[n_col - 2:]
    result_hbm, middle_hbm, out_hbm, refs = refs[0], refs[1], refs[2], refs[3:]
    grads_hbms, refs = refs[:n_dp], refs[n_dp:]
    down_outs, refs = refs[:n_col], refs[n_col:]
    (
        gain_out, tokens, cot, out_slab, up_slab, down_slab, out_w, up_w, down_w, out_t, up_t, down_t, out_half, up_half,
        down_half, att, scaled, normed, active, grad_hidden, branch, middle, grad, result, grad_att,
        grads, down_grads, square_send, square_recv, inner_send, inner_recv, inverse, narrow,
        send_sems, recv_sems, local_sems,
    ) = refs
    r, s = lax.axis_index("row"), lax.axis_index("cs")
    j, d = lax.axis_index("cp"), lax.axis_index("dp")
    width, here = tokens.shape
    pieces, _, piece = square_send.shape
    cols = att_hbm.shape[0]
    half = n_col * unit // 2
    rows_q = up_hbms[0].shape[1]
    rows_g = grads_hbms[0].shape[1]
    c_first = (s * n_pair + j) ^ (r * n_pair)
    sems = (send_sems, recv_sems)
    gain = column(half_row(gain_ref, r))
    counter, local_counter = iter(range(1000)), iter(range(1000))
    sent, stored = [], []

    def send(src, dst, device):
        copy = remote(src, dst, sems, next(counter), device)
        copy.start()
        sent.append(copy)
        return copy

    def move(src, dst):
        copy = pltpu.make_async_copy(src, dst, local_sems.at[next(local_counter)])
        copy.start()
        return copy

    def columns(u):
        return pl.ds(u * piece, piece)

    def span(u):
        return slice(u * piece, (u + 1) * piece)

    def down_rows(owner):
        return pl.ds(pl.multiple_of(owner * unit, 16), unit)

    def quarter_of(owner):
        return pl.ds(pl.multiple_of(owner * rows_q, 16), rows_q)

    quartered = (1, n_pair + 1)
    own_rows, other_rows = pl.ds(0, width), pl.ds(width, width)
    weight_loads = [
        move(out_all.at[m], out_slab.at[:, pl.ds(m * rows_q, rows_q)]) for m in range(n_dp)
    ] + [
        move(up_hbms[m].at[pl.ds(first, size)], target.at[:, quarter_of(d ^ m)])
        for m in range(n_dp)
        for first, size, target in ((0, n_col, up_slab), (n_col, 2, down_slab))
    ] + [
        move(ref, down_w.at[down_rows(c_first ^ m)])
        for m, ref in zip([m for m in range(n_col) if m not in quartered], down_hbms)
    ]
    att_loads = [
        move(
            att_hbm.at[:, pl.ds(pl.multiple_of(j * here + u * piece, 128), piece)],
            att.at[pl.ds(pl.multiple_of(j * cols, 16), cols), columns(u)],
        )
        for u in range(pieces)
    ]
    token_load = move(tokens_hbm, tokens)
    cot_loads = [move(cot_hbm, cot.at[own_rows]), move(cot_other, cot.at[other_rows])]
    sibling_id = {"row": 1 - r}
    pair_ids = [{"cp": j ^ m} for m in range(1, n_pair)]
    greet([sibling_id] + pair_ids)

    att_copies = {}
    for u in range(pieces):
        for m in range(1, n_pair):
            att_copies[u, m] = send(
                att_hbm.at[:, pl.ds(pl.multiple_of((j ^ m) * here + u * piece, 128), piece)],
                att.at[pl.ds(pl.multiple_of(j * cols, 16), cols), columns(u)],
                pair_ids[m - 1],
            )

    for copy in weight_loads:
        copy.wait()
    for m in range(n_col):
        at = slice(m * unit, (m + 1) * unit)
        out_w[at] = out_slab[m, :unit]
        up_w[at] = up_slab[m, :unit]
    for m, k in enumerate(quartered):
        down_w[down_rows(c_first ^ k)] = down_slab[m, :unit]
    cross_copies = []

    def cross(whole, part):
        cross_copies.append(send(whole.at[pl.ds(half, half)], part.at[:, other_rows], sibling_id))
        part[:, :width] = whole[:half]

    cross(up_w, up_half)
    cross(down_w, down_half)
    cross(out_w, out_half)
    out_t[...] = out_w[...].T
    narrow[...] = jnp.zeros_like(narrow)

    copies = {}

    def exchange(name, u, ref):
        copies[name, u] = send(
            ref.at[own_rows, columns(u)], ref.at[other_rows, columns(u)], sibling_id
        )

    def share_heads(u):
        att_loads[u].wait()
        for m in range(1, n_pair):
            att_copies[u, m].wait_recv()
        exchange("att", u, att)

    def first_branch(u):
        if u == 0:
            token_load.wait()
        copies["att", u].wait_recv()
        value = tokens[:, span(u)].astype(FULL) + jnp.dot(
            out_t[...], att[:, span(u)], preferred_element_type=FULL
        )
        scaled[:width, span(u)] = (value * gain).astype(LOW)
        exchange("scaled", u, scaled)
        square_send[u] = jnp.sum(value * value, axis=0, keepdims=True)
        copies["square", u] = send(square_send.at[u], square_recv.at[u], sibling_id)
        middle[:, span(u)] = value

    def hidden_units(u):
        if u == 0:
            for copy in cot_loads:
                copy.wait()
            for copy in cross_copies:
                copy.wait_recv()
            up_t[...] = up_w[...].T
            down_t[...] = down_w[...].T
        grad_active = jnp.dot(down_half[...], cot[:, span(u)], preferred_element_type=FULL)
        copies["scaled", u].wait_recv()
        copies["square", u].wait_recv()
        scale = lax.rsqrt((square_send[u] + square_recv[u]) / D + EPSILON)
        inverse[u] = scale
        hidden = scale * jnp.dot(up_half[...], scaled[:, span(u)], preferred_element_type=FULL)
        sigmoid = jax.nn.sigmoid(hidden)
        value = (grad_active * sigmoid * (1.0 + hidden * (1.0 - sigmoid))).astype(LOW)
        grad_hidden[:half, span(u)] = value
        exchange("grad_hidden", u, grad_hidden)
        active[:half, span(u)] = (hidden * sigmoid).astype(LOW)
        exchange("active", u, active)
        inner_send[u] = jnp.sum(value.astype(FULL) * hidden, axis=0, keepdims=True)
        copies["inner", u] = send(inner_send.at[u], inner_recv.at[u], sibling_id)
        normed[:, span(u)] = (middle[:, span(u)] * scale * gain).astype(LOW)

    def second_branch(u):
        copies["grad_hidden", u].wait_recv()
        copies["inner", u].wait_recv()
        scale = inverse[u]
        inner = scale * scale * ((inner_send[u] + inner_recv[u]) / D)
        back = jnp.dot(up_t[...], grad_hidden[:, span(u)], preferred_element_type=FULL)
        value = (
            cot[:width, span(u)].astype(FULL)
            + scale * (back * gain)
            - middle[:, span(u)] * inner
        )
        branch[:width, span(u)] = value.astype(LOW)
        exchange("branch", u, branch)
        grad[:, span(u)] = value
        stored.append(move(grad.at[:, columns(u)], middle_hbm.at[:, columns(u)]))
        product = back * middle[:, span(u)] * scale
        total = narrow[...]
        for v in range(piece // 128):
            total = total + product[:, v * 128:(v + 1) * 128]
        narrow[...] = total
        copies["active", u].wait_recv()
        result[:, span(u)] = middle[:, span(u)] + jnp.dot(
            down_t[...], active[:, span(u)], preferred_element_type=FULL
        )
        stored.append(move(result.at[:, columns(u)], result_hbm.at[:, columns(u)]))

    def heads_back(u):
        copies["branch", u].wait_recv()
        grad_att[:, span(u)] = jnp.dot(
            out_half[...], branch[:, span(u)], preferred_element_type=FULL
        ).astype(LOW)
        target = pl.ds(pl.multiple_of(j * here + u * piece, 128), piece)
        for m in range(n_pair):
            source = grad_att.at[
                pl.ds(pl.multiple_of((j ^ m) * cols, 16), cols), columns(u)
            ]
            if m:
                copies["out", u, m] = send(source, out_hbm.at[:, target], pair_ids[m - 1])
            else:
                stored.append(move(source, out_hbm.at[:, target]))

    stages = (share_heads, first_branch, hidden_units, second_branch, heads_back)
    turned = {}

    def product(name, first, left, right, target, at):
        if name not in turned:
            turned[name] = right[:width].T
        count = n_col // 2
        for n in range(0 if first else count, count if first else n_col):
            target[n, at:at + unit] = jnp.dot(
                left[n * unit:(n + 1) * unit], turned[name], preferred_element_type=FULL
            ).astype(LOW)

    if grads.shape[1] > 2 * unit:
        grads[...] = jnp.zeros_like(grads)
    if down_grads.shape[1] > unit:
        down_grads[...] = jnp.zeros_like(down_grads)
    for t in range(pieces + len(stages) - 1):
        for number in reversed(range(len(stages))):
            if 0 <= t - number < pieces:
                stages[number](t - number)
            if number == 4 and t == pieces + 2:
                product("down", True, active, cot, down_grads, 0)
        if t == pieces + 2:
            product("up", True, grad_hidden, normed, grads, unit)

    product("down", False, active, cot, down_grads, 0)
    for m in range(n_col):
        stored.append(move(down_grads.at[c_first ^ m], down_outs[m]))
    product("up", False, grad_hidden, normed, grads, unit)
    for first in (True, False):
        product("out", first, att, branch, grads, 0)
    for m in range(n_dp):
        at = pl.ds(pl.multiple_of((d ^ m) * rows_g, 16), rows_g)
        stored.append(move(grads.at[:, at], grads_hbms[m]))
    gain_out[...] = jnp.sum(narrow[...].T, axis=0, keepdims=True)

    for u in range(pieces):
        for m in range(1, n_pair):
            copies["out", u, m].wait_recv()
    for copy in stored:
        copy.wait()
    for copy in sent:
        copy.wait_send()


def middle_part(n_dp, n_pair, gain, attended, tokens, cotangent, cot_other, out_all, ups, downs):
    width, here = tokens.shape
    n_col = 2 * n_pair
    cols, length = attended.shape
    unit = downs[0].shape[0]
    half = n_col * unit // 2
    rows_q = ups[0].shape[1]
    rows_g = quarter_rows(2 * unit, n_dp)
    pieces = max(2, here // 256)
    piece = here // pieces
    count = 2 * pieces * (n_pair - 1) + 7 * pieces + 8
    moves = 4 * n_dp + 2 * n_col + 4 * pieces + 4
    hbm = pl.BlockSpec(memory_space=pl.ANY)
    vmem = pl.BlockSpec(memory_space=pltpu.VMEM)
    V = pltpu.VMEM
    S = jax.ShapeDtypeStruct
    weight = V((2 * half, width), LOW)
    weight_t = V((width, 2 * half), LOW)
    both = V((2 * width, here), LOW)
    whole = V((width, here), FULL)
    row = V((pieces, 1, piece), FULL)
    out = pl.pallas_call(
        functools.partial(middle_kernel, n_dp, n_pair, unit),
        out_shape=(
            S((width, here), FULL),
            S((width, here), FULL),
            S((cols, length), LOW),
        )
        + (S((n_col, rows_g, width), LOW),) * n_dp
        + (S((n_dp * quarter_rows(unit, n_dp), width), LOW),) * n_col
        + (S((1, width), FULL),),
        in_specs=[vmem] + [hbm] * (3 + n_dp + n_col),
        out_specs=(hbm,) * (3 + n_dp + n_col) + (vmem,),
        scratch_shapes=[
            V((width, here), LOW),
            both,
            V((n_col, n_dp * rows_q, width), LOW),
            V((n_col, n_dp * rows_q, width), LOW),
            V((2, n_dp * rows_q, width), LOW),
            weight,
            weight,
            weight,
            weight_t,
            weight_t,
            weight_t,
            V((half, 2 * width), LOW),
            V((half, 2 * width), LOW),
            V((half, 2 * width), LOW),
            both,
            both,
            V((width, here), LOW),
            V((2 * half, here), LOW),
            V((2 * half, here), LOW),
            both,
            whole,
            whole,
            whole,
            V((width, here), LOW),
            V((n_col, n_dp * rows_g, width), LOW),
            V((n_col, n_dp * quarter_rows(unit, n_dp), width), LOW),
            row,
            row,
            row,
            row,
            row,
            V((width, 128), FULL),
            pltpu.SemaphoreType.DMA((count,)),
            pltpu.SemaphoreType.DMA((count,)),
            pltpu.SemaphoreType.DMA((moves,)),
        ],
        compiler_params=pltpu.CompilerParams(
            collective_id=3, has_side_effects=True, vmem_limit_bytes=62 * 2**20
        ),
        cost_estimate=pl.CostEstimate(
            flops=18 * 2 * half * width * here, bytes_accessed=2**25, transcendentals=0
        ),
    )(gain, attended, tokens, cotangent, cot_other, out_all, *ups, *downs)
    return out[0], out[1], out[2], out[3:3 + n_dp], out[3 + n_dp:-1], out[-1]


def quarter_rows(rows, n_dp):
    return -(-rows // (16 * n_dp)) * 16


def tail_kernel(
    n_dp, n_pair, gain_ref, inverse_ref, sums_ref, qkv_hbm, dq_hbm, dk_hbm, dv_hbm, normed_hbm,
    tokens_hbm, middle_hbm, *refs,
):
    n_col = 2 * n_pair
    grads_hbms, refs = refs[:n_dp], refs[n_dp:]
    down_hbms, refs = refs[:n_col], refs[n_col:]
    (
        result_hbm, qkv_out, grads_out, down_out, sums_out,
        qkv, dproj, normed, tokens, middle, result, row_send, row_recv, own, pair_send, pair_recv,
        dp_send, dp_recv, dp_own, cross_send, cross_recv, cs_send, cs_recv, final, grads_parts,
        grads_send, grads_recv, grads_final, down_parts, down_send, down_recv, down_final,
        far_own, far_recv, far_send, far_parts,
        inner_send, inner_recv, sums_send, sums_recv, last_sums, send_sems, recv_sems, local_sems,
    ) = refs
    r, s = lax.axis_index("row"), lax.axis_index("cs")
    j, d = lax.axis_index("cp"), lax.axis_index("dp")
    width, here = tokens.shape
    cols = dq_hbm.shape[0]
    quartered = (1, n_pair + 1)
    whole = [k for k in range(n_col) if k not in quartered]
    share = width // n_dp
    part = share // 2
    rows_d = down_final.shape[0]
    subs = row_send.shape[1]
    piece = here // subs
    c_first = (s * n_pair + j) ^ (r * n_pair)
    near = r == s
    sems = (send_sems, recv_sems)
    gain = column(half_row(gain_ref, r))
    counter, local_counter = iter(range(1000)), iter(range(1000))
    sent, stored = [], []

    def send(src, dst, device):
        copy = remote(src, dst, sems, next(counter), device)
        copy.start()
        sent.append(copy)
        return copy

    def move(src, dst):
        copy = pltpu.make_async_copy(src, dst, local_sems.at[next(local_counter)])
        copy.start()
        return copy

    def down_rows(owner):
        return pl.ds(pl.multiple_of(owner * rows_d, 16), rows_d)

    load_grads = [move(grads_hbms[k], grads_parts.at[k]) for k in range(n_dp)]
    early = [
        move(dq_hbm, dproj.at[pl.ds(0, cols)]),
        move(dk_hbm, dproj.at[pl.ds(cols, cols)]),
        move(dv_hbm, dproj.at[pl.ds(2 * cols, cols)]),
        move(normed_hbm, normed),
    ]
    load_qkv = move(qkv_hbm, qkv)
    load_down = [move(down_hbms[k], down_parts.at[m]) for m, k in enumerate(whole)]
    load_far = [
        move(down_hbms[k].at[down_rows(d)], far_own.at[m]) for m, k in enumerate(quartered)
    ]
    late = [move(tokens_hbm, tokens), move(middle_hbm, middle)]

    sibling_id = {"row": 1 - r}
    cs_id = {"cs": 1 - s}
    dp_ids = [{"dp": d ^ k} for k in range(1, n_dp)]
    col_ids = [{"cs": s ^ (k // n_pair), "cp": j ^ (k % n_pair)} for k in range(1, n_col)]
    greet([sibling_id] + dp_ids + col_ids)


    for copy in load_grads:
        copy.wait()

    def summed(place_at):
        value = grads_parts[0, place_at].astype(FULL)
        for k in range(1, n_dp):
            value = value + grads_parts[k, place_at].astype(FULL)
        return value

    grads_copies = []
    for k in range(1, n_col):
        grads_send[k - 1] = summed(c_first ^ k).astype(LOW)
        grads_copies.append(send(grads_send.at[k - 1], grads_recv.at[k - 1], col_ids[k - 1]))
    far_copies = [
        send(down_hbms[k].at[down_rows(d ^ peer)], far_recv.at[peer - 1, m], dp_ids[peer - 1])
        for m, k in enumerate(quartered)
        for peer in range(1, n_dp)
    ]

    def quarter(half, owner):
        at = pl.ds(pl.multiple_of(half * width + owner * share, 32), share)
        return mm(normed[at, :], dproj[...], 1, 1)

    def rows_of(half, chunk, u):
        at = pl.ds(pl.multiple_of(chunk * here + u * piece, 128), piece)
        return jnp.dot(
            qkv[half * width:(half + 1) * width, :], dproj[:, at], preferred_element_type=FULL
        )

    dp_copies = {}

    def send_part(k, p):
        rows = pl.ds(p * part, part)
        dp_copies[k, p] = send(
            dp_send.at[k - 1, :, rows], dp_recv.at[k - 1, :, rows], dp_ids[k - 1]
        )

    def quarters(k):
        for half in range(2):
            dp_send[k - 1, half] = quarter(half, d ^ k).astype(LOW)
        send_part(k, 0)

    row_copies, pair_copies = {}, []
    for copy in early:
        copy.wait()
    for k in reversed(range(1, n_dp)):
        quarters(k)
    for k in reversed(range(1, n_dp)):
        send_part(k, 1)
    for copy in load_far:
        copy.wait()
    for copy in far_copies:
        copy.wait_recv()
    far_z = []
    for m, k in enumerate(quartered):
        value = far_own[m].astype(FULL)
        for peer in range(1, n_dp):
            value = value + far_recv[peer - 1, m].astype(FULL)
        far_send[m] = value.astype(LOW)
        far_z.append(send(far_send.at[m], far_parts.at[m], col_ids[k - 1]))
    load_qkv.wait()
    for k in range(1, n_pair):
        for u in range(subs):
            row_send[k, u] = rows_of(1, j ^ k, u).astype(LOW)
            row_copies[k, u] = send(row_send.at[k, u], row_recv.at[k, u], sibling_id)
    for k in range(1, n_pair):
        for u in range(subs):
            value = rows_of(0, j ^ k, u)
            row_copies[k, u].wait_recv()
            pair_send[k - 1, u] = (value + row_recv[k, u].astype(FULL)).astype(LOW)
            pair_copies.append(
                send(pair_send.at[k - 1, u], pair_recv.at[k - 1, u], {"cp": j ^ k})
            )
    for copy in load_down:
        copy.wait()
    value = down_parts[0].astype(FULL)
    for m in range(1, n_col - 2):
        value = value + down_parts[m].astype(FULL)
    down_send[...] = value.astype(LOW)

    down_copies = [
        send(down_send.at[down_rows(d ^ k)], down_recv.at[k - 1], dp_ids[k - 1])
        for k in range(1, n_dp)
    ]
    for half in range(2):
        dp_own[half] = quarter(half, d)

    for u in range(subs):
        row_send[0, u] = rows_of(1, j, u).astype(LOW)
        row_copies[0, u] = send(row_send.at[0, u], row_recv.at[0, u], sibling_id)
    for u in range(subs):
        own[u] = rows_of(0, j, u)

    cs_copies = []

    def reduce_part(p):
        rows = slice(p * part, (p + 1) * part)
        for k in range(1, n_dp):
            dp_copies[k, p].wait_recv()

        def total(half):
            value = dp_own[half, rows]
            for k in range(1, n_dp):
                value = value + dp_recv[k - 1, half, rows].astype(FULL)
            return value

        cross_send[p] = total(1).astype(LOW)
        cross_copy = send(cross_send.at[p], cross_recv.at[p], sibling_id)
        kept = total(0)
        cross_copy.wait_recv()
        crossed = cross_recv[p].astype(FULL)
        cs_send[p] = jnp.where(near, crossed, kept).astype(LOW)
        cs_copies.append(send(cs_send.at[p], cs_recv.at[p], cs_id))
        dp_own[0, rows] = jnp.where(near, kept, crossed)

    reduce_part(0)

    reduce_part(1)

    value = down_send[down_rows(d)].astype(FULL)
    for k in range(1, n_dp):
        down_copies[k - 1].wait_recv()
        value = value + down_recv[k - 1].astype(FULL)
    for m in range(2):
        far_z[m].wait_recv()
        value = value + far_parts[m].astype(FULL)
    down_final[...] = value.astype(LOW)
    out_copies = [send(down_final, down_out.at[d], peer) for peer in dp_ids]
    stored.append(move(down_final, down_out.at[d]))

    value = summed(c_first)
    for k in range(1, n_col):
        grads_copies[k - 1].wait_recv()
        value = value + grads_recv[k - 1].astype(FULL)
    grads_final[...] = value.astype(LOW)
    out_copies += [send(grads_final, grads_out.at[d], peer) for peer in dp_ids]
    stored.append(move(grads_final, grads_out.at[d]))

    for copy in late:
        copy.wait()
    for copy in pair_copies:
        copy.wait_recv()
    inverse = inverse_ref[...]
    for u in range(subs):
        row_copies[0, u].wait_recv()
        at = slice(u * piece, (u + 1) * piece)
        value = own[u] + row_recv[0, u].astype(FULL)
        for k in range(1, n_pair):
            value = value + pair_recv[k - 1, u].astype(FULL)
        own[u] = value
        inner_send[:, at] = jnp.sum(
            value * gain * tokens[:, at].astype(FULL), axis=0, keepdims=True
        )
    inner_copy = send(inner_send, inner_recv, sibling_id)

    def finish_part(p):
        cs_copies[p].wait_recv()
        rows = slice(p * part, (p + 1) * part)
        final[p] = (dp_own[0, rows] + cs_recv[p].astype(FULL)).astype(LOW)
        target = qkv_out.at[d, pl.ds(p * part, part)]
        out_copies.extend([send(final.at[p], target, peer) for peer in dp_ids])
        stored.append(move(final.at[p], target))

    finish_part(0)
    narrow = jnp.zeros((width, 128), FULL)
    for u in range(subs):
        at = slice(u * piece, (u + 1) * piece)
        wide = own[u] * tokens[:, at].astype(FULL) * inverse[:, at]
        for v in range(piece // 128):
            narrow = narrow + wide[:, v * 128:(v + 1) * 128]
    gain_part = jnp.sum(narrow.T, axis=0, keepdims=True)
    sums_send[0] = jnp.concatenate([gain_part, sums_ref[1:]], 0)
    sums_copies = {}

    def send_sums(step, peers):
        for k, peer in enumerate(peers):
            sums_copies[step, k] = send(sums_send.at[step], sums_recv.at[step, k], peer)

    def add_sums(step, members):
        value = sums_send[step]
        for k in range(members - 1):
            sums_copies[step, k].wait_recv()
            value = value + sums_recv[step, k]
        sums_send[step + 1] = value

    send_sums(0, dp_ids)
    inner_copy.wait_recv()
    inner = (inner_send[...] + inner_recv[...]) / D
    for u in range(subs):
        at = slice(u * piece, (u + 1) * piece)
        result[:, at] = (
            middle[:, at]
            + inverse[:, at] * (own[u] * gain)
            - tokens[:, at].astype(FULL)
            * (inverse[:, at] * inverse[:, at] * inverse[:, at] * inner[:, at])
        )
    stored.append(move(result, result_hbm))
    add_sums(0, n_dp)
    send_sums(1, col_ids)
    finish_part(1)

    add_sums(1, n_col)
    sums_copy = send(sums_send.at[2], last_sums, sibling_id)
    sums_copy.wait_recv()
    sums_out[0] = sums_send[2]
    sums_out[1] = last_sums[...]
    for copy in out_copies:
        copy.wait_recv()
    for copy in stored:
        copy.wait()
    for copy in sent:
        copy.wait_send()


def tail(n_dp, n_pair, gain, inverse, sums, qkv, dq, dk, dv, normed, tokens, middle, grads, downs):
    width, here = tokens.shape
    length = normed.shape[1]
    cols = dq.shape[0]
    unit = downs[0].shape[0]
    rows_d = unit // n_dp
    share = width // n_dp
    subs = 2
    piece = here // subs
    n_col = 2 * n_pair
    part = grads[0].shape[1:]
    wide = 3 * cols
    count = 2 * n_pair * subs + 10 * n_dp + 2 * n_col + 14
    moves = 15 + n_dp + n_col
    hbm = pl.BlockSpec(memory_space=pl.ANY)
    vmem = pl.BlockSpec(memory_space=pltpu.VMEM)
    V = pltpu.VMEM
    halves = V((2, share // 2, wide), LOW)
    return pl.pallas_call(
        functools.partial(tail_kernel, n_dp, n_pair),
        out_shape=(
            jax.ShapeDtypeStruct((width, here), FULL),
            jax.ShapeDtypeStruct((n_dp, share, wide), LOW),
            jax.ShapeDtypeStruct((n_dp,) + part, LOW),
            jax.ShapeDtypeStruct((n_dp, rows_d, width), LOW),
            jax.ShapeDtypeStruct((2,) + sums.shape, FULL),
        ),
        in_specs=[vmem] * 3 + [hbm] * (7 + n_dp + n_col),
        out_specs=(hbm,) * 4 + (vmem,),
        scratch_shapes=[
            V((2 * width, wide), LOW),
            V((wide, length), LOW),
            V((2 * width, length), LOW),
            V((width, here), LOW),
            V((width, here), FULL),
            V((width, here), FULL),
            V((n_pair, subs, width, piece), LOW),
            V((n_pair, subs, width, piece), LOW),
            V((subs, width, piece), FULL),
            V((n_pair - 1, subs, width, piece), LOW),
            V((n_pair - 1, subs, width, piece), LOW),
            V((n_dp - 1, 2, share, wide), LOW),
            V((n_dp - 1, 2, share, wide), LOW),
            V((2, share, wide), FULL),
            halves,
            halves,
            halves,
            halves,
            halves,
            V((n_dp, n_col) + part, LOW),
            V((n_col - 1,) + part, LOW),
            V((n_col - 1,) + part, LOW),
            V(part, LOW),
            V((n_col - 2, unit, width), LOW),
            V((n_dp * rows_d, width), LOW),
            V((n_dp - 1, rows_d, width), LOW),
            V((rows_d, width), LOW),
            V((2, rows_d, width), LOW),
            V((n_dp - 1, 2, rows_d, width), LOW),
            V((2, rows_d, width), LOW),
            V((2, rows_d, width), LOW),
            V((1, here), FULL),
            V((1, here), FULL),
            V((3,) + sums.shape, FULL),
            V((2, max(n_dp, n_col) - 1) + sums.shape, FULL),
            V(sums.shape, FULL),
            pltpu.SemaphoreType.DMA((count,)),
            pltpu.SemaphoreType.DMA((count,)),
            pltpu.SemaphoreType.DMA((moves,)),
        ],
        compiler_params=pltpu.CompilerParams(
            collective_id=1, has_side_effects=True, vmem_limit_bytes=62 * 2**20
        ),
        cost_estimate=pl.CostEstimate(
            flops=8 * wide * width * length, bytes_accessed=2**25, transcendentals=0
        ),
    )(gain, inverse, sums, qkv, dq, dk, dv, normed, tokens, middle, *grads, *downs)


def on_device(
    tokens,
    segment_ids,
    padding_mask,
    w_qkv,
    w_out,
    w_up,
    w_down,
    gain_attn,
    gain_mlp,
    scale_raw,
    cotangent,
):
    width, here = tokens.shape
    r, s = lax.axis_index("row"), lax.axis_index("cs")
    j, d = lax.axis_index("cp"), lax.axis_index("dp")
    n_pair, n_dp, n_col = lax.axis_size("cp"), lax.axis_size("dp"), lax.axis_size(COLS)
    c = s * n_pair + j
    head_cols = w_qkv.shape[0] // (3 * width)
    heads = head_cols // HEAD
    near = r == s

    ids = jnp.concatenate([segment_ids, padding_mask], 0)
    ids = jnp.where(s == r, ids, sibling(ids))
    segments, padding = ids[0], ids[1]
    length = segments.shape[0]
    firsts = segments[::BLOCK]
    starts = jnp.sum((segments[None, :] < firsts[:, None]).astype(jnp.int32), axis=1)
    filled = (jnp.sum(padding) + BLOCK - 1) // BLOCK
    blocks = jnp.arange(length // BLOCK, dtype=jnp.int32)
    lo = starts // BLOCK
    hi = jnp.minimum(blocks, filled)
    gain_one, gain_two = gain_attn[None, :], gain_mlp[None, :]
    scale_row = scale_raw[None, :]

    block = w_qkv.reshape(width, 3 * head_cols)
    down = w_down.reshape(-1, width)
    unit = down.shape[0]
    part_rows = quarter_rows(unit, n_dp)

    def quarters(matrix):
        padded = jnp.pad(matrix, ((0, n_dp * part_rows - unit), (0, 0)))
        return padded.reshape(n_dp, part_rows, width)

    out = lax.dynamic_index_in_dim(quarters(w_out.reshape(-1, width)), d, 0, keepdims=False)
    up = lax.dynamic_index_in_dim(quarters(w_up.reshape(width, -1).T), d, 0, keepdims=False)
    (
        queries, key_heads, values, query_raw, normed_one, qkv, out_all, ups, cot_other,
        inverse_one,
    ) = head(
        n_dp, n_pair, gain_one, scale_row, tokens, cotangent, block, out, up,
        quarters(down),
    )
    ups = gather(ups, "dp")
    downs = [down] + [
        lax.ppermute(down, COLS, [(i, i ^ k) for i in range(n_col)])
        for k in range(2, n_col)
        if k != n_pair + 1
    ]
    attended, logs = attention_forward(queries, key_heads, values, ids, ids, lo, hi)
    result, grad_middle, grad_attended, grads, down_grads, gain_two_part = middle_part(
        n_dp, n_pair, gain_two, attended, tokens, cotangent, cot_other, out_all, ups, downs
    )
    received = [grads[0]] + [shift(grads[k], "dp", k) for k in range(1, n_dp)]
    down_received = [
        down_grads[k]
        if k in (0, 1, n_pair + 1)
        else lax.ppermute(down_grads[k], COLS, [(i, i ^ k) for i in range(n_col)])
        for k in range(n_col)
    ]

    dq, dk, dv, sums = attention_backward(
        queries, key_heads, values, attended, grad_attended, logs, query_raw, scale_row, gain_two_part,
        ids, ids, lo, hi,
    )
    grad_tokens, grad_qkv, final, final_down, sums = tail(
        n_dp, n_pair, gain_one, inverse_one, sums, qkv, dq, dk, dv, normed_one, tokens,
        grad_middle, received, down_received,
    )
    grad_qkv = grad_qkv.astype(FULL)
    final = final.reshape(-1, width)
    final = [final[i * unit:(i + 1) * unit].astype(FULL) for i in range(2)]
    final.append(final_down.reshape(-1, width)[:unit].astype(FULL))
    own, other = sums[0], sums[1]
    first = r == 0
    gains = jnp.concatenate(
        [jnp.where(first, own[:2], other[:2]), jnp.where(first, other[:2], own[:2])], 1
    )
    scale_total = (own[2] + other[2])[:HEAD]
    return (
        result,
        grad_tokens,
        grad_qkv.reshape(-1),
        final[0].reshape(-1),
        final[1].T.reshape(-1),
        final[2].reshape(-1),
        gains[0],
        gains[1],
        scale_total,
    )


def solution(mesh):
    n_dp, n_row, n_col = (mesh.shape[name] for name in ("dp", "row", "col"))
    split = Mesh(
        np.asarray(mesh.devices).reshape(n_dp, n_row, n_row, n_col // n_row),
        ("dp", "row", "cs", "cp"),
    )
    rows = P("row", ("dp", "cs", "cp"))
    ids = P(("dp", "row"), None)
    blocks = P(("row", "cs", "cp"))
    return jax.shard_map(
        on_device,
        mesh=split,
        in_specs=(rows, ids, ids, blocks, blocks, blocks, blocks, P(), P(), P(), rows),
        out_specs=(rows, rows, blocks, blocks, blocks, blocks, P(), P(), P()),
        check_vma=False,
    )
```

```python
import functools
import math

import jax
import jax.numpy as jnp
import numpy as np
from jax import lax
from jax.experimental import pallas as pl
from jax.experimental.pallas import tpu as pltpu
from jax.sharding import Mesh, PartitionSpec as P

D = 1280
HEAD = 80
EPSILON = 1e-06
LOG_TWO_E = 1.442695041
BLOCK = 256
LOW = jnp.bfloat16
FULL = jnp.float32
COLS = ("cs", "cp")


def mm(left, right, left_axis, right_axis):
    return lax.dot_general(
        left, right, (((left_axis,), (right_axis,)), ((), ())), preferred_element_type=FULL
    )


def shift(x, axis, k):
    n = lax.axis_size(axis)
    return lax.ppermute(x, axis, [(i, i ^ k) for i in range(n)])


def sibling(x):
    return shift(x, "row", 1)


def cut(x, index, count, axis):
    step = x.shape[axis] // count
    return lax.dynamic_slice_in_dim(x, index * step, step, axis)


def gather(x, axis):
    return [x] + [shift(x, axis, k) for k in range(1, lax.axis_size(axis))]


def diag_mask(segq, segk):
    size = segk.shape[0], segq.shape[1]
    ki = lax.broadcasted_iota(jnp.int32, size, 0)
    qi = lax.broadcasted_iota(jnp.int32, size, 1)
    return ((segk == segq) & (ki <= qi)) | (ki == qi)


def softplus_scale(row):
    return LOG_TWO_E / math.sqrt(HEAD) * jnp.log1p(jnp.exp(row))


def half_row(ref, which):
    size = ref.shape[1] // 2
    return jnp.where(which == 0, ref[:, :size], ref[:, size:])


def column(row):
    return jnp.broadcast_to(row, (8, row.shape[1])).T[:, :1]


def rows_of(h):
    return slice(h * HEAD, (h + 1) * HEAD)


def forward_kernel(heads, lo_ref, hi_ref, q_ref, k_ref, v_ref, segq_ref, segk_ref, o_ref, log_ref, ks, segks):
    i = pl.program_id(0)

    here = pl.ds(pl.multiple_of(i * BLOCK, BLOCK), BLOCK)
    for h in range(heads):
        ks[h, here, :] = k_ref[rows_of(h), here].T
    segks[here, :] = column(jnp.where(segk_ref[1:, here] == 1, segk_ref[:1, here], -1).astype(FULL))
    segq = segq_ref[:1].astype(FULL)

    def visit(kb, carry, diagonal):
        at = pl.ds(pl.multiple_of(kb * BLOCK, BLOCK), BLOCK)
        segk = segks[at, :]
        mask = diag_mask(segq, segk) if diagonal else segk == segq
        scores = [
            jnp.dot(ks[h, at, :], q_ref[rows_of(h), :], preferred_element_type=FULL)
            for h in range(heads)
        ]
        peaks, totals, weights = [], [], []
        for h in range(heads):
            s = jnp.where(mask, scores[h], -1e30)
            peak = jnp.max(s, axis=0, keepdims=True)
            if not diagonal:
                peak = jnp.maximum(carry[h][0], peak)
            p = jnp.exp(s - peak)
            peaks.append(peak)
            totals.append(jnp.sum(p, axis=0, keepdims=True))
            weights.append(p.astype(LOW))
        out = []
        for h in range(heads):
            new = jnp.dot(v_ref[rows_of(h), at], weights[h], preferred_element_type=FULL)
            total = totals[h]
            if not diagonal:
                m, l, acc = carry[h]
                keep = jnp.exp(m - peaks[h])
                total = l * keep + total
                new = acc * keep + new
            out.append((peaks[h], total, new))
        return tuple(out)

    carry = visit(i, None, True)
    carry = lax.fori_loop(lo_ref[i], hi_ref[i], lambda kb, c: visit(kb, c, False), carry)
    for h in range(heads):
        m, l, acc = carry[h]
        o_ref[h * HEAD:(h + 1) * HEAD, :] = (acc / l).astype(LOW)
        log_ref[h] = m + jnp.log(l)


def attention_forward(q, k, v, segq, segk, lo, hi):
    cols, length = q.shape
    heads = cols // HEAD
    steps = length // BLOCK
    whole = pl.BlockSpec((cols, length), lambda i, *_: (0, 0))
    part = pl.BlockSpec((cols, BLOCK), lambda i, *_: (0, i))
    return pl.pallas_call(
        functools.partial(forward_kernel, heads),
        out_shape=(
            jax.ShapeDtypeStruct((cols, length), LOW),
            jax.ShapeDtypeStruct((heads, 1, length), FULL),
        ),
        grid_spec=pltpu.PrefetchScalarGridSpec(
            num_scalar_prefetch=2,
            grid=(steps,),
            in_specs=[
                part,
                whole,
                whole,
                pl.BlockSpec((2, BLOCK), lambda i, *_: (0, i)),
                pl.BlockSpec((2, length), lambda i, *_: (0, 0)),
            ],
            out_specs=(part, pl.BlockSpec((heads, 1, BLOCK), lambda i, *_: (0, 0, i))),
            scratch_shapes=[pltpu.VMEM((heads, length, HEAD), LOW), pltpu.VMEM((length, 1), FULL)],
        ),
        compiler_params=pltpu.CompilerParams(vmem_limit_bytes=62 * 2**20),
        cost_estimate=pl.CostEstimate(
            flops=8 * 2 * length * length * cols,
            bytes_accessed=4 * cols * length * 2,
            transcendentals=heads * length * length // 3,
        ),
    )(lo, hi, q, k, v, segq, segk)


def backward_kernel(
    heads, lo_ref, hi_ref, q_ref, k_ref, v_ref, o_ref, go_ref, log_ref, raw_ref, scale_ref,
    gain_ref, segq_ref, segk_ref, dq_ref, dk_ref, dv_ref, sums_ref, ks, vs, qs, gs, dks, dvs, dqs, segks, total,
):
    i = pl.program_id(0)

    @pl.when(i == 0)
    def _():
        sums_ref[...] = jnp.zeros_like(sums_ref)
        total[...] = jnp.zeros_like(total)

    here = pl.ds(pl.multiple_of(i * BLOCK, BLOCK), BLOCK)
    for h in range(heads):
        ks[h, here, :] = k_ref[rows_of(h), here].T
        vs[h, here, :] = v_ref[rows_of(h), here].T
    segks[here, :] = column(jnp.where(segk_ref[1:, here] == 1, segk_ref[:1, here], -1).astype(FULL))
    segq = segq_ref[:1].astype(FULL)
    inner = [
        jnp.sum(
            o_ref[h * HEAD:(h + 1) * HEAD, :].astype(FULL)
            * go_ref[h * HEAD:(h + 1) * HEAD, :].astype(FULL),
            axis=0,
            keepdims=True,
        )
        for h in range(heads)
    ]

    for h in range(heads):
        qs[h] = q_ref[rows_of(h), :].T
        gs[h] = go_ref[rows_of(h), :].T

    def visit(kb, diagonal):
        at = pl.ds(pl.multiple_of(kb * BLOCK, BLOCK), BLOCK)
        segk = segks[at, :]
        mask = diag_mask(segq, segk) if diagonal else segk == segq
        scores = [
            jnp.dot(ks[h, at, :], q_ref[rows_of(h), :], preferred_element_type=FULL)
            for h in range(heads)
        ]
        dps = [
            jnp.dot(vs[h, at, :], go_ref[rows_of(h), :], preferred_element_type=FULL)
            for h in range(heads)
        ]
        ps, dss = [], []
        for h in range(heads):
            p = jnp.where(mask, jnp.exp(scores[h] - log_ref[h]), 0.0)
            dss.append((p * (dps[h] - inner[h])).astype(LOW))
            ps.append(p.astype(LOW))
        for h in range(heads):
            new_v = jnp.dot(ps[h], gs[h], preferred_element_type=FULL)
            new_k = jnp.dot(dss[h], qs[h], preferred_element_type=FULL)
            new_q = jnp.dot(k_ref[rows_of(h), at], dss[h], preferred_element_type=FULL)
            if diagonal:
                dvs[h, at, :], dks[h, at, :], dqs[rows_of(h), :] = new_v, new_k, new_q
            else:
                dvs[h, at, :] += new_v
                dks[h, at, :] += new_k
                dqs[rows_of(h), :] += new_q

    visit(i, True)

    @pl.loop(lo_ref[i], hi_ref[i])
    def _(kb):
        visit(kb, False)

    factor = column(softplus_scale(scale_ref[...]))
    part = jnp.zeros((HEAD, 1), FULL)
    for h in range(heads):
        rows = slice(h * HEAD, (h + 1) * HEAD)
        dq = dqs[rows, :]
        part = part + jnp.sum(dq * raw_ref[rows, :], axis=1, keepdims=True)
        dq_ref[rows, :] = (dq * factor).astype(LOW)
    total[...] += part

    @pl.when(i == pl.num_programs(0) - 1)
    def _():
        for h in range(heads):
            dk_ref[rows_of(h), :] = dks[h].astype(LOW).T
            dv_ref[rows_of(h), :] = dvs[h].astype(LOW).T
        sums_ref[1:2, :] = gain_ref[...]
        row = jnp.broadcast_to(total[...], (HEAD, 128)).T[:1]
        slope = LOG_TWO_E / math.sqrt(HEAD) * jax.nn.sigmoid(scale_ref[...])
        sums_ref[2:3, :HEAD] = row * slope


def attention_backward(q, k, v, o, go, logs, raw, scale, gain_part, segq, segk, lo, hi):
    cols, length = q.shape
    heads = cols // HEAD
    steps = length // BLOCK
    whole = pl.BlockSpec((cols, length), lambda i, *_: (0, 0))
    part = pl.BlockSpec((cols, BLOCK), lambda i, *_: (0, i))
    width = gain_part.shape[1]
    total = pl.BlockSpec((8, width), lambda i, *_: (0, 0))
    shape = jax.ShapeDtypeStruct((cols, length), LOW)
    return pl.pallas_call(
        functools.partial(backward_kernel, heads),
        out_shape=(shape, shape, shape, jax.ShapeDtypeStruct((8, width), FULL)),
        grid_spec=pltpu.PrefetchScalarGridSpec(
            num_scalar_prefetch=2,
            grid=(steps,),
            in_specs=[
                part,
                whole,
                whole,
                part,
                part,
                pl.BlockSpec((heads, 1, BLOCK), lambda i, *_: (0, 0, i)),
                part,
                pl.BlockSpec((1, HEAD), lambda i, *_: (0, 0)),
                pl.BlockSpec((1, width), lambda i, *_: (0, 0)),
                pl.BlockSpec((2, BLOCK), lambda i, *_: (0, i)),
                pl.BlockSpec((2, length), lambda i, *_: (0, 0)),
            ],
            out_specs=(part, whole, whole, total),
            scratch_shapes=[
                pltpu.VMEM((heads, length, HEAD), LOW),
                pltpu.VMEM((heads, length, HEAD), LOW),
                pltpu.VMEM((heads, BLOCK, HEAD), LOW),
                pltpu.VMEM((heads, BLOCK, HEAD), LOW),
                pltpu.VMEM((heads, length, HEAD), FULL),
                pltpu.VMEM((heads, length, HEAD), FULL),
                pltpu.VMEM((cols, BLOCK), FULL),
                pltpu.VMEM((length, 1), FULL),
                pltpu.VMEM((HEAD, 1), FULL),
            ],
        ),
        compiler_params=pltpu.CompilerParams(vmem_limit_bytes=62 * 2**20),
        cost_estimate=pl.CostEstimate(
            flops=8 * 5 * length * length * cols,
            bytes_accessed=8 * cols * length * 2,
            transcendentals=heads * length * length // 3,
        ),
    )(lo, hi, q, k, v, o, go, logs, raw, scale, gain_part, segq, segk)


def remote(src, dst, sems, index, device):
    return pltpu.make_async_remote_copy(
        src_ref=src,
        dst_ref=dst,
        send_sem=sems[0].at[index],
        recv_sem=sems[1].at[index],
        device_id=device,
        device_id_type=pl.DeviceIdType.MESH,
    )


def greet(peers):
    barrier = pltpu.get_barrier_semaphore()
    for peer in peers:
        pl.semaphore_signal(barrier, inc=1, device_id=peer, device_id_type=pl.DeviceIdType.MESH)
    pl.semaphore_wait(barrier, len(peers))


def head_kernel(
    n_dp, n_pair, gain_ref, raw_ref, tokens_hbm, cot_hbm, block_hbm, out_hbm, up_hbm,
    down_hbm, q_hbm, k_hbm, v_hbm, raw_hbm, normed_hbm, qkv_hbm, out_all, ups_hbm, cot_out, inverse_ref,
    tokens, others, block, cs_recv, remote_block, pass_on, qkv, turned, normed, q, k, v, raw,
    send_sems, recv_sems, local_sems,
):
    r, s = lax.axis_index("row"), lax.axis_index("cs")
    j, d = lax.axis_index("cp"), lax.axis_index("dp")
    n_col = 2 * n_pair
    subs, width, piece = tokens.shape[1:]
    here = subs * piece
    share = cs_recv.shape[0]
    cols = q.shape[0]
    c_first = (s * n_pair + j) ^ (r * n_pair)
    near = r == s
    sems = (send_sems, recv_sems)
    counter, local_counter = iter(range(1000)), iter(range(1000))
    sent, stored = [], []

    def send(src, dst, device):
        copy = remote(src, dst, sems, next(counter), device)
        copy.start()
        sent.append(copy)
        return copy

    def move(src, dst):
        copy = pltpu.make_async_copy(src, dst, local_sems.at[next(local_counter)])
        copy.start()
        return copy

    def store(src, dst):
        stored.append(move(src, dst))

    def columns(u):
        return pl.ds(u * piece, piece)

    own_tokens = [move(tokens_hbm.at[:, columns(u)], tokens.at[0, u]) for u in range(subs)]
    own_block = move(block_hbm, block)
    own_out = move(out_hbm, out_all.at[d, c_first])
    store(up_hbm, ups_hbm.at[c_first])
    sibling_id = {"row": 1 - r}
    dp_ids = [{"dp": d ^ k} for k in range(1, n_dp)]
    col_ids = [{"cs": s ^ (k // n_pair), "cp": j ^ (k % n_pair)} for k in range(1, n_col)]
    greet([sibling_id] + dp_ids + col_ids)

    cs_copy = send(block_hbm.at[d], cs_recv, {"cs": 1 - s})
    down_ids = [col_ids[0], col_ids[n_pair]]
    down_copies = [
        send(down_hbm.at[d], ups_hbm.at[n_col + m], peer) for m, peer in enumerate(down_ids)
    ]
    out_copies = [send(out_hbm, out_all.at[d, c_first], peer) for peer in col_ids]
    other_copies = {}
    for u in range(subs):
        other_copies[0, u] = send(tokens_hbm.at[:, columns(u)], others.at[0, u], sibling_id)
    pair_copies = {}

    def send_pairs(u):
        for m in range(1, n_pair):
            pair_copies[m, u] = send(
                tokens_hbm.at[:, columns(u)], tokens.at[m, u], {"cp": j ^ m}
            )

    send_pairs(0)

    cot_copy = send(cot_hbm, cot_out, sibling_id)
    gain_own = column(half_row(gain_ref, r))
    gain_other = column(half_row(gain_ref, 1 - r))
    factor = jnp.concatenate([column(softplus_scale(raw_ref[...]))] * (cols // HEAD), 0)

    def norm(m, u):
        own, other = tokens[m, u].astype(FULL), others[m, u].astype(FULL)
        squares = jnp.sum(own * own, axis=0, keepdims=True)
        squares = squares + jnp.sum(other * other, axis=0, keepdims=True)
        inverse = lax.rsqrt(squares / D + EPSILON)
        at = pl.ds(pl.multiple_of((j ^ m) * here + u * piece, 128), piece)
        normed[:width, at] = (own * inverse * gain_own).astype(LOW)
        normed[width:, at] = (other * inverse * gain_other).astype(LOW)
        store(normed.at[:, at], normed_hbm.at[:, at])
        if m == 0:
            inverse_ref[:, columns(u)] = inverse

    def project(m, u):
        at = pl.ds(pl.multiple_of((j ^ m) * here + u * piece, 128), piece)
        for part, out in ((0, None), (1, k), (2, v)):
            value = jnp.dot(
                turned[part * cols:(part + 1) * cols, :], normed[:, at],
                preferred_element_type=FULL,
            )
            if part == 0:
                raw[:, at] = value
                q[:, at] = (value * factor).astype(LOW)
            else:
                out[:, at] = value.astype(LOW)
        for src, dst in ((q, q_hbm), (k, k_hbm), (v, v_hbm), (raw, raw_hbm)):
            store(src.at[:, at], dst.at[:, at])

    for u in range(subs):
        own_tokens[u].wait()
        other_copies[0, u].wait_recv()
        norm(0, u)
    own_block.wait()

    cs_copy.wait_recv()
    send_pairs(1)
    dp_copies = [send(cs_recv, remote_block.at[d], peer) for peer in dp_ids]
    own_out.wait()
    for copy in out_copies:
        copy.wait_recv()
    late_copies = [send(out_all.at[d], out_all.at[d], peer) for peer in dp_ids]
    remote_block[d] = cs_recv[...]
    for u in range(subs - 1):
        for m in range(1, n_pair):
            pair_copies[m, u].wait_recv()
            other_copies[m, u] = send(tokens.at[m, u], others.at[m, u], sibling_id)
    cross_copies = []
    for m in range(n_dp):
        owner = d ^ m
        if m:
            dp_copies[m - 1].wait_recv()
        mine, its = block[owner], remote_block[owner]
        at = pl.multiple_of(owner * share, 32)
        qkv[pl.ds(at, share)] = jnp.where(near, mine, its)
        pass_on[owner] = jnp.where(near, its, mine)
        cross_copies.append(
            send(pass_on.at[owner], qkv.at[pl.ds(width + at, share)], sibling_id)
        )
    u = subs - 1
    for m in range(1, n_pair):
        pair_copies[m, u].wait_recv()
        other_copies[m, u] = send(tokens.at[m, u], others.at[m, u], sibling_id)
    late_copies += [send(up_hbm, ups_hbm.at[c_first], peer) for peer in col_ids]
    turned[:, :width] = qkv[:width].T
    for copy in cross_copies:
        copy.wait_recv()
    turned[:, width:] = qkv[width:].T
    store(qkv, qkv_hbm)

    for u in range(subs):
        project(0, u)
    for u in range(subs):
        for m in range(1, n_pair):
            other_copies[m, u].wait_recv()
            norm(m, u)
            project(m, u)

    for copy in stored:
        copy.wait()
    for copy in late_copies + down_copies + [cot_copy]:
        copy.wait_recv()
    for copy in sent:
        copy.wait_send()


def head(n_dp, n_pair, gain, scale, tokens, cotangent, block, out, up, down):
    width, here = tokens.shape
    wide = block.shape[1]
    cols = wide // 3
    share = width // n_dp
    length = n_pair * here
    n_col = 2 * n_pair
    subs = 2
    piece = here // subs
    count = subs * n_pair * 2 + 4 * n_dp + 2 * n_col + 7
    moves = 4 + subs + 5 * subs * n_pair + 4
    hbm = pl.BlockSpec(memory_space=pl.ANY)
    vmem = pl.BlockSpec(memory_space=pltpu.VMEM)
    V = pltpu.VMEM
    shape = jax.ShapeDtypeStruct((cols, length), LOW)
    return pl.pallas_call(
        functools.partial(head_kernel, n_dp, n_pair),
        out_shape=(
            shape,
            shape,
            shape,
            jax.ShapeDtypeStruct((cols, length), FULL),
            jax.ShapeDtypeStruct((2 * width, length), LOW),
            jax.ShapeDtypeStruct((2 * width, wide), LOW),
            jax.ShapeDtypeStruct((n_dp, n_col) + out.shape, LOW),
            jax.ShapeDtypeStruct((n_col + 2,) + up.shape, LOW),
            jax.ShapeDtypeStruct((width, here), LOW),
            jax.ShapeDtypeStruct((1, here), FULL),
        ),
        in_specs=[vmem] * 2 + [hbm] * 6,
        out_specs=(hbm,) * 9 + (vmem,),
        scratch_shapes=[
            V((n_pair, subs, width, piece), LOW),
            V((n_pair, subs, width, piece), LOW),
            V((n_dp, share, wide), LOW),
            V((share, wide), LOW),
            V((n_dp, share, wide), LOW),
            V((n_dp, share, wide), LOW),
            V((2 * width, wide), LOW),
            V((wide, 2 * width), LOW),
            V((2 * width, length), LOW),
            V((cols, length), LOW),
            V((cols, length), LOW),
            V((cols, length), LOW),
            V((cols, length), FULL),
            pltpu.SemaphoreType.DMA((count,)),
            pltpu.SemaphoreType.DMA((count,)),
            pltpu.SemaphoreType.DMA((moves,)),
        ],
        compiler_params=pltpu.CompilerParams(
            collective_id=2, has_side_effects=True, vmem_limit_bytes=60 * 2**20
        ),
        cost_estimate=pl.CostEstimate(
            flops=4 * wide * width * length, bytes_accessed=2**25, transcendentals=0
        ),
    )(gain, scale, tokens, cotangent, block.reshape(n_dp, share, wide), out, up, down)


def middle_kernel(n_dp, n_pair, unit, gain_ref, att_hbm, tokens_hbm, cot_hbm, cot_other, out_all, *refs):
    n_col = 2 * n_pair
    up_hbms, refs = refs[:n_dp], refs[n_dp:]
    down_hbms, refs = refs[:n_col - 2], refs[n_col - 2:]
    result_hbm, middle_hbm, out_hbm, refs = refs[0], refs[1], refs[2], refs[3:]
    grads_hbms, refs = refs[:n_dp], refs[n_dp:]
    down_outs, refs = refs[:n_col], refs[n_col:]
    (
        gain_out, tokens, cot, out_slab, up_slab, down_slab, out_w, up_w, down_w, out_t, up_t, down_t, out_half, up_half,
        down_half, att, scaled, normed, active, grad_hidden, branch, middle, grad, result, grad_att,
        grads, down_grads, square_send, square_recv, inner_send, inner_recv, inverse, narrow,
        send_sems, recv_sems, local_sems,
    ) = refs
    r, s = lax.axis_index("row"), lax.axis_index("cs")
    j, d = lax.axis_index("cp"), lax.axis_index("dp")
    width, here = tokens.shape
    pieces, _, piece = square_send.shape
    cols = att_hbm.shape[0]
    half = n_col * unit // 2
    rows_q = up_hbms[0].shape[1]
    rows_g = grads_hbms[0].shape[1]
    c_first = (s * n_pair + j) ^ (r * n_pair)
    sems = (send_sems, recv_sems)
    gain = column(half_row(gain_ref, r))
    counter, local_counter = iter(range(1000)), iter(range(1000))
    sent, stored = [], []

    def send(src, dst, device):
        copy = remote(src, dst, sems, next(counter), device)
        copy.start()
        sent.append(copy)
        return copy

    def move(src, dst):
        copy = pltpu.make_async_copy(src, dst, local_sems.at[next(local_counter)])
        copy.start()
        return copy

    def columns(u):
        return pl.ds(u * piece, piece)

    def span(u):
        return slice(u * piece, (u + 1) * piece)

    def down_rows(owner):
        return pl.ds(pl.multiple_of(owner * unit, 16), unit)

    def quarter_of(owner):
        return pl.ds(pl.multiple_of(owner * rows_q, 16), rows_q)

    quartered = (1, n_pair + 1)
    own_rows, other_rows = pl.ds(0, width), pl.ds(width, width)
    weight_loads = [
        move(out_all.at[m], out_slab.at[:, pl.ds(m * rows_q, rows_q)]) for m in range(n_dp)
    ] + [
        move(up_hbms[m].at[pl.ds(first, size)], target.at[:, quarter_of(d ^ m)])
        for m in range(n_dp)
        for first, size, target in ((0, n_col, up_slab), (n_col, 2, down_slab))
    ] + [
        move(ref, down_w.at[down_rows(c_first ^ m)])
        for m, ref in zip([m for m in range(n_col) if m not in quartered], down_hbms)
    ]
    att_loads = [
        move(
            att_hbm.at[:, pl.ds(pl.multiple_of(j * here + u * piece, 128), piece)],
            att.at[pl.ds(pl.multiple_of(j * cols, 16), cols), columns(u)],
        )
        for u in range(pieces)
    ]
    token_load = move(tokens_hbm, tokens)
    cot_loads = [move(cot_hbm, cot.at[own_rows]), move(cot_other, cot.at[other_rows])]
    sibling_id = {"row": 1 - r}
    pair_ids = [{"cp": j ^ m} for m in range(1, n_pair)]
    greet([sibling_id] + pair_ids)

    att_copies = {}
    for u in range(pieces):
        for m in range(1, n_pair):
            att_copies[u, m] = send(
                att_hbm.at[:, pl.ds(pl.multiple_of((j ^ m) * here + u * piece, 128), piece)],
                att.at[pl.ds(pl.multiple_of(j * cols, 16), cols), columns(u)],
                pair_ids[m - 1],
            )

    for copy in weight_loads:
        copy.wait()
    for m in range(n_col):
        at = slice(m * unit, (m + 1) * unit)
        out_w[at] = out_slab[m, :unit]
        up_w[at] = up_slab[m, :unit]
    for m, k in enumerate(quartered):
        down_w[down_rows(c_first ^ k)] = down_slab[m, :unit]
    cross_copies = []

    def cross(whole, part):
        cross_copies.append(send(whole.at[pl.ds(half, half)], part.at[:, other_rows], sibling_id))
        part[:, :width] = whole[:half]

    cross(up_w, up_half)
    cross(down_w, down_half)
    cross(out_w, out_half)
    out_t[...] = out_w[...].T
    narrow[...] = jnp.zeros_like(narrow)

    copies = {}

    def exchange(name, u, ref):
        copies[name, u] = send(
            ref.at[own_rows, columns(u)], ref.at[other_rows, columns(u)], sibling_id
        )

    def share_heads(u):
        att_loads[u].wait()
        for m in range(1, n_pair):
            att_copies[u, m].wait_recv()
        exchange("att", u, att)

    def first_branch(u):
        if u == 0:
            token_load.wait()
        copies["att", u].wait_recv()
        value = tokens[:, span(u)].astype(FULL) + jnp.dot(
            out_t[...], att[:, span(u)], preferred_element_type=FULL
        )
        scaled[:width, span(u)] = (value * gain).astype(LOW)
        exchange("scaled", u, scaled)
        square_send[u] = jnp.sum(value * value, axis=0, keepdims=True)
        copies["square", u] = send(square_send.at[u], square_recv.at[u], sibling_id)
        middle[:, span(u)] = value

    def hidden_units(u):
        if u == 0:
            for copy in cot_loads:
                copy.wait()
            for copy in cross_copies:
                copy.wait_recv()
            up_t[...] = up_w[...].T
            down_t[...] = down_w[...].T
        grad_active = jnp.dot(down_half[...], cot[:, span(u)], preferred_element_type=FULL)
        copies["scaled", u].wait_recv()
        copies["square", u].wait_recv()
        scale = lax.rsqrt((square_send[u] + square_recv[u]) / D + EPSILON)
        inverse[u] = scale
        hidden = scale * jnp.dot(up_half[...], scaled[:, span(u)], preferred_element_type=FULL)
        sigmoid = jax.nn.sigmoid(hidden)
        value = (grad_active * sigmoid * (1.0 + hidden * (1.0 - sigmoid))).astype(LOW)
        grad_hidden[:half, span(u)] = value
        exchange("grad_hidden", u, grad_hidden)
        active[:half, span(u)] = (hidden * sigmoid).astype(LOW)
        exchange("active", u, active)
        inner_send[u] = jnp.sum(value.astype(FULL) * hidden, axis=0, keepdims=True)
        copies["inner", u] = send(inner_send.at[u], inner_recv.at[u], sibling_id)
        normed[:, span(u)] = (middle[:, span(u)] * scale * gain).astype(LOW)

    def second_branch(u):
        copies["grad_hidden", u].wait_recv()
        copies["inner", u].wait_recv()
        scale = inverse[u]
        inner = scale * scale * ((inner_send[u] + inner_recv[u]) / D)
        back = jnp.dot(up_t[...], grad_hidden[:, span(u)], preferred_element_type=FULL)
        value = (
            cot[:width, span(u)].astype(FULL)
            + scale * (back * gain)
            - middle[:, span(u)] * inner
        )
        branch[:width, span(u)] = value.astype(LOW)
        exchange("branch", u, branch)
        grad[:, span(u)] = value
        stored.append(move(grad.at[:, columns(u)], middle_hbm.at[:, columns(u)]))
        product = back * middle[:, span(u)] * scale
        total = narrow[...]
        for v in range(piece // 128):
            total = total + product[:, v * 128:(v + 1) * 128]
        narrow[...] = total
        copies["active", u].wait_recv()
        result[:, span(u)] = middle[:, span(u)] + jnp.dot(
            down_t[...], active[:, span(u)], preferred_element_type=FULL
        )
        stored.append(move(result.at[:, columns(u)], result_hbm.at[:, columns(u)]))

    def heads_back(u):
        copies["branch", u].wait_recv()
        grad_att[:, span(u)] = jnp.dot(
            out_half[...], branch[:, span(u)], preferred_element_type=FULL
        ).astype(LOW)
        target = pl.ds(pl.multiple_of(j * here + u * piece, 128), piece)
        for m in range(n_pair):
            source = grad_att.at[
                pl.ds(pl.multiple_of((j ^ m) * cols, 16), cols), columns(u)
            ]
            if m:
                copies["out", u, m] = send(source, out_hbm.at[:, target], pair_ids[m - 1])
            else:
                stored.append(move(source, out_hbm.at[:, target]))

    stages = (share_heads, first_branch, hidden_units, second_branch, heads_back)
    turned = {}

    def product(name, first, left, right, target, at):
        if name not in turned:
            turned[name] = right[:width].T
        count = n_col // 2
        for n in range(0 if first else count, count if first else n_col):
            target[n, at:at + unit] = jnp.dot(
                left[n * unit:(n + 1) * unit], turned[name], preferred_element_type=FULL
            ).astype(LOW)

    if grads.shape[1] > 2 * unit:
        grads[...] = jnp.zeros_like(grads)
    if down_grads.shape[1] > unit:
        down_grads[...] = jnp.zeros_like(down_grads)
    for t in range(pieces + len(stages) - 1):
        for number in reversed(range(len(stages))):
            if 0 <= t - number < pieces:
                stages[number](t - number)
            if number == 4 and t == pieces + 2:
                product("down", True, active, cot, down_grads, 0)
        if t == pieces + 2:
            product("up", True, grad_hidden, normed, grads, unit)

    product("down", False, active, cot, down_grads, 0)
    for m in range(n_col):
        stored.append(move(down_grads.at[c_first ^ m], down_outs[m]))
    product("up", False, grad_hidden, normed, grads, unit)
    for first in (True, False):
        product("out", first, att, branch, grads, 0)
    for m in range(n_dp):
        at = pl.ds(pl.multiple_of((d ^ m) * rows_g, 16), rows_g)
        stored.append(move(grads.at[:, at], grads_hbms[m]))
    gain_out[...] = jnp.sum(narrow[...].T, axis=0, keepdims=True)

    for u in range(pieces):
        for m in range(1, n_pair):
            copies["out", u, m].wait_recv()
    for copy in stored:
        copy.wait()
    for copy in sent:
        copy.wait_send()


def middle_part(n_dp, n_pair, gain, attended, tokens, cotangent, cot_other, out_all, ups, downs):
    width, here = tokens.shape
    n_col = 2 * n_pair
    cols, length = attended.shape
    unit = downs[0].shape[0]
    half = n_col * unit // 2
    rows_q = ups[0].shape[1]
    rows_g = quarter_rows(2 * unit, n_dp)
    pieces = max(2, here // 256)
    piece = here // pieces
    count = 2 * pieces * (n_pair - 1) + 7 * pieces + 8
    moves = 4 * n_dp + 2 * n_col + 4 * pieces + 4
    hbm = pl.BlockSpec(memory_space=pl.ANY)
    vmem = pl.BlockSpec(memory_space=pltpu.VMEM)
    V = pltpu.VMEM
    S = jax.ShapeDtypeStruct
    weight = V((2 * half, width), LOW)
    weight_t = V((width, 2 * half), LOW)
    both = V((2 * width, here), LOW)
    whole = V((width, here), FULL)
    row = V((pieces, 1, piece), FULL)
    out = pl.pallas_call(
        functools.partial(middle_kernel, n_dp, n_pair, unit),
        out_shape=(
            S((width, here), FULL),
            S((width, here), FULL),
            S((cols, length), LOW),
        )
        + (S((n_col, rows_g, width), LOW),) * n_dp
        + (S((n_dp * quarter_rows(unit, n_dp), width), LOW),) * n_col
        + (S((1, width), FULL),),
        in_specs=[vmem] + [hbm] * (3 + n_dp + n_col),
        out_specs=(hbm,) * (3 + n_dp + n_col) + (vmem,),
        scratch_shapes=[
            V((width, here), LOW),
            both,
            V((n_col, n_dp * rows_q, width), LOW),
            V((n_col, n_dp * rows_q, width), LOW),
            V((2, n_dp * rows_q, width), LOW),
            weight,
            weight,
            weight,
            weight_t,
            weight_t,
            weight_t,
            V((half, 2 * width), LOW),
            V((half, 2 * width), LOW),
            V((half, 2 * width), LOW),
            both,
            both,
            V((width, here), LOW),
            V((2 * half, here), LOW),
            V((2 * half, here), LOW),
            both,
            whole,
            whole,
            whole,
            V((width, here), LOW),
            V((n_col, n_dp * rows_g, width), LOW),
            V((n_col, n_dp * quarter_rows(unit, n_dp), width), LOW),
            row,
            row,
            row,
            row,
            row,
            V((width, 128), FULL),
            pltpu.SemaphoreType.DMA((count,)),
            pltpu.SemaphoreType.DMA((count,)),
            pltpu.SemaphoreType.DMA((moves,)),
        ],
        compiler_params=pltpu.CompilerParams(
            collective_id=3, has_side_effects=True, vmem_limit_bytes=62 * 2**20
        ),
        cost_estimate=pl.CostEstimate(
            flops=18 * 2 * half * width * here, bytes_accessed=2**25, transcendentals=0
        ),
    )(gain, attended, tokens, cotangent, cot_other, out_all, *ups, *downs)
    return out[0], out[1], out[2], out[3:3 + n_dp], out[3 + n_dp:-1], out[-1]


def quarter_rows(rows, n_dp):
    return -(-rows // (16 * n_dp)) * 16


def tail_kernel(
    n_dp, n_pair, gain_ref, inverse_ref, sums_ref, qkv_hbm, dq_hbm, dk_hbm, dv_hbm, normed_hbm,
    tokens_hbm, middle_hbm, *refs,
):
    n_col = 2 * n_pair
    grads_hbms, refs = refs[:n_dp], refs[n_dp:]
    down_hbms, refs = refs[:n_col], refs[n_col:]
    (
        result_hbm, qkv_out, grads_out, down_out, sums_out,
        qkv, dproj, normed, tokens, middle, result, row_send, row_recv, own, pair_send, pair_recv,
        dp_send, dp_recv, dp_own, cross_send, cross_recv, cs_send, cs_recv, final, grads_parts,
        grads_send, grads_recv, grads_final, down_parts, down_send, down_recv, down_final,
        far_own, far_recv, far_send, far_parts,
        inner_send, inner_recv, sums_send, sums_recv, last_sums, send_sems, recv_sems, local_sems,
    ) = refs
    r, s = lax.axis_index("row"), lax.axis_index("cs")
    j, d = lax.axis_index("cp"), lax.axis_index("dp")
    width, here = tokens.shape
    cols = dq_hbm.shape[0]
    quartered = (1, n_pair + 1)
    whole = [k for k in range(n_col) if k not in quartered]
    share = width // n_dp
    part = share // 2
    rows_d = down_final.shape[0]
    subs = row_send.shape[1]
    piece = here // subs
    c_first = (s * n_pair + j) ^ (r * n_pair)
    near = r == s
    sems = (send_sems, recv_sems)
    gain = column(half_row(gain_ref, r))
    counter, local_counter = iter(range(1000)), iter(range(1000))
    sent, stored = [], []

    def send(src, dst, device):
        copy = remote(src, dst, sems, next(counter), device)
        copy.start()
        sent.append(copy)
        return copy

    def move(src, dst):
        copy = pltpu.make_async_copy(src, dst, local_sems.at[next(local_counter)])
        copy.start()
        return copy

    def down_rows(owner):
        return pl.ds(pl.multiple_of(owner * rows_d, 16), rows_d)

    load_grads = [move(grads_hbms[k], grads_parts.at[k]) for k in range(n_dp)]
    early = [
        move(dq_hbm, dproj.at[pl.ds(0, cols)]),
        move(dk_hbm, dproj.at[pl.ds(cols, cols)]),
        move(dv_hbm, dproj.at[pl.ds(2 * cols, cols)]),
        move(normed_hbm, normed),
    ]
    load_qkv = move(qkv_hbm, qkv)
    load_down = [move(down_hbms[k], down_parts.at[m]) for m, k in enumerate(whole)]
    load_far = [
        move(down_hbms[k].at[down_rows(d)], far_own.at[m]) for m, k in enumerate(quartered)
    ]
    late = [move(tokens_hbm, tokens), move(middle_hbm, middle)]

    sibling_id = {"row": 1 - r}
    cs_id = {"cs": 1 - s}
    dp_ids = [{"dp": d ^ k} for k in range(1, n_dp)]
    col_ids = [{"cs": s ^ (k // n_pair), "cp": j ^ (k % n_pair)} for k in range(1, n_col)]
    greet([sibling_id] + dp_ids + col_ids)


    for copy in load_grads:
        copy.wait()

    def summed(place_at):
        value = grads_parts[0, place_at].astype(FULL)
        for k in range(1, n_dp):
            value = value + grads_parts[k, place_at].astype(FULL)
        return value

    grads_copies = []
    for k in range(1, n_col):
        grads_send[k - 1] = summed(c_first ^ k).astype(LOW)
        grads_copies.append(send(grads_send.at[k - 1], grads_recv.at[k - 1], col_ids[k - 1]))
    far_copies = [
        send(down_hbms[k].at[down_rows(d ^ peer)], far_recv.at[peer - 1, m], dp_ids[peer - 1])
        for m, k in enumerate(quartered)
        for peer in range(1, n_dp)
    ]

    def quarter(half, owner):
        at = pl.ds(pl.multiple_of(half * width + owner * share, 32), share)
        return mm(normed[at, :], dproj[...], 1, 1)

    def rows_of(half, chunk, u):
        at = pl.ds(pl.multiple_of(chunk * here + u * piece, 128), piece)
        return jnp.dot(
            qkv[half * width:(half + 1) * width, :], dproj[:, at], preferred_element_type=FULL
        )

    dp_copies = {}

    def send_part(k, p):
        rows = pl.ds(p * part, part)
        dp_copies[k, p] = send(
            dp_send.at[k - 1, :, rows], dp_recv.at[k - 1, :, rows], dp_ids[k - 1]
        )

    def quarters(k):
        for half in range(2):
            dp_send[k - 1, half] = quarter(half, d ^ k).astype(LOW)
        send_part(k, 0)

    row_copies, pair_copies = {}, []
    for copy in early:
        copy.wait()
    for k in reversed(range(1, n_dp)):
        quarters(k)
    for k in reversed(range(1, n_dp)):
        send_part(k, 1)
    for copy in load_far:
        copy.wait()
    for copy in far_copies:
        copy.wait_recv()
    far_z = []
    for m, k in enumerate(quartered):
        value = far_own[m].astype(FULL)
        for peer in range(1, n_dp):
            value = value + far_recv[peer - 1, m].astype(FULL)
        far_send[m] = value.astype(LOW)
        far_z.append(send(far_send.at[m], far_parts.at[m], col_ids[k - 1]))
    load_qkv.wait()
    for k in range(1, n_pair):
        for u in range(subs):
            row_send[k, u] = rows_of(1, j ^ k, u).astype(LOW)
            row_copies[k, u] = send(row_send.at[k, u], row_recv.at[k, u], sibling_id)
    for k in range(1, n_pair):
        for u in range(subs):
            value = rows_of(0, j ^ k, u)
            row_copies[k, u].wait_recv()
            pair_send[k - 1, u] = (value + row_recv[k, u].astype(FULL)).astype(LOW)
            pair_copies.append(
                send(pair_send.at[k - 1, u], pair_recv.at[k - 1, u], {"cp": j ^ k})
            )
    for copy in load_down:
        copy.wait()
    value = down_parts[0].astype(FULL)
    for m in range(1, n_col - 2):
        value = value + down_parts[m].astype(FULL)
    down_send[...] = value.astype(LOW)

    down_copies = [
        send(down_send.at[down_rows(d ^ k)], down_recv.at[k - 1], dp_ids[k - 1])
        for k in range(1, n_dp)
    ]
    for half in range(2):
        dp_own[half] = quarter(half, d)

    for u in range(subs):
        row_send[0, u] = rows_of(1, j, u).astype(LOW)
        row_copies[0, u] = send(row_send.at[0, u], row_recv.at[0, u], sibling_id)
    for u in range(subs):
        own[u] = rows_of(0, j, u)

    cs_copies = []

    def reduce_part(p):
        rows = slice(p * part, (p + 1) * part)
        for k in range(1, n_dp):
            dp_copies[k, p].wait_recv()

        def total(half):
            value = dp_own[half, rows]
            for k in range(1, n_dp):
                value = value + dp_recv[k - 1, half, rows].astype(FULL)
            return value

        cross_send[p] = total(1).astype(LOW)
        cross_copy = send(cross_send.at[p], cross_recv.at[p], sibling_id)
        kept = total(0)
        cross_copy.wait_recv()
        crossed = cross_recv[p].astype(FULL)
        cs_send[p] = jnp.where(near, crossed, kept).astype(LOW)
        cs_copies.append(send(cs_send.at[p], cs_recv.at[p], cs_id))
        dp_own[0, rows] = jnp.where(near, kept, crossed)

    reduce_part(0)

    reduce_part(1)

    value = down_send[down_rows(d)].astype(FULL)
    for k in range(1, n_dp):
        down_copies[k - 1].wait_recv()
        value = value + down_recv[k - 1].astype(FULL)
    for m in range(2):
        far_z[m].wait_recv()
        value = value + far_parts[m].astype(FULL)
    down_final[...] = value.astype(LOW)
    out_copies = [send(down_final, down_out.at[d], peer) for peer in dp_ids]
    stored.append(move(down_final, down_out.at[d]))

    value = summed(c_first)
    for k in range(1, n_col):
        grads_copies[k - 1].wait_recv()
        value = value + grads_recv[k - 1].astype(FULL)
    grads_final[...] = value.astype(LOW)
    out_copies += [send(grads_final, grads_out.at[d], peer) for peer in dp_ids]
    stored.append(move(grads_final, grads_out.at[d]))

    def finish_part(p):
        cs_copies[p].wait_recv()
        rows = slice(p * part, (p + 1) * part)
        final[p] = (dp_own[0, rows] + cs_recv[p].astype(FULL)).astype(LOW)
        target = qkv_out.at[d, pl.ds(p * part, part)]
        out_copies.extend([send(final.at[p], target, peer) for peer in dp_ids])
        stored.append(move(final.at[p], target))

    finish_part(0)

    for copy in late:
        copy.wait()
    for copy in pair_copies:
        copy.wait_recv()
    inverse = inverse_ref[...]
    for u in range(subs):
        row_copies[0, u].wait_recv()
        at = slice(u * piece, (u + 1) * piece)
        value = own[u] + row_recv[0, u].astype(FULL)
        for k in range(1, n_pair):
            value = value + pair_recv[k - 1, u].astype(FULL)
        own[u] = value
        inner_send[:, at] = jnp.sum(
            value * gain * tokens[:, at].astype(FULL), axis=0, keepdims=True
        )
    inner_copy = send(inner_send, inner_recv, sibling_id)

    narrow = jnp.zeros((width, 128), FULL)
    for u in range(subs):
        at = slice(u * piece, (u + 1) * piece)
        wide = own[u] * tokens[:, at].astype(FULL) * inverse[:, at]
        for v in range(piece // 128):
            narrow = narrow + wide[:, v * 128:(v + 1) * 128]
    gain_part = jnp.sum(narrow.T, axis=0, keepdims=True)
    sums_send[0] = jnp.concatenate([gain_part, sums_ref[1:]], 0)
    sums_copies = {}

    def send_sums(step, peers):
        for k, peer in enumerate(peers):
            sums_copies[step, k] = send(sums_send.at[step], sums_recv.at[step, k], peer)

    def add_sums(step, members):
        value = sums_send[step]
        for k in range(members - 1):
            sums_copies[step, k].wait_recv()
            value = value + sums_recv[step, k]
        sums_send[step + 1] = value

    send_sums(0, dp_ids)
    inner_copy.wait_recv()
    inner = (inner_send[...] + inner_recv[...]) / D
    for u in range(subs):
        at = slice(u * piece, (u + 1) * piece)
        result[:, at] = (
            middle[:, at]
            + inverse[:, at] * (own[u] * gain)
            - tokens[:, at].astype(FULL)
            * (inverse[:, at] * inverse[:, at] * inverse[:, at] * inner[:, at])
        )
    stored.append(move(result, result_hbm))
    add_sums(0, n_dp)
    send_sums(1, col_ids)
    finish_part(1)

    add_sums(1, n_col)
    sums_copy = send(sums_send.at[2], last_sums, sibling_id)
    sums_copy.wait_recv()
    sums_out[0] = sums_send[2]
    sums_out[1] = last_sums[...]
    for copy in out_copies:
        copy.wait_recv()
    for copy in stored:
        copy.wait()
    for copy in sent:
        copy.wait_send()


def tail(n_dp, n_pair, gain, inverse, sums, qkv, dq, dk, dv, normed, tokens, middle, grads, downs):
    width, here = tokens.shape
    length = normed.shape[1]
    cols = dq.shape[0]
    unit = downs[0].shape[0]
    rows_d = unit // n_dp
    share = width // n_dp
    subs = 2
    piece = here // subs
    n_col = 2 * n_pair
    part = grads[0].shape[1:]
    wide = 3 * cols
    count = 2 * n_pair * subs + 10 * n_dp + 2 * n_col + 14
    moves = 15 + n_dp + n_col
    hbm = pl.BlockSpec(memory_space=pl.ANY)
    vmem = pl.BlockSpec(memory_space=pltpu.VMEM)
    V = pltpu.VMEM
    halves = V((2, share // 2, wide), LOW)
    return pl.pallas_call(
        functools.partial(tail_kernel, n_dp, n_pair),
        out_shape=(
            jax.ShapeDtypeStruct((width, here), FULL),
            jax.ShapeDtypeStruct((n_dp, share, wide), LOW),
            jax.ShapeDtypeStruct((n_dp,) + part, LOW),
            jax.ShapeDtypeStruct((n_dp, rows_d, width), LOW),
            jax.ShapeDtypeStruct((2,) + sums.shape, FULL),
        ),
        in_specs=[vmem] * 3 + [hbm] * (7 + n_dp + n_col),
        out_specs=(hbm,) * 4 + (vmem,),
        scratch_shapes=[
            V((2 * width, wide), LOW),
            V((wide, length), LOW),
            V((2 * width, length), LOW),
            V((width, here), LOW),
            V((width, here), FULL),
            V((width, here), FULL),
            V((n_pair, subs, width, piece), LOW),
            V((n_pair, subs, width, piece), LOW),
            V((subs, width, piece), FULL),
            V((n_pair - 1, subs, width, piece), LOW),
            V((n_pair - 1, subs, width, piece), LOW),
            V((n_dp - 1, 2, share, wide), LOW),
            V((n_dp - 1, 2, share, wide), LOW),
            V((2, share, wide), FULL),
            halves,
            halves,
            halves,
            halves,
            halves,
            V((n_dp, n_col) + part, LOW),
            V((n_col - 1,) + part, LOW),
            V((n_col - 1,) + part, LOW),
            V(part, LOW),
            V((n_col - 2, unit, width), LOW),
            V((n_dp * rows_d, width), LOW),
            V((n_dp - 1, rows_d, width), LOW),
            V((rows_d, width), LOW),
            V((2, rows_d, width), LOW),
            V((n_dp - 1, 2, rows_d, width), LOW),
            V((2, rows_d, width), LOW),
            V((2, rows_d, width), LOW),
            V((1, here), FULL),
            V((1, here), FULL),
            V((3,) + sums.shape, FULL),
            V((2, max(n_dp, n_col) - 1) + sums.shape, FULL),
            V(sums.shape, FULL),
            pltpu.SemaphoreType.DMA((count,)),
            pltpu.SemaphoreType.DMA((count,)),
            pltpu.SemaphoreType.DMA((moves,)),
        ],
        compiler_params=pltpu.CompilerParams(
            collective_id=1, has_side_effects=True, vmem_limit_bytes=62 * 2**20
        ),
        cost_estimate=pl.CostEstimate(
            flops=8 * wide * width * length, bytes_accessed=2**25, transcendentals=0
        ),
    )(gain, inverse, sums, qkv, dq, dk, dv, normed, tokens, middle, *grads, *downs)


def on_device(
    tokens,
    segment_ids,
    padding_mask,
    w_qkv,
    w_out,
    w_up,
    w_down,
    gain_attn,
    gain_mlp,
    scale_raw,
    cotangent,
):
    width, here = tokens.shape
    r, s = lax.axis_index("row"), lax.axis_index("cs")
    j, d = lax.axis_index("cp"), lax.axis_index("dp")
    n_pair, n_dp, n_col = lax.axis_size("cp"), lax.axis_size("dp"), lax.axis_size(COLS)
    c = s * n_pair + j
    head_cols = w_qkv.shape[0] // (3 * width)
    heads = head_cols // HEAD
    near = r == s

    ids = jnp.concatenate([segment_ids, padding_mask], 0)
    ids = jnp.where(s == r, ids, sibling(ids))
    segments, padding = ids[0], ids[1]
    length = segments.shape[0]
    firsts = segments[::BLOCK]
    starts = jnp.sum((segments[None, :] < firsts[:, None]).astype(jnp.int32), axis=1)
    filled = (jnp.sum(padding) + BLOCK - 1) // BLOCK
    blocks = jnp.arange(length // BLOCK, dtype=jnp.int32)
    lo = starts // BLOCK
    hi = jnp.minimum(blocks, filled)
    gain_one, gain_two = gain_attn[None, :], gain_mlp[None, :]
    scale_row = scale_raw[None, :]

    block = w_qkv.reshape(width, 3 * head_cols)
    down = w_down.reshape(-1, width)
    unit = down.shape[0]
    part_rows = quarter_rows(unit, n_dp)

    def quarters(matrix):
        padded = jnp.pad(matrix, ((0, n_dp * part_rows - unit), (0, 0)))
        return padded.reshape(n_dp, part_rows, width)

    out = lax.dynamic_index_in_dim(quarters(w_out.reshape(-1, width)), d, 0, keepdims=False)
    up = lax.dynamic_index_in_dim(quarters(w_up.reshape(width, -1).T), d, 0, keepdims=False)
    (
        queries, key_heads, values, query_raw, normed_one, qkv, out_all, ups, cot_other,
        inverse_one,
    ) = head(
        n_dp, n_pair, gain_one, scale_row, tokens, cotangent, block, out, up,
        quarters(down),
    )
    ups = gather(ups, "dp")
    downs = [down] + [
        lax.ppermute(down, COLS, [(i, i ^ k) for i in range(n_col)])
        for k in range(2, n_col)
        if k != n_pair + 1
    ]
    attended, logs = attention_forward(queries, key_heads, values, ids, ids, lo, hi)
    result, grad_middle, grad_attended, grads, down_grads, gain_two_part = middle_part(
        n_dp, n_pair, gain_two, attended, tokens, cotangent, cot_other, out_all, ups, downs
    )
    received = [grads[0]] + [shift(grads[k], "dp", k) for k in range(1, n_dp)]
    down_received = [
        down_grads[k]
        if k in (0, 1, n_pair + 1)
        else lax.ppermute(down_grads[k], COLS, [(i, i ^ k) for i in range(n_col)])
        for k in range(n_col)
    ]

    dq, dk, dv, sums = attention_backward(
        queries, key_heads, values, attended, grad_attended, logs, query_raw, scale_row, gain_two_part,
        ids, ids, lo, hi,
    )
    grad_tokens, grad_qkv, final, final_down, sums = tail(
        n_dp, n_pair, gain_one, inverse_one, sums, qkv, dq, dk, dv, normed_one, tokens,
        grad_middle, received, down_received,
    )
    grad_qkv = grad_qkv.astype(FULL)
    final = final.reshape(-1, width)
    final = [final[i * unit:(i + 1) * unit].astype(FULL) for i in range(2)]
    final.append(final_down.reshape(-1, width)[:unit].astype(FULL))
    own, other = sums[0], sums[1]
    first = r == 0
    gains = jnp.concatenate(
        [jnp.where(first, own[:2], other[:2]), jnp.where(first, other[:2], own[:2])], 1
    )
    scale_total = (own[2] + other[2])[:HEAD]
    return (
        result,
        grad_tokens,
        grad_qkv.reshape(-1),
        final[0].reshape(-1),
        final[1].T.reshape(-1),
        final[2].reshape(-1),
        gains[0],
        gains[1],
        scale_total,
    )


def solution(mesh):
    n_dp, n_row, n_col = (mesh.shape[name] for name in ("dp", "row", "col"))
    split = Mesh(
        np.asarray(mesh.devices).reshape(n_dp, n_row, n_row, n_col // n_row),
        ("dp", "row", "cs", "cp"),
    )
    rows = P("row", ("dp", "cs", "cp"))
    ids = P(("dp", "row"), None)
    blocks = P(("row", "cs", "cp"))
    return jax.shard_map(
        on_device,
        mesh=split,
        in_specs=(rows, ids, ids, blocks, blocks, blocks, blocks, P(), P(), P(), rows),
        out_specs=(rows, rows, blocks, blocks, blocks, blocks, P(), P(), P()),
        check_vma=False,
    )
```
